32 devices in a mesh: stick: 8 (over z, y), band: 4 (over x, core).
Axes of the slice: x: 2, y: 2, z: 4, core: 2. Of those that a mesh axis runs over, the one named last changes fastest.
Arguments:
- sticks: float32 [32, 96, 1024], P('band', None, 'stick'), may hold values from -0.078125 to 0.078125
- stick_columns: int32 [1024], P('stick'), may hold values from -1 to 2303, as said below
Outputs:
- exchange_sticks: float32 [32, 96, 1024], P('band', None, 'stick')
The draws below stay inside these ranges and needn't reach their ends.
Inputs may be any that keep to these rules, and one draw needn't show every extreme that they name: `stick_columns`: each entry is -1 (an empty slot) or a grid column kx * 48 + ky, and no column appears twice. On each index of the stick axis its 128 slots hold the live sticks first and the empty ones after; one index holds 128 live sticks, another 128 / 4, the others from 32 to 128.
All inputs are finite; a program needn't handle non-finite values.
Results may differ from the reference program's by a relative error of at most 0.0003.
Values sent between devices are 32-bit elements; how exact they have to be, the bound alone decides.
No kernel may reach another device: no remote copies, remote signals or barrier semaphores. Data moves between devices by JAX's collectives and lax.ppermute only.
A program may use at most 64 MiB of HBM per device.

```python
import math
import jax
import jax.numpy as jnp
from jax import lax

G = 48
CAP = 128
HALF = 2
GROUPS = 4
GROUP_SIZE = 8
NBANDS = 32
STICKS = 1024


def draw_stick_columns(key, part):
    owner_count = STICKS // CAP
    key_order, key_count, key_full, key_light = jax.random.split(key, 4)
    column_order = jax.random.permutation(key_order, G * G).astype(jnp.int32)
    full_owner = jax.random.randint(key_full, (), 0, owner_count)
    light_owner = (full_owner + 1 + jax.random.randint(key_light, (), 0, owner_count - 1)) % owner_count
    last_column = G * G - 1
    last_place = jnp.argmax(column_order == last_column)
    target_slot = full_owner * CAP
    column_order = column_order.at[last_place].set(column_order[target_slot]).at[target_slot].set(last_column)
    owner_index = jnp.arange(owner_count)
    counts = jax.random.randint(key_count, (owner_count,), CAP // 4, CAP + 1)
    counts = jnp.where(owner_index == light_owner, CAP // 4, counts)
    counts = jnp.where(owner_index == full_owner, CAP, counts)
    slot_index = jnp.arange(STICKS)
    occupied = slot_index % CAP < counts[slot_index // CAP]
    return jnp.where(occupied, column_order[:STICKS], -1).astype(jnp.int32)


def block_scale(own_key, shape, cuts, least, largest):
    level = 1.0
    for dim, blocks in cuts:
        steps = jax.random.uniform(jax.random.fold_in(jax.random.fold_in(own_key, 6), dim), (blocks,), jnp.float32, least / len(cuts), largest / len(cuts))
        level = level * jnp.repeat(jnp.exp(steps), shape[dim] // blocks).reshape((-1,) + (1,) * (len(shape) - 1 - dim))
    return level


def centred(own_key, dims, spread, most, shards=(), kind=jnp.bfloat16):
    gain = block_scale(own_key, dims, shards, -0.22, 0.18) if shards else 1.0
    array = jax.random.normal(own_key, dims, jnp.float32) * spread * gain
    return jnp.minimum(jnp.maximum(array, -most), most).astype(kind)


def setup_inputs(seed: int = 0) -> dict:
    splits = jax.random.split(jax.random.key(seed), 3)
    sticks = centred(splits[0], (NBANDS, 2 * G, STICKS), ((1.6 / (STICKS * G)) ** 0.5), 0.078125, ((0, 4), (2, 8)), jnp.float32)
    stick_columns = draw_stick_columns(jax.random.fold_in(splits[2], 71), 0)
    return {"sticks": sticks, "stick_columns": stick_columns}


BOX_LENGTH = 18.0


def coulomb_kernel():
    half_count = G // 2 + 1
    frequency = jnp.arange(G, dtype=jnp.int32)
    folded = jnp.minimum(frequency, G - frequency)
    squares = folded * folded
    squared_sum = squares[:half_count, None, None] + squares[None, :, None] + squares[None, None, :]
    unit_square = (2.0 * math.pi / BOX_LENGTH) ** 2
    bounded = jnp.maximum(squared_sum, 1).astype(jnp.float32)
    return jnp.where(squared_sum > 0, 4.0 * math.pi / (unit_square * bounded), 0.0).astype(jnp.float32)


def orbital_field(band_rows, slot_rows):
    values = band_rows[:, :G] + 1j * band_rows[:, G:]
    grid = jnp.zeros((G * G + 1, G), values.dtype).at[slot_rows].set(values)[: G * G]
    return jnp.real(jnp.fft.ifftn(grid.reshape(G, G, G))) * float(G ** 3)


def potential(density, kernel):
    spectrum = jnp.fft.rfftn(density, axes=(2, 1, 0))
    return jnp.fft.irfftn(kernel * spectrum, s=(G, G, G), axes=(2, 1, 0))


def reference(sticks, stick_columns):
    slot_rows = jnp.where(stick_columns >= 0, stick_columns, G * G).astype(jnp.int32)
    kernel = coulomb_kernel()
    fields = lax.map(lambda band_rows: orbital_field(jnp.transpose(band_rows), slot_rows), sticks)
    fields = fields.reshape(GROUPS, GROUP_SIZE, G, G, G)

    def exchange_band(band_index):
        group_index = band_index // GROUP_SIZE
        member = band_index % GROUP_SIZE
        own_field = fields[group_index, member]
        exchange_sum = jnp.zeros((G, G, G), own_field.dtype)
        for offset in range(-HALF, HALF + 1):
            source = fields[(group_index + offset) % GROUPS, member]
            exchange_sum = exchange_sum + potential(own_field * source, kernel) * source
        spectrum = jnp.fft.fftn(exchange_sum) * (G ** -1.5)
        padded = jnp.concatenate([spectrum.reshape(G * G, G), jnp.zeros((1, G), spectrum.dtype)], axis=0)
        picked = padded[slot_rows]
        return jnp.transpose(jnp.concatenate([jnp.real(picked), jnp.imag(picked)], axis=1))

    return lax.map(exchange_band, jnp.arange(NBANDS, dtype=jnp.int32))
```

```python
import functools
import math

import jax
import jax.numpy as jnp
import numpy as np
from jax import lax
from jax.experimental import pallas as pl
from jax.experimental.pallas import tpu as pltpu
from jax.sharding import PartitionSpec as P

HALF = 2
BOX_LENGTH = 18.0
LANES = 128
MID = 64
CHUNK = 8

F32 = jnp.float32
BF16 = jnp.bfloat16


def rounded_parts(table):
    high = table.astype(BF16)
    low = (table - high.astype(np.float64)).astype(BF16)
    return high, low


def trig(g):
    angle = 2.0 * np.pi / g * (np.outer(np.arange(g), np.arange(g)) % g)
    return np.cos(angle), np.sin(angle)


def stacked_left(table):
    high, low = rounded_parts(table)
    return np.concatenate(
        [np.concatenate([high, high], 1), np.concatenate([low, np.zeros_like(low)], 1)], 0
    )


def stacked_right(table):
    high, low = rounded_parts(table)
    return np.concatenate(
        [np.concatenate([high, low], 1), np.concatenate([high, np.zeros_like(low)], 1)], 0
    )


def make_tables(g):
    c, s = trig(g)
    forward = stacked_left(np.concatenate([c, -s], 1))
    backward = stacked_left(np.concatenate([c, s], 1))

    def lane_table(sign, scale):
        out = np.zeros((LANES, LANES))
        out[:g, :g] = c
        out[:g, MID : MID + g] = sign * s
        out[MID : MID + g, :g] = -sign * s
        out[MID : MID + g, MID : MID + g] = c
        return out * scale

    z_forward = stacked_right(lane_table(-1.0, 1.0))
    z_backward = stacked_right(lane_table(1.0, 1.0 / g**3))
    spread = np.zeros((LANES, 2 * g))
    spread[:g, :g] = c
    spread[:g, g:] = -s
    spread[MID : MID + g, :g] = s
    spread[MID : MID + g, g:] = c
    stick_in = stacked_left(spread)
    pick = np.zeros((2 * g, LANES))
    pick[:g, :g] = c
    pick[:g, MID : MID + g] = s
    pick[g:, :g] = -s
    pick[g:, MID : MID + g] = c
    stick_out = stacked_left(pick * g**-1.5)
    freq = np.arange(g)
    square = np.minimum(freq, g - freq) ** 2
    total = square[:, None, None] + square[None, :, None] + square[None, None, :]
    unit = (2.0 * math.pi / BOX_LENGTH) ** 2
    kernel = np.where(total > 0, 4.0 * math.pi / (unit * np.maximum(total, 1)), 0.0)
    coulomb = np.zeros((g, g, LANES), np.float32)
    coulomb[:, :, :g] = kernel
    coulomb[:, :, MID : MID + g] = kernel
    return dict(
        forward=forward,
        backward=backward,
        z_forward=z_forward,
        z_backward=z_backward,
        stick_in=stick_in,
        stick_out=stick_out,
        coulomb=coulomb,
    )


def split(x):
    high = x.astype(BF16)
    low = (x - high.astype(F32)).astype(BF16)
    return high, low


def dot(a, b):
    return jnp.dot(a, b, preferred_element_type=F32)


def lower_lanes(shape):
    return lax.broadcasted_iota(jnp.int32, shape, len(shape) - 1) % LANES < MID


def turned(x):
    rolled = pltpu.roll(x, MID, 1)
    return jnp.where(lower_lanes(x.shape), -rolled, rolled)


def left_pair(table, first, second):
    u = jnp.concatenate([first[0], second[0]], 1)
    v = jnp.concatenate([first[1], second[1]], 1)
    u_high, u_low = split(u)
    v_high, v_low = split(v)
    data = jnp.concatenate([u_high, v_high, u_low, v_low], 0)
    both = dot(table, data)
    g = both.shape[0] // 2
    out = both[:g] + both[g:]
    return out[:, :LANES], out[:, LANES:]


def left_all(table, slabs, expand):
    results = []
    for k in range(0, len(slabs), 2):
        results += left_pair(table, expand(slabs[k]), expand(slabs[k + 1]))
    return results


def complex_slab(x):
    return x, turned(x)


def right(x, table):
    high, low = split(x)
    both = dot(jnp.concatenate([high, low], 1), table)
    return both[:, :LANES] + both[:, LANES:]


def chunks(g, body):
    @pl.loop(0, g // CHUNK)
    def _(step):
        body(step * CHUNK)


def strided_slabs(ref, first, g):
    return [ref[pl.ds(first + k, g, stride=g), :] for k in range(CHUNK)]


def slabs_at(ref, first, g):
    rows = pl.ds(pl.multiple_of(first * g, CHUNK * g), CHUNK * g)
    block = ref[rows, :]
    return [block[k * g : (k + 1) * g] for k in range(CHUNK)]


def store_slabs(ref, first, g, slabs):
    rows = pl.ds(pl.multiple_of(first * g, CHUNK * g), CHUNK * g)
    ref[rows, :] = jnp.concatenate(slabs, 0)


def one_hot(columns, first, rows):
    index = lax.broadcasted_iota(jnp.int32, (rows, columns.shape[1]), 0)
    return jnp.where(index == columns - first, 1.0, 0.0).astype(BF16)


def all_columns(received_ref, row):
    count = received_ref.shape[0]
    rows = [received_ref[k, row : row + 1, :] for k in range(count)]
    return jnp.concatenate(rows, 1).astype(jnp.int32)


def field_kernel(g, received_ref, stick_in_ref, backward_ref, phi_ref, packed_ref, work_a, work_b):
    count = received_ref.shape[0]
    columns = all_columns(received_ref, 2 * g)
    stick_in = stick_in_ref[...]
    backward = backward_ref[...]
    pieces = []
    for k in range(0, count, 2):
        block = jnp.concatenate([received_ref[k, : 2 * g, :], received_ref[k + 1, : 2 * g, :]], 1)
        both = dot(stick_in, jnp.concatenate(split(block), 0))
        lined = both[:LANES] + both[LANES:]
        pieces.append(jnp.concatenate(split(lined.T), 1))
    sticks = jnp.concatenate(pieces, 0)

    def scatter(first):
        rows = CHUNK * g
        hot = one_hot(columns, first * g, rows)
        both = dot(hot, sticks)
        placed = both[:, :LANES] + both[:, LANES:]
        slabs = [placed[k * g : (k + 1) * g] for k in range(CHUNK)]
        store_slabs(work_b, first, g, left_all(backward, slabs, complex_slab))

    chunks(g, scatter)

    def real_slab(x):
        rolled = pltpu.roll(x, MID, 1)
        lower = lower_lanes(x.shape)
        return jnp.where(lower, x, rolled), -jnp.where(lower, rolled, x)

    def finish(first):
        slabs = strided_slabs(work_b, first, g)
        store_slabs(phi_ref, first, g, left_all(backward, slabs, real_slab))

    chunks(g, finish)
    half_rows = g * g // 2
    lower = phi_ref[:half_rows, :]
    packed_ref[...] = jnp.where(lower_lanes(lower.shape), lower, phi_ref[half_rows:, :])


def potentials(g, phi_ref, pair_ref, tables, work_a, work_b, emit):
    forward_ref, backward_ref, z_forward_ref, z_backward_ref, coulomb_ref = tables
    forward = forward_ref[...]
    backward = backward_ref[...]

    def first_steps(first):
        rows = pl.ds(pl.multiple_of(first * g, CHUNK * g), CHUNK * g)
        density = phi_ref[rows, :] * pair_ref[rows, :]
        spectrum = right(density, z_forward_ref[...])
        slabs = [spectrum[k * g : (k + 1) * g] for k in range(CHUNK)]
        store_slabs(work_a, first, g, left_all(forward, slabs, complex_slab))

    chunks(g, first_steps)

    def middle(first):
        slabs = left_all(forward, strided_slabs(work_a, first, g), complex_slab)
        slabs = [slab * coulomb_ref[first + k] for k, slab in enumerate(slabs)]
        store_slabs(work_b, first, g, left_all(backward, slabs, complex_slab))

    chunks(g, middle)

    def last_steps(first):
        slabs = left_all(backward, strided_slabs(work_b, first, g), complex_slab)
        emit(first, right(jnp.concatenate(slabs, 0), z_backward_ref[...]))

    chunks(g, last_steps)


def pair_fields(g, first_ref, second_ref, pair_ref):
    half_rows = g * g // 2
    first, second = first_ref[...], second_ref[...]
    lower = lower_lanes(first.shape)
    pair_ref[:half_rows, :] = jnp.where(lower, first, pltpu.roll(second, MID, 1))
    pair_ref[half_rows:, :] = jnp.where(lower, pltpu.roll(first, MID, 1), second)


def near_kernel(g, phi_ref, other_ref, forward_ref, backward_ref, z_forward_ref, z_backward_ref, coulomb_ref, sum_ref, pair_ref, work_a, work_b):
    half_rows = g * g // 2
    other = other_ref[...]
    own = phi_ref[...]
    lower = lower_lanes(other.shape)
    pair_ref[:half_rows, :] = jnp.where(lower, own[:half_rows], pltpu.roll(other, MID, 1))
    pair_ref[half_rows:, :] = jnp.where(lower, own[half_rows:], other)

    def emit(first, potential):
        rows = pl.ds(pl.multiple_of(first * g, CHUNK * g), CHUNK * g)
        sum_ref[rows, :] = potential * pair_ref[rows, :]

    tables = (forward_ref, backward_ref, z_forward_ref, z_backward_ref, coulomb_ref)
    potentials(g, phi_ref, pair_ref, tables, work_a, work_b, emit)


def middle_kernel(g, phi_ref, first_ref, second_ref, before_ref, forward_ref, backward_ref, z_forward_ref, z_backward_ref, coulomb_ref, sum_ref, pair_ref, work_a, work_b):
    pair_fields(g, first_ref, second_ref, pair_ref)

    def emit(first, potential):
        rows = pl.ds(pl.multiple_of(first * g, CHUNK * g), CHUNK * g)
        sum_ref[rows, :] = potential * pair_ref[rows, :] + before_ref[rows, :]

    tables = (forward_ref, backward_ref, z_forward_ref, z_backward_ref, coulomb_ref)
    potentials(g, phi_ref, pair_ref, tables, work_a, work_b, emit)


def far_kernel(g, weights, phi_ref, first_ref, second_ref, sum_ref, received_ref, forward_ref, backward_ref, z_forward_ref, z_backward_ref, stick_out_ref, coulomb_ref, out_ref, pair_ref, work_a, work_b, picked):
    pair_fields(g, first_ref, second_ref, pair_ref)
    forward = forward_ref[...]

    def emit(first, potential):
        rows = pl.ds(pl.multiple_of(first * g, CHUNK * g), CHUNK * g)
        lower = lower_lanes(potential.shape)
        weight = jnp.where(lower, weights[0], weights[1])
        total = potential * pair_ref[rows, :] * weight + sum_ref[rows, :]
        total = total + pltpu.roll(total, MID, 1)
        slabs = [total[k * g : (k + 1) * g] for k in range(CHUNK)]

        def expand(x):
            low = lower_lanes(x.shape)
            return jnp.where(low, x, 0.0), jnp.where(low, 0.0, x)

        store_slabs(work_a, first, g, left_all(forward, slabs, expand))

    tables = (forward_ref, backward_ref, z_forward_ref, z_backward_ref, coulomb_ref)
    potentials(g, phi_ref, pair_ref, tables, work_a, work_b, emit)

    columns = all_columns(received_ref, 2 * g)
    picked[...] = jnp.zeros_like(picked)

    def pick(first):
        slabs = left_all(forward, strided_slabs(work_a, first, g), complex_slab)
        rows = CHUNK * g
        parts = jnp.concatenate(split(jnp.concatenate(slabs, 0)), 1)
        hot = one_hot(columns, first * g, rows)
        both = lax.dot_general(parts, hot, (((0,), (0,)), ((), ())), preferred_element_type=F32)
        picked[...] += both[:LANES] + both[LANES:]

    chunks(g, pick)
    result = dot(stick_out_ref[...], jnp.concatenate(split(picked[...]), 0))
    result = result[: 2 * g] + result[2 * g :]
    for k in range(out_ref.shape[0]):
        out_ref[k] = result[:, k * LANES : (k + 1) * LANES]


def call(kernel, out_shapes, scratch, flops, *operands):
    vmem = pl.BlockSpec(memory_space=pltpu.VMEM)
    moved = sum(x.size * x.dtype.itemsize for x in operands)
    return pl.pallas_call(
        kernel,
        out_shape=out_shapes,
        in_specs=[vmem] * len(operands),
        out_specs=jax.tree.map(lambda _: vmem, out_shapes),
        scratch_shapes=scratch,
        compiler_params=pltpu.CompilerParams(vmem_limit_bytes=40 * 2**20),
        cost_estimate=pl.CostEstimate(flops=flops, bytes_accessed=moved, transcendentals=0),
    )(*operands)


def on_device(sticks, stick_columns):
    g = sticks.shape[1] // 2
    owners = lax.axis_size("stick")
    groups = lax.axis_size("band")
    t = {name: jnp.asarray(value) for name, value in make_tables(g).items()}
    rows = g * g
    field = jax.ShapeDtypeStruct((rows, LANES), F32)
    half_field = jax.ShapeDtypeStruct((rows // 2, LANES), F32)
    scratch = pltpu.VMEM((rows, LANES), F32)
    pot_flops = 6 * 2 * rows * 256 * 256

    column_rows = jnp.broadcast_to(stick_columns.astype(F32)[None, None, :], (owners, 8, stick_columns.shape[0]))
    payload = jnp.concatenate([sticks, column_rows], 1)
    received = lax.all_to_all(payload, "stick", split_axis=0, concat_axis=0, tiled=True)
    phi, packed = call(
        functools.partial(field_kernel, g),
        (field, half_field),
        [scratch, scratch],
        10**9,
        received,
        t["stick_in"],
        t["backward"],
    )
    pot_tables = [t["forward"], t["backward"], t["z_forward"], t["z_backward"]]
    swap = [(i, i ^ 1) for i in range(groups)]

    def fetched(distance):
        return lax.ppermute(packed, "band", [(i, (i - distance) % groups) for i in range(groups)])

    near = lax.ppermute(packed, "band", swap)
    ahead = fetched(HALF)
    total = call(
        functools.partial(near_kernel, g),
        field,
        [scratch] * 3,
        pot_flops,
        phi,
        near,
        *pot_tables,
        t["coulomb"],
    )
    if groups == 2 * HALF:
        weights = (2.0, 1.0)
        first, second = ahead, lax.ppermute(ahead, "band", swap)
    else:
        weights = (1.0, 0.0)
        behind = fetched(-HALF)
        odd = lax.axis_index("band") % 2 == 1
        first = second = lax.ppermute(jnp.where(odd, behind, ahead), "band", swap)
        total = call(
            functools.partial(middle_kernel, g),
            field,
            [scratch] * 3,
            pot_flops,
            phi,
            ahead,
            behind,
            total,
            *pot_tables,
            t["coulomb"],
        )
    result = call(
        functools.partial(far_kernel, g, weights),
        jax.ShapeDtypeStruct(sticks.shape, F32),
        [scratch] * 3 + [pltpu.VMEM((LANES, owners * stick_columns.shape[0]), F32)],
        pot_flops,
        phi,
        first,
        second,
        total,
        received,
        *pot_tables,
        t["stick_out"],
        t["coulomb"],
    )
    return lax.all_to_all(result, "stick", split_axis=0, concat_axis=0, tiled=True)


def solution(mesh):
    return jax.shard_map(
        on_device,
        mesh=mesh,
        in_specs=(P("band", None, "stick"), P("stick")),
        out_specs=P("band", None, "stick"),
        check_vma=False,
    )
```

```python
import functools
import math

import jax
import jax.numpy as jnp
import numpy as np
from jax import lax
from jax.experimental import pallas as pl
from jax.experimental.pallas import tpu as pltpu
from jax.sharding import PartitionSpec as P

HALF = 2
BOX_LENGTH = 18.0
LANES = 128
MID = 64
CHUNK = 8

F32 = jnp.float32
BF16 = jnp.bfloat16


def rounded_parts(table):
    high = table.astype(BF16)
    low = (table - high.astype(np.float64)).astype(BF16)
    return high, low


def trig(g):
    angle = 2.0 * np.pi / g * (np.outer(np.arange(g), np.arange(g)) % g)
    return np.cos(angle), np.sin(angle)


def stacked_left(table):
    high, low = rounded_parts(table)
    return np.concatenate(
        [np.concatenate([high, high], 1), np.concatenate([low, np.zeros_like(low)], 1)], 0
    )


def stacked_right(table):
    high, low = rounded_parts(table)
    return np.concatenate(
        [np.concatenate([high, low], 1), np.concatenate([high, np.zeros_like(low)], 1)], 0
    )


def make_tables(g):
    c, s = trig(g)
    forward = stacked_left(np.concatenate([c, -s], 1))
    backward = stacked_left(np.concatenate([c, s], 1))

    def lane_table(sign, scale):
        out = np.zeros((LANES, LANES))
        out[:g, :g] = c
        out[:g, MID : MID + g] = sign * s
        out[MID : MID + g, :g] = -sign * s
        out[MID : MID + g, MID : MID + g] = c
        return out * scale

    z_forward = stacked_right(lane_table(-1.0, 1.0))
    z_backward = stacked_right(lane_table(1.0, 1.0 / g**3))
    spread = np.zeros((LANES, 2 * g))
    spread[:g, :g] = c
    spread[:g, g:] = -s
    spread[MID : MID + g, :g] = s
    spread[MID : MID + g, g:] = c
    stick_in = stacked_left(spread)
    pick = np.zeros((2 * g, LANES))
    pick[:g, :g] = c
    pick[:g, MID : MID + g] = s
    pick[g:, :g] = -s
    pick[g:, MID : MID + g] = c
    stick_out = stacked_left(pick * g**-1.5)
    freq = np.arange(g)
    square = np.minimum(freq, g - freq) ** 2
    total = square[:, None, None] + square[None, :, None] + square[None, None, :]
    unit = (2.0 * math.pi / BOX_LENGTH) ** 2
    kernel = np.where(total > 0, 4.0 * math.pi / (unit * np.maximum(total, 1)), 0.0)
    coulomb = np.zeros((g, g, LANES), np.float32)
    coulomb[:, :, :g] = kernel
    coulomb[:, :, MID : MID + g] = kernel
    return dict(
        forward=forward,
        backward=backward,
        z_forward=z_forward,
        z_backward=z_backward,
        stick_in=stick_in,
        stick_out=stick_out,
        coulomb=coulomb,
    )


def split(x):
    high = x.astype(BF16)
    low = (x - high.astype(F32)).astype(BF16)
    return high, low


def dot(a, b):
    return jnp.dot(a, b, preferred_element_type=F32)


def lower_lanes(shape):
    return lax.broadcasted_iota(jnp.int32, shape, len(shape) - 1) % LANES < MID


def turned(x):
    rolled = pltpu.roll(x, MID, 1)
    return jnp.where(lower_lanes(x.shape), -rolled, rolled)


def left_pair(table, first, second):
    u = jnp.concatenate([first[0], second[0]], 1)
    v = jnp.concatenate([first[1], second[1]], 1)
    u_high, u_low = split(u)
    v_high, v_low = split(v)
    data = jnp.concatenate([u_high, v_high, u_low, v_low], 0)
    both = dot(table, data)
    g = both.shape[0] // 2
    out = both[:g] + both[g:]
    return out[:, :LANES], out[:, LANES:]


def left_all(table, slabs, expand):
    results = []
    for k in range(0, len(slabs), 2):
        results += left_pair(table, expand(slabs[k]), expand(slabs[k + 1]))
    return results


def complex_slab(x):
    return x, turned(x)


def right(x, table):
    high, low = split(x)
    both = dot(jnp.concatenate([high, low], 1), table)
    return both[:, :LANES] + both[:, LANES:]


def chunks(g, body):
    for step in range(g // CHUNK):
        body(step * CHUNK)


def strided_slabs(ref, first, g):
    return [ref[pl.ds(first + k, g, stride=g), :] for k in range(CHUNK)]


def slabs_at(ref, first, g):
    rows = pl.ds(first * g, CHUNK * g)
    block = ref[rows, :]
    return [block[k * g : (k + 1) * g] for k in range(CHUNK)]


def store_slabs(ref, first, g, slabs):
    rows = pl.ds(first * g, CHUNK * g)
    ref[rows, :] = jnp.concatenate(slabs, 0)


def one_hot(columns, first, rows):
    index = lax.broadcasted_iota(jnp.int32, (rows, columns.shape[1]), 0)
    return jnp.where(index == columns - first, 1.0, 0.0).astype(BF16)


def all_columns(received_ref, row):
    count = received_ref.shape[0]
    rows = [received_ref[k, row : row + 1, :] for k in range(count)]
    return jnp.concatenate(rows, 1).astype(jnp.int32)


def field_kernel(g, received_ref, stick_in_ref, backward_ref, phi_ref, packed_ref, work_a, work_b):
    count = received_ref.shape[0]
    columns = all_columns(received_ref, 2 * g)
    stick_in = stick_in_ref[...]
    backward = backward_ref[...]
    pieces = []
    for k in range(0, count, 2):
        block = jnp.concatenate([received_ref[k, : 2 * g, :], received_ref[k + 1, : 2 * g, :]], 1)
        both = dot(stick_in, jnp.concatenate(split(block), 0))
        lined = both[:LANES] + both[LANES:]
        pieces.append(jnp.concatenate(split(lined.T), 1))
    sticks = jnp.concatenate(pieces, 0)

    def scatter(first):
        rows = CHUNK * g
        hot = one_hot(columns, first * g, rows)
        both = dot(hot, sticks)
        placed = both[:, :LANES] + both[:, LANES:]
        slabs = [placed[k * g : (k + 1) * g] for k in range(CHUNK)]
        store_slabs(work_b, first, g, left_all(backward, slabs, complex_slab))

    chunks(g, scatter)

    def real_slab(x):
        rolled = pltpu.roll(x, MID, 1)
        lower = lower_lanes(x.shape)
        return jnp.where(lower, x, rolled), -jnp.where(lower, rolled, x)

    def finish(first):
        slabs = strided_slabs(work_b, first, g)
        store_slabs(phi_ref, first, g, left_all(backward, slabs, real_slab))

    chunks(g, finish)
    half_rows = g * g // 2
    lower = phi_ref[:half_rows, :]
    packed_ref[...] = jnp.where(lower_lanes(lower.shape), lower, phi_ref[half_rows:, :])


def potentials(g, phi_ref, pair_ref, tables, work_a, work_b, emit):
    forward_ref, backward_ref, z_forward_ref, z_backward_ref, coulomb_ref = tables
    forward = forward_ref[...]
    backward = backward_ref[...]

    def first_steps(first):
        rows = pl.ds(first * g, CHUNK * g)
        density = phi_ref[rows, :] * pair_ref[rows, :]
        spectrum = right(density, z_forward_ref[...])
        slabs = [spectrum[k * g : (k + 1) * g] for k in range(CHUNK)]
        store_slabs(work_a, first, g, left_all(forward, slabs, complex_slab))

    chunks(g, first_steps)

    def middle(first):
        slabs = left_all(forward, strided_slabs(work_a, first, g), complex_slab)
        slabs = [slab * coulomb_ref[first + k] for k, slab in enumerate(slabs)]
        store_slabs(work_b, first, g, left_all(backward, slabs, complex_slab))

    chunks(g, middle)

    def last_steps(first):
        slabs = left_all(backward, strided_slabs(work_b, first, g), complex_slab)
        emit(first, right(jnp.concatenate(slabs, 0), z_backward_ref[...]))

    chunks(g, last_steps)


def pair_fields(g, first_ref, second_ref, pair_ref):
    half_rows = g * g // 2
    first, second = first_ref[...], second_ref[...]
    lower = lower_lanes(first.shape)
    pair_ref[:half_rows, :] = jnp.where(lower, first, pltpu.roll(second, MID, 1))
    pair_ref[half_rows:, :] = jnp.where(lower, pltpu.roll(first, MID, 1), second)


def near_kernel(g, phi_ref, other_ref, forward_ref, backward_ref, z_forward_ref, z_backward_ref, coulomb_ref, sum_ref, pair_ref, work_a, work_b):
    half_rows = g * g // 2
    other = other_ref[...]
    own = phi_ref[...]
    lower = lower_lanes(other.shape)
    pair_ref[:half_rows, :] = jnp.where(lower, own[:half_rows], pltpu.roll(other, MID, 1))
    pair_ref[half_rows:, :] = jnp.where(lower, own[half_rows:], other)

    def emit(first, potential):
        rows = pl.ds(first * g, CHUNK * g)
        sum_ref[rows, :] = potential * pair_ref[rows, :]

    tables = (forward_ref, backward_ref, z_forward_ref, z_backward_ref, coulomb_ref)
    potentials(g, phi_ref, pair_ref, tables, work_a, work_b, emit)


def middle_kernel(g, phi_ref, first_ref, second_ref, before_ref, forward_ref, backward_ref, z_forward_ref, z_backward_ref, coulomb_ref, sum_ref, pair_ref, work_a, work_b):
    pair_fields(g, first_ref, second_ref, pair_ref)

    def emit(first, potential):
        rows = pl.ds(first * g, CHUNK * g)
        sum_ref[rows, :] = potential * pair_ref[rows, :] + before_ref[rows, :]

    tables = (forward_ref, backward_ref, z_forward_ref, z_backward_ref, coulomb_ref)
    potentials(g, phi_ref, pair_ref, tables, work_a, work_b, emit)


def far_kernel(g, weights, phi_ref, first_ref, second_ref, sum_ref, received_ref, forward_ref, backward_ref, z_forward_ref, z_backward_ref, stick_out_ref, coulomb_ref, out_ref, pair_ref, work_a, work_b, picked):
    pair_fields(g, first_ref, second_ref, pair_ref)
    forward = forward_ref[...]

    def emit(first, potential):
        rows = pl.ds(first * g, CHUNK * g)
        lower = lower_lanes(potential.shape)
        weight = jnp.where(lower, weights[0], weights[1])
        total = potential * pair_ref[rows, :] * weight + sum_ref[rows, :]
        total = total + pltpu.roll(total, MID, 1)
        slabs = [total[k * g : (k + 1) * g] for k in range(CHUNK)]

        def expand(x):
            low = lower_lanes(x.shape)
            return jnp.where(low, x, 0.0), jnp.where(low, 0.0, x)

        store_slabs(work_a, first, g, left_all(forward, slabs, expand))

    tables = (forward_ref, backward_ref, z_forward_ref, z_backward_ref, coulomb_ref)
    potentials(g, phi_ref, pair_ref, tables, work_a, work_b, emit)

    columns = all_columns(received_ref, 2 * g)
    picked[...] = jnp.zeros_like(picked)

    def pick(first):
        slabs = left_all(forward, strided_slabs(work_a, first, g), complex_slab)
        rows = CHUNK * g
        parts = jnp.concatenate(split(jnp.concatenate(slabs, 0)), 1)
        hot = one_hot(columns, first * g, rows)
        both = lax.dot_general(parts, hot, (((0,), (0,)), ((), ())), preferred_element_type=F32)
        picked[...] += both[:LANES] + both[LANES:]

    chunks(g, pick)
    result = dot(stick_out_ref[...], jnp.concatenate(split(picked[...]), 0))
    result = result[: 2 * g] + result[2 * g :]
    for k in range(out_ref.shape[0]):
        out_ref[k] = result[:, k * LANES : (k + 1) * LANES]


def call(kernel, out_shapes, scratch, flops, *operands):
    vmem = pl.BlockSpec(memory_space=pltpu.VMEM)
    moved = sum(x.size * x.dtype.itemsize for x in operands)
    return pl.pallas_call(
        kernel,
        out_shape=out_shapes,
        in_specs=[vmem] * len(operands),
        out_specs=jax.tree.map(lambda _: vmem, out_shapes),
        scratch_shapes=scratch,
        compiler_params=pltpu.CompilerParams(vmem_limit_bytes=40 * 2**20),
        cost_estimate=pl.CostEstimate(flops=flops, bytes_accessed=moved, transcendentals=0),
    )(*operands)


def on_device(sticks, stick_columns):
    g = sticks.shape[1] // 2
    owners = lax.axis_size("stick")
    groups = lax.axis_size("band")
    t = {name: jnp.asarray(value) for name, value in make_tables(g).items()}
    rows = g * g
    field = jax.ShapeDtypeStruct((rows, LANES), F32)
    half_field = jax.ShapeDtypeStruct((rows // 2, LANES), F32)
    scratch = pltpu.VMEM((rows, LANES), F32)
    pot_flops = 6 * 2 * rows * 256 * 256

    column_rows = jnp.broadcast_to(stick_columns.astype(F32)[None, None, :], (owners, 8, stick_columns.shape[0]))
    payload = jnp.concatenate([sticks, column_rows], 1)
    received = lax.all_to_all(payload, "stick", split_axis=0, concat_axis=0, tiled=True)
    phi, packed = call(
        functools.partial(field_kernel, g),
        (field, half_field),
        [scratch, scratch],
        10**9,
        received,
        t["stick_in"],
        t["backward"],
    )
    pot_tables = [t["forward"], t["backward"], t["z_forward"], t["z_backward"]]
    swap = [(i, i ^ 1) for i in range(groups)]

    def fetched(distance):
        return lax.ppermute(packed, "band", [(i, (i - distance) % groups) for i in range(groups)])

    near = lax.ppermute(packed, "band", swap)
    ahead = fetched(HALF)
    total = call(
        functools.partial(near_kernel, g),
        field,
        [scratch] * 3,
        pot_flops,
        phi,
        near,
        *pot_tables,
        t["coulomb"],
    )
    ahead, total = lax.optimization_barrier((ahead, total))
    if groups == 2 * HALF:
        weights = (2.0, 1.0)
        first, second = ahead, lax.ppermute(ahead, "band", swap)
    else:
        weights = (1.0, 0.0)
        behind = fetched(-HALF)
        odd = lax.axis_index("band") % 2 == 1
        first = second = lax.ppermute(jnp.where(odd, behind, ahead), "band", swap)
        total = call(
            functools.partial(middle_kernel, g),
            field,
            [scratch] * 3,
            pot_flops,
            phi,
            ahead,
            behind,
            total,
            *pot_tables,
            t["coulomb"],
        )
    result = call(
        functools.partial(far_kernel, g, weights),
        jax.ShapeDtypeStruct(sticks.shape, F32),
        [scratch] * 3 + [pltpu.VMEM((LANES, owners * stick_columns.shape[0]), F32)],
        pot_flops,
        phi,
        first,
        second,
        total,
        received,
        *pot_tables,
        t["stick_out"],
        t["coulomb"],
    )
    return lax.all_to_all(result, "stick", split_axis=0, concat_axis=0, tiled=True)


def solution(mesh):
    return jax.shard_map(
        on_device,
        mesh=mesh,
        in_specs=(P("band", None, "stick"), P("stick")),
        out_specs=P("band", None, "stick"),
        check_vma=False,
    )
```

```python
import functools
import math

import jax
import jax.numpy as jnp
import numpy as np
from jax import lax
from jax.experimental import pallas as pl
from jax.experimental.pallas import tpu as pltpu
from jax.sharding import PartitionSpec as P

HALF = 2
BOX_LENGTH = 18.0
LANES = 128
MID = 64
CHUNK = 8

F32 = jnp.float32
BF16 = jnp.bfloat16


def rounded_parts(table):
    high = table.astype(BF16)
    low = (table - high.astype(np.float64)).astype(BF16)
    return high, low


def trig(g):
    angle = 2.0 * np.pi / g * (np.outer(np.arange(g), np.arange(g)) % g)
    return np.cos(angle), np.sin(angle)


def stacked_left(table):
    high, low = rounded_parts(table)
    return np.concatenate(
        [np.concatenate([high, high], 1), np.concatenate([low, np.zeros_like(low)], 1)], 0
    )


def stacked_right(table):
    high, low = rounded_parts(table)
    return np.concatenate(
        [np.concatenate([high, low], 1), np.concatenate([high, np.zeros_like(low)], 1)], 0
    )


def make_tables(g):
    c, s = trig(g)
    forward = stacked_left(np.concatenate([c, -s], 1))
    backward = stacked_left(np.concatenate([c, s], 1))

    def lane_table(sign, scale):
        out = np.zeros((LANES, LANES))
        out[:g, :g] = c
        out[:g, MID : MID + g] = sign * s
        out[MID : MID + g, :g] = -sign * s
        out[MID : MID + g, MID : MID + g] = c
        return out * scale

    z_forward = stacked_right(lane_table(-1.0, 1.0))
    z_backward = stacked_right(lane_table(1.0, 1.0 / g**3))
    spread = np.zeros((LANES, 2 * g))
    spread[:g, :g] = c
    spread[:g, g:] = -s
    spread[MID : MID + g, :g] = s
    spread[MID : MID + g, g:] = c
    stick_in = stacked_left(spread)
    pick = np.zeros((2 * g, LANES))
    pick[:g, :g] = c
    pick[:g, MID : MID + g] = s
    pick[g:, :g] = -s
    pick[g:, MID : MID + g] = c
    stick_out = stacked_left(pick * g**-1.5)
    freq = np.arange(g)
    square = np.minimum(freq, g - freq) ** 2
    total = square[:, None, None] + square[None, :, None] + square[None, None, :]
    unit = (2.0 * math.pi / BOX_LENGTH) ** 2
    kernel = np.where(total > 0, 4.0 * math.pi / (unit * np.maximum(total, 1)), 0.0)
    coulomb = np.zeros((g, g, LANES), np.float32)
    coulomb[:, :, :g] = kernel
    coulomb[:, :, MID : MID + g] = kernel
    return dict(
        forward=forward,
        backward=backward,
        z_forward=z_forward,
        z_backward=z_backward,
        stick_in=stick_in,
        stick_out=stick_out,
        coulomb=coulomb,
    )


def split(x):
    high = x.astype(BF16)
    low = (x - high.astype(F32)).astype(BF16)
    return high, low


def dot(a, b):
    return jnp.dot(a, b, preferred_element_type=F32)


def lower_lanes(shape):
    return lax.broadcasted_iota(jnp.int32, shape, len(shape) - 1) % LANES < MID


def turned(x):
    rolled = pltpu.roll(x, MID, 1)
    return jnp.where(lower_lanes(x.shape), -rolled, rolled)


def left_pair(table, first, second):
    u = jnp.concatenate([first[0], second[0]], 1)
    v = jnp.concatenate([first[1], second[1]], 1)
    u_high, u_low = split(u)
    v_high, v_low = split(v)
    data = jnp.concatenate([u_high, v_high, u_low, v_low], 0)
    both = dot(table, data)
    g = both.shape[0] // 2
    out = both[:g] + both[g:]
    return out[:, :LANES], out[:, LANES:]


def left_all(table, slabs, expand):
    results = []
    for k in range(0, len(slabs), 2):
        results += left_pair(table, expand(slabs[k]), expand(slabs[k + 1]))
    return results


def complex_slab(x):
    return x, turned(x)


def right(x, table):
    high, low = split(x)
    both = dot(jnp.concatenate([high, low], 1), table)
    return both[:, :LANES] + both[:, LANES:]


def chunks(g, body):
    for step in range(g // CHUNK):
        body(step * CHUNK)


def strided_slabs(ref, first, g):
    return [ref[pl.ds(first + k, g, stride=g), :] for k in range(CHUNK)]


def slabs_at(ref, first, g):
    rows = pl.ds(first * g, CHUNK * g)
    block = ref[rows, :]
    return [block[k * g : (k + 1) * g] for k in range(CHUNK)]


def store_slabs(ref, first, g, slabs):
    rows = pl.ds(first * g, CHUNK * g)
    ref[rows, :] = jnp.concatenate(slabs, 0)


def one_hot(columns, first, rows):
    index = lax.broadcasted_iota(jnp.int32, (rows, columns.shape[1]), 0)
    return jnp.where(index == columns - first, 1.0, 0.0).astype(BF16)


def send_kernel(g, sticks_ref, columns_ref, *block_refs):
    own = lax.axis_index("stick")
    columns = jnp.broadcast_to(columns_ref[...].astype(F32), (8, LANES))
    for d, block_ref in enumerate(block_refs):
        block_ref[: 2 * g, :] = sticks_ref[own ^ d]
        block_ref[2 * g :, :] = columns


def place_kernel(*refs):
    own = lax.axis_index("stick")
    out_ref = refs[-1]
    for d, block_ref in enumerate(refs[:-1]):
        out_ref[own ^ d] = block_ref[...]


def field_kernel(g, count, *refs):
    received, (stick_in_ref, backward_ref, phi_ref, packed_ref, columns_ref, work_a, work_b) = refs[:count], refs[count:]
    columns = jnp.concatenate([ref[2 * g : 2 * g + 1, :] for ref in received], 1).astype(jnp.int32)
    columns_ref[...] = jnp.broadcast_to(columns, columns_ref.shape)
    stick_in = stick_in_ref[...]
    backward = backward_ref[...]
    pieces = []
    for k in range(0, count, 2):
        block = jnp.concatenate([received[k][: 2 * g, :], received[k + 1][: 2 * g, :]], 1)
        both = dot(stick_in, jnp.concatenate(split(block), 0))
        lined = both[:LANES] + both[LANES:]
        pieces.append(jnp.concatenate(split(lined.T), 1))
    sticks = jnp.concatenate(pieces, 0)

    def scatter(first):
        rows = CHUNK * g
        hot = one_hot(columns, first * g, rows)
        both = dot(hot, sticks)
        placed = both[:, :LANES] + both[:, LANES:]
        slabs = [placed[k * g : (k + 1) * g] for k in range(CHUNK)]
        store_slabs(work_b, first, g, left_all(backward, slabs, complex_slab))

    chunks(g, scatter)

    def real_slab(x):
        rolled = pltpu.roll(x, MID, 1)
        lower = lower_lanes(x.shape)
        return jnp.where(lower, x, rolled), -jnp.where(lower, rolled, x)

    def finish(first):
        slabs = strided_slabs(work_b, first, g)
        store_slabs(phi_ref, first, g, left_all(backward, slabs, real_slab))

    chunks(g, finish)
    half_rows = g * g // 2
    lower = phi_ref[:half_rows, :]
    packed_ref[...] = jnp.where(lower_lanes(lower.shape), lower, phi_ref[half_rows:, :])


def potentials(g, phi_ref, pair_ref, tables, work_a, work_b, emit):
    forward_ref, backward_ref, z_forward_ref, z_backward_ref, coulomb_ref = tables
    forward = forward_ref[...]
    backward = backward_ref[...]

    def first_steps(first):
        rows = pl.ds(first * g, CHUNK * g)
        density = phi_ref[rows, :] * pair_ref[rows, :]
        spectrum = right(density, z_forward_ref[...])
        slabs = [spectrum[k * g : (k + 1) * g] for k in range(CHUNK)]
        store_slabs(work_a, first, g, left_all(forward, slabs, complex_slab))

    chunks(g, first_steps)

    def middle(first):
        slabs = left_all(forward, strided_slabs(work_a, first, g), complex_slab)
        slabs = [slab * coulomb_ref[first + k] for k, slab in enumerate(slabs)]
        store_slabs(work_b, first, g, left_all(backward, slabs, complex_slab))

    chunks(g, middle)

    def last_steps(first):
        slabs = left_all(backward, strided_slabs(work_b, first, g), complex_slab)
        emit(first, right(jnp.concatenate(slabs, 0), z_backward_ref[...]))

    chunks(g, last_steps)


def pair_fields(g, first_ref, second_ref, pair_ref):
    half_rows = g * g // 2
    first, second = first_ref[...], second_ref[...]
    lower = lower_lanes(first.shape)
    pair_ref[:half_rows, :] = jnp.where(lower, first, pltpu.roll(second, MID, 1))
    pair_ref[half_rows:, :] = jnp.where(lower, pltpu.roll(first, MID, 1), second)


def near_kernel(g, phi_ref, other_ref, forward_ref, backward_ref, z_forward_ref, z_backward_ref, coulomb_ref, sum_ref, pair_ref, work_a, work_b):
    half_rows = g * g // 2
    other = other_ref[...]
    own = phi_ref[...]
    lower = lower_lanes(other.shape)
    pair_ref[:half_rows, :] = jnp.where(lower, own[:half_rows], pltpu.roll(other, MID, 1))
    pair_ref[half_rows:, :] = jnp.where(lower, own[half_rows:], other)

    def emit(first, potential):
        rows = pl.ds(first * g, CHUNK * g)
        sum_ref[rows, :] = potential * pair_ref[rows, :]

    tables = (forward_ref, backward_ref, z_forward_ref, z_backward_ref, coulomb_ref)
    potentials(g, phi_ref, pair_ref, tables, work_a, work_b, emit)


def middle_kernel(g, phi_ref, first_ref, second_ref, before_ref, forward_ref, backward_ref, z_forward_ref, z_backward_ref, coulomb_ref, sum_ref, pair_ref, work_a, work_b):
    pair_fields(g, first_ref, second_ref, pair_ref)

    def emit(first, potential):
        rows = pl.ds(first * g, CHUNK * g)
        sum_ref[rows, :] = potential * pair_ref[rows, :] + before_ref[rows, :]

    tables = (forward_ref, backward_ref, z_forward_ref, z_backward_ref, coulomb_ref)
    potentials(g, phi_ref, pair_ref, tables, work_a, work_b, emit)


def far_kernel(g, weights, phi_ref, first_ref, second_ref, sum_ref, columns_ref, forward_ref, backward_ref, z_forward_ref, z_backward_ref, stick_out_ref, coulomb_ref, *rest):
    out_refs, (pair_ref, work_a, work_b, picked) = rest[:-4], rest[-4:]
    pair_fields(g, first_ref, second_ref, pair_ref)
    forward = forward_ref[...]

    def emit(first, potential):
        rows = pl.ds(first * g, CHUNK * g)
        lower = lower_lanes(potential.shape)
        weight = jnp.where(lower, weights[0], weights[1])
        total = potential * pair_ref[rows, :] * weight + sum_ref[rows, :]
        total = total + pltpu.roll(total, MID, 1)
        slabs = [total[k * g : (k + 1) * g] for k in range(CHUNK)]

        def expand(x):
            low = lower_lanes(x.shape)
            return jnp.where(low, x, 0.0), jnp.where(low, 0.0, x)

        store_slabs(work_a, first, g, left_all(forward, slabs, expand))

    tables = (forward_ref, backward_ref, z_forward_ref, z_backward_ref, coulomb_ref)
    potentials(g, phi_ref, pair_ref, tables, work_a, work_b, emit)

    columns = columns_ref[:1, :]
    picked[...] = jnp.zeros_like(picked)

    def pick(first):
        slabs = left_all(forward, strided_slabs(work_a, first, g), complex_slab)
        rows = CHUNK * g
        parts = jnp.concatenate(split(jnp.concatenate(slabs, 0)), 1)
        hot = one_hot(columns, first * g, rows)
        both = lax.dot_general(parts, hot, (((0,), (0,)), ((), ())), preferred_element_type=F32)
        picked[...] += both[:LANES] + both[LANES:]

    chunks(g, pick)
    result = dot(stick_out_ref[...], jnp.concatenate(split(picked[...]), 0))
    result = result[: 2 * g] + result[2 * g :]
    for k, out_ref in enumerate(out_refs):
        out_ref[...] = result[:, k * LANES : (k + 1) * LANES]


def call(kernel, out_shapes, scratch, flops, *operands):
    vmem = pl.BlockSpec(memory_space=pltpu.VMEM)
    moved = sum(x.size * x.dtype.itemsize for x in operands)
    return pl.pallas_call(
        kernel,
        out_shape=out_shapes,
        in_specs=[vmem] * len(operands),
        out_specs=jax.tree.map(lambda _: vmem, out_shapes),
        scratch_shapes=scratch,
        compiler_params=pltpu.CompilerParams(vmem_limit_bytes=40 * 2**20),
        cost_estimate=pl.CostEstimate(flops=flops, bytes_accessed=moved, transcendentals=0),
    )(*operands)


def exchanged(blocks):
    owners = len(blocks)
    moved = {}
    for d in range(owners - 1, 0, -1):
        moved[d] = lax.ppermute(blocks[d], "stick", [(i, i ^ d) for i in range(owners)])
    return [blocks[0]] + [moved[d] for d in range(1, owners)]


def on_device(sticks, stick_columns):
    g = sticks.shape[1] // 2
    owners = lax.axis_size("stick")
    groups = lax.axis_size("band")
    t = {name: jnp.asarray(value) for name, value in make_tables(g).items()}
    rows = g * g
    field = jax.ShapeDtypeStruct((rows, LANES), F32)
    half_field = jax.ShapeDtypeStruct((rows // 2, LANES), F32)
    scratch = pltpu.VMEM((rows, LANES), F32)
    pot_flops = 6 * 2 * rows * 256 * 256

    slots = stick_columns.shape[0]
    sent = call(
        functools.partial(send_kernel, g),
        [jax.ShapeDtypeStruct((2 * g + 8, slots), F32)] * owners,
        [],
        10**6,
        sticks,
        stick_columns[None, :],
    )
    received = exchanged(sent)
    phi, packed, columns = call(
        functools.partial(field_kernel, g, owners),
        [field, half_field, jax.ShapeDtypeStruct((8, owners * slots), jnp.int32)],
        [scratch, scratch],
        10**9,
        *received,
        t["stick_in"],
        t["backward"],
    )
    pot_tables = [t["forward"], t["backward"], t["z_forward"], t["z_backward"]]
    swap = [(i, i ^ 1) for i in range(groups)]

    def fetched(distance):
        return lax.ppermute(packed, "band", [(i, (i - distance) % groups) for i in range(groups)])

    near = lax.ppermute(packed, "band", swap)
    ahead = fetched(HALF)
    total = call(
        functools.partial(near_kernel, g),
        field,
        [scratch] * 3,
        pot_flops,
        phi,
        near,
        *pot_tables,
        t["coulomb"],
    )
    ahead, total = lax.optimization_barrier((ahead, total))
    if groups == 2 * HALF:
        weights = (2.0, 1.0)
        first, second = ahead, lax.ppermute(ahead, "band", swap)
    else:
        weights = (1.0, 0.0)
        behind = fetched(-HALF)
        odd = lax.axis_index("band") % 2 == 1
        first = second = lax.ppermute(jnp.where(odd, behind, ahead), "band", swap)
        total = call(
            functools.partial(middle_kernel, g),
            field,
            [scratch] * 3,
            pot_flops,
            phi,
            ahead,
            behind,
            total,
            *pot_tables,
            t["coulomb"],
        )
    result = call(
        functools.partial(far_kernel, g, weights),
        [jax.ShapeDtypeStruct((2 * g, slots), F32)] * owners,
        [scratch] * 3 + [pltpu.VMEM((LANES, owners * slots), F32)],
        pot_flops,
        phi,
        first,
        second,
        total,
        columns,
        *pot_tables,
        t["stick_out"],
        t["coulomb"],
    )
    return call(place_kernel, jax.ShapeDtypeStruct(sticks.shape, F32), [], 10**6, *exchanged(result))


def solution(mesh):
    return jax.shard_map(
        on_device,
        mesh=mesh,
        in_specs=(P("band", None, "stick"), P("stick")),
        out_specs=P("band", None, "stick"),
        check_vma=False,
    )
```

```python
import functools
import math

import jax
import jax.numpy as jnp
import numpy as np
from jax import lax
from jax.experimental import pallas as pl
from jax.experimental.pallas import tpu as pltpu
from jax.sharding import PartitionSpec as P

HALF = 2
BOX_LENGTH = 18.0
LANES = 128
MID = 64
PAIRS = 4
FOLD = 3

F32 = jnp.float32
BF16 = jnp.bfloat16


def rounded_parts(table):
    high = table.astype(BF16).astype(np.float64)
    low = (table - high).astype(BF16).astype(np.float64)
    return high, low


def across(table):
    high, low = rounded_parts(table)
    return np.concatenate([high, high, low], 1).astype(np.float32)


def down(table):
    high, low = rounded_parts(table)
    return np.concatenate([high, high, low], 0).astype(np.float32)


def make_tables(g):
    angle = 2.0 * np.pi / g * (np.outer(np.arange(g), np.arange(g)) % g)
    c, s = np.cos(angle), np.sin(angle)
    lower, upper = slice(0, g), slice(MID, MID + g)

    z_forward = np.zeros((2 * LANES, 2 * LANES))
    z_backward = np.zeros((2 * LANES, 2 * LANES))
    for slab, half in enumerate((lower, upper)):
        base = slab * LANES
        real, imag = slice(base, base + g), slice(base + MID, base + MID + g)
        one, two = half, slice(LANES + half.start, LANES + half.stop)
        z_forward[one, real], z_forward[one, imag] = c, -s
        z_forward[two, real], z_forward[two, imag] = s, c
        z_backward[real, one], z_backward[real, two] = c, s
        z_backward[imag, one], z_backward[imag, two] = -s, c

    stick_in = np.zeros((LANES, 2 * g))
    stick_in[lower, :g], stick_in[lower, g:] = c, -s
    stick_in[upper, :g], stick_in[upper, g:] = s, c
    stick_out = np.block([[c, s], [-s, c]]) * g**-1.5

    freq = np.arange(g)
    square = np.minimum(freq, g - freq) ** 2
    total = square[:, None, None] + square[None, :, None] + square[None, None, :]
    unit = (2.0 * math.pi / BOX_LENGTH) ** 2
    kernel = np.where(total > 0, 4.0 * math.pi / (unit * np.maximum(total, 1)), 0.0)
    coulomb = np.zeros((g, g, LANES), np.float32)
    coulomb[:, :, lower] = kernel
    coulomb[:, :, upper] = kernel
    return dict(
        forward=across(np.concatenate([c, -s], 0)),
        backward=across(np.concatenate([c, s], 0)),
        z_forward=down(z_forward),
        z_backward=down(z_backward / g**3),
        stick_in=across(stick_in),
        stick_out=across(stick_out),
        coulomb=coulomb,
    )


def split(x):
    high = x.astype(BF16)
    low = (x - high.astype(F32)).astype(BF16)
    return high, low


def stacked(x):
    high, low = split(x)
    return jnp.concatenate([high, low, high], 0)


def dot(a, b):
    return jnp.dot(a, b, preferred_element_type=F32)


def lane_halves(shape):
    return lax.broadcasted_iota(jnp.int32, shape, 1) % LANES < MID


def turned(x):
    return jnp.concatenate(
        [pltpu.roll(x[:, k : k + LANES], MID, 1) for k in range(0, x.shape[1], LANES)], 1
    )


def left(table, x):
    both = dot(table, stacked(x))
    g = both.shape[0] // 2
    return both[:g], both[g:]


def left_complex(table, x):
    cos, sin = left(table, x)
    sign = jnp.where(lane_halves((1, x.shape[1])), -1.0, 1.0)
    return cos + turned(sin) * sign


def halves(x):
    return x[:, :LANES], x[:, LANES:]


def beside(a, b):
    return jnp.concatenate([a, b], 1)


def right(parts, table):
    high, low = zip(*[split(x) for x in parts])
    return dot(jnp.concatenate(high + low + high, 1), table)


def strided(ref, first, g):
    return ref[pl.ds(first, g, stride=g), :]


def slab_rows(index, g, count=1):
    return pl.ds(index * g, count * g)


def one_hot(columns, first, rows):
    index = lax.broadcasted_iota(jnp.int16, (rows, columns.shape[1]), 0)
    wanted = (columns - first).astype(jnp.int16)
    return jnp.where(index == wanted, jnp.asarray(1, BF16), jnp.asarray(0, BF16))


def send_kernel(g, sticks_ref, columns_ref, *refs):
    block_refs, (row_ref, sems, row_sem) = refs[:-3], refs[-3:]
    own = lax.axis_index("stick")
    copies = [
        pltpu.make_async_copy(sticks_ref.at[own ^ d], ref.at[pl.ds(0, 2 * g)], sems.at[d])
        for d, ref in enumerate(block_refs)
    ]
    row_copy = pltpu.make_async_copy(columns_ref, row_ref, row_sem)
    row_copy.start()
    for copy in copies:
        copy.start()
    row_copy.wait()
    columns = jnp.broadcast_to(row_ref[...].astype(F32), (8, LANES))
    for ref in block_refs:
        ref[2 * g :, :] = columns
    for copy in copies:
        copy.wait()


def table_kernel(*refs):
    count = len(refs) // 2
    for table_ref, out_ref in zip(refs[:count], refs[count:]):
        out_ref[...] = table_ref[...].astype(BF16)


def place_kernel(*refs):
    own = lax.axis_index("stick")
    out_ref = refs[-1]
    for d, block_ref in enumerate(refs[:-1]):
        out_ref[own ^ d] = block_ref[...]


def fold(field_ref, folded_ref, g):
    rows = folded_ref.shape[0] // FOLD
    used = lax.broadcasted_iota(jnp.int32, (rows, LANES), 1) % MID < g
    last = field_ref[FOLD * rows :, :]
    width = g // FOLD
    for k in range(FOLD):
        part = slice(k * rows, (k + 1) * rows)
        folded_ref[part, :] = jnp.where(used, field_ref[part, :], pltpu.roll(last, g - k * width, 1))


def unfold(folded_ref, field_ref, g):
    rows = folded_ref.shape[0] // FOLD
    lane = lax.broadcasted_iota(jnp.int32, (rows, LANES), 1) % MID
    width = g // FOLD
    last = None
    for k in range(FOLD):
        part = folded_ref[k * rows : (k + 1) * rows, :]
        field_ref[k * rows : (k + 1) * rows, :] = part
        piece = pltpu.roll(part, LANES - (g - k * width), 1)
        last = piece if last is None else jnp.where(lane >= k * width, piece, last)
    field_ref[FOLD * rows :, :] = last


def field_kernel(g, count, *refs):
    received = refs[:count]
    stick_in_ref, backward_ref, phi_ref, folded_ref, columns_ref, work_a = refs[count:]
    columns = jnp.concatenate([ref[2 * g : 2 * g + 1, :] for ref in received], 1).astype(jnp.int32)
    columns_ref[...] = jnp.broadcast_to(columns, columns_ref.shape)
    stick_in, backward = stick_in_ref[...], backward_ref[...]
    pieces = []
    for k in range(0, count, 2):
        block = beside(received[k][: 2 * g, :], received[k + 1][: 2 * g, :])
        pieces.append(beside(*split(dot(stick_in, stacked(block)).T)))
    sticks = jnp.concatenate(pieces, 0)

    for first in range(0, g, 2 * PAIRS):
        both = dot(one_hot(columns, first * g, 2 * PAIRS * g), sticks)
        placed = both[:, :LANES] + both[:, LANES:]
        for k in range(0, 2 * PAIRS, 2):
            x = beside(placed[k * g : (k + 1) * g], placed[(k + 1) * g : (k + 2) * g])
            for j, slab in enumerate(halves(left_complex(backward, x))):
                work_a[slab_rows(first + k + j, g), :] = slab

    for pair in range(g // 2):
        x = beside(strided(work_a, pair, g), strided(work_a, pair + g // 2, g))
        (cos, cos_up), (sin, sin_up) = map(halves, left(backward, x))
        lower = cos - pltpu.roll(sin, MID, 1)
        upper = pltpu.roll(cos_up, MID, 1) - sin_up
        phi_ref[slab_rows(pair, g), :] = jnp.where(lane_halves(lower.shape), lower, upper)
    fold(phi_ref, folded_ref, g)


def potentials(g, phi_ref, first_ref, second_ref, tables, work_a, work_b, emit):
    forward, backward, z_forward, z_backward = [ref[...].astype(BF16) for ref in tables[:4]]
    coulomb_ref = tables[4]
    half = g // 2
    for start in range(0, half, PAIRS):
        rows = slab_rows(start, g, PAIRS)
        phi = phi_ref[rows, :]
        spectrum = right([phi * first_ref[rows, :], phi * second_ref[rows, :]], z_forward)
        for k in range(PAIRS):
            slabs = halves(left_complex(forward, spectrum[k * g : (k + 1) * g]))
            work_a[slab_rows(start + k, g), :] = slabs[0]
            work_a[slab_rows(start + k + half, g), :] = slabs[1]

    for kx in range(0, g, 2):
        x = left_complex(forward, beside(strided(work_a, kx, g), strided(work_a, kx + 1, g)))
        x = left_complex(backward, x * beside(coulomb_ref[kx], coulomb_ref[kx + 1]))
        for j, slab in enumerate(halves(x)):
            work_b[slab_rows(kx + j, g), :] = slab

    for start in range(0, half, PAIRS):
        slabs = [
            left_complex(backward, beside(strided(work_b, pair, g), strided(work_b, pair + half, g)))
            for pair in range(start, start + PAIRS)
        ]
        emit(start, *halves(right([jnp.concatenate(slabs, 0)], z_backward)))


def near_kernel(g, phi_ref, near_ref, *refs):
    tables, (sum_ref, other_ref, work_a, work_b) = refs[:5], refs[5:]
    unfold(near_ref, other_ref, g)

    def emit(start, own, other):
        rows = slab_rows(start, g, PAIRS)
        sum_ref[rows, :] = own * phi_ref[rows, :] + other * other_ref[rows, :]

    potentials(g, phi_ref, phi_ref, other_ref, tables, work_a, work_b, emit)


def middle_kernel(g, phi_ref, ahead_ref, behind_ref, before_ref, *refs):
    tables, (sum_ref, first_ref, second_ref, work_a, work_b) = refs[:5], refs[5:]
    unfold(ahead_ref, first_ref, g)
    unfold(behind_ref, second_ref, g)

    def emit(start, first, second):
        rows = slab_rows(start, g, PAIRS)
        sum_ref[rows, :] = before_ref[rows, :] + first * first_ref[rows, :] + second * second_ref[rows, :]

    potentials(g, phi_ref, first_ref, second_ref, tables, work_a, work_b, emit)


def far_kernel(g, weights, phi_ref, ahead_ref, across_ref, before_ref, columns_ref, stick_out_ref, *refs):
    tables, out_refs = refs[:5], refs[5:-5]
    first_ref, second_ref, work_a, work_b, parts_ref = refs[-5:]
    unfold(ahead_ref, first_ref, g)
    unfold(across_ref, second_ref, g)
    forward = tables[0][...].astype(BF16)
    half = g // 2

    def emit(start, first, second):
        rows = slab_rows(start, g, PAIRS)
        total = before_ref[rows, :] + weights[0] * (first * first_ref[rows, :])
        total = total + weights[1] * (second * second_ref[rows, :])
        for k in range(0, PAIRS, 2):
            cos, sin = left(forward, beside(total[k * g : (k + 1) * g], total[(k + 1) * g : (k + 2) * g]))
            low = lane_halves(cos.shape)
            lower, upper = halves(jnp.where(low, cos, turned(sin))), halves(jnp.where(low, turned(cos), sin))
            for j in range(2):
                work_a[slab_rows(start + k + j, g), :] = lower[j]
                work_a[slab_rows(start + k + j + half, g), :] = upper[j]

    potentials(g, phi_ref, first_ref, second_ref, tables, work_a, work_b, emit)

    for first in range(0, g, 2 * PAIRS):
        slabs = []
        for kx in range(first, first + 2 * PAIRS, 2):
            slabs += halves(left_complex(forward, beside(strided(work_a, kx, g), strided(work_a, kx + 1, g))))
        lined = jnp.concatenate(slabs, 0).T
        lined = jnp.concatenate([lined[:g], lined[MID : MID + g]], 0)
        parts_ref[:, first * g : (first + 2 * PAIRS) * g] = jnp.concatenate(split(lined), 0)

    parts = parts_ref[...]
    stick_out = stick_out_ref[...].astype(BF16)
    for k in range(0, len(out_refs), 2):
        hot = one_hot(columns_ref[:1, k * LANES : (k + 2) * LANES], 0, g * g)
        both = dot(parts, hot)
        picked = both[: 2 * g] + both[2 * g :]
        out_refs[k][...], out_refs[k + 1][...] = halves(dot(stick_out, stacked(picked)))


def call(kernel, out_shapes, scratch, flops, *operands, space=pltpu.VMEM):
    vmem = pl.BlockSpec(memory_space=pltpu.VMEM)
    moved = sum(x.size * x.dtype.itemsize for x in operands)
    return pl.pallas_call(
        kernel,
        out_shape=out_shapes,
        in_specs=[pl.BlockSpec(memory_space=space)] * len(operands),
        out_specs=jax.tree.map(lambda _: vmem, out_shapes),
        scratch_shapes=scratch,
        compiler_params=pltpu.CompilerParams(vmem_limit_bytes=40 * 2**20),
        cost_estimate=pl.CostEstimate(flops=flops, bytes_accessed=moved, transcendentals=0),
    )(*operands)


def exchanged(blocks):
    owners = len(blocks)
    moved = {}
    for d in range(owners - 1, 0, -1):
        moved[d] = lax.ppermute(blocks[d], "stick", [(i, i ^ d) for i in range(owners)])
    return [blocks[0]] + [moved[d] for d in range(1, owners)]


def on_device(sticks, stick_columns):
    g = sticks.shape[1] // 2
    slots = stick_columns.shape[0]
    owners = lax.axis_size("stick")
    groups = lax.axis_size("band")
    t = {name: jnp.asarray(value) for name, value in make_tables(g).items()}
    rows = g * g
    field = jax.ShapeDtypeStruct((rows // 2, LANES), F32)
    folded = jax.ShapeDtypeStruct((rows // 2 * FOLD // (FOLD + 1), LANES), F32)
    field_scratch = pltpu.VMEM((rows // 2, LANES), F32)
    work = pltpu.VMEM((rows, LANES), F32)
    pot_flops = 6 * 2 * rows * 256 * 256

    sent = call(
        functools.partial(send_kernel, g),
        [jax.ShapeDtypeStruct((2 * g + 8, slots), F32)] * owners,
        [pltpu.VMEM((1, slots), jnp.int32), pltpu.SemaphoreType.DMA((owners,)), pltpu.SemaphoreType.DMA],
        10**6,
        sticks,
        stick_columns[None, :],
        space=pltpu.HBM,
    )
    received = exchanged(sent)
    first_tables = lax.optimization_barrier((t["stick_in"], t["backward"], sent[0]))[:2]
    first_tables = call(
        table_kernel, [jax.ShapeDtypeStruct(x.shape, BF16) for x in first_tables], [], 10**9, *first_tables
    )
    phi, packed, columns = call(
        functools.partial(field_kernel, g, owners),
        [field, folded, jax.ShapeDtypeStruct((8, owners * slots), jnp.int32)],
        [work],
        10**9,
        *received,
        *first_tables,
    )
    pot_tables = [t["forward"], t["backward"], t["z_forward"], t["z_backward"], t["coulomb"]]
    swap = [(i, i ^ 1) for i in range(groups)]

    def fetched(distance):
        return lax.ppermute(packed, "band", [(i, (i - distance) % groups) for i in range(groups)])

    near = lax.ppermute(packed, "band", swap)
    ahead = fetched(HALF)
    total = call(
        functools.partial(near_kernel, g), field, [field_scratch, work, work], pot_flops, phi, near, *pot_tables
    )
    ahead, total = lax.optimization_barrier((ahead, total))
    if groups == 2 * HALF:
        weights = (2.0, 1.0)
        first, second = ahead, lax.ppermute(ahead, "band", swap)
    else:
        weights = (1.0, 0.0)
        behind = fetched(-HALF)
        odd = lax.axis_index("band") % 2 == 1
        first = second = lax.ppermute(jnp.where(odd, behind, ahead), "band", swap)
        total = call(
            functools.partial(middle_kernel, g),
            field,
            [field_scratch, field_scratch, work, work],
            pot_flops,
            phi,
            ahead,
            behind,
            total,
            *pot_tables,
        )
    result = call(
        functools.partial(far_kernel, g, weights),
        [jax.ShapeDtypeStruct((2 * g, slots), F32)] * owners,
        [field_scratch, field_scratch, work, work, pltpu.VMEM((4 * g, rows), BF16)],
        pot_flops,
        phi,
        first,
        second,
        total,
        columns,
        t["stick_out"],
        *pot_tables,
    )
    return call(place_kernel, jax.ShapeDtypeStruct(sticks.shape, F32), [], 10**6, *exchanged(result))


def solution(mesh):
    return jax.shard_map(
        on_device,
        mesh=mesh,
        in_specs=(P("band", None, "stick"), P("stick")),
        out_specs=P("band", None, "stick"),
        check_vma=False,
    )
```

```python
import functools
import math

import jax
import jax.numpy as jnp
import numpy as np
from jax import lax
from jax.experimental import pallas as pl
from jax.experimental.pallas import tpu as pltpu
from jax.sharding import PartitionSpec as P

HALF = 2
BOX_LENGTH = 18.0
LANES = 128
MID = 64
PAIRS = 4

F32 = jnp.float32
BF16 = jnp.bfloat16


def rounded_parts(table):
    high = table.astype(BF16).astype(np.float64)
    low = (table - high).astype(BF16).astype(np.float64)
    return high, low


def across(table):
    high, low = rounded_parts(table)
    return np.concatenate([high, high, low], 1).astype(np.float32)


def down(table):
    high, low = rounded_parts(table)
    return np.concatenate([high, high, low], 0).astype(np.float32)


def make_tables(g):
    angle = 2.0 * np.pi / g * (np.outer(np.arange(g), np.arange(g)) % g)
    c, s = np.cos(angle), np.sin(angle)
    lower, upper = slice(0, g), slice(MID, MID + g)

    z_forward = np.zeros((2 * LANES, 2 * LANES))
    z_backward = np.zeros((2 * LANES, 2 * LANES))
    for slab, half in enumerate((lower, upper)):
        base = slab * LANES
        real, imag = slice(base, base + g), slice(base + MID, base + MID + g)
        one, two = half, slice(LANES + half.start, LANES + half.stop)
        z_forward[one, real], z_forward[one, imag] = c, -s
        z_forward[two, real], z_forward[two, imag] = s, c
        z_backward[real, one], z_backward[real, two] = c, s
        z_backward[imag, one], z_backward[imag, two] = -s, c

    stick_in = np.zeros((LANES, 2 * g))
    stick_in[lower, :g], stick_in[lower, g:] = c, -s
    stick_in[upper, :g], stick_in[upper, g:] = s, c
    stick_out = np.block([[c, s], [-s, c]]) * g**-1.5

    freq = np.arange(g)
    square = np.minimum(freq, g - freq) ** 2
    total = square[:, None, None] + square[None, :, None] + square[None, None, :]
    unit = (2.0 * math.pi / BOX_LENGTH) ** 2
    kernel = np.where(total > 0, 4.0 * math.pi / (unit * np.maximum(total, 1)), 0.0)
    coulomb = np.zeros((g, g, LANES), np.float32)
    coulomb[:, :, lower] = kernel
    coulomb[:, :, upper] = kernel
    return dict(
        forward=across(np.concatenate([c, -s], 0)),
        backward=across(np.concatenate([c, s], 0)),
        z_forward=down(z_forward),
        z_backward=down(z_backward / g**3),
        stick_in=across(stick_in),
        stick_out=across(stick_out),
        coulomb=coulomb,
    )


def split(x):
    high = x.astype(BF16)
    low = (x - high.astype(F32)).astype(BF16)
    return high, low


def stacked(x):
    high, low = split(x)
    return jnp.concatenate([high, low, high], 0)


def dot(a, b):
    return jnp.dot(a, b, preferred_element_type=F32)


def lane_halves(shape):
    return lax.broadcasted_iota(jnp.int32, shape, 1) % LANES < MID


def turned(x):
    return jnp.concatenate(
        [pltpu.roll(x[:, k : k + LANES], MID, 1) for k in range(0, x.shape[1], LANES)], 1
    )


def left(table, x):
    both = dot(table, stacked(x))
    g = both.shape[0] // 2
    return both[:g], both[g:]


def left_complex(table, x):
    cos, sin = left(table, x)
    sign = jnp.where(lane_halves((1, x.shape[1])), -1.0, 1.0)
    return cos + turned(sin) * sign


def halves(x):
    return x[:, :LANES], x[:, LANES:]


def beside(a, b):
    return jnp.concatenate([a, b], 1)


def right(parts, table):
    high, low = zip(*[split(x) for x in parts])
    return dot(jnp.concatenate(high + low + high, 1), table)


def strided(ref, first, g):
    return ref[pl.ds(first, g, stride=g), :]


def slab_rows(index, g, count=1):
    return pl.ds(index * g, count * g)


def one_hot(columns, first, rows):
    index = lax.broadcasted_iota(jnp.int16, (rows, columns.shape[1]), 0)
    wanted = (columns - first).astype(jnp.int16)
    return jnp.where(index == wanted, jnp.asarray(1, BF16), jnp.asarray(0, BF16))


def send_kernel(g, sticks_ref, columns_ref, first_ref, second_ref):
    first_ref[:, :g, :] = sticks_ref[:, :g, :]
    first_ref[:, g:, :] = jnp.broadcast_to(columns_ref[...].astype(F32), (first_ref.shape[0], 8, LANES))
    second_ref[...] = sticks_ref[:, g:, :]


def table_kernel(*refs):
    count = len(refs) // 2
    for table_ref, out_ref in zip(refs[:count], refs[count:]):
        out_ref[...] = table_ref[...].astype(BF16)


def field_kernel(g, first_ref, second_ref, stick_in_ref, backward_ref, phi_ref, columns_ref, work_a):
    count = first_ref.shape[0]
    columns = jnp.concatenate([first_ref[k, g : g + 1, :] for k in range(count)], 1).astype(jnp.int32)
    columns_ref[...] = jnp.broadcast_to(columns, columns_ref.shape)
    stick_in, backward = stick_in_ref[...], backward_ref[...]
    pieces = []
    for k in range(0, count, 2):
        blocks = [jnp.concatenate([first_ref[k + j, :g, :], second_ref[k + j]], 0) for j in range(2)]
        block = beside(*blocks)
        pieces.append(beside(*split(dot(stick_in, stacked(block)).T)))
    sticks = jnp.concatenate(pieces, 0)

    for first in range(0, g, 2 * PAIRS):
        both = dot(one_hot(columns, first * g, 2 * PAIRS * g), sticks)
        placed = both[:, :LANES] + both[:, LANES:]
        for k in range(0, 2 * PAIRS, 2):
            x = beside(placed[k * g : (k + 1) * g], placed[(k + 1) * g : (k + 2) * g])
            for j, slab in enumerate(halves(left_complex(backward, x))):
                work_a[slab_rows(first + k + j, g), :] = slab

    for pair in range(g // 2):
        x = beside(strided(work_a, pair, g), strided(work_a, pair + g // 2, g))
        (cos, cos_up), (sin, sin_up) = map(halves, left(backward, x))
        lower = cos - pltpu.roll(sin, MID, 1)
        upper = pltpu.roll(cos_up, MID, 1) - sin_up
        phi_ref[slab_rows(pair, g), :] = jnp.where(lane_halves(lower.shape), lower, upper)


def potentials(g, phi_ref, first_ref, second_ref, tables, work_a, work_b, emit):
    forward, backward, z_forward, z_backward = [ref[...].astype(BF16) for ref in tables[:4]]
    coulomb_ref = tables[4]
    half = g // 2
    for start in range(0, half, PAIRS):
        rows = slab_rows(start, g, PAIRS)
        phi = phi_ref[rows, :]
        spectrum = right([phi * first_ref[rows, :], phi * second_ref[rows, :]], z_forward)
        for k in range(PAIRS):
            slabs = halves(left_complex(forward, spectrum[k * g : (k + 1) * g]))
            work_a[slab_rows(start + k, g), :] = slabs[0]
            work_a[slab_rows(start + k + half, g), :] = slabs[1]

    for kx in range(0, g, 2):
        x = left_complex(forward, beside(strided(work_a, kx, g), strided(work_a, kx + 1, g)))
        x = left_complex(backward, x * beside(coulomb_ref[kx], coulomb_ref[kx + 1]))
        for j, slab in enumerate(halves(x)):
            work_b[slab_rows(kx + j, g), :] = slab

    for start in range(0, half, PAIRS):
        slabs = [
            left_complex(backward, beside(strided(work_b, pair, g), strided(work_b, pair + half, g)))
            for pair in range(start, start + PAIRS)
        ]
        emit(start, *halves(right([jnp.concatenate(slabs, 0)], z_backward)))


def near_kernel(g, phi_ref, other_ref, *refs):
    tables, (sum_ref, work_a, work_b) = refs[:5], refs[5:]

    def emit(start, own, other):
        rows = slab_rows(start, g, PAIRS)
        sum_ref[rows, :] = own * phi_ref[rows, :] + other * other_ref[rows, :]

    potentials(g, phi_ref, phi_ref, other_ref, tables, work_a, work_b, emit)


def middle_kernel(g, phi_ref, first_ref, second_ref, before_ref, *refs):
    tables, (sum_ref, work_a, work_b) = refs[:5], refs[5:]

    def emit(start, first, second):
        rows = slab_rows(start, g, PAIRS)
        sum_ref[rows, :] = before_ref[rows, :] + first * first_ref[rows, :] + second * second_ref[rows, :]

    potentials(g, phi_ref, first_ref, second_ref, tables, work_a, work_b, emit)


def far_kernel(g, weights, phi_ref, first_ref, second_ref, before_ref, columns_ref, stick_out_ref, *refs):
    tables, (out_ref, work_a, work_b, parts_ref) = refs[:5], refs[5:]
    forward = tables[0][...].astype(BF16)
    half = g // 2

    def emit(start, first, second):
        rows = slab_rows(start, g, PAIRS)
        total = before_ref[rows, :] + weights[0] * (first * first_ref[rows, :])
        total = total + weights[1] * (second * second_ref[rows, :])
        for k in range(0, PAIRS, 2):
            cos, sin = left(forward, beside(total[k * g : (k + 1) * g], total[(k + 1) * g : (k + 2) * g]))
            low = lane_halves(cos.shape)
            lower, upper = halves(jnp.where(low, cos, turned(sin))), halves(jnp.where(low, turned(cos), sin))
            for j in range(2):
                work_a[slab_rows(start + k + j, g), :] = lower[j]
                work_a[slab_rows(start + k + j + half, g), :] = upper[j]

    potentials(g, phi_ref, first_ref, second_ref, tables, work_a, work_b, emit)

    for first in range(0, g, 2 * PAIRS):
        slabs = []
        for kx in range(first, first + 2 * PAIRS, 2):
            slabs += halves(left_complex(forward, beside(strided(work_a, kx, g), strided(work_a, kx + 1, g))))
        lined = jnp.concatenate(slabs, 0).T
        lined = jnp.concatenate([lined[:g], lined[MID : MID + g]], 0)
        parts_ref[:, first * g : (first + 2 * PAIRS) * g] = jnp.concatenate(split(lined), 0)

    parts = parts_ref[...]
    stick_out = stick_out_ref[...].astype(BF16)
    for k in range(0, out_ref.shape[0], 2):
        hot = one_hot(columns_ref[:1, k * LANES : (k + 2) * LANES], 0, g * g)
        both = dot(parts, hot)
        picked = both[: 2 * g] + both[2 * g :]
        out_ref[k], out_ref[k + 1] = halves(dot(stick_out, stacked(picked)))


def call(kernel, out_shapes, scratch, flops, *operands):
    vmem = pl.BlockSpec(memory_space=pltpu.VMEM)
    moved = sum(x.size * x.dtype.itemsize for x in operands)
    return pl.pallas_call(
        kernel,
        out_shape=out_shapes,
        in_specs=[vmem] * len(operands),
        out_specs=jax.tree.map(lambda _: vmem, out_shapes),
        scratch_shapes=scratch,
        compiler_params=pltpu.CompilerParams(vmem_limit_bytes=40 * 2**20),
        cost_estimate=pl.CostEstimate(flops=flops, bytes_accessed=moved, transcendentals=0),
    )(*operands)


def exchanged(blocks):
    return lax.all_to_all(blocks, "stick", split_axis=0, concat_axis=0, tiled=True)


def on_device(sticks, stick_columns):
    g = sticks.shape[1] // 2
    slots = stick_columns.shape[0]
    owners = lax.axis_size("stick")
    groups = lax.axis_size("band")
    t = {name: jnp.asarray(value) for name, value in make_tables(g).items()}
    rows = g * g
    field = jax.ShapeDtypeStruct((rows // 2, LANES), F32)
    work = pltpu.VMEM((rows, LANES), F32)
    pot_flops = 6 * 2 * rows * 256 * 256

    def shifted(x, distance):
        return lax.ppermute(x, "band", [(i, (i - distance) % groups) for i in range(groups)])

    def swapped(x):
        return lax.ppermute(x, "band", [(i, i ^ 1) for i in range(groups)])

    sent = call(
        functools.partial(send_kernel, g),
        [jax.ShapeDtypeStruct((owners, g + 8, slots), F32), jax.ShapeDtypeStruct((owners, g, slots), F32)],
        [],
        10**6,
        sticks,
        stick_columns[None, :],
    )
    first_tables = lax.optimization_barrier((t["stick_in"], t["backward"], sent[0]))[:2]
    first_tables = call(
        table_kernel, [jax.ShapeDtypeStruct(x.shape, BF16) for x in first_tables], [], 10**9, *first_tables
    )
    distances = (HALF,) if groups == 2 * HALF else (HALF, -HALF)
    own, far = [], {distance: [] for distance in distances}
    for block in sent:
        own.append(exchanged(block))
        for distance in distances:
            far[distance].append(shifted(own[-1], distance))

    def orbital(blocks):
        return call(
            functools.partial(field_kernel, g),
            [field, jax.ShapeDtypeStruct((8, owners * slots), jnp.int32)],
            [work],
            10**9,
            *blocks,
            *first_tables,
        )

    phi, columns = orbital(own)
    near = swapped(phi)
    fields = [orbital(far[distance])[0] for distance in distances]
    pot_tables = [t["forward"], t["backward"], t["z_forward"], t["z_backward"], t["coulomb"]]

    def potential_sum(kernel, *operands):
        return call(functools.partial(kernel, g), field, [work, work], pot_flops, phi, *operands, *pot_tables)

    if groups == 2 * HALF:
        weights = (2.0, 1.0)
        first, second = fields[0], swapped(fields[0])
        near, first = lax.optimization_barrier((near, first))
        total = potential_sum(near_kernel, near)
    else:
        weights = (1.0, 0.0)
        odd = lax.axis_index("band") % 2 == 1
        first = second = swapped(jnp.where(odd, fields[1], fields[0]))
        total = potential_sum(near_kernel, near)
        total = potential_sum(middle_kernel, *fields, total)
    result = call(
        functools.partial(far_kernel, g, weights),
        jax.ShapeDtypeStruct(sticks.shape, F32),
        [work, work, pltpu.VMEM((4 * g, rows), BF16)],
        pot_flops,
        phi,
        first,
        second,
        total,
        columns,
        t["stick_out"],
        *pot_tables,
    )
    return exchanged(result)


def solution(mesh):
    return jax.shard_map(
        on_device,
        mesh=mesh,
        in_specs=(P("band", None, "stick"), P("stick")),
        out_specs=P("band", None, "stick"),
        check_vma=False,
    )
```

```python
import functools
import math

import jax
import jax.numpy as jnp
import numpy as np
from jax import lax
from jax.experimental import pallas as pl
from jax.experimental.pallas import tpu as pltpu
from jax.sharding import PartitionSpec as P

HALF = 2
BOX_LENGTH = 18.0
LANES = 128
MID = 64
PAIRS = 4
FOLD = 3

F32 = jnp.float32
BF16 = jnp.bfloat16


def rounded_parts(table):
    high = table.astype(BF16).astype(np.float64)
    low = (table - high).astype(BF16).astype(np.float64)
    return high, low


def across(table):
    high, low = rounded_parts(table)
    return np.concatenate([high, high, low], 1).astype(np.float32)


def down(table):
    high, low = rounded_parts(table)
    return np.block([[high, low], [high, np.zeros_like(low)]]).astype(np.float32)


def make_tables(g):
    angle = 2.0 * np.pi / g * (np.outer(np.arange(g), np.arange(g)) % g)
    c, s = np.cos(angle), np.sin(angle)
    lower, upper = slice(0, g), slice(MID, MID + g)

    forward, backward, real_back = np.zeros((3, LANES, LANES))
    forward[lower, lower], forward[lower, upper] = c, -s
    forward[upper, lower], forward[upper, upper] = s, c
    backward[lower, lower], backward[lower, upper] = c, s
    backward[upper, lower], backward[upper, upper] = -s, c
    for half in (lower, upper):
        real_back[:, half] = backward[:, lower]
    real_forward = np.zeros((LANES, 2 * LANES))
    real_forward[lower, :LANES] = forward[lower]
    real_forward[upper, LANES:] = forward[lower]

    stick_in = np.zeros((LANES, 2 * g))
    stick_in[lower, :g], stick_in[lower, g:] = c, -s
    stick_in[upper, :g], stick_in[upper, g:] = s, c
    stick_out = np.block([[c, s], [-s, c]]) * g**-1.5

    freq = np.arange(g)
    square = np.minimum(freq, g - freq) ** 2
    total = square[:, None, None] + square[None, :, None] + square[None, None, :]
    unit = (2.0 * math.pi / BOX_LENGTH) ** 2
    kernel = np.where(total > 0, 4.0 * math.pi / (unit * np.maximum(total, 1)), 0.0)
    coulomb = np.zeros((g, g, LANES), np.float32)
    coulomb[:, :, lower] = kernel
    coulomb[:, :, upper] = kernel
    return dict(
        forward=down(forward),
        backward=down(backward),
        last_backward=down(backward / g**3),
        real_back=down(real_back),
        real_forward=down(real_forward),
        stick_in=across(stick_in),
        stick_out=across(stick_out),
        coulomb=coulomb.reshape(g * g, LANES),
    )


def split(x):
    high = x.astype(BF16)
    low = (x - high.astype(F32)).astype(BF16)
    return high, low


def stacked(x):
    high, low = split(x)
    return jnp.concatenate([high, low, high], 0)


def dot(a, b):
    return jnp.dot(a, b, preferred_element_type=F32)


def lane_halves(shape):
    return lax.broadcasted_iota(jnp.int32, shape, 1) % LANES < MID


def turned(x):
    return pltpu.roll(x, MID, 1)


def regrouped(a, b):
    low = lane_halves(a.shape)
    return jnp.where(low, a, turned(b)), jnp.where(low, turned(a), b)


def transposed(a, b):
    g = a.shape[0]
    pad = jnp.zeros((MID - g, LANES), F32)
    both = jnp.concatenate([a, pad, b, pad], 0).T
    return regrouped(both[:g], both[MID : MID + g])


def pairwise(function, slabs):
    results = []
    for k in range(0, len(slabs), 2):
        results += function(slabs[k], slabs[k + 1])
    return results


def beside(a, b):
    return jnp.concatenate([a, b], 1)


def right(x, table):
    both = dot(beside(*split(x)), table)
    width = both.shape[1] // 2
    return both[:, :width] + both[:, width:]


def right_slabs(slabs, table):
    g = slabs[0].shape[0]
    out = right(jnp.concatenate(slabs, 0), table)
    return [out[k : k + g] for k in range(0, out.shape[0], g)]


def strided(ref, first, g):
    return ref[pl.ds(first, g, stride=g), :]


def slab_rows(index, g, count=1):
    return pl.ds(index * g, count * g)


def one_hot(columns, first, rows):
    index = lax.broadcasted_iota(jnp.int16, (rows, columns.shape[1]), 0)
    wanted = (columns - first).astype(jnp.int16)
    return jnp.where(index == wanted, jnp.asarray(1, BF16), jnp.asarray(0, BF16))


def send_kernel(g, sticks_ref, columns_ref, *refs):
    block_refs, (row_ref, sems, row_sem) = refs[:-3], refs[-3:]
    own = lax.axis_index("stick")
    copies = [
        pltpu.make_async_copy(sticks_ref.at[own ^ d], ref.at[pl.ds(0, 2 * g)], sems.at[d])
        for d, ref in enumerate(block_refs)
    ]
    row_copy = pltpu.make_async_copy(columns_ref, row_ref, row_sem)
    row_copy.start()
    for copy in copies:
        copy.start()
    row_copy.wait()
    columns = jnp.broadcast_to(row_ref[...].astype(F32), (8, LANES))
    for ref in block_refs:
        ref[2 * g :, :] = columns
    for copy in copies:
        copy.wait()


def table_kernel(*refs):
    count = len(refs) // 2
    for table_ref, out_ref in zip(refs[:count], refs[count:]):
        out_ref[...] = table_ref[...].astype(BF16)


def place_kernel(*refs):
    own = lax.axis_index("stick")
    out_ref = refs[-1]
    for d, block_ref in enumerate(refs[:-1]):
        out_ref[own ^ d] = block_ref[...]


def folded_parts(parts, g):
    used = lax.broadcasted_iota(jnp.int32, parts[0].shape, 1) % MID < g
    width = g // FOLD
    return [jnp.where(used, parts[k], pltpu.roll(parts[FOLD], g - k * width, 1)) for k in range(FOLD)]


def folded_position(columns, g):
    kx = lax.div(columns, g)
    ky = columns - kx * g
    group, member = lax.div(kx, 2 * FOLD + 2), lax.rem(kx, 2 * FOLD + 2)
    pair, half = lax.div(member, 2), lax.rem(member, 2)
    width = g // FOLD
    piece = lax.div(ky, width)
    last = pair == FOLD
    row = group * FOLD + jnp.where(last, piece, pair)
    lane = half * MID + jnp.where(last, g + ky - piece * width, ky)
    return jnp.where(columns < 0, -1, row * LANES + lane)


def fold(field_ref, folded_ref, g):
    rows = folded_ref.shape[0] // FOLD
    parts = [field_ref[k * rows : (k + 1) * rows, :] for k in range(FOLD + 1)]
    folded_ref[...] = jnp.concatenate(folded_parts(parts, g), 0)


def unfold(folded_ref, field_ref, g):
    rows = folded_ref.shape[0] // FOLD
    lane = lax.broadcasted_iota(jnp.int32, (rows, LANES), 1) % MID
    width = g // FOLD
    last = None
    for k in range(FOLD):
        part = folded_ref[k * rows : (k + 1) * rows, :]
        field_ref[k * rows : (k + 1) * rows, :] = part
        piece = pltpu.roll(part, LANES - (g - k * width), 1)
        last = piece if last is None else jnp.where(lane >= k * width, piece, last)
    field_ref[FOLD * rows :, :] = last


def store(ref, first, slabs):
    g = slabs[0].shape[0]
    for k, slab in enumerate(slabs):
        ref[slab_rows(first + k, g), :] = slab


def field_kernel(g, count, *refs):
    received = refs[:count]
    stick_in_ref, backward_ref, real_back_ref, phi_ref, folded_ref, positions_ref, work_a = refs[count:]
    columns = jnp.concatenate([ref[2 * g : 2 * g + 1, :] for ref in received], 1).astype(jnp.int32)
    positions_ref[...] = jnp.broadcast_to(folded_position(columns, g), positions_ref.shape)
    stick_in, backward, real_back = stick_in_ref[...], backward_ref[...], real_back_ref[...]
    pieces = []
    for k in range(0, count, 2):
        block = beside(received[k][: 2 * g, :], received[k + 1][: 2 * g, :])
        pieces.append(beside(*split(dot(stick_in, stacked(block)).T)))
    sticks = jnp.concatenate(pieces, 0)

    step = g // 4
    for first in range(0, g, step):
        both = dot(one_hot(columns, first * g, step * g), sticks)
        placed = both[:, :LANES] + both[:, LANES:]
        slabs = pairwise(transposed, [placed[k * g : (k + 1) * g] for k in range(step)])
        store(work_a, first, right_slabs(slabs, backward))

    half = g // 2
    for start in range(0, half, PAIRS):
        slabs = []
        for z in range(start, start + PAIRS):
            slabs += transposed(strided(work_a, z, g), strided(work_a, z + half, g))
        slabs = right_slabs(slabs, real_back)
        low = lane_halves(slabs[0].shape)
        store(phi_ref, start, pairwise(lambda a, b: [jnp.where(low, a, b)], slabs))
    fold(phi_ref, folded_ref, g)


def potentials(g, phi_ref, first_ref, second_ref, tables, work_a, work_b, emit):
    forward, backward, last_backward = [ref[...].astype(BF16) for ref in tables[:3]]
    coulomb_ref = tables[3]
    half = g // 2
    for start in range(0, half, PAIRS):
        rows = slab_rows(start, g, PAIRS)
        phi = phi_ref[rows, :]
        lower, upper = regrouped(phi * first_ref[rows, :], phi * second_ref[rows, :])
        spectrum = right(jnp.concatenate([lower, upper], 0), forward)
        slabs = pairwise(transposed, [spectrum[k * g : (k + 1) * g] for k in range(2 * PAIRS)])
        slabs = right_slabs(slabs, forward)
        store(work_a, start, slabs[:PAIRS])
        store(work_a, start + half, slabs[PAIRS:])

    for first in range(0, g, 2 * PAIRS):
        slabs = pairwise(transposed, [strided(work_a, first + k, g) for k in range(2 * PAIRS)])
        spectrum = right(jnp.concatenate(slabs, 0), forward) * coulomb_ref[slab_rows(first, g, 2 * PAIRS), :]
        spectrum = right(spectrum, backward)
        slabs = pairwise(transposed, [spectrum[k * g : (k + 1) * g] for k in range(2 * PAIRS)])
        store(work_b, first, right_slabs(slabs, backward))

    for start in range(0, half, PAIRS):
        slabs = [strided(work_b, start + k, g) for k in range(PAIRS)]
        slabs += [strided(work_b, start + k + half, g) for k in range(PAIRS)]
        out = right(jnp.concatenate(pairwise(transposed, slabs), 0), last_backward)
        emit(start, *regrouped(out[: PAIRS * g], out[PAIRS * g :]))


def near_kernel(g, phi_ref, near_ref, *refs):
    tables, (sum_ref, other_ref, work_a, work_b) = refs[:4], refs[4:]
    unfold(near_ref, other_ref, g)

    def emit(start, own, other):
        rows = slab_rows(start, g, PAIRS)
        sum_ref[rows, :] = own * phi_ref[rows, :] + other * other_ref[rows, :]

    potentials(g, phi_ref, phi_ref, other_ref, tables, work_a, work_b, emit)


def middle_kernel(g, phi_ref, ahead_ref, behind_ref, before_ref, *refs):
    tables, (sum_ref, first_ref, second_ref, work_a, work_b) = refs[:4], refs[4:]
    unfold(ahead_ref, first_ref, g)
    unfold(behind_ref, second_ref, g)

    def emit(start, first, second):
        rows = slab_rows(start, g, PAIRS)
        sum_ref[rows, :] = before_ref[rows, :] + first * first_ref[rows, :] + second * second_ref[rows, :]

    potentials(g, phi_ref, first_ref, second_ref, tables, work_a, work_b, emit)


def far_kernel(g, weights, phi_ref, ahead_ref, across_ref, before_ref, positions_ref, stick_out_ref, real_forward_ref, *refs):
    tables, out_refs = refs[:4], refs[4:-5]
    first_ref, second_ref, work_a, work_b, parts_ref = refs[-5:]
    unfold(ahead_ref, first_ref, g)
    unfold(across_ref, second_ref, g)
    forward, real_forward = tables[0][...].astype(BF16), real_forward_ref[...].astype(BF16)
    half = g // 2

    def emit(start, first, second):
        rows = slab_rows(start, g, PAIRS)
        total = before_ref[rows, :] + weights[0] * (first * first_ref[rows, :])
        total = total + weights[1] * (second * second_ref[rows, :])
        spectrum = right(total, real_forward)
        spectrum = jnp.concatenate([spectrum[:, :LANES], spectrum[:, LANES:]], 0)
        slabs = pairwise(transposed, [spectrum[k * g : (k + 1) * g] for k in range(2 * PAIRS)])
        slabs = right_slabs(slabs, forward)
        store(work_a, start, slabs[:PAIRS])
        store(work_a, start + half, slabs[PAIRS:])

    potentials(g, phi_ref, first_ref, second_ref, tables, work_a, work_b, emit)

    many = 2 * FOLD + 2
    width = FOLD * LANES
    for group in range(g // many):
        parts = []
        for kx in range(group * many, (group + 1) * many, 2):
            parts.append(jnp.concatenate(regrouped(strided(work_a, kx, g), strided(work_a, kx + 1, g)), 0))
        line = jnp.concatenate(folded_parts(parts, g), 1)
        parts_ref[:, group * width : (group + 1) * width] = jnp.concatenate(split(line), 0)

    parts = parts_ref[...]
    stick_out = stick_out_ref[...].astype(BF16)
    for k in range(0, len(out_refs), 2):
        hot = one_hot(positions_ref[:1, k * LANES : (k + 2) * LANES], 0, g * g)
        both = dot(parts, hot)
        picked = dot(stick_out, stacked(both[: 2 * g] + both[2 * g :]))
        out_refs[k][...], out_refs[k + 1][...] = picked[:, :LANES], picked[:, LANES:]


def call(kernel, out_shapes, scratch, flops, *operands, space=pltpu.VMEM):
    vmem = pl.BlockSpec(memory_space=pltpu.VMEM)
    moved = sum(x.size * x.dtype.itemsize for x in operands)
    return pl.pallas_call(
        kernel,
        out_shape=out_shapes,
        in_specs=[pl.BlockSpec(memory_space=space)] * len(operands),
        out_specs=jax.tree.map(lambda _: vmem, out_shapes),
        scratch_shapes=scratch,
        compiler_params=pltpu.CompilerParams(vmem_limit_bytes=40 * 2**20),
        cost_estimate=pl.CostEstimate(flops=flops, bytes_accessed=moved, transcendentals=0),
    )(*operands)


def exchanged(blocks):
    owners = len(blocks)
    moved = {}
    for d in range(owners - 1, 0, -1):
        moved[d] = lax.ppermute(blocks[d], "stick", [(i, i ^ d) for i in range(owners)])
    return [blocks[0]] + [moved[d] for d in range(1, owners)]


def on_device(sticks, stick_columns):
    g = sticks.shape[1] // 2
    slots = stick_columns.shape[0]
    owners = lax.axis_size("stick")
    groups = lax.axis_size("band")
    t = {name: jnp.asarray(value) for name, value in make_tables(g).items()}
    rows = g * g
    field = jax.ShapeDtypeStruct((rows // 2, LANES), F32)
    folded = jax.ShapeDtypeStruct((rows // 2 * FOLD // (FOLD + 1), LANES), F32)
    field_scratch = pltpu.VMEM((rows // 2, LANES), F32)
    work = pltpu.VMEM((rows, LANES), F32)
    pot_flops = 6 * 2 * rows * 256 * 256

    sent = call(
        functools.partial(send_kernel, g),
        [jax.ShapeDtypeStruct((2 * g + 8, slots), F32)] * owners,
        [pltpu.VMEM((1, slots), jnp.int32), pltpu.SemaphoreType.DMA((owners,)), pltpu.SemaphoreType.DMA],
        10**6,
        sticks,
        stick_columns[None, :],
        space=pltpu.HBM,
    )
    received = exchanged(sent)
    first_tables = lax.optimization_barrier((t["stick_in"], t["backward"], t["real_back"], sent[0]))[:3]
    first_tables = call(
        table_kernel, [jax.ShapeDtypeStruct(x.shape, BF16) for x in first_tables], [], 10**9, *first_tables
    )
    phi, packed, positions = call(
        functools.partial(field_kernel, g, owners),
        [field, folded, jax.ShapeDtypeStruct((8, owners * slots), jnp.int32)],
        [work],
        10**9,
        *received,
        *first_tables,
    )
    pot_tables = [t["forward"], t["backward"], t["last_backward"], t["coulomb"]]
    swap = [(i, i ^ 1) for i in range(groups)]

    def fetched(distance):
        return lax.ppermute(packed, "band", [(i, (i - distance) % groups) for i in range(groups)])

    near = lax.ppermute(packed, "band", swap)
    ahead = fetched(HALF)
    total = call(
        functools.partial(near_kernel, g), field, [field_scratch, work, work], pot_flops, phi, near, *pot_tables
    )
    ahead, total = lax.optimization_barrier((ahead, total))
    if groups == 2 * HALF:
        weights = (2.0, 1.0)
        first, second = ahead, lax.ppermute(ahead, "band", swap)
    else:
        weights = (1.0, 0.0)
        behind = fetched(-HALF)
        odd = lax.axis_index("band") % 2 == 1
        first = second = lax.ppermute(jnp.where(odd, behind, ahead), "band", swap)
        total = call(
            functools.partial(middle_kernel, g),
            field,
            [field_scratch, field_scratch, work, work],
            pot_flops,
            phi,
            ahead,
            behind,
            total,
            *pot_tables,
        )
    result = call(
        functools.partial(far_kernel, g, weights),
        [jax.ShapeDtypeStruct((2 * g, slots), F32)] * owners,
        [field_scratch, field_scratch, work, work, pltpu.VMEM((4 * g, rows), BF16)],
        pot_flops,
        phi,
        first,
        second,
        total,
        positions,
        t["stick_out"],
        t["real_forward"],
        *pot_tables,
    )
    return call(place_kernel, jax.ShapeDtypeStruct(sticks.shape, F32), [], 10**6, *exchanged(result))


def solution(mesh):
    return jax.shard_map(
        on_device,
        mesh=mesh,
        in_specs=(P("band", None, "stick"), P("stick")),
        out_specs=P("band", None, "stick"),
        check_vma=False,
    )
```

```python
import functools
import math

import jax
import jax.numpy as jnp
import numpy as np
from jax import lax
from jax.experimental import pallas as pl
from jax.experimental.pallas import tpu as pltpu
from jax.sharding import PartitionSpec as P

HALF = 2
BOX_LENGTH = 18.0
LANES = 128
MID = 64
PAIRS = 4
FOLD = 3

F32 = jnp.float32
BF16 = jnp.bfloat16


def rounded_parts(table):
    high = table.astype(BF16).astype(np.float64)
    low = (table - high).astype(BF16).astype(np.float64)
    return high, low


def across(table):
    high, low = rounded_parts(table)
    return np.concatenate([high, high, low], 1).astype(np.float32)


def down(table):
    high, low = rounded_parts(table)
    return np.concatenate([high, high, low], 0).astype(np.float32)


def make_tables(g):
    angle = 2.0 * np.pi / g * (np.outer(np.arange(g), np.arange(g)) % g)
    c, s = np.cos(angle), np.sin(angle)
    lower, upper = slice(0, g), slice(MID, MID + g)

    z_forward = np.zeros((2 * LANES, 2 * LANES))
    z_backward = np.zeros((2 * LANES, 2 * LANES))
    for slab, half in enumerate((lower, upper)):
        base = slab * LANES
        real, imag = slice(base, base + g), slice(base + MID, base + MID + g)
        one, two = half, slice(LANES + half.start, LANES + half.stop)
        z_forward[one, real], z_forward[one, imag] = c, -s
        z_forward[two, real], z_forward[two, imag] = s, c
        z_backward[real, one], z_backward[real, two] = c, s
        z_backward[imag, one], z_backward[imag, two] = -s, c

    stick_in = np.zeros((LANES, 2 * g))
    stick_in[lower, :g], stick_in[lower, g:] = c, -s
    stick_in[upper, :g], stick_in[upper, g:] = s, c
    stick_out = np.block([[c, s], [-s, c]]) * g**-1.5

    freq = np.arange(g)
    square = np.minimum(freq, g - freq) ** 2
    total = square[:, None, None] + square[None, :, None] + square[None, None, :]
    unit = (2.0 * math.pi / BOX_LENGTH) ** 2
    kernel = np.where(total > 0, 4.0 * math.pi / (unit * np.maximum(total, 1)), 0.0)
    coulomb = np.zeros((g, g, LANES), np.float32)
    coulomb[:, :, lower] = kernel
    coulomb[:, :, upper] = kernel
    return dict(
        forward=across(np.concatenate([c, -s], 0)),
        backward=across(np.concatenate([c, s], 0)),
        z_forward=down(z_forward),
        z_backward=down(z_backward / g**3),
        stick_in=across(stick_in),
        stick_out=across(stick_out),
        coulomb=coulomb,
    )


def split(x):
    high = x.astype(BF16)
    low = (x - high.astype(F32)).astype(BF16)
    return high, low


def stacked(x):
    high, low = split(x)
    return jnp.concatenate([high, low, high], 0)


def dot(a, b):
    return jnp.dot(a, b, preferred_element_type=F32)


def lane_halves(shape):
    return lax.broadcasted_iota(jnp.int32, shape, 1) % LANES < MID


def turned(x):
    return jnp.concatenate(
        [pltpu.roll(x[:, k : k + LANES], MID, 1) for k in range(0, x.shape[1], LANES)], 1
    )


def left(table, x):
    both = dot(table, stacked(x))
    g = both.shape[0] // 2
    return both[:g], both[g:]


def left_complex(table, x):
    cos, sin = left(table, x)
    sign = jnp.where(lane_halves((1, x.shape[1])), -1.0, 1.0)
    return cos + turned(sin) * sign


def halves(x):
    return x[:, :LANES], x[:, LANES:]


def beside(a, b):
    return jnp.concatenate([a, b], 1)


def right(parts, table):
    high, low = zip(*[split(x) for x in parts])
    return dot(jnp.concatenate(high + low + high, 1), table)


def pitch(g):
    return g + 1


def strided(ref, first, g):
    return ref[pl.ds(first, g, stride=pitch(g)), :]


def work_rows(index, g):
    return pl.ds(index * pitch(g), g)


def slab_rows(index, g, count=1):
    return pl.ds(index * g, count * g)


def one_hot(columns, first, rows):
    index = lax.broadcasted_iota(jnp.int16, (rows, columns.shape[1]), 0)
    wanted = (columns - first).astype(jnp.int16)
    return jnp.where(index == wanted, jnp.asarray(1, BF16), jnp.asarray(0, BF16))


def send_kernel(g, sticks_ref, columns_ref, *refs):
    block_refs, (row_ref, sems, row_sem) = refs[:-3], refs[-3:]
    own = lax.axis_index("stick")
    copies = [
        pltpu.make_async_copy(sticks_ref.at[own ^ d], ref.at[pl.ds(0, 2 * g)], sems.at[d])
        for d, ref in enumerate(block_refs)
    ]
    row_copy = pltpu.make_async_copy(columns_ref, row_ref, row_sem)
    row_copy.start()
    for copy in copies:
        copy.start()
    row_copy.wait()
    columns = jnp.broadcast_to(row_ref[...].astype(F32), (8, LANES))
    for ref in block_refs:
        ref[2 * g :, :] = columns
    for copy in copies:
        copy.wait()


def table_kernel(*refs):
    count = len(refs) // 2
    for table_ref, out_ref in zip(refs[:count], refs[count:]):
        out_ref[...] = table_ref[...].astype(BF16)


def place_kernel(*refs):
    own = lax.axis_index("stick")
    out_ref = refs[-1]
    for d, block_ref in enumerate(refs[:-1]):
        out_ref[own ^ d] = block_ref[...]


def fold(field_ref, folded_ref, g):
    rows = folded_ref.shape[0] // FOLD
    used = lax.broadcasted_iota(jnp.int32, (rows, LANES), 1) % MID < g
    last = field_ref[FOLD * rows :, :]
    width = g // FOLD
    for k in range(FOLD):
        part = slice(k * rows, (k + 1) * rows)
        folded_ref[part, :] = jnp.where(used, field_ref[part, :], pltpu.roll(last, g - k * width, 1))


def unfold(folded_ref, field_ref, g):
    rows = folded_ref.shape[0] // FOLD
    lane = lax.broadcasted_iota(jnp.int32, (rows, LANES), 1) % MID
    width = g // FOLD
    last = None
    for k in range(FOLD):
        part = folded_ref[k * rows : (k + 1) * rows, :]
        field_ref[k * rows : (k + 1) * rows, :] = part
        piece = pltpu.roll(part, LANES - (g - k * width), 1)
        last = piece if last is None else jnp.where(lane >= k * width, piece, last)
    field_ref[FOLD * rows :, :] = last


def field_kernel(g, count, *refs):
    received = refs[:count]
    stick_in_ref, backward_ref, phi_ref, folded_ref, columns_ref, work_a = refs[count:]
    columns = jnp.concatenate([ref[2 * g : 2 * g + 1, :] for ref in received], 1).astype(jnp.int32)
    columns_ref[...] = jnp.broadcast_to(columns, columns_ref.shape)
    stick_in, backward = stick_in_ref[...], backward_ref[...]
    pieces = []
    for k in range(0, count, 2):
        block = beside(received[k][: 2 * g, :], received[k + 1][: 2 * g, :])
        pieces.append(beside(*split(dot(stick_in, stacked(block)).T)))
    sticks = jnp.concatenate(pieces, 0)

    for first in range(0, g, 2 * PAIRS):
        both = dot(one_hot(columns, first * g, 2 * PAIRS * g), sticks)
        placed = both[:, :LANES] + both[:, LANES:]
        for k in range(0, 2 * PAIRS, 2):
            x = beside(placed[k * g : (k + 1) * g], placed[(k + 1) * g : (k + 2) * g])
            for j, slab in enumerate(halves(left_complex(backward, x))):
                work_a[work_rows(first + k + j, g), :] = slab

    for pair in range(g // 2):
        x = beside(strided(work_a, pair, g), strided(work_a, pair + g // 2, g))
        (cos, cos_up), (sin, sin_up) = map(halves, left(backward, x))
        lower = cos - pltpu.roll(sin, MID, 1)
        upper = pltpu.roll(cos_up, MID, 1) - sin_up
        phi_ref[slab_rows(pair, g), :] = jnp.where(lane_halves(lower.shape), lower, upper)
    fold(phi_ref, folded_ref, g)


def potentials(g, phi_ref, first_ref, second_ref, tables, work_a, work_b, emit):
    forward, backward, z_forward, z_backward = [ref[...].astype(BF16) for ref in tables[:4]]
    coulomb_ref = tables[4]
    half = g // 2
    for start in range(0, half, PAIRS):
        rows = slab_rows(start, g, PAIRS)
        phi = phi_ref[rows, :]
        spectrum = right([phi * first_ref[rows, :], phi * second_ref[rows, :]], z_forward)
        for k in range(PAIRS):
            slabs = halves(left_complex(forward, spectrum[k * g : (k + 1) * g]))
            work_a[work_rows(start + k, g), :] = slabs[0]
            work_a[work_rows(start + k + half, g), :] = slabs[1]

    for kx in range(0, g, 2):
        x = left_complex(forward, beside(strided(work_a, kx, g), strided(work_a, kx + 1, g)))
        x = left_complex(backward, x * beside(coulomb_ref[kx], coulomb_ref[kx + 1]))
        for j, slab in enumerate(halves(x)):
            work_b[work_rows(kx + j, g), :] = slab

    for start in range(0, half, PAIRS):
        slabs = [
            left_complex(backward, beside(strided(work_b, pair, g), strided(work_b, pair + half, g)))
            for pair in range(start, start + PAIRS)
        ]
        emit(start, *halves(right([jnp.concatenate(slabs, 0)], z_backward)))


def near_kernel(g, phi_ref, near_ref, *refs):
    tables, (sum_ref, other_ref, work_a, work_b) = refs[:5], refs[5:]
    unfold(near_ref, other_ref, g)

    def emit(start, own, other):
        rows = slab_rows(start, g, PAIRS)
        sum_ref[rows, :] = own * phi_ref[rows, :] + other * other_ref[rows, :]

    potentials(g, phi_ref, phi_ref, other_ref, tables, work_a, work_b, emit)


def middle_kernel(g, phi_ref, ahead_ref, behind_ref, before_ref, *refs):
    tables, (sum_ref, first_ref, second_ref, work_a, work_b) = refs[:5], refs[5:]
    unfold(ahead_ref, first_ref, g)
    unfold(behind_ref, second_ref, g)

    def emit(start, first, second):
        rows = slab_rows(start, g, PAIRS)
        sum_ref[rows, :] = before_ref[rows, :] + first * first_ref[rows, :] + second * second_ref[rows, :]

    potentials(g, phi_ref, first_ref, second_ref, tables, work_a, work_b, emit)


def far_kernel(g, weights, phi_ref, ahead_ref, across_ref, before_ref, columns_ref, stick_out_ref, *refs):
    tables, out_refs = refs[:5], refs[5:-5]
    first_ref, second_ref, work_a, work_b, parts_ref = refs[-5:]
    unfold(ahead_ref, first_ref, g)
    unfold(across_ref, second_ref, g)
    forward = tables[0][...].astype(BF16)
    half = g // 2

    def emit(start, first, second):
        rows = slab_rows(start, g, PAIRS)
        total = before_ref[rows, :] + weights[0] * (first * first_ref[rows, :])
        total = total + weights[1] * (second * second_ref[rows, :])
        for k in range(0, PAIRS, 2):
            cos, sin = left(forward, beside(total[k * g : (k + 1) * g], total[(k + 1) * g : (k + 2) * g]))
            low = lane_halves(cos.shape)
            lower, upper = halves(jnp.where(low, cos, turned(sin))), halves(jnp.where(low, turned(cos), sin))
            for j in range(2):
                work_a[work_rows(start + k + j, g), :] = lower[j]
                work_a[work_rows(start + k + j + half, g), :] = upper[j]

    potentials(g, phi_ref, first_ref, second_ref, tables, work_a, work_b, emit)

    for first in range(0, g, 2 * PAIRS):
        slabs = []
        for kx in range(first, first + 2 * PAIRS, 2):
            slabs += halves(left_complex(forward, beside(strided(work_a, kx, g), strided(work_a, kx + 1, g))))
        lined = jnp.concatenate(slabs, 0).T
        lined = jnp.concatenate([lined[:g], lined[MID : MID + g]], 0)
        parts_ref[:, first * g : (first + 2 * PAIRS) * g] = jnp.concatenate(split(lined), 0)

    parts = parts_ref[...]
    stick_out = stick_out_ref[...].astype(BF16)
    for k in range(0, len(out_refs), 2):
        hot = one_hot(columns_ref[:1, k * LANES : (k + 2) * LANES], 0, g * g)
        both = dot(parts, hot)
        picked = both[: 2 * g] + both[2 * g :]
        out_refs[k][...], out_refs[k + 1][...] = halves(dot(stick_out, stacked(picked)))


def call(kernel, out_shapes, scratch, flops, *operands, space=pltpu.VMEM):
    vmem = pl.BlockSpec(memory_space=pltpu.VMEM)
    moved = sum(x.size * x.dtype.itemsize for x in operands)
    return pl.pallas_call(
        kernel,
        out_shape=out_shapes,
        in_specs=[pl.BlockSpec(memory_space=space)] * len(operands),
        out_specs=jax.tree.map(lambda _: vmem, out_shapes),
        scratch_shapes=scratch,
        compiler_params=pltpu.CompilerParams(vmem_limit_bytes=40 * 2**20),
        cost_estimate=pl.CostEstimate(flops=flops, bytes_accessed=moved, transcendentals=0),
    )(*operands)


def exchanged(blocks):
    owners = len(blocks)
    moved = {}
    for d in range(owners - 1, 0, -1):
        moved[d] = lax.ppermute(blocks[d], "stick", [(i, i ^ d) for i in range(owners)])
    return [blocks[0]] + [moved[d] for d in range(1, owners)]


def on_device(sticks, stick_columns):
    g = sticks.shape[1] // 2
    slots = stick_columns.shape[0]
    owners = lax.axis_size("stick")
    groups = lax.axis_size("band")
    t = {name: jnp.asarray(value) for name, value in make_tables(g).items()}
    rows = g * g
    field = jax.ShapeDtypeStruct((rows // 2, LANES), F32)
    folded = jax.ShapeDtypeStruct((rows // 2 * FOLD // (FOLD + 1), LANES), F32)
    field_scratch = pltpu.VMEM((rows // 2, LANES), F32)
    work = pltpu.VMEM((g * pitch(g), LANES), F32)
    pot_flops = 6 * 2 * rows * 256 * 256

    sent = call(
        functools.partial(send_kernel, g),
        [jax.ShapeDtypeStruct((2 * g + 8, slots), F32)] * owners,
        [pltpu.VMEM((1, slots), jnp.int32), pltpu.SemaphoreType.DMA((owners,)), pltpu.SemaphoreType.DMA],
        10**6,
        sticks,
        stick_columns[None, :],
        space=pltpu.HBM,
    )
    received = exchanged(sent)
    first_tables = lax.optimization_barrier((t["stick_in"], t["backward"], sent[0]))[:2]
    first_tables = call(
        table_kernel, [jax.ShapeDtypeStruct(x.shape, BF16) for x in first_tables], [], 10**9, *first_tables
    )
    phi, packed, columns = call(
        functools.partial(field_kernel, g, owners),
        [field, folded, jax.ShapeDtypeStruct((8, owners * slots), jnp.int32)],
        [work],
        10**9,
        *received,
        *first_tables,
    )
    pot_tables = [t["forward"], t["backward"], t["z_forward"], t["z_backward"], t["coulomb"]]
    swap = [(i, i ^ 1) for i in range(groups)]

    def fetched(distance):
        return lax.ppermute(packed, "band", [(i, (i - distance) % groups) for i in range(groups)])

    near = lax.ppermute(packed, "band", swap)
    ahead = fetched(HALF)
    total = call(
        functools.partial(near_kernel, g), field, [field_scratch, work, work], pot_flops, phi, near, *pot_tables
    )
    ahead, total = lax.optimization_barrier((ahead, total))
    if groups == 2 * HALF:
        weights = (2.0, 1.0)
        first, second = ahead, lax.ppermute(ahead, "band", swap)
    else:
        weights = (1.0, 0.0)
        behind = fetched(-HALF)
        odd = lax.axis_index("band") % 2 == 1
        first = second = lax.ppermute(jnp.where(odd, behind, ahead), "band", swap)
        total = call(
            functools.partial(middle_kernel, g),
            field,
            [field_scratch, field_scratch, work, work],
            pot_flops,
            phi,
            ahead,
            behind,
            total,
            *pot_tables,
        )
    result = call(
        functools.partial(far_kernel, g, weights),
        [jax.ShapeDtypeStruct((2 * g, slots), F32)] * owners,
        [field_scratch, field_scratch, work, work, pltpu.VMEM((4 * g, rows), BF16)],
        pot_flops,
        phi,
        first,
        second,
        total,
        columns,
        t["stick_out"],
        *pot_tables,
    )
    return call(place_kernel, jax.ShapeDtypeStruct(sticks.shape, F32), [], 10**6, *exchanged(result))


def solution(mesh):
    return jax.shard_map(
        on_device,
        mesh=mesh,
        in_specs=(P("band", None, "stick"), P("stick")),
        out_specs=P("band", None, "stick"),
        check_vma=False,
    )
```

```python
import functools
import math

import jax
import jax.numpy as jnp
import numpy as np
from jax import lax
from jax.experimental import pallas as pl
from jax.experimental.pallas import tpu as pltpu
from jax.sharding import PartitionSpec as P

HALF = 2
BOX_LENGTH = 18.0
LANES = 128
MID = 64
PAIRS = 6
FOLD = 3

F32 = jnp.float32
BF16 = jnp.bfloat16


def rounded_parts(table):
    high = table.astype(BF16).astype(np.float64)
    low = (table - high).astype(BF16).astype(np.float64)
    return high, low


def across(table):
    high, low = rounded_parts(table)
    return np.concatenate([high, high, low], 1).astype(np.float32)


def down(table):
    high, low = rounded_parts(table)
    return np.block([[high, low], [high, np.zeros_like(low)]]).astype(np.float32)


def make_tables(g):
    angle = 2.0 * np.pi / g * (np.outer(np.arange(g), np.arange(g)) % g)
    c, s = np.cos(angle), np.sin(angle)
    lower, upper = slice(0, g), slice(MID, MID + g)

    forward, backward = np.zeros((2, LANES, LANES))
    forward[lower, lower], forward[lower, upper] = c, -s
    forward[upper, lower], forward[upper, upper] = s, c
    backward[lower, lower], backward[lower, upper] = c, s
    backward[upper, lower], backward[upper, upper] = -s, c
    real_forward = np.zeros((LANES, 2 * LANES))
    real_forward[lower, :LANES] = forward[lower]
    real_forward[upper, LANES:] = forward[lower]

    stick_in = np.block([[c, -s], [s, c]])
    stick_out = np.block([[c, s], [-s, c]]) * g**-1.5

    freq = np.arange(g)
    square = np.minimum(freq, g - freq) ** 2
    total = square[:, None, None] + square[None, :, None] + square[None, None, :]
    unit = (2.0 * math.pi / BOX_LENGTH) ** 2
    kernel = np.where(total > 0, 4.0 * math.pi / (unit * np.maximum(total, 1)), 0.0)
    coulomb = np.zeros((g, g, LANES), np.float32)
    coulomb[:, :, lower] = kernel
    coulomb[:, :, upper] = kernel
    return dict(
        forward=down(forward),
        backward=down(backward),
        last_backward=down(backward / g**3),
        left_forward=across(np.concatenate([c, -s], 0)),
        left_backward=across(np.concatenate([c, s], 0)),
        real_forward=down(real_forward),
        stick_in=across(stick_in),
        stick_out=across(stick_out),
        coulomb=coulomb.reshape(g * g, LANES),
    )


def split(x):
    high = x.astype(BF16)
    low = (x - high.astype(F32)).astype(BF16)
    return high, low


def stacked(x):
    high, low = split(x)
    return jnp.concatenate([high, low, high], 0)


def dot(a, b):
    return jnp.dot(a, b, preferred_element_type=F32)


def lane_halves(shape):
    return lax.broadcasted_iota(jnp.int32, shape, 1) % LANES < MID


def turned(x):
    return pltpu.roll(x, MID, 1)


def regrouped(a, b):
    low = lane_halves(a.shape)
    return jnp.where(low, a, turned(b)), jnp.where(low, turned(a), b)


def transposed(a, b):
    g = a.shape[0]
    pad = jnp.zeros((MID - g, LANES), F32)
    both = jnp.concatenate([a, pad, b, pad], 0).T
    return regrouped(both[:g], both[MID : MID + g])


def pairwise(function, slabs):
    results = []
    for k in range(0, len(slabs), 2):
        results += function(slabs[k], slabs[k + 1])
    return results


def beside(a, b):
    return jnp.concatenate([a, b], 1)


def halves(x):
    return x[:, :LANES], x[:, LANES:]


def left(table, x):
    both = dot(table, stacked(x))
    g = both.shape[0] // 2
    return both[:g], both[g:]


def left_complex(table, a, b):
    cos, sin = left(table, beside(a, b))
    sign = jnp.where(lane_halves((1, LANES)), -1.0, 1.0)
    return [p + turned(q) * sign for p, q in zip(halves(cos), halves(sin))]


def right(x, table):
    both = dot(beside(*split(x)), table)
    width = both.shape[1] // 2
    return both[:, :width] + both[:, width:]


def right_slabs(slabs, table):
    g = slabs[0].shape[0]
    out = right(jnp.concatenate(slabs, 0), table)
    return [out[k : k + g] for k in range(0, out.shape[0], g)]


def strided(ref, first, g):
    return ref[pl.ds(first, g, stride=g), :]


def slab_rows(index, g, count=1):
    return pl.ds(index * g, count * g)


def one_hot(columns, first, rows):
    index = lax.broadcasted_iota(jnp.int16, (rows, columns.shape[1]), 0)
    wanted = (columns - first).astype(jnp.int16)
    return jnp.where(index == wanted, jnp.asarray(1, BF16), jnp.asarray(0, BF16))


def send_kernel(g, sticks_ref, columns_ref, *refs):
    block_refs, (row_ref, sems, row_sem) = refs[:-3], refs[-3:]
    own = lax.axis_index("stick")
    copies = [
        pltpu.make_async_copy(sticks_ref.at[own ^ d], ref.at[pl.ds(0, 2 * g)], sems.at[d])
        for d, ref in enumerate(block_refs)
    ]
    row_copy = pltpu.make_async_copy(columns_ref, row_ref, row_sem)
    row_copy.start()
    for copy in copies:
        copy.start()
    row_copy.wait()
    columns = jnp.broadcast_to(row_ref[...].astype(F32), (8, LANES))
    for ref in block_refs:
        ref[2 * g :, :] = columns
    for copy in copies:
        copy.wait()


def table_kernel(*refs):
    count = len(refs) // 2
    for table_ref, out_ref in zip(refs[:count], refs[count:]):
        out_ref[...] = table_ref[...].astype(BF16)


def place_kernel(*refs):
    own = lax.axis_index("stick")
    out_ref = refs[-1]
    for d, block_ref in enumerate(refs[:-1]):
        out_ref[own ^ d] = block_ref[...]


def folded_parts(parts, g):
    used = lax.broadcasted_iota(jnp.int32, parts[0].shape, 1) % MID < g
    width = g // FOLD
    return [jnp.where(used, parts[k], pltpu.roll(parts[FOLD], g - k * width, 1)) for k in range(FOLD)]


def folded_position(columns, g):
    kx = lax.div(columns, g)
    ky = columns - kx * g
    group, member = lax.div(ky, 2 * FOLD + 2), lax.rem(ky, 2 * FOLD + 2)
    pair, half = lax.div(member, 2), lax.rem(member, 2)
    width = g // FOLD
    piece = lax.div(kx, width)
    last = pair == FOLD
    row = group * FOLD + jnp.where(last, piece, pair)
    lane = half * MID + jnp.where(last, g + kx - piece * width, kx)
    return jnp.where(columns < 0, -1, row * LANES + lane)


def paired_position(columns, g):
    kx = lax.div(columns, g)
    return jnp.where(columns < 0, -1, lax.div(kx, 2) * LANES + lax.rem(kx, 2) * MID + columns - kx * g)


def fold(field_ref, folded_ref, g):
    rows = folded_ref.shape[0] // FOLD
    parts = [field_ref[k * rows : (k + 1) * rows, :] for k in range(FOLD + 1)]
    folded_ref[...] = jnp.concatenate(folded_parts(parts, g), 0)


def unfold(folded_ref, field_ref, g):
    rows = folded_ref.shape[0] // FOLD
    lane = lax.broadcasted_iota(jnp.int32, (rows, LANES), 1) % MID
    width = g // FOLD
    last = None
    for k in range(FOLD):
        part = folded_ref[k * rows : (k + 1) * rows, :]
        field_ref[k * rows : (k + 1) * rows, :] = part
        piece = pltpu.roll(part, LANES - (g - k * width), 1)
        last = piece if last is None else jnp.where(lane >= k * width, piece, last)
    field_ref[FOLD * rows :, :] = last


def store(ref, first, slabs):
    g = slabs[0].shape[0]
    for k, slab in enumerate(slabs):
        ref[slab_rows(first + k, g), :] = slab


def field_kernel(g, count, *refs):
    received = refs[:count]
    stick_in_ref, backward_ref, left_ref, phi_ref, folded_ref, positions_ref, work_a = refs[count:]
    columns = jnp.concatenate([ref[2 * g : 2 * g + 1, :] for ref in received], 1).astype(jnp.int32)
    positions_ref[...] = jnp.broadcast_to(folded_position(columns, g), positions_ref.shape)
    stick_in, backward, left_backward = stick_in_ref[...], backward_ref[...], left_ref[...]
    sticks, rows = [], []
    for k in range(0, count, 2):
        block = beside(received[k][: 2 * g, :], received[k + 1][: 2 * g, :])
        sticks.append(jnp.concatenate(split(dot(stick_in, stacked(block))), 0))
        for ref in received[k : k + 2]:
            ids = paired_position(ref[2 * g : 2 * g + 8, :].astype(jnp.int32), g).astype(F32)
            ids = jnp.concatenate([ids] * (LANES // 8), 0).T
            rows.append(jnp.concatenate([ids, ids], 1).astype(jnp.int32).astype(jnp.int16))
    sticks = jnp.concatenate(sticks, 1)
    rows = jnp.concatenate(rows, 0)

    lane = lax.broadcasted_iota(jnp.int16, rows.shape, 1)
    step = 2 * PAIRS
    for first in range(0, g, step):
        slabs = []
        for kx in range(first, first + step, 4):
            start = jnp.asarray(kx // 2 * LANES, jnp.int16)
            hot = jnp.where(rows == lane + start, jnp.asarray(1, BF16), jnp.asarray(0, BF16))
            both = dot(sticks, hot)
            placed = both[: 2 * g] + both[2 * g :]
            for part in halves(placed):
                slabs += regrouped(part[:g], part[g:])
        store(work_a, first, right_slabs(slabs, backward))

    half = g // 2
    for z in range(half):
        x = beside(strided(work_a, z, g), strided(work_a, z + half, g))
        (cos, cos_up), (sin, sin_up) = map(halves, left(left_backward, x))
        low = lane_halves(cos.shape)
        store(phi_ref, z, [jnp.where(low, cos - turned(sin), turned(cos_up) - sin_up)])
    fold(phi_ref, folded_ref, g)


def potentials(g, phi_ref, first_ref, second_ref, tables, work_a, work_b, emit):
    forward, last_backward, left_forward, left_backward = [ref[...].astype(BF16) for ref in tables[:4]]
    coulomb_ref = tables[4]
    half = g // 2
    for start in range(0, half, PAIRS):
        rows = slab_rows(start, g, PAIRS)
        phi = phi_ref[rows, :]
        lower, upper = regrouped(phi * first_ref[rows, :], phi * second_ref[rows, :])
        spectrum = right(jnp.concatenate([lower, upper], 0), forward)
        for k in range(PAIRS):
            a, b = left_complex(left_forward, *(spectrum[j * g : (j + 1) * g] for j in (k, k + PAIRS)))
            store(work_a, start + k, [a])
            store(work_a, start + k + half, [b])

    for kx in range(0, g, 2):
        slabs = left_complex(left_forward, strided(work_a, kx, g), strided(work_a, kx + 1, g))
        slabs = [slab * coulomb_ref[slab_rows(kx + j, g), :] for j, slab in enumerate(slabs)]
        store(work_b, kx, left_complex(left_backward, *slabs))

    for start in range(0, half, PAIRS):
        lower, upper = [], []
        for z in range(start, start + PAIRS):
            a, b = left_complex(left_backward, strided(work_b, z, g), strided(work_b, z + half, g))
            lower.append(a)
            upper.append(b)
        out = right(jnp.concatenate(lower + upper, 0), last_backward)
        emit(start, *regrouped(out[: PAIRS * g], out[PAIRS * g :]))


def near_kernel(g, phi_ref, near_ref, *refs):
    tables, (sum_ref, other_ref, work_a, work_b) = refs[:5], refs[5:]
    unfold(near_ref, other_ref, g)

    def emit(start, own, other):
        rows = slab_rows(start, g, PAIRS)
        sum_ref[rows, :] = own * phi_ref[rows, :] + other * other_ref[rows, :]

    potentials(g, phi_ref, phi_ref, other_ref, tables, work_a, work_b, emit)


def middle_kernel(g, phi_ref, ahead_ref, behind_ref, before_ref, *refs):
    tables, (sum_ref, first_ref, second_ref, work_a, work_b) = refs[:5], refs[5:]
    unfold(ahead_ref, first_ref, g)
    unfold(behind_ref, second_ref, g)

    def emit(start, first, second):
        rows = slab_rows(start, g, PAIRS)
        sum_ref[rows, :] = before_ref[rows, :] + first * first_ref[rows, :] + second * second_ref[rows, :]

    potentials(g, phi_ref, first_ref, second_ref, tables, work_a, work_b, emit)


def far_kernel(g, weights, phi_ref, ahead_ref, across_ref, before_ref, positions_ref, stick_out_ref, real_forward_ref, *refs):
    tables, out_refs = refs[:5], refs[5:-5]
    first_ref, second_ref, work_a, work_b, parts_ref = refs[-5:]
    unfold(ahead_ref, first_ref, g)
    unfold(across_ref, second_ref, g)
    forward, real_forward = tables[0][...].astype(BF16), real_forward_ref[...].astype(BF16)
    half = g // 2

    def emit(start, first, second):
        rows = slab_rows(start, g, PAIRS)
        total = before_ref[rows, :] + weights[0] * (first * first_ref[rows, :])
        total = total + weights[1] * (second * second_ref[rows, :])
        spectrum = right(total, real_forward)
        spectrum = jnp.concatenate([spectrum[:, :LANES], spectrum[:, LANES:]], 0)
        slabs = pairwise(transposed, [spectrum[k * g : (k + 1) * g] for k in range(2 * PAIRS)])
        slabs = right_slabs(slabs, forward)
        store(work_a, start, slabs[:PAIRS])
        store(work_a, start + half, slabs[PAIRS:])

    potentials(g, phi_ref, first_ref, second_ref, tables, work_a, work_b, emit)

    many = 2 * FOLD + 2
    width = FOLD * LANES
    for group in range(g // many):
        parts = []
        for ky in range(group * many, (group + 1) * many, 2):
            parts.append(jnp.concatenate(regrouped(strided(work_a, ky, g), strided(work_a, ky + 1, g)), 0))
        line = jnp.concatenate(folded_parts(parts, g), 1)
        parts_ref[:, group * width : (group + 1) * width] = jnp.concatenate(split(line), 0)

    parts = parts_ref[...]
    stick_out = stick_out_ref[...].astype(BF16)
    for k in range(0, len(out_refs), 2):
        hot = one_hot(positions_ref[:1, k * LANES : (k + 2) * LANES], 0, g * g)
        both = dot(parts, hot)
        picked = dot(stick_out, stacked(both[: 2 * g] + both[2 * g :]))
        out_refs[k][...], out_refs[k + 1][...] = picked[:, :LANES], picked[:, LANES:]


def call(kernel, out_shapes, scratch, flops, *operands, space=pltpu.VMEM):
    vmem = pl.BlockSpec(memory_space=pltpu.VMEM)
    moved = sum(x.size * x.dtype.itemsize for x in operands)
    return pl.pallas_call(
        kernel,
        out_shape=out_shapes,
        in_specs=[pl.BlockSpec(memory_space=space)] * len(operands),
        out_specs=jax.tree.map(lambda _: vmem, out_shapes),
        scratch_shapes=scratch,
        compiler_params=pltpu.CompilerParams(vmem_limit_bytes=40 * 2**20),
        cost_estimate=pl.CostEstimate(flops=flops, bytes_accessed=moved, transcendentals=0),
    )(*operands)


def exchanged(blocks):
    owners = len(blocks)
    moved = {}
    for d in range(owners - 1, 0, -1):
        moved[d] = lax.ppermute(blocks[d], "stick", [(i, i ^ d) for i in range(owners)])
    return [blocks[0]] + [moved[d] for d in range(1, owners)]


def on_device(sticks, stick_columns):
    g = sticks.shape[1] // 2
    slots = stick_columns.shape[0]
    owners = lax.axis_size("stick")
    groups = lax.axis_size("band")
    t = {name: jnp.asarray(value) for name, value in make_tables(g).items()}
    rows = g * g
    field = jax.ShapeDtypeStruct((rows // 2, LANES), F32)
    folded = jax.ShapeDtypeStruct((rows // 2 * FOLD // (FOLD + 1), LANES), F32)
    field_scratch = pltpu.VMEM((rows // 2, LANES), F32)
    work = pltpu.VMEM((rows, LANES), F32)
    pot_flops = 6 * 2 * rows * 256 * 256

    sent = call(
        functools.partial(send_kernel, g),
        [jax.ShapeDtypeStruct((2 * g + 8, slots), F32)] * owners,
        [pltpu.VMEM((1, slots), jnp.int32), pltpu.SemaphoreType.DMA((owners,)), pltpu.SemaphoreType.DMA],
        10**6,
        sticks,
        stick_columns[None, :],
        space=pltpu.HBM,
    )
    received = exchanged(sent)
    first_tables = lax.optimization_barrier((t["stick_in"], t["backward"], t["left_backward"], sent[0]))[:3]
    first_tables = call(
        table_kernel, [jax.ShapeDtypeStruct(x.shape, BF16) for x in first_tables], [], 10**9, *first_tables
    )
    phi, packed, positions = call(
        functools.partial(field_kernel, g, owners),
        [field, folded, jax.ShapeDtypeStruct((8, owners * slots), jnp.int32)],
        [work],
        10**9,
        *received,
        *first_tables,
    )
    pot_tables = [t["forward"], t["last_backward"], t["left_forward"], t["left_backward"], t["coulomb"]]
    swap = [(i, i ^ 1) for i in range(groups)]

    def fetched(distance):
        return lax.ppermute(packed, "band", [(i, (i - distance) % groups) for i in range(groups)])

    near = lax.ppermute(packed, "band", swap)
    ahead = fetched(HALF)
    total = call(
        functools.partial(near_kernel, g), field, [field_scratch, work, work], pot_flops, phi, near, *pot_tables
    )
    ahead, total = lax.optimization_barrier((ahead, total))
    if groups == 2 * HALF:
        weights = (2.0, 1.0)
        first, second = ahead, lax.ppermute(ahead, "band", swap)
    else:
        weights = (1.0, 0.0)
        behind = fetched(-HALF)
        odd = lax.axis_index("band") % 2 == 1
        first = second = lax.ppermute(jnp.where(odd, behind, ahead), "band", swap)
        total = call(
            functools.partial(middle_kernel, g),
            field,
            [field_scratch, field_scratch, work, work],
            pot_flops,
            phi,
            ahead,
            behind,
            total,
            *pot_tables,
        )
    result = call(
        functools.partial(far_kernel, g, weights),
        [jax.ShapeDtypeStruct((2 * g, slots), F32)] * owners,
        [field_scratch, field_scratch, work, work, pltpu.VMEM((4 * g, rows), BF16)],
        pot_flops,
        phi,
        first,
        second,
        total,
        positions,
        t["stick_out"],
        t["real_forward"],
        *pot_tables,
    )
    return call(place_kernel, jax.ShapeDtypeStruct(sticks.shape, F32), [], 10**6, *exchanged(result))


def solution(mesh):
    return jax.shard_map(
        on_device,
        mesh=mesh,
        in_specs=(P("band", None, "stick"), P("stick")),
        out_specs=P("band", None, "stick"),
        check_vma=False,
    )
```

```python
import functools
import math

import jax
import jax.numpy as jnp
import numpy as np
from jax import lax
from jax.experimental import pallas as pl
from jax.experimental.pallas import tpu as pltpu
from jax.sharding import PartitionSpec as P

HALF = 2
BOX_LENGTH = 18.0
LANES = 128
MID = 64
PAIRS = 6
FOLD = 3

F32 = jnp.float32
BF16 = jnp.bfloat16


def rounded_parts(table):
    high = table.astype(BF16).astype(np.float64)
    low = (table - high).astype(BF16).astype(np.float64)
    return high, low


def across(table):
    high, low = rounded_parts(table)
    return np.concatenate([high, high, low], 1).astype(np.float32)


def down(table):
    high, low = rounded_parts(table)
    return np.block([[high, low], [high, np.zeros_like(low)]]).astype(np.float32)


def make_tables(g):
    angle = 2.0 * np.pi / g * (np.outer(np.arange(g), np.arange(g)) % g)
    c, s = np.cos(angle), np.sin(angle)
    lower, upper = slice(0, g), slice(MID, MID + g)

    forward, backward = np.zeros((2, LANES, LANES))
    forward[lower, lower], forward[lower, upper] = c, -s
    forward[upper, lower], forward[upper, upper] = s, c
    backward[lower, lower], backward[lower, upper] = c, s
    backward[upper, lower], backward[upper, upper] = -s, c
    stick_in = np.zeros((LANES, 2 * g))
    stick_in[lower, :g], stick_in[lower, g:] = c, -s
    stick_in[upper, :g], stick_in[upper, g:] = s, c
    stick_out = np.zeros((2 * g, LANES))
    stick_out[:g, lower], stick_out[:g, upper] = c, s
    stick_out[g:, lower], stick_out[g:, upper] = -s, c

    freq = np.arange(g)
    square = np.minimum(freq, g - freq) ** 2
    total = square[:, None, None] + square[None, :, None] + square[None, None, :]
    unit = (2.0 * math.pi / BOX_LENGTH) ** 2
    kernel = np.where(total > 0, 4.0 * math.pi / (unit * np.maximum(total, 1)), 0.0)
    coulomb = np.zeros((g, g, LANES), np.float32)
    coulomb[:, :, lower] = kernel
    coulomb[:, :, upper] = kernel
    return dict(
        forward=down(forward),
        last_backward=down(backward / g**3),
        left_forward=across(np.concatenate([c, -s], 0)),
        left_backward=across(np.concatenate([c, s], 0)),
        stick_in=across(stick_in),
        stick_out=across(stick_out * g**-1.5),
        coulomb=coulomb.reshape(g * g, LANES),
    )


def split(x):
    high = x.astype(BF16)
    low = (x - high.astype(F32)).astype(BF16)
    return high, low


def stacked(x):
    high, low = split(x)
    return jnp.concatenate([high, low, high], 0)


def dot(a, b):
    return jnp.dot(a, b, preferred_element_type=F32)


def lane_halves(shape):
    return lax.broadcasted_iota(jnp.int32, shape, 1) % LANES < MID


def turned(x):
    return pltpu.roll(x, MID, 1)


def regrouped(a, b):
    low = lane_halves(a.shape)
    return jnp.where(low, a, turned(b)), jnp.where(low, turned(a), b)


def beside(a, b):
    return jnp.concatenate([a, b], 1)


def halves(x):
    return x[:, :LANES], x[:, LANES:]


def left(table, x):
    both = dot(table, stacked(x))
    g = both.shape[0] // 2
    return both[:g], both[g:]


def left_complex(table, a, b):
    cos, sin = left(table, beside(a, b))
    sign = jnp.where(lane_halves((1, LANES)), -1.0, 1.0)
    return [p + turned(q) * sign for p, q in zip(halves(cos), halves(sin))]


def right(x, table):
    both = dot(beside(*split(x)), table)
    width = both.shape[1] // 2
    return both[:, :width] + both[:, width:]


def strided(ref, first, g):
    return ref[pl.ds(first, g, stride=g), :]


def slab_rows(index, g, count=1):
    return pl.ds(index * g, count * g)


def one_hot(index, wanted):
    return jnp.where(index == wanted, jnp.asarray(1, BF16), jnp.asarray(0, BF16))


def send_kernel(g, sticks_ref, columns_ref, *refs):
    block_refs, (row_ref, sems, row_sem) = refs[:-3], refs[-3:]
    own = lax.axis_index("stick")
    copies = [
        pltpu.make_async_copy(sticks_ref.at[own ^ d], ref.at[pl.ds(0, 2 * g)], sems.at[d])
        for d, ref in enumerate(block_refs)
    ]
    row_copy = pltpu.make_async_copy(columns_ref, row_ref, row_sem)
    row_copy.start()
    for copy in copies:
        copy.start()
    row_copy.wait()
    columns = jnp.broadcast_to(row_ref[...].astype(F32), (8, LANES))
    for ref in block_refs:
        ref[2 * g :, :] = columns
    for copy in copies:
        copy.wait()


def table_kernel(*refs):
    count = len(refs) // 2
    for table_ref, out_ref in zip(refs[:count], refs[count:]):
        out_ref[...] = table_ref[...].astype(BF16)


def place_kernel(*refs):
    own = lax.axis_index("stick")
    out_ref = refs[-1]
    for d, block_ref in enumerate(refs[:-1]):
        out_ref[own ^ d] = block_ref[...]


def fold(field_ref, folded_ref, g):
    rows = folded_ref.shape[0] // FOLD
    used = lax.broadcasted_iota(jnp.int32, (rows, LANES), 1) % MID < g
    last = field_ref[FOLD * rows :, :]
    width = g // FOLD
    for k in range(FOLD):
        part = slice(k * rows, (k + 1) * rows)
        folded_ref[part, :] = jnp.where(used, field_ref[part, :], pltpu.roll(last, g - k * width, 1))


def unfold(folded_ref, field_ref, g):
    rows = folded_ref.shape[0] // FOLD
    lane = lax.broadcasted_iota(jnp.int32, (rows, LANES), 1) % MID
    width = g // FOLD
    last = None
    for k in range(FOLD):
        part = folded_ref[k * rows : (k + 1) * rows, :]
        field_ref[k * rows : (k + 1) * rows, :] = part
        piece = pltpu.roll(part, LANES - (g - k * width), 1)
        last = piece if last is None else jnp.where(lane >= k * width, piece, last)
    field_ref[FOLD * rows :, :] = last


def store(ref, first, slabs):
    g = slabs[0].shape[0]
    for k, slab in enumerate(slabs):
        ref[slab_rows(first + k, g), :] = slab


def field_kernel(g, count, *refs):
    received = refs[:count]
    stick_in_ref, left_ref, phi_ref, folded_ref, columns_ref, work_a = refs[count:]
    columns = jnp.concatenate([ref[2 * g : 2 * g + 1, :] for ref in received], 1)
    columns_ref[...] = jnp.broadcast_to(columns, columns_ref.shape)
    columns = columns.astype(jnp.int32)
    stick_in, backward = stick_in_ref[...], left_ref[...]
    sticks = []
    for k in range(0, count, 2):
        block = beside(received[k][: 2 * g, :], received[k + 1][: 2 * g, :])
        sticks.append(beside(*split(dot(stick_in, stacked(block)).T)))
    sticks = jnp.concatenate(sticks, 0)

    half = g // 2
    index = lax.broadcasted_iota(jnp.int16, (half * g, columns.shape[1]), 0)
    for first in (0, half):
        both = dot(one_hot(index, (columns - first * g).astype(jnp.int16)), sticks)
        placed = both[:, :LANES] + both[:, LANES:]
        for k in range(0, half, 2):
            slabs = left_complex(backward, placed[k * g : (k + 1) * g], placed[(k + 1) * g : (k + 2) * g])
            store(work_a, first + k, slabs)

    for y in range(half):
        x = beside(strided(work_a, y, g), strided(work_a, y + half, g))
        (cos, cos_up), (sin, sin_up) = map(halves, left(backward, x))
        low = lane_halves(cos.shape)
        store(phi_ref, y, [jnp.where(low, cos - turned(sin), turned(cos_up) - sin_up)])
    fold(phi_ref, folded_ref, g)


def pick_kernel(g, columns_ref, hot_ref):
    for k in range(0, columns_ref.shape[1], LANES):
        block = columns_ref[:, k : k + LANES]
        wanted = jnp.concatenate([block] * (LANES // block.shape[0]), 0).T.astype(jnp.int32)
        for c in range(0, hot_ref.shape[1], LANES):
            index = lax.broadcasted_iota(jnp.int16, (LANES, LANES), 1)
            hot_ref[k : k + LANES, c : c + LANES] = one_hot(index, (wanted - c).astype(jnp.int16))


def potentials(g, phi_ref, first_ref, second_ref, tables, work_a, work_b, emit):
    forward, last_backward, left_forward, left_backward = [ref[...].astype(BF16) for ref in tables[:4]]
    coulomb_ref = tables[4]
    half = g // 2
    for start in range(0, half, PAIRS):
        rows = slab_rows(start, g, PAIRS)
        phi = phi_ref[rows, :]
        lower, upper = regrouped(phi * first_ref[rows, :], phi * second_ref[rows, :])
        spectrum = right(jnp.concatenate([lower, upper], 0), forward)
        for k in range(PAIRS):
            a, b = left_complex(left_forward, *(spectrum[j * g : (j + 1) * g] for j in (k, k + PAIRS)))
            store(work_a, start + k, [a])
            store(work_a, start + k + half, [b])

    for kx in range(0, g, 2):
        slabs = left_complex(left_forward, strided(work_a, kx, g), strided(work_a, kx + 1, g))
        slabs = [slab * coulomb_ref[slab_rows(kx + j, g), :] for j, slab in enumerate(slabs)]
        store(work_b, kx, left_complex(left_backward, *slabs))

    for start in range(0, half, PAIRS):
        lower, upper = [], []
        for z in range(start, start + PAIRS):
            a, b = left_complex(left_backward, strided(work_b, z, g), strided(work_b, z + half, g))
            lower.append(a)
            upper.append(b)
        out = right(jnp.concatenate(lower + upper, 0), last_backward)
        emit(start, *regrouped(out[: PAIRS * g], out[PAIRS * g :]))


def near_kernel(g, phi_ref, near_ref, *refs):
    tables, (sum_ref, other_ref, work_a, work_b) = refs[:5], refs[5:]
    unfold(near_ref, other_ref, g)

    def emit(start, own, other):
        rows = slab_rows(start, g, PAIRS)
        sum_ref[rows, :] = own * phi_ref[rows, :] + other * other_ref[rows, :]

    potentials(g, phi_ref, phi_ref, other_ref, tables, work_a, work_b, emit)


def middle_kernel(g, phi_ref, ahead_ref, behind_ref, before_ref, *refs):
    tables, (sum_ref, first_ref, second_ref, work_a, work_b) = refs[:5], refs[5:]
    unfold(ahead_ref, first_ref, g)
    unfold(behind_ref, second_ref, g)

    def emit(start, first, second):
        rows = slab_rows(start, g, PAIRS)
        sum_ref[rows, :] = before_ref[rows, :] + first * first_ref[rows, :] + second * second_ref[rows, :]

    potentials(g, phi_ref, first_ref, second_ref, tables, work_a, work_b, emit)


def far_kernel(g, weights, phi_ref, ahead_ref, across_ref, before_ref, hot_ref, stick_out_ref, *refs):
    tables, out_refs = refs[:5], refs[5:-5]
    first_ref, second_ref, work_a, work_b, picked_ref = refs[-5:]
    unfold(ahead_ref, first_ref, g)
    unfold(across_ref, second_ref, g)
    forward = tables[2][...].astype(BF16)
    half = g // 2

    def emit(start, first, second):
        rows = slab_rows(start, g, PAIRS)
        total = before_ref[rows, :] + weights[0] * (first * first_ref[rows, :])
        total = total + weights[1] * (second * second_ref[rows, :])
        for k in range(0, PAIRS, 2):
            cos, sin = left(forward, beside(total[k * g : (k + 1) * g], total[(k + 1) * g : (k + 2) * g]))
            for j, (real, imag) in enumerate(zip(halves(cos), halves(sin))):
                lower, upper = regrouped(real, imag)
                store(work_a, start + k + j, [lower])
                store(work_a, start + k + j + half, [upper])

    potentials(g, phi_ref, first_ref, second_ref, tables, work_a, work_b, emit)

    step = g // 3
    for first in range(0, g, step):
        slabs = []
        for kx in range(first, first + step, 2):
            slabs += left_complex(forward, strided(work_a, kx, g), strided(work_a, kx + 1, g))
        spectrum = beside(*split(jnp.concatenate(slabs, 0)))
        both = dot(hot_ref[:, first * g : (first + step) * g], spectrum)
        both = both[:, :LANES] + both[:, LANES:]
        picked_ref[...] = both if first == 0 else picked_ref[...] + both

    stick_out = stick_out_ref[...].astype(BF16)
    for k in range(0, len(out_refs), 2):
        high, low = split(picked_ref[k * LANES : (k + 2) * LANES, :])
        lined = jnp.concatenate([high, low, high], 1)
        out = lax.dot_general(stick_out, lined, (((1,), (1,)), ((), ())), preferred_element_type=F32)
        out_refs[k][...], out_refs[k + 1][...] = halves(out)


def call(kernel, out_shapes, scratch, flops, *operands, space=pltpu.VMEM):
    vmem = pl.BlockSpec(memory_space=pltpu.VMEM)
    moved = sum(x.size * x.dtype.itemsize for x in operands)
    return pl.pallas_call(
        kernel,
        out_shape=out_shapes,
        in_specs=[pl.BlockSpec(memory_space=space)] * len(operands),
        out_specs=jax.tree.map(lambda _: vmem, out_shapes),
        scratch_shapes=scratch,
        compiler_params=pltpu.CompilerParams(vmem_limit_bytes=40 * 2**20),
        cost_estimate=pl.CostEstimate(flops=flops, bytes_accessed=moved, transcendentals=0),
    )(*operands)


def exchanged(blocks):
    owners = len(blocks)
    moved = {}
    for d in range(owners - 1, 0, -1):
        moved[d] = lax.ppermute(blocks[d], "stick", [(i, i ^ d) for i in range(owners)])
    return [blocks[0]] + [moved[d] for d in range(1, owners)]


def on_device(sticks, stick_columns):
    g = sticks.shape[1] // 2
    slots = stick_columns.shape[0]
    owners = lax.axis_size("stick")
    groups = lax.axis_size("band")
    t = {name: jnp.asarray(value) for name, value in make_tables(g).items()}
    rows = g * g
    field = jax.ShapeDtypeStruct((rows // 2, LANES), F32)
    folded = jax.ShapeDtypeStruct((rows // 2 * FOLD // (FOLD + 1), LANES), F32)
    field_scratch = pltpu.VMEM((rows // 2, LANES), F32)
    work = pltpu.VMEM((rows, LANES), F32)
    pot_flops = 6 * 2 * rows * 256 * 256

    sent = call(
        functools.partial(send_kernel, g),
        [jax.ShapeDtypeStruct((2 * g + 8, slots), F32)] * owners,
        [pltpu.VMEM((1, slots), jnp.int32), pltpu.SemaphoreType.DMA((owners,)), pltpu.SemaphoreType.DMA],
        10**6,
        sticks,
        stick_columns[None, :],
        space=pltpu.HBM,
    )
    received = exchanged(sent)
    first_tables = lax.optimization_barrier((t["stick_in"], t["left_backward"], sent[0]))[:2]
    first_tables = call(
        table_kernel, [jax.ShapeDtypeStruct(x.shape, BF16) for x in first_tables], [], 10**9, *first_tables
    )
    phi, packed, columns = call(
        functools.partial(field_kernel, g, owners),
        [field, folded, jax.ShapeDtypeStruct((8, owners * slots), F32)],
        [work],
        10**9,
        *received,
        *first_tables,
    )
    pot_tables = [t["forward"], t["last_backward"], t["left_forward"], t["left_backward"], t["coulomb"]]
    swap = [(i, i ^ 1) for i in range(groups)]

    def fetched(distance):
        return lax.ppermute(packed, "band", [(i, (i - distance) % groups) for i in range(groups)])

    near = lax.ppermute(packed, "band", swap)
    ahead = fetched(HALF)
    total = call(
        functools.partial(near_kernel, g), field, [field_scratch, work, work], pot_flops, phi, near, *pot_tables
    )
    hot = call(
        functools.partial(pick_kernel, g), jax.ShapeDtypeStruct((owners * slots, rows), BF16), [], pot_flops, columns
    )
    ahead, total, hot = lax.optimization_barrier((ahead, total, hot))
    if groups == 2 * HALF:
        weights = (2.0, 1.0)
        first, second = ahead, lax.ppermute(ahead, "band", swap)
    else:
        weights = (1.0, 0.0)
        behind = fetched(-HALF)
        odd = lax.axis_index("band") % 2 == 1
        first = second = lax.ppermute(jnp.where(odd, behind, ahead), "band", swap)
        total = call(
            functools.partial(middle_kernel, g),
            field,
            [field_scratch, field_scratch, work, work],
            pot_flops,
            phi,
            ahead,
            behind,
            total,
            *pot_tables,
        )
    result = call(
        functools.partial(far_kernel, g, weights),
        [jax.ShapeDtypeStruct((2 * g, slots), F32)] * owners,
        [field_scratch, field_scratch, work, work, pltpu.VMEM((owners * slots, LANES), F32)],
        pot_flops,
        phi,
        first,
        second,
        total,
        hot,
        t["stick_out"],
        *pot_tables,
    )
    return call(place_kernel, jax.ShapeDtypeStruct(sticks.shape, F32), [], 10**6, *exchanged(result))


def solution(mesh):
    return jax.shard_map(
        on_device,
        mesh=mesh,
        in_specs=(P("band", None, "stick"), P("stick")),
        out_specs=P("band", None, "stick"),
        check_vma=False,
    )
```

```python
import functools
import math

import jax
import jax.numpy as jnp
import numpy as np
from jax import lax
from jax.experimental import pallas as pl
from jax.experimental.pallas import tpu as pltpu
from jax.sharding import PartitionSpec as P

HALF = 2
BOX_LENGTH = 18.0
LANES = 128
MID = 64
SEND_GRANT = 60
PAIRS = 6

F32 = jnp.float32
BF16 = jnp.bfloat16


def rounded_parts(table):
    high = table.astype(BF16).astype(np.float64)
    low = (table - high).astype(BF16).astype(np.float64)
    return high, low


def across(table):
    high, low = rounded_parts(table)
    return np.concatenate([high, high, low], 1).astype(np.float32)


def down(table):
    high, low = rounded_parts(table)
    return np.block([[high, low], [high, np.zeros_like(low)]]).astype(np.float32)


def make_tables(g):
    angle = 2.0 * np.pi / g * (np.outer(np.arange(g), np.arange(g)) % g)
    c, s = np.cos(angle), np.sin(angle)
    lower, upper = slice(0, g), slice(MID, MID + g)

    forward, backward = np.zeros((2, LANES, LANES))
    forward[lower, lower], forward[lower, upper] = c, -s
    forward[upper, lower], forward[upper, upper] = s, c
    backward[lower, lower], backward[lower, upper] = c, s
    backward[upper, lower], backward[upper, upper] = -s, c
    stick_in = np.zeros((LANES, 2 * g))
    stick_in[lower, :g], stick_in[lower, g:] = c, -s
    stick_in[upper, :g], stick_in[upper, g:] = s, c
    stick_out = np.zeros((2 * g, LANES))
    stick_out[:g, lower], stick_out[:g, upper] = c, s
    stick_out[g:, lower], stick_out[g:, upper] = -s, c

    freq = np.arange(g)
    square = np.minimum(freq, g - freq) ** 2
    total = square[:, None, None] + square[None, :, None] + square[None, None, :]
    unit = (2.0 * math.pi / BOX_LENGTH) ** 2
    kernel = np.where(total > 0, 4.0 * math.pi / (unit * np.maximum(total, 1)), 0.0)
    coulomb = np.zeros((g, g, LANES), np.float32)
    coulomb[:, :, lower] = kernel
    coulomb[:, :, upper] = kernel
    return dict(
        forward=down(forward),
        last_backward=down(backward / g**3),
        left_forward=across(np.concatenate([c, -s], 0)),
        left_backward=across(np.concatenate([c, s], 0)),
        stick_in=across(stick_in),
        stick_out=across(stick_out * g**-1.5),
        coulomb=coulomb.reshape(g * g, LANES),
    )


def split(x):
    high = x.astype(BF16)
    low = (x - high.astype(F32)).astype(BF16)
    return high, low


def stacked(x):
    high, low = split(x)
    return jnp.concatenate([high, low, high], 0)


def dot(a, b):
    return jnp.dot(a, b, preferred_element_type=F32)


def lane_halves(shape):
    return lax.broadcasted_iota(jnp.int32, shape, 1) % LANES < MID


def turned(x):
    return pltpu.roll(x, MID, 1)


def regrouped(a, b):
    low = lane_halves(a.shape)
    return jnp.where(low, a, turned(b)), jnp.where(low, turned(a), b)


def beside(a, b):
    return jnp.concatenate([a, b], 1)


def halves(x):
    return x[:, :LANES], x[:, LANES:]


def left(table, x):
    both = dot(table, stacked(x))
    g = both.shape[0] // 2
    return both[:g], both[g:]


def left_complex(table, a, b):
    cos, sin = left(table, beside(a, b))
    sign = jnp.where(lane_halves((1, LANES)), -1.0, 1.0)
    return [p + turned(q) * sign for p, q in zip(halves(cos), halves(sin))]


def right(x, table):
    both = dot(beside(*split(x)), table)
    width = both.shape[1] // 2
    return both[:, :width] + both[:, width:]


def strided(ref, first, g):
    return ref[pl.ds(first, g, stride=g), :]


def slab_rows(index, g, count=1):
    return pl.ds(index * g, count * g)


def one_hot(index, wanted):
    return jnp.where(index == wanted, jnp.asarray(1, BF16), jnp.asarray(0, BF16))


def send_kernel(g, sticks_ref, columns_ref, *refs):
    block_refs, (row_ref, rows_ref, sems, row_sem) = refs[:-4], refs[-4:]
    own = lax.axis_index("stick")
    count = len(block_refs)
    row_copy = pltpu.make_async_copy(columns_ref, row_ref, row_sem)
    row_copy.start()
    copies = [
        pltpu.make_async_copy(sticks_ref.at[own ^ d], ref.at[pl.ds(0, 2 * g)], sems.at[d])
        for d, ref in enumerate(block_refs)
    ]
    for copy in copies:
        copy.start()
    row_copy.wait()
    rows_ref[...] = jnp.broadcast_to(row_ref[...].astype(F32), rows_ref.shape)
    row_copies = [
        pltpu.make_async_copy(rows_ref, ref.at[pl.ds(2 * g, 8)], sems.at[count + d])
        for d, ref in enumerate(block_refs)
    ]
    for copy in row_copies:
        copy.start()
    for copy in copies + row_copies:
        copy.wait()


def table_kernel(*refs):
    count = len(refs) // 2
    for table_ref, out_ref in zip(refs[:count], refs[count:]):
        out_ref[...] = table_ref[...].astype(BF16)


def place_kernel(*refs):
    own = lax.axis_index("stick")
    out_ref = refs[-1]
    for d, block_ref in enumerate(refs[:-1]):
        out_ref[own ^ d] = block_ref[...]


def store(ref, first, slabs):
    g = slabs[0].shape[0]
    for k, slab in enumerate(slabs):
        ref[slab_rows(first + k, g), :] = slab


def relay_kernel(g, *refs):
    blocks, (coefficients_ref, columns_ref) = refs[:-2], refs[-2:]
    for k, ref in enumerate(blocks):
        coefficients_ref[k * 2 * g : (k + 1) * 2 * g, :] = ref[: 2 * g, :]
        columns_ref[:, k * LANES : (k + 1) * LANES] = ref[2 * g :, :]


def field_kernel(g, first_ref, second_ref, first_columns_ref, second_columns_ref, stick_in_ref, left_ref, phi_ref, work_a):
    columns = beside(first_columns_ref[:1, :], second_columns_ref[:1, :]).astype(jnp.int32)
    stick_in, backward = stick_in_ref[...], left_ref[...]
    blocks = []
    for ref in (first_ref, second_ref):
        blocks += [ref[k : k + 2 * g, :] for k in range(0, ref.shape[0], 2 * g)]
    sticks = []
    for k in range(0, len(blocks), 2):
        sticks.append(beside(*split(dot(stick_in, stacked(beside(blocks[k], blocks[k + 1]))).T)))
    sticks = jnp.concatenate(sticks, 0)

    half = g // 2
    index = lax.broadcasted_iota(jnp.int16, (half * g, columns.shape[1]), 0)
    for first in (0, half):
        both = dot(one_hot(index, (columns - first * g).astype(jnp.int16)), sticks)
        placed = both[:, :LANES] + both[:, LANES:]
        for k in range(0, half, 2):
            slabs = left_complex(backward, placed[k * g : (k + 1) * g], placed[(k + 1) * g : (k + 2) * g])
            store(work_a, first + k, slabs)

    for y in range(half):
        x = beside(strided(work_a, y, g), strided(work_a, y + half, g))
        (cos, cos_up), (sin, sin_up) = map(halves, left(backward, x))
        low = lane_halves(cos.shape)
        store(phi_ref, y, [jnp.where(low, cos - turned(sin), turned(cos_up) - sin_up)])


def pick_kernel(g, first_columns_ref, second_columns_ref, hot_ref):
    columns = beside(first_columns_ref[...], second_columns_ref[...])
    for k in range(0, columns.shape[1], LANES):
        block = columns[:, k : k + LANES]
        wanted = jnp.concatenate([block] * (LANES // block.shape[0]), 0).T.astype(jnp.int32)
        for c in range(0, hot_ref.shape[1], LANES):
            index = lax.broadcasted_iota(jnp.int16, (LANES, LANES), 1)
            hot_ref[k : k + LANES, c : c + LANES] = one_hot(index, (wanted - c).astype(jnp.int16))


def potentials(g, phi_ref, first_ref, second_ref, tables, work_a, work_b, emit):
    forward, last_backward, left_forward, left_backward = [ref[...].astype(BF16) for ref in tables[:4]]
    coulomb_ref = tables[4]
    half = g // 2
    for start in range(0, half, PAIRS):
        rows = slab_rows(start, g, PAIRS)
        phi = phi_ref[rows, :]
        lower, upper = regrouped(phi * first_ref[rows, :], phi * second_ref[rows, :])
        spectrum = right(jnp.concatenate([lower, upper], 0), forward)
        for k in range(PAIRS):
            a, b = left_complex(left_forward, *(spectrum[j * g : (j + 1) * g] for j in (k, k + PAIRS)))
            store(work_a, start + k, [a])
            store(work_a, start + k + half, [b])

    for kx in range(0, g, 2):
        slabs = left_complex(left_forward, strided(work_a, kx, g), strided(work_a, kx + 1, g))
        slabs = [slab * coulomb_ref[slab_rows(kx + j, g), :] for j, slab in enumerate(slabs)]
        store(work_b, kx, left_complex(left_backward, *slabs))

    for start in range(0, half, PAIRS):
        lower, upper = [], []
        for z in range(start, start + PAIRS):
            a, b = left_complex(left_backward, strided(work_b, z, g), strided(work_b, z + half, g))
            lower.append(a)
            upper.append(b)
        out = right(jnp.concatenate(lower + upper, 0), last_backward)
        emit(start, *regrouped(out[: PAIRS * g], out[PAIRS * g :]))


def near_kernel(g, phi_ref, other_ref, *refs):
    tables, (sum_ref, work_a, work_b) = refs[:5], refs[5:]

    def emit(start, own, other):
        rows = slab_rows(start, g, PAIRS)
        sum_ref[rows, :] = own * phi_ref[rows, :] + other * other_ref[rows, :]

    potentials(g, phi_ref, phi_ref, other_ref, tables, work_a, work_b, emit)


def middle_kernel(g, phi_ref, first_ref, second_ref, before_ref, *refs):
    tables, (sum_ref, work_a, work_b) = refs[:5], refs[5:]

    def emit(start, first, second):
        rows = slab_rows(start, g, PAIRS)
        sum_ref[rows, :] = before_ref[rows, :] + first * first_ref[rows, :] + second * second_ref[rows, :]

    potentials(g, phi_ref, first_ref, second_ref, tables, work_a, work_b, emit)


def far_kernel(g, weights, phi_ref, first_ref, second_ref, before_ref, hot_ref, stick_out_ref, *refs):
    tables, out_refs = refs[:5], refs[5:-3]
    work_a, work_b, picked_ref = refs[-3:]
    forward = tables[2][...].astype(BF16)
    half = g // 2

    def emit(start, first, second):
        rows = slab_rows(start, g, PAIRS)
        total = before_ref[rows, :] + weights[0] * (first * first_ref[rows, :])
        total = total + weights[1] * (second * second_ref[rows, :])
        for k in range(0, PAIRS, 2):
            cos, sin = left(forward, beside(total[k * g : (k + 1) * g], total[(k + 1) * g : (k + 2) * g]))
            for j, (real, imag) in enumerate(zip(halves(cos), halves(sin))):
                lower, upper = regrouped(real, imag)
                store(work_a, start + k + j, [lower])
                store(work_a, start + k + j + half, [upper])

    potentials(g, phi_ref, first_ref, second_ref, tables, work_a, work_b, emit)

    step = g // 3
    for first in range(0, g, step):
        slabs = []
        for kx in range(first, first + step, 2):
            slabs += left_complex(forward, strided(work_a, kx, g), strided(work_a, kx + 1, g))
        spectrum = beside(*split(jnp.concatenate(slabs, 0)))
        both = dot(hot_ref[:, first * g : (first + step) * g], spectrum)
        both = both[:, :LANES] + both[:, LANES:]
        picked_ref[...] = both if first == 0 else picked_ref[...] + both

    stick_out = stick_out_ref[...].astype(BF16)
    for k in range(0, len(out_refs), 2):
        high, low = split(picked_ref[k * LANES : (k + 2) * LANES, :])
        lined = jnp.concatenate([high, low, high], 1)
        out = lax.dot_general(stick_out, lined, (((1,), (1,)), ((), ())), preferred_element_type=F32)
        out_refs[k][...], out_refs[k + 1][...] = halves(out)


def call(kernel, out_shapes, scratch, flops, *operands, space=pltpu.VMEM, out_space=pltpu.VMEM, grant=40):
    moved = sum(x.size * x.dtype.itemsize for x in operands)
    out_spec = pl.BlockSpec(memory_space=out_space)
    return pl.pallas_call(
        kernel,
        out_shape=out_shapes,
        in_specs=[pl.BlockSpec(memory_space=space)] * len(operands),
        out_specs=jax.tree.map(lambda _: out_spec, out_shapes),
        scratch_shapes=scratch,
        compiler_params=pltpu.CompilerParams(vmem_limit_bytes=grant * 2**20),
        cost_estimate=pl.CostEstimate(flops=flops, bytes_accessed=moved, transcendentals=0),
    )(*operands)


def exchanged(blocks):
    owners = len(blocks)
    moved = {}
    for d in range(owners - 1, 0, -1):
        moved[d] = lax.ppermute(blocks[d], "stick", [(i, i ^ d) for i in range(owners)])
    return [blocks[0]] + [moved[d] for d in range(1, owners)]


def on_device(sticks, stick_columns):
    g = sticks.shape[1] // 2
    slots = stick_columns.shape[0]
    owners = lax.axis_size("stick")
    groups = lax.axis_size("band")
    t = {name: jnp.asarray(value) for name, value in make_tables(g).items()}
    rows = g * g
    field = jax.ShapeDtypeStruct((rows // 2, LANES), F32)
    work = pltpu.VMEM((rows, LANES), F32)
    pot_flops = 6 * 2 * rows * 256 * 256

    def shifted(x, distance):
        return lax.ppermute(x, "band", [(i, (i - distance) % groups) for i in range(groups)])

    def swapped(x):
        return lax.ppermute(x, "band", [(i, i ^ 1) for i in range(groups)])

    sent = call(
        functools.partial(send_kernel, g),
        [jax.ShapeDtypeStruct((2 * g + 8, slots), F32)] * owners,
        [
            pltpu.VMEM((1, slots), jnp.int32),
            pltpu.VMEM((8, slots), F32),
            pltpu.SemaphoreType.DMA((2 * owners,)),
            pltpu.SemaphoreType.DMA,
        ],
        10**6,
        sticks,
        stick_columns[None, :],
        space=pltpu.HBM,
        out_space=pltpu.HBM,
        grant=SEND_GRANT,
    )
    received = exchanged(sent)
    first_tables = lax.optimization_barrier((t["stick_in"], t["left_backward"], sent[0]))[:2]
    first_tables = call(
        table_kernel, [jax.ShapeDtypeStruct(x.shape, BF16) for x in first_tables], [], 10**9, *first_tables
    )

    half = owners // 2
    order = [0] + list(range(half, owners)) + list(range(1, half))
    relays, columns = [], []
    for part in (order[: half + 1], order[half + 1 :]):
        shapes = [(len(part) * 2 * g, slots), (8, len(part) * slots)]
        shapes = [jax.ShapeDtypeStruct(shape, F32) for shape in shapes]
        relay, column = call(functools.partial(relay_kernel, g), shapes, [], 10**6, *[received[d] for d in part])
        relays.append(relay)
        columns.append(column)

    def orbital(blocks):
        return call(functools.partial(field_kernel, g), field, [work], 10**9, *blocks, *columns, *first_tables)

    phi = orbital(relays)
    near = swapped(phi)
    hot = call(
        functools.partial(pick_kernel, g), jax.ShapeDtypeStruct((owners * slots, rows), BF16), [], pot_flops, *columns
    )
    distances = (HALF,) if groups == 2 * HALF else (HALF, -HALF)
    fields = [orbital([shifted(x, distance) for x in relays]) for distance in distances]
    pot_tables = [t["forward"], t["last_backward"], t["left_forward"], t["left_backward"], t["coulomb"]]

    def potential_sum(kernel, *operands):
        return call(functools.partial(kernel, g), field, [work, work], pot_flops, phi, *operands, *pot_tables)

    if groups == 2 * HALF:
        weights = (2.0, 1.0)
        first, second = fields[0], swapped(fields[0])
        near, first = lax.optimization_barrier((near, first))
        total = potential_sum(near_kernel, near)
    else:
        weights = (1.0, 0.0)
        odd = lax.axis_index("band") % 2 == 1
        first = second = swapped(jnp.where(odd, fields[1], fields[0]))
        total = potential_sum(near_kernel, near)
        total = potential_sum(middle_kernel, *fields, total)
    order_back = {d: k for k, d in enumerate(order)}
    result = call(
        functools.partial(far_kernel, g, weights),
        [jax.ShapeDtypeStruct((2 * g, slots), F32)] * owners,
        [work, work, pltpu.VMEM((owners * slots, LANES), F32)],
        pot_flops,
        phi,
        first,
        second,
        total,
        hot,
        t["stick_out"],
        *pot_tables,
    )
    result = [result[order_back[d]] for d in range(owners)]
    return call(place_kernel, jax.ShapeDtypeStruct(sticks.shape, F32), [], 10**6, *exchanged(result))


def solution(mesh):
    return jax.shard_map(
        on_device,
        mesh=mesh,
        in_specs=(P("band", None, "stick"), P("stick")),
        out_specs=P("band", None, "stick"),
        check_vma=False,
    )
```

```python
import functools
import math

import jax
import jax.numpy as jnp
import numpy as np
from jax import lax
from jax.experimental import pallas as pl
from jax.experimental.pallas import tpu as pltpu
from jax.sharding import PartitionSpec as P

HALF = 2
BOX_LENGTH = 18.0
LANES = 128
MID = 64
SEND_GRANT = 60
PAIRS = 6

F32 = jnp.float32
BF16 = jnp.bfloat16


def rounded_parts(table):
    high = table.astype(BF16).astype(np.float64)
    low = (table - high).astype(BF16).astype(np.float64)
    return high, low


def across(table):
    high, low = rounded_parts(table)
    return np.concatenate([high, high, low], 1).astype(np.float32)


def down(table):
    high, low = rounded_parts(table)
    return np.block([[high, low], [high, np.zeros_like(low)]]).astype(np.float32)


def make_tables(g):
    angle = 2.0 * np.pi / g * (np.outer(np.arange(g), np.arange(g)) % g)
    c, s = np.cos(angle), np.sin(angle)
    lower, upper = slice(0, g), slice(MID, MID + g)

    forward, backward = np.zeros((2, LANES, LANES))
    forward[lower, lower], forward[lower, upper] = c, -s
    forward[upper, lower], forward[upper, upper] = s, c
    backward[lower, lower], backward[lower, upper] = c, s
    backward[upper, lower], backward[upper, upper] = -s, c
    stick_in = np.zeros((LANES, 2 * g))
    stick_in[lower, :g], stick_in[lower, g:] = c, -s
    stick_in[upper, :g], stick_in[upper, g:] = s, c
    stick_out = np.zeros((2 * g, LANES))
    stick_out[:g, lower], stick_out[:g, upper] = c, s
    stick_out[g:, lower], stick_out[g:, upper] = -s, c

    freq = np.arange(g)
    square = np.minimum(freq, g - freq) ** 2
    total = square[:, None, None] + square[None, :, None] + square[None, None, :]
    unit = (2.0 * math.pi / BOX_LENGTH) ** 2
    kernel = np.where(total > 0, 4.0 * math.pi / (unit * np.maximum(total, 1)), 0.0)
    coulomb = np.zeros((g, g, LANES), np.float32)
    coulomb[:, :, lower] = kernel
    coulomb[:, :, upper] = kernel
    return dict(
        forward=down(forward),
        last_backward=down(backward / g**3),
        left_forward=across(np.concatenate([c, -s], 0)),
        left_backward=across(np.concatenate([c, s], 0)),
        stick_in=across(stick_in),
        stick_out=across(stick_out * g**-1.5),
        coulomb=coulomb.reshape(g * g, LANES),
    )


def split(x):
    high = x.astype(BF16)
    low = (x - high.astype(F32)).astype(BF16)
    return high, low


def stacked(x):
    high, low = split(x)
    return jnp.concatenate([high, low, high], 0)


def dot(a, b):
    return jnp.dot(a, b, preferred_element_type=F32)


def lane_halves(shape):
    return lax.broadcasted_iota(jnp.int32, shape, 1) % LANES < MID


def turned(x):
    return pltpu.roll(x, MID, 1)


def regrouped(a, b):
    low = lane_halves(a.shape)
    return jnp.where(low, a, turned(b)), jnp.where(low, turned(a), b)


def beside(a, b):
    return jnp.concatenate([a, b], 1)


def halves(x):
    return x[:, :LANES], x[:, LANES:]


def left(table, x):
    both = dot(table, stacked(x))
    g = both.shape[0] // 2
    return both[:g], both[g:]


def left_complex(table, a, b):
    cos, sin = left(table, beside(a, b))
    sign = jnp.where(lane_halves((1, LANES)), -1.0, 1.0)
    return [p + turned(q) * sign for p, q in zip(halves(cos), halves(sin))]


def right(x, table):
    both = dot(beside(*split(x)), table)
    width = both.shape[1] // 2
    return both[:, :width] + both[:, width:]


def strided(ref, first, g):
    return ref[pl.ds(first, g, stride=g), :]


def slab_rows(index, g, count=1):
    return pl.ds(index * g, count * g)


def one_hot(index, wanted):
    return jnp.where(index == wanted, jnp.asarray(1, BF16), jnp.asarray(0, BF16))


def send_kernel(g, sticks_ref, columns_ref, *refs):
    block_refs, (row_ref, sems, row_sem) = refs[:-3], refs[-3:]
    own = lax.axis_index("stick")
    row_copy = pltpu.make_async_copy(columns_ref, row_ref, row_sem)
    row_copy.start()
    copies = [
        pltpu.make_async_copy(sticks_ref.at[own ^ d], ref.at[pl.ds(0, 2 * g)], sems.at[d])
        for d, ref in enumerate(block_refs)
    ]
    for copy in copies:
        copy.start()
    row_copy.wait()
    columns = jnp.broadcast_to(row_ref[...].astype(F32), (8, LANES))
    for ref in block_refs:
        ref[2 * g :, :] = columns
    for copy in copies:
        copy.wait()


def table_kernel(*refs):
    count = len(refs) // 2
    for table_ref, out_ref in zip(refs[:count], refs[count:]):
        out_ref[...] = table_ref[...].astype(BF16)


def place_kernel(*refs):
    own = lax.axis_index("stick")
    out_ref = refs[-1]
    for d, block_ref in enumerate(refs[:-1]):
        out_ref[own ^ d] = block_ref[...]


def store(ref, first, slabs):
    g = slabs[0].shape[0]
    for k, slab in enumerate(slabs):
        ref[slab_rows(first + k, g), :] = slab


def relay_kernel(g, *refs):
    blocks, (coefficients_ref, columns_ref) = refs[:-2], refs[-2:]
    for k, ref in enumerate(blocks):
        coefficients_ref[k * 2 * g : (k + 1) * 2 * g, :] = ref[: 2 * g, :]
        columns_ref[:, k * LANES : (k + 1) * LANES] = ref[2 * g :, :]


def field_kernel(g, first_ref, second_ref, first_columns_ref, second_columns_ref, stick_in_ref, left_ref, phi_ref, work_a):
    columns = beside(first_columns_ref[:1, :], second_columns_ref[:1, :]).astype(jnp.int32)
    stick_in, backward = stick_in_ref[...], left_ref[...]
    blocks = []
    for ref in (first_ref, second_ref):
        blocks += [ref[k : k + 2 * g, :] for k in range(0, ref.shape[0], 2 * g)]
    sticks = []
    for k in range(0, len(blocks), 2):
        sticks.append(beside(*split(dot(stick_in, stacked(beside(blocks[k], blocks[k + 1]))).T)))
    sticks = jnp.concatenate(sticks, 0)

    half = g // 2
    index = lax.broadcasted_iota(jnp.int16, (half * g, columns.shape[1]), 0)
    for first in (0, half):
        both = dot(one_hot(index, (columns - first * g).astype(jnp.int16)), sticks)
        placed = both[:, :LANES] + both[:, LANES:]
        for k in range(0, half, 2):
            slabs = left_complex(backward, placed[k * g : (k + 1) * g], placed[(k + 1) * g : (k + 2) * g])
            store(work_a, first + k, slabs)

    for y in range(half):
        x = beside(strided(work_a, y, g), strided(work_a, y + half, g))
        (cos, cos_up), (sin, sin_up) = map(halves, left(backward, x))
        low = lane_halves(cos.shape)
        store(phi_ref, y, [jnp.where(low, cos - turned(sin), turned(cos_up) - sin_up)])


def pick_kernel(g, first_columns_ref, second_columns_ref, hot_ref):
    columns = beside(first_columns_ref[...], second_columns_ref[...])
    for k in range(0, columns.shape[1], LANES):
        block = columns[:, k : k + LANES]
        wanted = jnp.concatenate([block] * (LANES // block.shape[0]), 0).T.astype(jnp.int32)
        for c in range(0, hot_ref.shape[1], LANES):
            index = lax.broadcasted_iota(jnp.int16, (LANES, LANES), 1)
            hot_ref[k : k + LANES, c : c + LANES] = one_hot(index, (wanted - c).astype(jnp.int16))


def potentials(g, phi_ref, first_ref, second_ref, tables, work_a, work_b, emit):
    forward, last_backward, left_forward, left_backward = [ref[...].astype(BF16) for ref in tables[:4]]
    coulomb_ref = tables[4]
    half = g // 2
    for start in range(0, half, PAIRS):
        rows = slab_rows(start, g, PAIRS)
        phi = phi_ref[rows, :]
        lower, upper = regrouped(phi * first_ref[rows, :], phi * second_ref[rows, :])
        spectrum = right(jnp.concatenate([lower, upper], 0), forward)
        for k in range(PAIRS):
            a, b = left_complex(left_forward, *(spectrum[j * g : (j + 1) * g] for j in (k, k + PAIRS)))
            store(work_a, start + k, [a])
            store(work_a, start + k + half, [b])

    for kx in range(0, g, 2):
        slabs = left_complex(left_forward, strided(work_a, kx, g), strided(work_a, kx + 1, g))
        slabs = [slab * coulomb_ref[slab_rows(kx + j, g), :] for j, slab in enumerate(slabs)]
        store(work_b, kx, left_complex(left_backward, *slabs))

    for start in range(0, half, PAIRS):
        lower, upper = [], []
        for z in range(start, start + PAIRS):
            a, b = left_complex(left_backward, strided(work_b, z, g), strided(work_b, z + half, g))
            lower.append(a)
            upper.append(b)
        out = right(jnp.concatenate(lower + upper, 0), last_backward)
        emit(start, *regrouped(out[: PAIRS * g], out[PAIRS * g :]))


def near_kernel(g, phi_ref, other_ref, *refs):
    tables, (sum_ref, work_a, work_b) = refs[:5], refs[5:]

    def emit(start, own, other):
        rows = slab_rows(start, g, PAIRS)
        sum_ref[rows, :] = own * phi_ref[rows, :] + other * other_ref[rows, :]

    potentials(g, phi_ref, phi_ref, other_ref, tables, work_a, work_b, emit)


def middle_kernel(g, phi_ref, first_ref, second_ref, before_ref, *refs):
    tables, (sum_ref, work_a, work_b) = refs[:5], refs[5:]

    def emit(start, first, second):
        rows = slab_rows(start, g, PAIRS)
        sum_ref[rows, :] = before_ref[rows, :] + first * first_ref[rows, :] + second * second_ref[rows, :]

    potentials(g, phi_ref, first_ref, second_ref, tables, work_a, work_b, emit)


def far_kernel(g, weights, phi_ref, first_ref, second_ref, before_ref, hot_ref, stick_out_ref, *refs):
    tables, out_refs = refs[:5], refs[5:-3]
    work_a, work_b, picked_ref = refs[-3:]
    forward = tables[2][...].astype(BF16)
    half = g // 2

    def emit(start, first, second):
        rows = slab_rows(start, g, PAIRS)
        total = before_ref[rows, :] + weights[0] * (first * first_ref[rows, :])
        total = total + weights[1] * (second * second_ref[rows, :])
        for k in range(0, PAIRS, 2):
            cos, sin = left(forward, beside(total[k * g : (k + 1) * g], total[(k + 1) * g : (k + 2) * g]))
            for j, (real, imag) in enumerate(zip(halves(cos), halves(sin))):
                lower, upper = regrouped(real, imag)
                store(work_a, start + k + j, [lower])
                store(work_a, start + k + j + half, [upper])

    potentials(g, phi_ref, first_ref, second_ref, tables, work_a, work_b, emit)

    step = g // 3
    for first in range(0, g, step):
        slabs = []
        for kx in range(first, first + step, 2):
            slabs += left_complex(forward, strided(work_a, kx, g), strided(work_a, kx + 1, g))
        spectrum = beside(*split(jnp.concatenate(slabs, 0)))
        both = dot(hot_ref[:, first * g : (first + step) * g], spectrum)
        both = both[:, :LANES] + both[:, LANES:]
        picked_ref[...] = both if first == 0 else picked_ref[...] + both

    stick_out = stick_out_ref[...].astype(BF16)
    for k in range(0, len(out_refs), 2):
        high, low = split(picked_ref[k * LANES : (k + 2) * LANES, :])
        lined = jnp.concatenate([high, low, high], 1)
        out = lax.dot_general(stick_out, lined, (((1,), (1,)), ((), ())), preferred_element_type=F32)
        out_refs[k][...], out_refs[k + 1][...] = halves(out)


def call(kernel, out_shapes, scratch, flops, *operands, space=pltpu.VMEM, out_space=pltpu.VMEM, grant=40):
    moved = sum(x.size * x.dtype.itemsize for x in operands)
    out_spec = pl.BlockSpec(memory_space=out_space)
    return pl.pallas_call(
        kernel,
        out_shape=out_shapes,
        in_specs=[pl.BlockSpec(memory_space=space)] * len(operands),
        out_specs=jax.tree.map(lambda _: out_spec, out_shapes),
        scratch_shapes=scratch,
        compiler_params=pltpu.CompilerParams(vmem_limit_bytes=grant * 2**20),
        cost_estimate=pl.CostEstimate(flops=flops, bytes_accessed=moved, transcendentals=0),
    )(*operands)


def exchanged(blocks):
    owners = len(blocks)
    half = owners // 2
    blocks = list(blocks)

    def moved(d):
        return lax.ppermute(blocks[d], "stick", [(i, i ^ d) for i in range(owners)])

    far = [moved(d) for d in range(half, owners)]
    *blocks[1:half], far[0] = lax.optimization_barrier((*blocks[1:half], far[0]))
    return [blocks[0]] + [moved(d) for d in range(1, half)] + far


def on_device(sticks, stick_columns):
    g = sticks.shape[1] // 2
    slots = stick_columns.shape[0]
    owners = lax.axis_size("stick")
    groups = lax.axis_size("band")
    t = {name: jnp.asarray(value) for name, value in make_tables(g).items()}
    rows = g * g
    field = jax.ShapeDtypeStruct((rows // 2, LANES), F32)
    work = pltpu.VMEM((rows, LANES), F32)
    pot_flops = 6 * 2 * rows * 256 * 256

    def shifted(x, distance):
        return lax.ppermute(x, "band", [(i, (i - distance) % groups) for i in range(groups)])

    def swapped(x):
        return lax.ppermute(x, "band", [(i, i ^ 1) for i in range(groups)])

    sent = call(
        functools.partial(send_kernel, g),
        [jax.ShapeDtypeStruct((2 * g + 8, slots), F32)] * owners,
        [
            pltpu.VMEM((1, slots), jnp.int32),
            pltpu.SemaphoreType.DMA((owners,)),
            pltpu.SemaphoreType.DMA,
        ],
        10**6,
        sticks,
        stick_columns[None, :],
        space=pltpu.HBM,
        grant=SEND_GRANT,
    )
    received = exchanged(sent)
    first_tables = lax.optimization_barrier((t["stick_in"], t["left_backward"], sent[0]))[:2]
    first_tables = call(
        table_kernel, [jax.ShapeDtypeStruct(x.shape, BF16) for x in first_tables], [], 10**9, *first_tables
    )

    half = owners // 2
    order = [0] + list(range(half, owners)) + list(range(1, half))
    relays, columns = [], []
    for part in (order[: half + 1], order[half + 1 :]):
        shapes = [(len(part) * 2 * g, slots), (8, len(part) * slots)]
        shapes = [jax.ShapeDtypeStruct(shape, F32) for shape in shapes]
        relay, column = call(functools.partial(relay_kernel, g), shapes, [], 10**6, *[received[d] for d in part])
        relays.append(relay)
        columns.append(column)

    def orbital(blocks):
        return call(functools.partial(field_kernel, g), field, [work], 10**9, *blocks, *columns, *first_tables)

    phi = orbital(relays)
    near = swapped(phi)
    hot = call(
        functools.partial(pick_kernel, g), jax.ShapeDtypeStruct((owners * slots, rows), BF16), [], pot_flops, *columns
    )
    distances = (HALF,) if groups == 2 * HALF else (HALF, -HALF)
    fields = [orbital([shifted(x, distance) for x in relays]) for distance in distances]
    pot_tables = [t["forward"], t["last_backward"], t["left_forward"], t["left_backward"], t["coulomb"]]

    def potential_sum(kernel, *operands):
        return call(functools.partial(kernel, g), field, [work, work], pot_flops, phi, *operands, *pot_tables)

    if groups == 2 * HALF:
        weights = (2.0, 1.0)
        first, second = fields[0], swapped(fields[0])
        near, first = lax.optimization_barrier((near, first))
        total = potential_sum(near_kernel, near)
    else:
        weights = (1.0, 0.0)
        odd = lax.axis_index("band") % 2 == 1
        first = second = swapped(jnp.where(odd, fields[1], fields[0]))
        total = potential_sum(near_kernel, near)
        total = potential_sum(middle_kernel, *fields, total)
    order_back = {d: k for k, d in enumerate(order)}
    result = call(
        functools.partial(far_kernel, g, weights),
        [jax.ShapeDtypeStruct((2 * g, slots), F32)] * owners,
        [work, work, pltpu.VMEM((owners * slots, LANES), F32)],
        pot_flops,
        phi,
        first,
        second,
        total,
        hot,
        t["stick_out"],
        *pot_tables,
    )
    result = [result[order_back[d]] for d in range(owners)]
    return call(place_kernel, jax.ShapeDtypeStruct(sticks.shape, F32), [], 10**6, *exchanged(result))


def solution(mesh):
    return jax.shard_map(
        on_device,
        mesh=mesh,
        in_specs=(P("band", None, "stick"), P("stick")),
        out_specs=P("band", None, "stick"),
        check_vma=False,
    )
```

```python
import functools
import math

import jax
import jax.numpy as jnp
import numpy as np
from jax import lax
from jax.experimental import pallas as pl
from jax.experimental.pallas import tpu as pltpu
from jax.sharding import PartitionSpec as P

HALF = 2
BOX_LENGTH = 18.0
LANES = 128
MID = 64
WINDOW = 5
SEND_GRANT = 60
PAIRS = 6

F32 = jnp.float32
BF16 = jnp.bfloat16


def rounded_parts(table):
    high = table.astype(BF16).astype(np.float64)
    low = (table - high).astype(BF16).astype(np.float64)
    return high, low


def across(table):
    high, low = rounded_parts(table)
    return np.concatenate([high, high, low], 1).astype(np.float32)


def down(table):
    high, low = rounded_parts(table)
    return np.block([[high, low], [high, np.zeros_like(low)]]).astype(np.float32)


def make_tables(g):
    angle = 2.0 * np.pi / g * (np.outer(np.arange(g), np.arange(g)) % g)
    c, s = np.cos(angle), np.sin(angle)
    lower, upper = slice(0, g), slice(MID, MID + g)

    forward, backward = np.zeros((2, LANES, LANES))
    forward[lower, lower], forward[lower, upper] = c, -s
    forward[upper, lower], forward[upper, upper] = s, c
    backward[lower, lower], backward[lower, upper] = c, s
    backward[upper, lower], backward[upper, upper] = -s, c
    stick_in = np.zeros((LANES, 2 * g))
    stick_in[lower, :g], stick_in[lower, g:] = c, -s
    stick_in[upper, :g], stick_in[upper, g:] = s, c
    stick_out = np.zeros((2 * g, LANES))
    stick_out[:g, lower], stick_out[:g, upper] = c, s
    stick_out[g:, lower], stick_out[g:, upper] = -s, c

    freq = np.arange(g)
    square = np.minimum(freq, g - freq) ** 2
    total = square[:, None, None] + square[None, :, None] + square[None, None, :]
    unit = (2.0 * math.pi / BOX_LENGTH) ** 2
    kernel = np.where(total > 0, 4.0 * math.pi / (unit * np.maximum(total, 1)), 0.0)
    coulomb = np.zeros((g, g, LANES), np.float32)
    coulomb[:, :, lower] = kernel
    coulomb[:, :, upper] = kernel
    stick_in, left_backward = across(stick_in), across(np.concatenate([c, s], 0))
    early = np.zeros((LANES + 2 * g, stick_in.shape[1]), np.float32)
    early[:LANES], early[LANES:, : left_backward.shape[1]] = stick_in, left_backward
    return dict(
        forward=down(forward),
        last_backward=down(backward / g**3),
        left_forward=across(np.concatenate([c, -s], 0)),
        left_backward=left_backward,
        early=early,
        stick_out=across(stick_out * g**-1.5),
        coulomb=coulomb.reshape(g * g, LANES),
    )


def split(x):
    high = x.astype(BF16)
    low = (x - high.astype(F32)).astype(BF16)
    return high, low


def stacked(x):
    high, low = split(x)
    return jnp.concatenate([high, low, high], 0)


def dot(a, b):
    return jnp.dot(a, b, preferred_element_type=F32)


def lane_halves(shape):
    return lax.broadcasted_iota(jnp.int32, shape, 1) % LANES < MID


def turned(x):
    return pltpu.roll(x, MID, 1)


def regrouped(a, b):
    low = lane_halves(a.shape)
    return jnp.where(low, a, turned(b)), jnp.where(low, turned(a), b)


def beside(a, b):
    return jnp.concatenate([a, b], 1)


def halves(x):
    return x[:, :LANES], x[:, LANES:]


def left(table, x):
    both = dot(table, stacked(x))
    g = both.shape[0] // 2
    return both[:g], both[g:]


def left_complex(table, a, b):
    cos, sin = left(table, beside(a, b))
    sign = jnp.where(lane_halves((1, LANES)), -1.0, 1.0)
    return [p + turned(q) * sign for p, q in zip(halves(cos), halves(sin))]


def right(x, table):
    both = dot(beside(*split(x)), table)
    width = both.shape[1] // 2
    return both[:, :width] + both[:, width:]


def strided(ref, first, g):
    return ref[pl.ds(first, g, stride=g), :]


def slab_rows(index, g, count=1):
    return pl.ds(index * g, count * g)


def one_hot(index, wanted):
    return jnp.where(index == wanted, jnp.asarray(1, BF16), jnp.asarray(0, BF16))


def send_kernel(g, sticks_ref, columns_ref, *refs):
    block_refs, (row_ref, sems, row_sem) = refs[:-3], refs[-3:]
    own = lax.axis_index("stick")
    row_copy = pltpu.make_async_copy(columns_ref, row_ref, row_sem)
    row_copy.start()
    copies = [
        pltpu.make_async_copy(sticks_ref.at[own ^ d], ref.at[pl.ds(0, 2 * g)], sems.at[d])
        for d, ref in enumerate(block_refs)
    ]
    for copy in copies:
        copy.start()
    row_copy.wait()
    columns = jnp.broadcast_to(row_ref[...].astype(F32), (8, LANES))
    for ref in block_refs:
        ref[2 * g :, :] = columns
    for copy in copies:
        copy.wait()


def early_kernel(g, own_ref, tables_ref, staged_ref, stick_in_ref, left_ref):
    staged_ref[...] = own_ref[...]
    stick_in_ref[...] = tables_ref[:LANES, : stick_in_ref.shape[1]].astype(BF16)
    left_ref[...] = tables_ref[LANES:, : left_ref.shape[1]].astype(BF16)


def place_kernel(order, *refs):
    own = lax.axis_index("stick")
    out_ref = refs[-1]
    for d, block_ref in zip(order, refs[:-1]):
        out_ref[own ^ d] = block_ref[...]


def store(ref, first, slabs):
    g = slabs[0].shape[0]
    for k, slab in enumerate(slabs):
        ref[slab_rows(first + k, g), :] = slab


def relay_kernel(g, *refs):
    blocks, (coefficients_ref, columns_ref) = refs[:-2], refs[-2:]
    for k, ref in enumerate(blocks):
        coefficients_ref[k * 2 * g : (k + 1) * 2 * g, :] = ref[: 2 * g, :]
        columns_ref[:, k * LANES : (k + 1) * LANES] = ref[2 * g :, :]


def field_kernel(g, blocks_ref, columns_ref, stick_in_ref, left_ref, phi_ref, work_a):
    columns = columns_ref[:1, :].astype(jnp.int32)
    stick_in, backward = stick_in_ref[...], left_ref[...]
    blocks = [blocks_ref[k : k + 2 * g, :] for k in range(0, blocks_ref.shape[0], 2 * g)]
    sticks = []
    for k in range(0, len(blocks), 2):
        sticks.append(beside(*split(dot(stick_in, stacked(beside(blocks[k], blocks[k + 1]))).T)))
    sticks = jnp.concatenate(sticks, 0)

    half = g // 2
    index = lax.broadcasted_iota(jnp.int16, (half * g, columns.shape[1]), 0)
    for first in (0, half):
        both = dot(one_hot(index, (columns - first * g).astype(jnp.int16)), sticks)
        placed = both[:, :LANES] + both[:, LANES:]
        for k in range(0, half, 2):
            slabs = left_complex(backward, placed[k * g : (k + 1) * g], placed[(k + 1) * g : (k + 2) * g])
            store(work_a, first + k, slabs)

    for y in range(half):
        x = beside(strided(work_a, y, g), strided(work_a, y + half, g))
        (cos, cos_up), (sin, sin_up) = map(halves, left(backward, x))
        low = lane_halves(cos.shape)
        store(phi_ref, y, [jnp.where(low, cos - turned(sin), turned(cos_up) - sin_up)])


def pick_kernel(g, columns_ref, hot_ref):
    for k in range(0, columns_ref.shape[1], LANES):
        block = columns_ref[:, k : k + LANES]
        wanted = jnp.concatenate([block] * (LANES // block.shape[0]), 0).T.astype(jnp.int32)
        for c in range(0, hot_ref.shape[1], LANES):
            index = lax.broadcasted_iota(jnp.int16, (LANES, LANES), 1)
            hot_ref[k : k + LANES, c : c + LANES] = one_hot(index, (wanted - c).astype(jnp.int16))


def potentials(g, phi_ref, first_ref, second_ref, tables, work_a, work_b, emit):
    forward, last_backward, left_forward, left_backward = [ref[...].astype(BF16) for ref in tables[:4]]
    coulomb_ref = tables[4]
    half = g // 2
    for start in range(0, half, PAIRS):
        rows = slab_rows(start, g, PAIRS)
        phi = phi_ref[rows, :]
        lower, upper = regrouped(phi * first_ref[rows, :], phi * second_ref[rows, :])
        spectrum = right(jnp.concatenate([lower, upper], 0), forward)
        for k in range(PAIRS):
            a, b = left_complex(left_forward, *(spectrum[j * g : (j + 1) * g] for j in (k, k + PAIRS)))
            store(work_a, start + k, [a])
            store(work_a, start + k + half, [b])

    for kx in range(0, g, 2):
        slabs = left_complex(left_forward, strided(work_a, kx, g), strided(work_a, kx + 1, g))
        slabs = [slab * coulomb_ref[slab_rows(kx + j, g), :] for j, slab in enumerate(slabs)]
        store(work_b, kx, left_complex(left_backward, *slabs))

    for start in range(0, half, PAIRS):
        lower, upper = [], []
        for z in range(start, start + PAIRS):
            a, b = left_complex(left_backward, strided(work_b, z, g), strided(work_b, z + half, g))
            lower.append(a)
            upper.append(b)
        out = right(jnp.concatenate(lower + upper, 0), last_backward)
        emit(start, *regrouped(out[: PAIRS * g], out[PAIRS * g :]))


def near_kernel(g, phi_ref, other_ref, *refs):
    tables, (sum_ref, work_a, work_b) = refs[:5], refs[5:]

    def emit(start, own, other):
        rows = slab_rows(start, g, PAIRS)
        sum_ref[rows, :] = own * phi_ref[rows, :] + other * other_ref[rows, :]

    potentials(g, phi_ref, phi_ref, other_ref, tables, work_a, work_b, emit)


def middle_kernel(g, phi_ref, first_ref, second_ref, before_ref, *refs):
    tables, (sum_ref, work_a, work_b) = refs[:5], refs[5:]

    def emit(start, first, second):
        rows = slab_rows(start, g, PAIRS)
        sum_ref[rows, :] = before_ref[rows, :] + first * first_ref[rows, :] + second * second_ref[rows, :]

    potentials(g, phi_ref, first_ref, second_ref, tables, work_a, work_b, emit)


def far_kernel(g, weights, phi_ref, first_ref, second_ref, before_ref, hot_ref, stick_out_ref, *refs):
    tables, out_refs = refs[:5], refs[5:-3]
    work_a, work_b, picked_ref = refs[-3:]
    forward = tables[2][...].astype(BF16)
    half = g // 2

    def emit(start, first, second):
        rows = slab_rows(start, g, PAIRS)
        total = before_ref[rows, :] + weights[0] * (first * first_ref[rows, :])
        total = total + weights[1] * (second * second_ref[rows, :])
        for k in range(0, PAIRS, 2):
            cos, sin = left(forward, beside(total[k * g : (k + 1) * g], total[(k + 1) * g : (k + 2) * g]))
            for j, (real, imag) in enumerate(zip(halves(cos), halves(sin))):
                lower, upper = regrouped(real, imag)
                store(work_a, start + k + j, [lower])
                store(work_a, start + k + j + half, [upper])

    potentials(g, phi_ref, first_ref, second_ref, tables, work_a, work_b, emit)

    step = g // 3
    for first in range(0, g, step):
        slabs = []
        for kx in range(first, first + step, 2):
            slabs += left_complex(forward, strided(work_a, kx, g), strided(work_a, kx + 1, g))
        spectrum = beside(*split(jnp.concatenate(slabs, 0)))
        both = dot(hot_ref[:, first * g : (first + step) * g], spectrum)
        both = both[:, :LANES] + both[:, LANES:]
        picked_ref[...] = both if first == 0 else picked_ref[...] + both

    stick_out = stick_out_ref[...].astype(BF16)
    for k in range(0, len(out_refs), 2):
        high, low = split(picked_ref[k * LANES : (k + 2) * LANES, :])
        lined = jnp.concatenate([high, low, high], 1)
        out = lax.dot_general(stick_out, lined, (((1,), (1,)), ((), ())), preferred_element_type=F32)
        out_refs[k][...], out_refs[k + 1][...] = halves(out)


def call(kernel, out_shapes, scratch, flops, *operands, space=pltpu.VMEM, out_space=pltpu.VMEM, grant=40):
    out_spec = pl.BlockSpec(memory_space=out_space)
    return pl.pallas_call(
        kernel,
        out_shape=out_shapes,
        in_specs=[pl.BlockSpec(memory_space=space)] * len(operands),
        out_specs=jax.tree.map(lambda _: out_spec, out_shapes),
        scratch_shapes=scratch,
        compiler_params=pltpu.CompilerParams(vmem_limit_bytes=grant * 2**20),
        cost_estimate=pl.CostEstimate(flops=flops, bytes_accessed=flops, transcendentals=0),
    )(*operands)


def after(x, *others):
    return lax.optimization_barrier((x, *others))[0]


def exchanged(blocks, order, before):
    owners = len(blocks)
    moved = [blocks[0]] + [None] * (owners - 1)
    for d in order:
        others = [moved[x] if isinstance(x, int) else x for x in before.get(d, ())]
        block = after(blocks[d], *others) if others else blocks[d]
        moved[d] = lax.ppermute(block, "stick", [(i, i ^ d) for i in range(owners)])
    return moved


def on_device(sticks, stick_columns):
    g = sticks.shape[1] // 2
    slots = stick_columns.shape[0]
    owners = lax.axis_size("stick")
    groups = lax.axis_size("band")
    t = {name: jnp.asarray(value) for name, value in make_tables(g).items()}
    rows = g * g
    field = jax.ShapeDtypeStruct((rows // 2, LANES), F32)
    work = pltpu.VMEM((rows, LANES), F32)
    pot_flops = 1

    def shifted(x, distance):
        return lax.ppermute(x, "band", [(i, (i - distance) % groups) for i in range(groups)])

    def swapped(x):
        return lax.ppermute(x, "band", [(i, i ^ 1) for i in range(groups)])

    sent = call(
        functools.partial(send_kernel, g),
        [jax.ShapeDtypeStruct((2 * g + 8, slots), F32)] * owners,
        [
            pltpu.VMEM((1, slots), jnp.int32),
            pltpu.SemaphoreType.DMA((owners,)),
            pltpu.SemaphoreType.DMA,
        ],
        1,
        sticks,
        stick_columns[None, :],
        space=pltpu.HBM,
        grant=SEND_GRANT,
    )
    shapes = [(2 * g + 8, slots), (LANES, 6 * g), (2 * g, 3 * g)]
    staged, *first_tables = call(
        functools.partial(early_kernel, g),
        [jax.ShapeDtypeStruct(shape, kind) for shape, kind in zip(shapes, (F32, BF16, BF16))],
        [],
        1,
        sent[0],
        after(t["early"], sent[0]),
    )
    half = owners // 2
    distant, close = list(range(half, owners)), list(range(1, half))
    received = exchanged(sent, distant + close, {d: (half, staged, *first_tables) for d in close})
    received[0] = staged
    order = [0] + distant + close
    relay, columns = call(
        functools.partial(relay_kernel, g),
        [jax.ShapeDtypeStruct((owners * 2 * g, slots), F32), jax.ShapeDtypeStruct((8, owners * slots), F32)],
        [],
        1,
        *[received[d] for d in order],
    )

    def orbital(blocks):
        return call(functools.partial(field_kernel, g), field, [work], 1, blocks, columns, *first_tables)

    phi = orbital(relay)
    near = swapped(phi)
    hot = call(
        functools.partial(pick_kernel, g), jax.ShapeDtypeStruct((owners * slots, rows), BF16), [], pot_flops, columns
    )
    pot_tables = [t["forward"], t["last_backward"], t["left_forward"], t["left_backward"], t["coulomb"]]

    def potential_sum(kernel, *operands):
        return call(functools.partial(kernel, g), field, [work, work], pot_flops, phi, *operands, *pot_tables)

    distances = (HALF,) if groups == 2 * HALF else (HALF, -HALF)
    fields = [orbital(after(shifted(relay, distance), hot)) for distance in distances]
    total = potential_sum(near_kernel, after(near, *fields))
    if groups == 2 * HALF:
        weights = (2.0, 1.0)
        first, second = fields[0], swapped(fields[0])
    else:
        weights = (1.0, 0.0)
        odd = lax.axis_index("band") % 2 == 1
        first = second = swapped(jnp.where(odd, fields[1], fields[0]))
        total = potential_sum(middle_kernel, *fields, total)
    result = call(
        functools.partial(far_kernel, g, weights),
        [jax.ShapeDtypeStruct((2 * g, slots), F32)] * owners,
        [work, work, pltpu.VMEM((owners * slots, LANES), F32)],
        pot_flops,
        phi,
        first,
        second,
        total,
        hot,
        t["stick_out"],
        *pot_tables,
    )
    result = [result[order.index(d)] for d in range(owners)]
    mixed = [distant[0]] + [d for pair in zip(close, distant[1:]) for d in pair]
    before = {mixed[k]: (mixed[k - 3 - k % 2],) for k in range(WINDOW, len(mixed))}
    result = exchanged(result, mixed, before)
    return call(
        functools.partial(place_kernel, order),
        jax.ShapeDtypeStruct(sticks.shape, F32),
        [],
        1,
        *[result[d] for d in order],
    )


def solution(mesh):
    return jax.shard_map(
        on_device,
        mesh=mesh,
        in_specs=(P("band", None, "stick"), P("stick")),
        out_specs=P("band", None, "stick"),
        check_vma=False,
    )
```

```python
import functools
import math

import jax
import jax.numpy as jnp
import numpy as np
from jax import lax
from jax.experimental import pallas as pl
from jax.experimental.pallas import tpu as pltpu
from jax.sharding import PartitionSpec as P

HALF = 2
BOX_LENGTH = 18.0
LANES = 128
MID = 64
SEND_GRANT = 60
PAIRS = 6

F32 = jnp.float32
BF16 = jnp.bfloat16


def rounded_parts(table):
    high = table.astype(BF16).astype(np.float64)
    low = (table - high).astype(BF16).astype(np.float64)
    return high, low


def across(table):
    high, low = rounded_parts(table)
    return np.concatenate([high, high, low], 1).astype(np.float32)


def down(table):
    high, low = rounded_parts(table)
    return np.block([[high, low], [high, np.zeros_like(low)]]).astype(np.float32)


def make_tables(g):
    angle = 2.0 * np.pi / g * (np.outer(np.arange(g), np.arange(g)) % g)
    c, s = np.cos(angle), np.sin(angle)
    lower, upper = slice(0, g), slice(MID, MID + g)

    forward, backward = np.zeros((2, LANES, LANES))
    forward[lower, lower], forward[lower, upper] = c, -s
    forward[upper, lower], forward[upper, upper] = s, c
    backward[lower, lower], backward[lower, upper] = c, s
    backward[upper, lower], backward[upper, upper] = -s, c
    stick_in = np.zeros((LANES, 2 * g))
    stick_in[lower, :g], stick_in[lower, g:] = c, -s
    stick_in[upper, :g], stick_in[upper, g:] = s, c
    stick_out = np.zeros((2 * g, LANES))
    stick_out[:g, lower], stick_out[:g, upper] = c, s
    stick_out[g:, lower], stick_out[g:, upper] = -s, c

    freq = np.arange(g)
    square = np.minimum(freq, g - freq) ** 2
    total = square[:, None, None] + square[None, :, None] + square[None, None, :]
    unit = (2.0 * math.pi / BOX_LENGTH) ** 2
    kernel = np.where(total > 0, 4.0 * math.pi / (unit * np.maximum(total, 1)), 0.0)
    coulomb = np.zeros((g, g, LANES), np.float32)
    coulomb[:, :, lower] = kernel
    coulomb[:, :, upper] = kernel
    stick_in, left_backward = across(stick_in), across(np.concatenate([c, s], 0))
    early = np.zeros((LANES + 2 * g, stick_in.shape[1]), np.float32)
    early[:LANES], early[LANES:, : left_backward.shape[1]] = stick_in, left_backward
    return dict(
        forward=down(forward),
        last_backward=down(backward / g**3),
        left_forward=across(np.concatenate([c, -s], 0)),
        left_backward=left_backward,
        early=early,
        stick_out=across(stick_out * g**-1.5),
        coulomb=coulomb.reshape(g * g, LANES),
    )


def split(x):
    high = x.astype(BF16)
    low = (x - high.astype(F32)).astype(BF16)
    return high, low


def stacked(x):
    high, low = split(x)
    return jnp.concatenate([high, low, high], 0)


def dot(a, b):
    return jnp.dot(a, b, preferred_element_type=F32)


def lane_halves(shape):
    return lax.broadcasted_iota(jnp.int32, shape, 1) % LANES < MID


def turned(x):
    return pltpu.roll(x, MID, 1)


def regrouped(a, b):
    low = lane_halves(a.shape)
    return jnp.where(low, a, turned(b)), jnp.where(low, turned(a), b)


def beside(a, b):
    return jnp.concatenate([a, b], 1)


def halves(x):
    return x[:, :LANES], x[:, LANES:]


def left(table, x):
    both = dot(table, stacked(x))
    g = both.shape[0] // 2
    return both[:g], both[g:]


def left_complex(table, a, b):
    cos, sin = left(table, beside(a, b))
    sign = jnp.where(lane_halves((1, LANES)), -1.0, 1.0)
    return [p + turned(q) * sign for p, q in zip(halves(cos), halves(sin))]


def right(x, table):
    both = dot(beside(*split(x)), table)
    width = both.shape[1] // 2
    return both[:, :width] + both[:, width:]


def strided(ref, first, g):
    return ref[pl.ds(first, g, stride=g), :]


def slab_rows(index, g, count=1):
    return pl.ds(index * g, count * g)


def one_hot(index, wanted):
    return jnp.where(index == wanted, jnp.asarray(1, BF16), jnp.asarray(0, BF16))


def send_kernel(g, sticks_ref, columns_ref, *refs):
    block_refs, (row_ref, sems, row_sem) = refs[:-3], refs[-3:]
    own = lax.axis_index("stick")
    row_copy = pltpu.make_async_copy(columns_ref, row_ref, row_sem)
    row_copy.start()
    copies = [
        pltpu.make_async_copy(sticks_ref.at[own ^ d], ref.at[pl.ds(0, 2 * g)], sems.at[d])
        for d, ref in enumerate(block_refs)
    ]
    for copy in copies:
        copy.start()
    row_copy.wait()
    columns = jnp.broadcast_to(row_ref[...].astype(F32), (8, LANES))
    for ref in block_refs:
        ref[2 * g :, :] = columns
    for copy in copies:
        copy.wait()


def early_kernel(g, own_ref, tables_ref, staged_ref, stick_in_ref, left_ref):
    staged_ref[...] = own_ref[...]
    stick_in_ref[...] = tables_ref[:LANES, : stick_in_ref.shape[1]].astype(BF16)
    left_ref[...] = tables_ref[LANES:, : left_ref.shape[1]].astype(BF16)


def place_kernel(order, *refs):
    own = lax.axis_index("stick")
    out_ref = refs[-1]
    for d, block_ref in zip(order, refs[:-1]):
        out_ref[own ^ d] = block_ref[...]


def store(ref, first, slabs):
    g = slabs[0].shape[0]
    for k, slab in enumerate(slabs):
        ref[slab_rows(first + k, g), :] = slab


def relay_kernel(g, *refs):
    blocks, (coefficients_ref, columns_ref) = refs[:-2], refs[-2:]
    for k, ref in enumerate(blocks):
        coefficients_ref[k * 2 * g : (k + 1) * 2 * g, :] = ref[: 2 * g, :]
        columns_ref[:, k * LANES : (k + 1) * LANES] = ref[2 * g :, :]


def field_kernel(g, blocks_ref, columns_ref, stick_in_ref, left_ref, phi_ref, work_a):
    columns = columns_ref[:1, :].astype(jnp.int32)
    stick_in, backward = stick_in_ref[...], left_ref[...]
    blocks = [blocks_ref[k : k + 2 * g, :] for k in range(0, blocks_ref.shape[0], 2 * g)]
    sticks = []
    for k in range(0, len(blocks), 2):
        sticks.append(beside(*split(dot(stick_in, stacked(beside(blocks[k], blocks[k + 1]))).T)))
    sticks = jnp.concatenate(sticks, 0)

    half = g // 2
    index = lax.broadcasted_iota(jnp.int16, (half * g, columns.shape[1]), 0)
    for first in (0, half):
        both = dot(one_hot(index, (columns - first * g).astype(jnp.int16)), sticks)
        placed = both[:, :LANES] + both[:, LANES:]
        for k in range(0, half, 2):
            slabs = left_complex(backward, placed[k * g : (k + 1) * g], placed[(k + 1) * g : (k + 2) * g])
            store(work_a, first + k, slabs)

    for y in range(half):
        x = beside(strided(work_a, y, g), strided(work_a, y + half, g))
        (cos, cos_up), (sin, sin_up) = map(halves, left(backward, x))
        low = lane_halves(cos.shape)
        store(phi_ref, y, [jnp.where(low, cos - turned(sin), turned(cos_up) - sin_up)])


def hot_kernel(g, columns_ref, *hot_refs):
    first = 0
    for hot_ref in hot_refs:
        for k in range(0, hot_ref.shape[0], LANES):
            block = columns_ref[:, first + k : first + k + LANES]
            wanted = jnp.concatenate([block] * (LANES // block.shape[0]), 0).T.astype(jnp.int32)
            for c in range(0, hot_ref.shape[1], LANES):
                index = lax.broadcasted_iota(jnp.int16, (LANES, LANES), 1)
                hot_ref[k : k + LANES, c : c + LANES] = one_hot(index, (wanted - c).astype(jnp.int16))
        first += hot_ref.shape[0]


def potentials(g, phi_ref, first_ref, second_ref, tables, work_a, work_b, emit):
    forward, last_backward, left_forward, left_backward = [ref[...].astype(BF16) for ref in tables[:4]]
    coulomb_ref = tables[4]
    half = g // 2
    for start in range(0, half, PAIRS):
        rows = slab_rows(start, g, PAIRS)
        phi = phi_ref[rows, :]
        lower, upper = regrouped(phi * first_ref[rows, :], phi * second_ref[rows, :])
        spectrum = right(jnp.concatenate([lower, upper], 0), forward)
        for k in range(PAIRS):
            a, b = left_complex(left_forward, *(spectrum[j * g : (j + 1) * g] for j in (k, k + PAIRS)))
            store(work_a, start + k, [a])
            store(work_a, start + k + half, [b])

    for kx in range(0, g, 2):
        slabs = left_complex(left_forward, strided(work_a, kx, g), strided(work_a, kx + 1, g))
        slabs = [slab * coulomb_ref[slab_rows(kx + j, g), :] for j, slab in enumerate(slabs)]
        store(work_b, kx, left_complex(left_backward, *slabs))

    for start in range(0, half, PAIRS):
        lower, upper = [], []
        for z in range(start, start + PAIRS):
            a, b = left_complex(left_backward, strided(work_b, z, g), strided(work_b, z + half, g))
            lower.append(a)
            upper.append(b)
        out = right(jnp.concatenate(lower + upper, 0), last_backward)
        emit(start, *regrouped(out[: PAIRS * g], out[PAIRS * g :]))


def near_kernel(g, phi_ref, other_ref, *refs):
    tables, (sum_ref, work_a, work_b) = refs[:5], refs[5:]

    def emit(start, own, other):
        rows = slab_rows(start, g, PAIRS)
        sum_ref[rows, :] = own * phi_ref[rows, :] + other * other_ref[rows, :]

    potentials(g, phi_ref, phi_ref, other_ref, tables, work_a, work_b, emit)


def middle_kernel(g, phi_ref, first_ref, second_ref, before_ref, *refs):
    tables, (sum_ref, work_a, work_b) = refs[:5], refs[5:]

    def emit(start, first, second):
        rows = slab_rows(start, g, PAIRS)
        sum_ref[rows, :] = before_ref[rows, :] + first * first_ref[rows, :] + second * second_ref[rows, :]

    potentials(g, phi_ref, first_ref, second_ref, tables, work_a, work_b, emit)


def far_kernel(g, weights, phi_ref, first_ref, second_ref, before_ref, *refs):
    tables, (spectrum_ref, work_a, work_b) = refs[:5], refs[5:]
    forward = tables[2][...].astype(BF16)
    half = g // 2

    def emit(start, first, second):
        rows = slab_rows(start, g, PAIRS)
        total = before_ref[rows, :] + weights[0] * (first * first_ref[rows, :])
        total = total + weights[1] * (second * second_ref[rows, :])
        for k in range(0, PAIRS, 2):
            cos, sin = left(forward, beside(total[k * g : (k + 1) * g], total[(k + 1) * g : (k + 2) * g]))
            for j, (real, imag) in enumerate(zip(halves(cos), halves(sin))):
                lower, upper = regrouped(real, imag)
                store(work_a, start + k + j, [lower])
                store(work_a, start + k + j + half, [upper])

    potentials(g, phi_ref, first_ref, second_ref, tables, work_a, work_b, emit)

    for kx in range(0, g, 2):
        slabs = left_complex(forward, strided(work_a, kx, g), strided(work_a, kx + 1, g))
        spectrum_ref[slab_rows(kx, g, 2), :] = beside(*split(jnp.concatenate(slabs, 0)))


def pick_kernel(g, spectrum_ref, hot_ref, stick_out_ref, *out_refs):
    both = dot(hot_ref[...], spectrum_ref[...])
    picked = both[:, :LANES] + both[:, LANES:]
    stick_out = stick_out_ref[...].astype(BF16)
    for k in range(0, len(out_refs), 2):
        lined = beside(*[picked[j * LANES : (j + 1) * LANES].T for j in (k, k + 1)])
        out_refs[k][...], out_refs[k + 1][...] = halves(dot(stick_out, stacked(lined)))


def call(kernel, out_shapes, scratch, flops, *operands, space=pltpu.VMEM, out_space=pltpu.VMEM, grant=40):
    out_spec = pl.BlockSpec(memory_space=out_space)
    return pl.pallas_call(
        kernel,
        out_shape=out_shapes,
        in_specs=[pl.BlockSpec(memory_space=space)] * len(operands),
        out_specs=jax.tree.map(lambda _: out_spec, out_shapes),
        scratch_shapes=scratch,
        compiler_params=pltpu.CompilerParams(vmem_limit_bytes=grant * 2**20),
        cost_estimate=pl.CostEstimate(flops=flops, bytes_accessed=flops, transcendentals=0),
    )(*operands)


def after(x, *others):
    return lax.optimization_barrier((x, *others))[0]


def moved(block, d, owners):
    return lax.ppermute(block, "stick", [(i, i ^ d) for i in range(owners)])


def on_device(sticks, stick_columns):
    g = sticks.shape[1] // 2
    slots = stick_columns.shape[0]
    owners = lax.axis_size("stick")
    groups = lax.axis_size("band")
    t = {name: jnp.asarray(value) for name, value in make_tables(g).items()}
    rows = g * g
    field = jax.ShapeDtypeStruct((rows // 2, LANES), F32)
    work = pltpu.VMEM((rows, LANES), F32)
    pot_flops = 1

    def shifted(x, distance):
        return lax.ppermute(x, "band", [(i, (i - distance) % groups) for i in range(groups)])

    def swapped(x):
        return lax.ppermute(x, "band", [(i, i ^ 1) for i in range(groups)])

    sent = call(
        functools.partial(send_kernel, g),
        [jax.ShapeDtypeStruct((2 * g + 8, slots), F32)] * owners,
        [
            pltpu.VMEM((1, slots), jnp.int32),
            pltpu.SemaphoreType.DMA((owners,)),
            pltpu.SemaphoreType.DMA,
        ],
        1,
        sticks,
        stick_columns[None, :],
        space=pltpu.HBM,
        grant=SEND_GRANT,
    )
    shapes = [(2 * g + 8, slots), (LANES, 6 * g), (2 * g, 3 * g)]
    staged, *first_tables = call(
        functools.partial(early_kernel, g),
        [jax.ShapeDtypeStruct(shape, kind) for shape, kind in zip(shapes, (F32, BF16, BF16))],
        [],
        1,
        sent[0],
        after(t["early"], sent[0]),
    )
    half = owners // 2
    distant, close = list(range(half, owners)), list(range(1, half))
    received = {0: staged}
    for d in distant:
        received[d] = moved(sent[d], d, owners)
    for d in close:
        received[d] = moved(after(sent[d], received[half], staged, *first_tables), d, owners)
    order = distant + close + [0]
    relay, columns = call(
        functools.partial(relay_kernel, g),
        [jax.ShapeDtypeStruct((owners * 2 * g, slots), F32), jax.ShapeDtypeStruct((8, owners * slots), F32)],
        [],
        1,
        *[received[d] for d in order],
    )

    def orbital(blocks):
        return call(functools.partial(field_kernel, g), field, [work], 1, blocks, columns, *first_tables)

    phi = orbital(relay)
    near = swapped(phi)
    hot = call(
        functools.partial(hot_kernel, g),
        [jax.ShapeDtypeStruct((half * slots, rows), BF16)] * 2,
        [],
        pot_flops,
        columns,
    )
    pot_tables = [t["forward"], t["last_backward"], t["left_forward"], t["left_backward"], t["coulomb"]]

    def potential_sum(kernel, *operands):
        return call(functools.partial(kernel, g), field, [work, work], pot_flops, phi, *operands, *pot_tables)

    distances = (HALF,) if groups == 2 * HALF else (HALF, -HALF)
    fields = [orbital(after(shifted(relay, distance), *hot)) for distance in distances]
    total = potential_sum(near_kernel, after(near, *fields))
    if groups == 2 * HALF:
        weights = (2.0, 1.0)
        first, second = fields[0], swapped(fields[0])
    else:
        weights = (1.0, 0.0)
        odd = lax.axis_index("band") % 2 == 1
        first = second = swapped(jnp.where(odd, fields[1], fields[0]))
        total = potential_sum(middle_kernel, *fields, total)
    spectrum = call(
        functools.partial(far_kernel, g, weights),
        jax.ShapeDtypeStruct((rows, 2 * LANES), BF16),
        [work, work],
        pot_flops,
        phi,
        first,
        second,
        total,
        *pot_tables,
    )

    def picked(spectrum, hot):
        shapes = [jax.ShapeDtypeStruct((2 * g, slots), F32)] * half
        return call(functools.partial(pick_kernel, g), shapes, [], 1, spectrum, hot, t["stick_out"])

    result = {}
    for d, block in zip(distant, picked(spectrum, hot[0])):
        result[d] = moved(block, d, owners)
    *blocks, result[0] = picked(after(spectrum, result[half]), hot[1])
    for k, block in enumerate(blocks):
        result[close[k]] = moved(block, close[k], owners)
    return call(
        functools.partial(place_kernel, order),
        jax.ShapeDtypeStruct(sticks.shape, F32),
        [],
        1,
        *[result[d] for d in order],
    )


def solution(mesh):
    return jax.shard_map(
        on_device,
        mesh=mesh,
        in_specs=(P("band", None, "stick"), P("stick")),
        out_specs=P("band", None, "stick"),
        check_vma=False,
    )
```

```python
import functools
import math

import jax
import jax.numpy as jnp
import numpy as np
from jax import lax
from jax.experimental import pallas as pl
from jax.experimental.pallas import tpu as pltpu
from jax.sharding import PartitionSpec as P

HALF = 2
BOX_LENGTH = 18.0
LANES = 128
MID = 64
WINDOW = 5
SEND_GRANT = 60
PAIRS = 4
WIDE = 8

F32 = jnp.float32
BF16 = jnp.bfloat16


def rounded_parts(table):
    high = table.astype(BF16).astype(np.float64)
    low = (table - high).astype(BF16).astype(np.float64)
    return high, low


def across(table):
    high, low = rounded_parts(table)
    return np.concatenate([high, high, low], 1).astype(np.float32)


def down(table):
    high, low = rounded_parts(table)
    return np.block([[high, low], [high, np.zeros_like(low)]]).astype(np.float32)


def make_tables(g):
    angle = 2.0 * np.pi / g * (np.outer(np.arange(g), np.arange(g)) % g)
    c, s = np.cos(angle), np.sin(angle)
    lower, upper = slice(0, g), slice(MID, MID + g)

    forward, backward = np.zeros((2, LANES, LANES))
    forward[lower, lower], forward[lower, upper] = c, -s
    forward[upper, lower], forward[upper, upper] = s, c
    backward[lower, lower], backward[lower, upper] = c, s
    backward[upper, lower], backward[upper, upper] = -s, c
    stick_in = np.zeros((LANES, 2 * g))
    stick_in[lower, :g], stick_in[lower, g:] = c, -s
    stick_in[upper, :g], stick_in[upper, g:] = s, c
    stick_out = np.zeros((2 * g, LANES))
    stick_out[:g, lower], stick_out[:g, upper] = c, s
    stick_out[g:, lower], stick_out[g:, upper] = -s, c

    freq = np.arange(g)
    square = np.minimum(freq, g - freq) ** 2
    total = square[:, None, None] + square[None, :, None] + square[None, None, :]
    unit = (2.0 * math.pi / BOX_LENGTH) ** 2
    kernel = np.where(total > 0, 4.0 * math.pi / (unit * np.maximum(total, 1)), 0.0)
    coulomb = np.zeros((g, g, LANES), np.float32)
    coulomb[:, :, lower] = kernel
    coulomb[:, :, upper] = kernel
    stick_in, left_backward = across(stick_in), across(np.concatenate([c, s], 0))
    early = np.zeros((LANES + 2 * g, stick_in.shape[1]), np.float32)
    early[:LANES], early[LANES:, : left_backward.shape[1]] = stick_in, left_backward
    return dict(
        forward=down(forward),
        last_backward=down(backward / g**3),
        left_forward=across(np.concatenate([c, -s], 0)),
        left_backward=left_backward,
        early=early,
        stick_out=across(stick_out * g**-1.5),
        coulomb=coulomb.reshape(g * g, LANES),
    )


def split(x):
    high = x.astype(BF16)
    low = (x - high.astype(F32)).astype(BF16)
    return high, low


def stacked(x):
    high, low = split(x)
    return jnp.concatenate([high, low, high], 0)


def dot(a, b):
    return jnp.dot(a, b, preferred_element_type=F32)


def lane_halves(shape):
    return lax.broadcasted_iota(jnp.int32, shape, 1) % LANES < MID


def turned(x):
    return pltpu.roll(x, MID, 1)


def regrouped(a, b):
    low = lane_halves(a.shape)
    return jnp.where(low, a, turned(b)), jnp.where(low, turned(a), b)


def beside(a, b):
    return jnp.concatenate([a, b], 1)


def pieces(x):
    return [x[:, k : k + LANES] for k in range(0, x.shape[1], LANES)]


def left(table, slabs):
    both = dot(table, stacked(jnp.concatenate(slabs, 1)))
    g = both.shape[0] // 2
    return pieces(both[:g]), pieces(both[g:])


def left_complex(table, slabs):
    sign = jnp.where(lane_halves((1, LANES)), -1.0, 1.0)
    return [cos + turned(sin) * sign for cos, sin in zip(*left(table, slabs))]


def right(x, table):
    both = dot(beside(*split(x)), table)
    width = both.shape[1] // 2
    return both[:, :width] + both[:, width:]


def strided(ref, first, g):
    return ref[pl.ds(first, g, stride=g), :]


def slab_rows(index, g, count=1):
    return pl.ds(index * g, count * g)


def one_hot(index, wanted):
    return jnp.where(index == wanted, jnp.asarray(1, BF16), jnp.asarray(0, BF16))


def send_kernel(g, sticks_ref, columns_ref, *refs):
    block_refs, (row_ref, sems, row_sem) = refs[:-3], refs[-3:]
    own = lax.axis_index("stick")
    row_copy = pltpu.make_async_copy(columns_ref, row_ref, row_sem)
    row_copy.start()
    copies = [
        pltpu.make_async_copy(sticks_ref.at[own ^ d], ref.at[pl.ds(0, 2 * g)], sems.at[d])
        for d, ref in enumerate(block_refs)
    ]
    for copy in copies:
        copy.start()
    row_copy.wait()
    columns = jnp.broadcast_to(row_ref[...].astype(F32), (8, LANES))
    for ref in block_refs:
        ref[2 * g :, :] = columns
    for copy in copies:
        copy.wait()


def early_kernel(g, own_ref, tables_ref, staged_ref, stick_in_ref, left_ref):
    staged_ref[...] = own_ref[...]
    stick_in_ref[...] = tables_ref[:LANES, : stick_in_ref.shape[1]].astype(BF16)
    left_ref[...] = tables_ref[LANES:, : left_ref.shape[1]].astype(BF16)


def place_kernel(order, *refs):
    own = lax.axis_index("stick")
    out_ref = refs[-1]
    for d, block_ref in zip(order, refs[:-1]):
        out_ref[own ^ d] = block_ref[...]


def store(ref, first, slabs):
    g = slabs[0].shape[0]
    for k, slab in enumerate(slabs):
        ref[slab_rows(first + k, g), :] = slab


def relay_kernel(g, *refs):
    blocks, (coefficients_ref, columns_ref) = refs[:-2], refs[-2:]
    for k, ref in enumerate(blocks):
        coefficients_ref[k * 2 * g : (k + 1) * 2 * g, :] = ref[: 2 * g, :]
        columns_ref[:, k * LANES : (k + 1) * LANES] = ref[2 * g :, :]


def field_kernel(g, blocks_ref, columns_ref, stick_in_ref, left_ref, phi_ref, work_a):
    columns = columns_ref[:1, :].astype(jnp.int32)
    stick_in, backward = stick_in_ref[...], left_ref[...]
    blocks = [blocks_ref[k : k + 2 * g, :] for k in range(0, blocks_ref.shape[0], 2 * g)]
    sticks = []
    for k in range(0, len(blocks), 2):
        sticks.append(beside(*split(dot(stick_in, stacked(beside(blocks[k], blocks[k + 1]))).T)))
    sticks = jnp.concatenate(sticks, 0)

    half = g // 2
    index = lax.broadcasted_iota(jnp.int16, (half * g, columns.shape[1]), 0)
    for first in (0, half):
        both = dot(one_hot(index, (columns - first * g).astype(jnp.int16)), sticks)
        placed = both[:, :LANES] + both[:, LANES:]
        for k in range(0, half, WIDE):
            slabs = left_complex(backward, [placed[j * g : (j + 1) * g] for j in range(k, k + WIDE)])
            store(work_a, first + k, slabs)

    low = lane_halves((g, LANES))
    for first in range(0, half, WIDE // 2):
        lower = [strided(work_a, y, g) for y in range(first, first + WIDE // 2)]
        upper = [strided(work_a, y + half, g) for y in range(first, first + WIDE // 2)]
        cos, sin = left(backward, lower + upper)
        for k in range(WIDE // 2):
            j = k + WIDE // 2
            field = jnp.where(low, cos[k] - turned(sin[k]), turned(cos[j]) - sin[j])
            store(phi_ref, first + k, [field])


def pick_kernel(g, columns_ref, hot_ref):
    for k in range(0, columns_ref.shape[1], LANES):
        block = columns_ref[:, k : k + LANES]
        wanted = jnp.concatenate([block] * (LANES // block.shape[0]), 0).T.astype(jnp.int32)
        for c in range(0, hot_ref.shape[1], LANES):
            index = lax.broadcasted_iota(jnp.int16, (LANES, LANES), 1)
            hot_ref[k : k + LANES, c : c + LANES] = one_hot(index, (wanted - c).astype(jnp.int16))


def potentials(g, phi_ref, first_ref, second_ref, tables, work_a, work_b, emit):
    forward, last_backward, left_forward, left_backward = [ref[...].astype(BF16) for ref in tables[:4]]
    coulomb_ref = tables[4]
    half = g // 2
    for start in range(0, half, PAIRS):
        rows = slab_rows(start, g, PAIRS)
        phi = phi_ref[rows, :]
        lower, upper = regrouped(phi * first_ref[rows, :], phi * second_ref[rows, :])
        spectrum = right(jnp.concatenate([lower, upper], 0), forward)
        for k in range(0, PAIRS, WIDE // 2):
            chosen = list(range(k, k + WIDE // 2)) + list(range(k + PAIRS, k + PAIRS + WIDE // 2))
            slabs = left_complex(left_forward, [spectrum[j * g : (j + 1) * g] for j in chosen])
            store(work_a, start + k, slabs[: WIDE // 2])
            store(work_a, start + k + half, slabs[WIDE // 2 :])

    for kx in range(0, g, WIDE):
        slabs = left_complex(left_forward, [strided(work_a, kx + j, g) for j in range(WIDE)])
        slabs = [slab * coulomb_ref[slab_rows(kx + j, g), :] for j, slab in enumerate(slabs)]
        store(work_b, kx, left_complex(left_backward, slabs))

    for start in range(0, half, PAIRS):
        lower, upper = [], []
        for y in range(start, start + PAIRS, WIDE // 2):
            chosen = list(range(y, y + WIDE // 2))
            slabs = left_complex(left_backward, [strided(work_b, j, g) for j in chosen + [j + half for j in chosen]])
            lower += slabs[: WIDE // 2]
            upper += slabs[WIDE // 2 :]
        out = right(jnp.concatenate(lower + upper, 0), last_backward)
        emit(start, *regrouped(out[: PAIRS * g], out[PAIRS * g :]))


def near_kernel(g, phi_ref, other_ref, *refs):
    tables, (sum_ref, work_a, work_b) = refs[:5], refs[5:]

    def emit(start, own, other):
        rows = slab_rows(start, g, PAIRS)
        sum_ref[rows, :] = own * phi_ref[rows, :] + other * other_ref[rows, :]

    potentials(g, phi_ref, phi_ref, other_ref, tables, work_a, work_b, emit)


def middle_kernel(g, phi_ref, first_ref, second_ref, before_ref, *refs):
    tables, (sum_ref, work_a, work_b) = refs[:5], refs[5:]

    def emit(start, first, second):
        rows = slab_rows(start, g, PAIRS)
        sum_ref[rows, :] = before_ref[rows, :] + first * first_ref[rows, :] + second * second_ref[rows, :]

    potentials(g, phi_ref, first_ref, second_ref, tables, work_a, work_b, emit)


def far_kernel(g, weights, phi_ref, first_ref, second_ref, before_ref, hot_ref, stick_out_ref, *refs):
    tables, out_refs = refs[:5], refs[5:-3]
    work_a, work_b, picked_ref = refs[-3:]
    forward = tables[2][...].astype(BF16)
    half = g // 2

    def emit(start, first, second):
        rows = slab_rows(start, g, PAIRS)
        total = before_ref[rows, :] + weights[0] * (first * first_ref[rows, :])
        total = total + weights[1] * (second * second_ref[rows, :])
        cos, sin = left(forward, [total[k * g : (k + 1) * g] for k in range(PAIRS)])
        for k, (real, imag) in enumerate(zip(cos, sin)):
            lower, upper = regrouped(real, imag)
            store(work_a, start + k, [lower])
            store(work_a, start + k + half, [upper])

    potentials(g, phi_ref, first_ref, second_ref, tables, work_a, work_b, emit)

    step = g // 3
    for first in range(0, g, step):
        slabs = []
        for kx in range(first, first + step, WIDE):
            slabs += left_complex(forward, [strided(work_a, kx + j, g) for j in range(WIDE)])
        spectrum = beside(*split(jnp.concatenate(slabs, 0)))
        both = dot(hot_ref[:, first * g : (first + step) * g], spectrum)
        both = both[:, :LANES] + both[:, LANES:]
        picked_ref[...] = both if first == 0 else picked_ref[...] + both

    stick_out = stick_out_ref[...].astype(BF16)
    for k in range(0, len(out_refs), 2):
        lined = beside(*[picked_ref[j * LANES : (j + 1) * LANES, :].T for j in (k, k + 1)])
        out_refs[k][...], out_refs[k + 1][...] = pieces(dot(stick_out, stacked(lined)))


def call(kernel, out_shapes, scratch, flops, *operands, space=pltpu.VMEM, out_space=pltpu.VMEM, grant=40):
    out_spec = pl.BlockSpec(memory_space=out_space)
    return pl.pallas_call(
        kernel,
        out_shape=out_shapes,
        in_specs=[pl.BlockSpec(memory_space=space)] * len(operands),
        out_specs=jax.tree.map(lambda _: out_spec, out_shapes),
        scratch_shapes=scratch,
        compiler_params=pltpu.CompilerParams(vmem_limit_bytes=grant * 2**20),
        cost_estimate=pl.CostEstimate(flops=flops, bytes_accessed=flops, transcendentals=0),
    )(*operands)


def after(x, *others):
    return lax.optimization_barrier((x, *others))[0]


def exchanged(blocks, order, before):
    owners = len(blocks)
    moved = [blocks[0]] + [None] * (owners - 1)
    for d in order:
        others = [moved[x] if isinstance(x, int) else x for x in before.get(d, ())]
        block = after(blocks[d], *others) if others else blocks[d]
        moved[d] = lax.ppermute(block, "stick", [(i, i ^ d) for i in range(owners)])
    return moved


def on_device(sticks, stick_columns):
    g = sticks.shape[1] // 2
    slots = stick_columns.shape[0]
    owners = lax.axis_size("stick")
    groups = lax.axis_size("band")
    t = {name: jnp.asarray(value) for name, value in make_tables(g).items()}
    rows = g * g
    field = jax.ShapeDtypeStruct((rows // 2, LANES), F32)
    work = pltpu.VMEM((rows, LANES), F32)
    pot_flops = 1

    def shifted(x, distance):
        return lax.ppermute(x, "band", [(i, (i - distance) % groups) for i in range(groups)])

    def swapped(x):
        return lax.ppermute(x, "band", [(i, i ^ 1) for i in range(groups)])

    sent = call(
        functools.partial(send_kernel, g),
        [jax.ShapeDtypeStruct((2 * g + 8, slots), F32)] * owners,
        [
            pltpu.VMEM((1, slots), jnp.int32),
            pltpu.SemaphoreType.DMA((owners,)),
            pltpu.SemaphoreType.DMA,
        ],
        1,
        sticks,
        stick_columns[None, :],
        space=pltpu.HBM,
        grant=SEND_GRANT,
    )
    shapes = [(2 * g + 8, slots), (LANES, 6 * g), (2 * g, 3 * g)]
    staged, *first_tables = call(
        functools.partial(early_kernel, g),
        [jax.ShapeDtypeStruct(shape, kind) for shape, kind in zip(shapes, (F32, BF16, BF16))],
        [],
        1,
        sent[0],
        after(t["early"], sent[0]),
    )
    half = owners // 2
    distant, close = list(range(half, owners)), list(range(1, half))
    mixed = [distant[0]] + [d for pair in zip(close, distant[1:]) for d in pair]
    before = {mixed[k]: (mixed[k - 3 - k % 2],) for k in range(WINDOW, len(mixed))}
    last = mixed[WINDOW]
    received = exchanged(sent, mixed, {**before, last: (*before[last], staged, *first_tables)})
    received[0] = staged
    order = [0] + distant + close
    relay, columns = call(
        functools.partial(relay_kernel, g),
        [jax.ShapeDtypeStruct((owners * 2 * g, slots), F32), jax.ShapeDtypeStruct((8, owners * slots), F32)],
        [],
        1,
        *[received[d] for d in order],
    )

    def orbital(blocks):
        return call(functools.partial(field_kernel, g), field, [work], 1, blocks, columns, *first_tables)

    phi = orbital(relay)
    near = swapped(phi)
    hot = call(
        functools.partial(pick_kernel, g), jax.ShapeDtypeStruct((owners * slots, rows), BF16), [], pot_flops, columns
    )
    pot_tables = [t["forward"], t["last_backward"], t["left_forward"], t["left_backward"], t["coulomb"]]

    def potential_sum(kernel, *operands):
        return call(functools.partial(kernel, g), field, [work, work], pot_flops, phi, *operands, *pot_tables)

    distances = (HALF,) if groups == 2 * HALF else (HALF, -HALF)
    fields = [orbital(after(shifted(relay, distance), hot)) for distance in distances]
    total = potential_sum(near_kernel, after(near, *fields))
    if groups == 2 * HALF:
        weights = (2.0, 1.0)
        first, second = fields[0], swapped(fields[0])
    else:
        weights = (1.0, 0.0)
        odd = lax.axis_index("band") % 2 == 1
        first = second = swapped(jnp.where(odd, fields[1], fields[0]))
        total = potential_sum(middle_kernel, *fields, total)
    result = call(
        functools.partial(far_kernel, g, weights),
        [jax.ShapeDtypeStruct((2 * g, slots), F32)] * owners,
        [work, work, pltpu.VMEM((owners * slots, LANES), F32)],
        pot_flops,
        phi,
        first,
        second,
        total,
        hot,
        t["stick_out"],
        *pot_tables,
    )
    result = [result[order.index(d)] for d in range(owners)]
    result = exchanged(result, mixed, before)
    return call(
        functools.partial(place_kernel, order),
        jax.ShapeDtypeStruct(sticks.shape, F32),
        [],
        1,
        *[result[d] for d in order],
    )


def solution(mesh):
    return jax.shard_map(
        on_device,
        mesh=mesh,
        in_specs=(P("band", None, "stick"), P("stick")),
        out_specs=P("band", None, "stick"),
        check_vma=False,
    )
```

```python
import functools
import math

import jax
import jax.numpy as jnp
import numpy as np
from jax import lax
from jax.experimental import pallas as pl
from jax.experimental.pallas import tpu as pltpu
from jax.sharding import PartitionSpec as P

HALF = 2
BOX_LENGTH = 18.0
LANES = 128
MID = 64
WINDOW = 5
SEND_GRANT = 60
PAIRS = 4

F32 = jnp.float32
BF16 = jnp.bfloat16


def rounded_parts(table):
    high = table.astype(BF16).astype(np.float64)
    low = (table - high).astype(BF16).astype(np.float64)
    return high, low


def across(table):
    high, low = rounded_parts(table)
    return np.concatenate([high, high, low], 1).astype(np.float32)


def down(table):
    high, low = rounded_parts(table)
    return np.block([[high, low], [high, np.zeros_like(low)]]).astype(np.float32)


def make_tables(g):
    angle = 2.0 * np.pi / g * (np.outer(np.arange(g), np.arange(g)) % g)
    c, s = np.cos(angle), np.sin(angle)
    lower, upper = slice(0, g), slice(MID, MID + g)

    forward, backward = np.zeros((2, LANES, LANES))
    forward[lower, lower], forward[lower, upper] = c, -s
    forward[upper, lower], forward[upper, upper] = s, c
    backward[lower, lower], backward[lower, upper] = c, s
    backward[upper, lower], backward[upper, upper] = -s, c
    stick_in = np.zeros((LANES, 2 * g))
    stick_in[lower, :g], stick_in[lower, g:] = c, -s
    stick_in[upper, :g], stick_in[upper, g:] = s, c
    stick_out = np.zeros((2 * g, LANES))
    stick_out[:g, lower], stick_out[:g, upper] = c, s
    stick_out[g:, lower], stick_out[g:, upper] = -s, c

    freq = np.arange(g)
    square = np.minimum(freq, g - freq) ** 2
    total = square[:, None, None] + square[None, :, None] + square[None, None, :]
    unit = (2.0 * math.pi / BOX_LENGTH) ** 2
    kernel = np.where(total > 0, 4.0 * math.pi / (unit * np.maximum(total, 1)), 0.0)
    coulomb = np.zeros((g, g, LANES), np.float32)
    coulomb[:, :, lower] = kernel
    coulomb[:, :, upper] = kernel
    stick_in, left_backward = across(stick_in), across(np.concatenate([c, s], 0))
    early = np.zeros((LANES + 2 * g, stick_in.shape[1]), np.float32)
    early[:LANES], early[LANES:, : left_backward.shape[1]] = stick_in, left_backward
    return dict(
        forward=down(forward),
        last_backward=down(backward / g**3),
        left_forward=across(np.concatenate([c, -s], 0)),
        left_backward=left_backward,
        early=early,
        stick_out=across(stick_out * g**-1.5),
        coulomb=coulomb.reshape(g * g, LANES),
    )


def split(x):
    high = x.astype(BF16)
    low = (x - high.astype(F32)).astype(BF16)
    return high, low


def stacked(x):
    high, low = split(x)
    return jnp.concatenate([high, low, high], 0)


def dot(a, b):
    return jnp.dot(a, b, preferred_element_type=F32)


def lane_halves(shape):
    return lax.broadcasted_iota(jnp.int32, shape, 1) % LANES < MID


def turned(x):
    return pltpu.roll(x, MID, 1)


def regrouped(a, b):
    low = lane_halves(a.shape)
    return jnp.where(low, a, turned(b)), jnp.where(low, turned(a), b)


def beside(a, b):
    return jnp.concatenate([a, b], 1)


def halves(x):
    return x[:, :LANES], x[:, LANES:]


def left(table, x):
    both = dot(table, stacked(x))
    g = both.shape[0] // 2
    return both[:g], both[g:]


def left_complex(table, a, b):
    cos, sin = left(table, beside(a, b))
    sign = jnp.where(lane_halves((1, LANES)), -1.0, 1.0)
    return [p + turned(q) * sign for p, q in zip(halves(cos), halves(sin))]


def right(x, table):
    both = dot(beside(*split(x)), table)
    width = both.shape[1] // 2
    return both[:, :width] + both[:, width:]


def strided(ref, first, g):
    return ref[pl.ds(first, g, stride=g), :]


def slab_rows(index, g, count=1):
    return pl.ds(index * g, count * g)


def one_hot(index, wanted):
    return jnp.where(index == wanted, jnp.asarray(1, BF16), jnp.asarray(0, BF16))


def send_kernel(g, sticks_ref, columns_ref, *refs):
    block_refs, (row_ref, sems, row_sem) = refs[:-3], refs[-3:]
    own = lax.axis_index("stick")
    row_copy = pltpu.make_async_copy(columns_ref, row_ref, row_sem)
    row_copy.start()
    copies = [
        pltpu.make_async_copy(sticks_ref.at[own ^ d], ref.at[pl.ds(0, 2 * g)], sems.at[d])
        for d, ref in enumerate(block_refs)
    ]
    for copy in copies:
        copy.start()
    row_copy.wait()
    columns = jnp.broadcast_to(row_ref[...].astype(F32), (8, LANES))
    for ref in block_refs:
        ref[2 * g :, :] = columns
    for copy in copies:
        copy.wait()


def early_kernel(g, own_ref, tables_ref, staged_ref, stick_in_ref, left_ref):
    staged_ref[...] = own_ref[...]
    stick_in_ref[...] = tables_ref[:LANES, : stick_in_ref.shape[1]].astype(BF16)
    left_ref[...] = tables_ref[LANES:, : left_ref.shape[1]].astype(BF16)


def place_kernel(order, *refs):
    own = lax.axis_index("stick")
    out_ref = refs[-1]
    for d, block_ref in zip(order, refs[:-1]):
        out_ref[own ^ d] = block_ref[...]


def store(ref, first, slabs):
    g = slabs[0].shape[0]
    for k, slab in enumerate(slabs):
        ref[slab_rows(first + k, g), :] = slab


def relay_kernel(g, *refs):
    blocks, (coefficients_ref, columns_ref) = refs[:-2], refs[-2:]
    for k, ref in enumerate(blocks):
        coefficients_ref[k * 2 * g : (k + 1) * 2 * g, :] = ref[: 2 * g, :]
        columns_ref[:, k * LANES : (k + 1) * LANES] = ref[2 * g :, :]


def field_kernel(g, blocks_ref, columns_ref, stick_in_ref, left_ref, phi_ref, work_a):
    columns = columns_ref[:1, :].astype(jnp.int32)
    stick_in, backward = stick_in_ref[...], left_ref[...]
    blocks = [blocks_ref[k : k + 2 * g, :] for k in range(0, blocks_ref.shape[0], 2 * g)]
    sticks = []
    for k in range(0, len(blocks), 2):
        sticks.append(beside(*split(dot(stick_in, stacked(beside(blocks[k], blocks[k + 1]))).T)))
    sticks = jnp.concatenate(sticks, 0)

    half = g // 2
    index = lax.broadcasted_iota(jnp.int16, (half * g, columns.shape[1]), 0)
    for first in (0, half):
        both = dot(one_hot(index, (columns - first * g).astype(jnp.int16)), sticks)
        placed = both[:, :LANES] + both[:, LANES:]
        for k in range(0, half, 2):
            slabs = left_complex(backward, placed[k * g : (k + 1) * g], placed[(k + 1) * g : (k + 2) * g])
            store(work_a, first + k, slabs)

    for y in range(half):
        x = beside(strided(work_a, y, g), strided(work_a, y + half, g))
        (cos, cos_up), (sin, sin_up) = map(halves, left(backward, x))
        low = lane_halves(cos.shape)
        store(phi_ref, y, [jnp.where(low, cos - turned(sin), turned(cos_up) - sin_up)])


def pick_kernel(g, columns_ref, hot_ref):
    for k in range(0, columns_ref.shape[1], LANES):
        block = columns_ref[:, k : k + LANES]
        wanted = jnp.concatenate([block] * (LANES // block.shape[0]), 0).T.astype(jnp.int32)
        for c in range(0, hot_ref.shape[1], LANES):
            index = lax.broadcasted_iota(jnp.int16, (LANES, LANES), 1)
            hot_ref[k : k + LANES, c : c + LANES] = one_hot(index, (wanted - c).astype(jnp.int16))


def potentials(g, phi_ref, first_ref, second_ref, tables, work_a, work_b, emit):
    forward, last_backward, left_forward, left_backward = [ref[...].astype(BF16) for ref in tables[:4]]
    coulomb_ref = tables[4]
    half = g // 2
    for start in range(0, half, PAIRS):
        rows = slab_rows(start, g, PAIRS)
        phi = phi_ref[rows, :]
        lower, upper = regrouped(phi * first_ref[rows, :], phi * second_ref[rows, :])
        spectrum = right(jnp.concatenate([lower, upper], 0), forward)
        for k in range(PAIRS):
            a, b = left_complex(left_forward, *(spectrum[j * g : (j + 1) * g] for j in (k, k + PAIRS)))
            store(work_a, start + k, [a])
            store(work_a, start + k + half, [b])

    for kx in range(0, g, 2):
        slabs = left_complex(left_forward, strided(work_a, kx, g), strided(work_a, kx + 1, g))
        slabs = [slab * coulomb_ref[slab_rows(kx + j, g), :] for j, slab in enumerate(slabs)]
        store(work_b, kx, left_complex(left_backward, *slabs))

    for start in range(0, half, PAIRS):
        lower, upper = [], []
        for z in range(start, start + PAIRS):
            a, b = left_complex(left_backward, strided(work_b, z, g), strided(work_b, z + half, g))
            lower.append(a)
            upper.append(b)
        out = right(jnp.concatenate(lower + upper, 0), last_backward)
        emit(start, *regrouped(out[: PAIRS * g], out[PAIRS * g :]))


def near_kernel(g, phi_ref, other_ref, *refs):
    tables, (sum_ref, work_a, work_b) = refs[:5], refs[5:]

    def emit(start, own, other):
        rows = slab_rows(start, g, PAIRS)
        sum_ref[rows, :] = own * phi_ref[rows, :] + other * other_ref[rows, :]

    potentials(g, phi_ref, phi_ref, other_ref, tables, work_a, work_b, emit)


def middle_kernel(g, phi_ref, first_ref, second_ref, before_ref, *refs):
    tables, (sum_ref, work_a, work_b) = refs[:5], refs[5:]

    def emit(start, first, second):
        rows = slab_rows(start, g, PAIRS)
        sum_ref[rows, :] = before_ref[rows, :] + first * first_ref[rows, :] + second * second_ref[rows, :]

    potentials(g, phi_ref, first_ref, second_ref, tables, work_a, work_b, emit)


def far_kernel(g, weights, phi_ref, first_ref, second_ref, before_ref, hot_ref, stick_out_ref, *refs):
    tables, out_refs = refs[:5], refs[5:-3]
    work_a, work_b, picked_ref = refs[-3:]
    forward = tables[2][...].astype(BF16)
    half = g // 2

    def emit(start, first, second):
        rows = slab_rows(start, g, PAIRS)
        total = before_ref[rows, :] + weights[0] * (first * first_ref[rows, :])
        total = total + weights[1] * (second * second_ref[rows, :])
        for k in range(0, PAIRS, 2):
            cos, sin = left(forward, beside(total[k * g : (k + 1) * g], total[(k + 1) * g : (k + 2) * g]))
            for j, (real, imag) in enumerate(zip(halves(cos), halves(sin))):
                lower, upper = regrouped(real, imag)
                store(work_a, start + k + j, [lower])
                store(work_a, start + k + j + half, [upper])

    potentials(g, phi_ref, first_ref, second_ref, tables, work_a, work_b, emit)

    step = g // 3
    for first in range(0, g, step):
        slabs = []
        for kx in range(first, first + step, 2):
            slabs += left_complex(forward, strided(work_a, kx, g), strided(work_a, kx + 1, g))
        spectrum = beside(*split(jnp.concatenate(slabs, 0)))
        both = dot(hot_ref[:, first * g : (first + step) * g], spectrum)
        both = both[:, :LANES] + both[:, LANES:]
        picked_ref[...] = both if first == 0 else picked_ref[...] + both

    stick_out = stick_out_ref[...].astype(BF16)
    for k in range(0, len(out_refs), 2):
        high, low = split(picked_ref[k * LANES : (k + 2) * LANES, :])
        lined = jnp.concatenate([high, low, high], 1)
        out = lax.dot_general(stick_out, lined, (((1,), (1,)), ((), ())), preferred_element_type=F32)
        out_refs[k][...], out_refs[k + 1][...] = halves(out)


def call(kernel, out_shapes, scratch, flops, *operands, space=pltpu.VMEM, out_space=pltpu.VMEM, grant=40):
    out_spec = pl.BlockSpec(memory_space=out_space)
    return pl.pallas_call(
        kernel,
        out_shape=out_shapes,
        in_specs=[pl.BlockSpec(memory_space=space)] * len(operands),
        out_specs=jax.tree.map(lambda _: out_spec, out_shapes),
        scratch_shapes=scratch,
        compiler_params=pltpu.CompilerParams(vmem_limit_bytes=grant * 2**20),
        cost_estimate=pl.CostEstimate(flops=flops, bytes_accessed=flops, transcendentals=0),
    )(*operands)


def after(x, *others):
    return lax.optimization_barrier((x, *others))[0]


def exchanged(blocks, order, before):
    owners = len(blocks)
    moved = [blocks[0]] + [None] * (owners - 1)
    for d in order:
        others = [moved[x] if isinstance(x, int) else x for x in before.get(d, ())]
        block = after(blocks[d], *others) if others else blocks[d]
        moved[d] = lax.ppermute(block, "stick", [(i, i ^ d) for i in range(owners)])
    return moved


def on_device(sticks, stick_columns):
    g = sticks.shape[1] // 2
    slots = stick_columns.shape[0]
    owners = lax.axis_size("stick")
    groups = lax.axis_size("band")
    t = {name: jnp.asarray(value) for name, value in make_tables(g).items()}
    rows = g * g
    field = jax.ShapeDtypeStruct((rows // 2, LANES), F32)
    work = pltpu.VMEM((rows, LANES), F32)
    pot_flops = 1

    def shifted(x, distance):
        return lax.ppermute(x, "band", [(i, (i - distance) % groups) for i in range(groups)])

    def swapped(x):
        return lax.ppermute(x, "band", [(i, i ^ 1) for i in range(groups)])

    sent = call(
        functools.partial(send_kernel, g),
        [jax.ShapeDtypeStruct((2 * g + 8, slots), F32)] * owners,
        [
            pltpu.VMEM((1, slots), jnp.int32),
            pltpu.SemaphoreType.DMA((owners,)),
            pltpu.SemaphoreType.DMA,
        ],
        1,
        sticks,
        stick_columns[None, :],
        space=pltpu.HBM,
        grant=SEND_GRANT,
    )
    shapes = [(2 * g + 8, slots), (LANES, 6 * g), (2 * g, 3 * g)]
    staged, *first_tables = call(
        functools.partial(early_kernel, g),
        [jax.ShapeDtypeStruct(shape, kind) for shape, kind in zip(shapes, (F32, BF16, BF16))],
        [],
        1,
        sent[0],
        after(t["early"], sent[0]),
    )
    half = owners // 2
    distant, close = list(range(half, owners)), list(range(1, half))
    mixed = [distant[0]] + [d for pair in zip(close, distant[1:]) for d in pair]
    before = {mixed[k]: (half,) for k in range(WINDOW, len(mixed))}
    last = mixed[WINDOW]
    received = exchanged(sent, mixed, {**before, last: (*before[last], staged, *first_tables)})
    received[0] = staged
    order = [0] + mixed
    relay, columns = call(
        functools.partial(relay_kernel, g),
        [jax.ShapeDtypeStruct((owners * 2 * g, slots), F32), jax.ShapeDtypeStruct((8, owners * slots), F32)],
        [],
        1,
        *[received[d] for d in order],
    )

    def orbital(blocks):
        return call(functools.partial(field_kernel, g), field, [work], 1, blocks, columns, *first_tables)

    phi = orbital(relay)
    near = swapped(phi)
    hot = call(
        functools.partial(pick_kernel, g), jax.ShapeDtypeStruct((owners * slots, rows), BF16), [], pot_flops, columns
    )
    pot_tables = [t["forward"], t["last_backward"], t["left_forward"], t["left_backward"], t["coulomb"]]

    def potential_sum(kernel, *operands):
        return call(functools.partial(kernel, g), field, [work, work], pot_flops, phi, *operands, *pot_tables)

    distances = (HALF,) if groups == 2 * HALF else (HALF, -HALF)
    fields = [orbital(after(shifted(relay, distance), hot)) for distance in distances]
    total = potential_sum(near_kernel, after(near, *fields))
    if groups == 2 * HALF:
        weights = (2.0, 1.0)
        first, second = fields[0], swapped(fields[0])
    else:
        weights = (1.0, 0.0)
        odd = lax.axis_index("band") % 2 == 1
        first = second = swapped(jnp.where(odd, fields[1], fields[0]))
        total = potential_sum(middle_kernel, *fields, total)
    result = call(
        functools.partial(far_kernel, g, weights),
        [jax.ShapeDtypeStruct((2 * g, slots), F32)] * owners,
        [work, work, pltpu.VMEM((owners * slots, LANES), F32)],
        pot_flops,
        phi,
        first,
        second,
        total,
        hot,
        t["stick_out"],
        *pot_tables,
    )
    result = [result[order.index(d)] for d in range(owners)]
    result = exchanged(result, mixed, before)
    return call(
        functools.partial(place_kernel, order),
        jax.ShapeDtypeStruct(sticks.shape, F32),
        [],
        1,
        *[result[d] for d in order],
    )


def solution(mesh):
    return jax.shard_map(
        on_device,
        mesh=mesh,
        in_specs=(P("band", None, "stick"), P("stick")),
        out_specs=P("band", None, "stick"),
        check_vma=False,
    )
```

```python
import functools
import math

import jax
import jax.numpy as jnp
import numpy as np
from jax import lax
from jax.experimental import pallas as pl
from jax.experimental.pallas import tpu as pltpu
from jax.sharding import PartitionSpec as P

HALF = 2
BOX_LENGTH = 18.0
LANES = 128
MID = 64
WINDOW = 5
SEND_GRANT = 60
PAIRS = 12

F32 = jnp.float32
BF16 = jnp.bfloat16


def rounded_parts(table):
    high = table.astype(BF16).astype(np.float64)
    low = (table - high).astype(BF16).astype(np.float64)
    return high, low


def across(table):
    high, low = rounded_parts(table)
    return np.concatenate([high, high, low], 1).astype(np.float32)


def down(table):
    high, low = rounded_parts(table)
    return np.block([[high, low], [high, np.zeros_like(low)]]).astype(np.float32)


def make_tables(g):
    angle = 2.0 * np.pi / g * (np.outer(np.arange(g), np.arange(g)) % g)
    c, s = np.cos(angle), np.sin(angle)
    lower, upper = slice(0, g), slice(MID, MID + g)

    forward, backward = np.zeros((2, LANES, LANES))
    forward[lower, lower], forward[lower, upper] = c, -s
    forward[upper, lower], forward[upper, upper] = s, c
    backward[lower, lower], backward[lower, upper] = c, s
    backward[upper, lower], backward[upper, upper] = -s, c
    stick_in = np.zeros((LANES, 2 * g))
    stick_in[lower, :g], stick_in[lower, g:] = c, -s
    stick_in[upper, :g], stick_in[upper, g:] = s, c
    stick_out = np.zeros((2 * g, LANES))
    stick_out[:g, lower], stick_out[:g, upper] = c, s
    stick_out[g:, lower], stick_out[g:, upper] = -s, c

    freq = np.arange(g)
    square = np.minimum(freq, g - freq) ** 2
    total = square[:, None, None] + square[None, :, None] + square[None, None, :]
    unit = (2.0 * math.pi / BOX_LENGTH) ** 2
    kernel = np.where(total > 0, 4.0 * math.pi / (unit * np.maximum(total, 1)), 0.0)
    coulomb = np.zeros((g, g, LANES), np.float32)
    coulomb[:, :, lower] = kernel
    coulomb[:, :, upper] = kernel
    stick_in, left_backward = across(stick_in), across(np.concatenate([c, s], 0))
    early = np.zeros((LANES + 2 * g, stick_in.shape[1]), np.float32)
    early[:LANES], early[LANES:, : left_backward.shape[1]] = stick_in, left_backward
    return dict(
        forward=down(forward),
        last_backward=down(backward / g**3),
        left_forward=across(np.concatenate([c, -s], 0)),
        left_backward=left_backward,
        early=early,
        stick_out=across(stick_out * g**-1.5),
        coulomb=coulomb.reshape(g * g, LANES),
    )


def split(x):
    high = x.astype(BF16)
    low = (x - high.astype(F32)).astype(BF16)
    return high, low


def stacked(x):
    high, low = split(x)
    return jnp.concatenate([high, low, high], 0)


def dot(a, b):
    return jnp.dot(a, b, preferred_element_type=F32)


def lane_halves(shape):
    return lax.broadcasted_iota(jnp.int32, shape, 1) % LANES < MID


def turned(x):
    return pltpu.roll(x, MID, 1)


def regrouped(a, b):
    low = lane_halves(a.shape)
    return jnp.where(low, a, turned(b)), jnp.where(low, turned(a), b)


def beside(a, b):
    return jnp.concatenate([a, b], 1)


def halves(x):
    return x[:, :LANES], x[:, LANES:]


def left(table, x):
    both = dot(table, stacked(x))
    g = both.shape[0] // 2
    return both[:g], both[g:]


def left_complex(table, a, b):
    cos, sin = left(table, beside(a, b))
    sign = jnp.where(lane_halves((1, LANES)), -1.0, 1.0)
    return [p + turned(q) * sign for p, q in zip(halves(cos), halves(sin))]


def right(x, table):
    both = dot(beside(*split(x)), table)
    width = both.shape[1] // 2
    return both[:, :width] + both[:, width:]


def strided(ref, first, g):
    return ref[pl.ds(first, g, stride=g), :]


def slab_rows(index, g, count=1):
    return pl.ds(index * g, count * g)


def one_hot(index, wanted):
    return jnp.where(index == wanted, jnp.asarray(1, BF16), jnp.asarray(0, BF16))


def send_kernel(g, sticks_ref, columns_ref, *refs):
    block_refs, (row_ref, sems, row_sem) = refs[:-3], refs[-3:]
    own = lax.axis_index("stick")
    row_copy = pltpu.make_async_copy(columns_ref, row_ref, row_sem)
    row_copy.start()
    copies = [
        pltpu.make_async_copy(sticks_ref.at[own ^ d], ref.at[pl.ds(0, 2 * g)], sems.at[d])
        for d, ref in enumerate(block_refs)
    ]
    for copy in copies:
        copy.start()
    row_copy.wait()
    columns = jnp.broadcast_to(row_ref[...].astype(F32), (8, LANES))
    for ref in block_refs:
        ref[2 * g :, :] = columns
    for copy in copies:
        copy.wait()


def early_kernel(g, own_ref, tables_ref, staged_ref, stick_in_ref, left_ref):
    staged_ref[...] = own_ref[...]
    stick_in_ref[...] = tables_ref[:LANES, : stick_in_ref.shape[1]].astype(BF16)
    left_ref[...] = tables_ref[LANES:, : left_ref.shape[1]].astype(BF16)


def place_kernel(order, *refs):
    own = lax.axis_index("stick")
    out_ref = refs[-1]
    for d, block_ref in zip(order, refs[:-1]):
        out_ref[own ^ d] = block_ref[...]


def store(ref, first, slabs):
    g = slabs[0].shape[0]
    for k, slab in enumerate(slabs):
        ref[slab_rows(first + k, g), :] = slab


def relay_kernel(g, *refs):
    blocks, (coefficients_ref, columns_ref) = refs[:-2], refs[-2:]
    for k, ref in enumerate(blocks):
        coefficients_ref[k * 2 * g : (k + 1) * 2 * g, :] = ref[: 2 * g, :]
        columns_ref[:, k * LANES : (k + 1) * LANES] = ref[2 * g :, :]


def field_kernel(g, blocks_ref, columns_ref, stick_in_ref, left_ref, phi_ref, work_a):
    columns = columns_ref[:1, :].astype(jnp.int32)
    stick_in, backward = stick_in_ref[...], left_ref[...]
    blocks = [blocks_ref[k : k + 2 * g, :] for k in range(0, blocks_ref.shape[0], 2 * g)]
    sticks = []
    for k in range(0, len(blocks), 2):
        sticks.append(beside(*split(dot(stick_in, stacked(beside(blocks[k], blocks[k + 1]))).T)))
    sticks = jnp.concatenate(sticks, 0)

    half = g // 2
    index = lax.broadcasted_iota(jnp.int16, (half * g, columns.shape[1]), 0)
    for first in (0, half):
        both = dot(one_hot(index, (columns - first * g).astype(jnp.int16)), sticks)
        placed = both[:, :LANES] + both[:, LANES:]
        for k in range(0, half, 2):
            slabs = left_complex(backward, placed[k * g : (k + 1) * g], placed[(k + 1) * g : (k + 2) * g])
            store(work_a, first + k, slabs)

    for y in range(half):
        x = beside(strided(work_a, y, g), strided(work_a, y + half, g))
        (cos, cos_up), (sin, sin_up) = map(halves, left(backward, x))
        low = lane_halves(cos.shape)
        store(phi_ref, y, [jnp.where(low, cos - turned(sin), turned(cos_up) - sin_up)])


def pick_kernel(g, columns_ref, hot_ref):
    for k in range(0, columns_ref.shape[1], LANES):
        block = columns_ref[:, k : k + LANES]
        wanted = jnp.concatenate([block] * (LANES // block.shape[0]), 0).T.astype(jnp.int32)
        for c in range(0, hot_ref.shape[1], LANES):
            index = lax.broadcasted_iota(jnp.int16, (LANES, LANES), 1)
            hot_ref[k : k + LANES, c : c + LANES] = one_hot(index, (wanted - c).astype(jnp.int16))


def potentials(g, phi_ref, first_ref, second_ref, tables, work_a, work_b, emit):
    forward, last_backward, left_forward, left_backward = [ref[...].astype(BF16) for ref in tables[:4]]
    coulomb_ref = tables[4]
    half = g // 2
    for start in range(0, half, PAIRS):
        rows = slab_rows(start, g, PAIRS)
        phi = phi_ref[rows, :]
        lower, upper = regrouped(phi * first_ref[rows, :], phi * second_ref[rows, :])
        spectrum = right(jnp.concatenate([lower, upper], 0), forward)
        for k in range(PAIRS):
            a, b = left_complex(left_forward, *(spectrum[j * g : (j + 1) * g] for j in (k, k + PAIRS)))
            store(work_a, start + k, [a])
            store(work_a, start + k + half, [b])

    for kx in range(0, g, 2):
        slabs = left_complex(left_forward, strided(work_a, kx, g), strided(work_a, kx + 1, g))
        slabs = [slab * coulomb_ref[slab_rows(kx + j, g), :] for j, slab in enumerate(slabs)]
        store(work_b, kx, left_complex(left_backward, *slabs))

    for start in range(0, half, PAIRS):
        lower, upper = [], []
        for z in range(start, start + PAIRS):
            a, b = left_complex(left_backward, strided(work_b, z, g), strided(work_b, z + half, g))
            lower.append(a)
            upper.append(b)
        out = right(jnp.concatenate(lower + upper, 0), last_backward)
        emit(start, *regrouped(out[: PAIRS * g], out[PAIRS * g :]))


def near_kernel(g, phi_ref, other_ref, *refs):
    tables, (sum_ref, work_a, work_b) = refs[:5], refs[5:]

    def emit(start, own, other):
        rows = slab_rows(start, g, PAIRS)
        sum_ref[rows, :] = own * phi_ref[rows, :] + other * other_ref[rows, :]

    potentials(g, phi_ref, phi_ref, other_ref, tables, work_a, work_b, emit)


def middle_kernel(g, phi_ref, first_ref, second_ref, before_ref, *refs):
    tables, (sum_ref, work_a, work_b) = refs[:5], refs[5:]

    def emit(start, first, second):
        rows = slab_rows(start, g, PAIRS)
        sum_ref[rows, :] = before_ref[rows, :] + first * first_ref[rows, :] + second * second_ref[rows, :]

    potentials(g, phi_ref, first_ref, second_ref, tables, work_a, work_b, emit)


def far_kernel(g, weights, phi_ref, first_ref, second_ref, before_ref, hot_ref, stick_out_ref, *refs):
    tables, out_refs = refs[:5], refs[5:-3]
    work_a, work_b, picked_ref = refs[-3:]
    forward = tables[2][...].astype(BF16)
    half = g // 2

    def emit(start, first, second):
        rows = slab_rows(start, g, PAIRS)
        total = before_ref[rows, :] + weights[0] * (first * first_ref[rows, :])
        total = total + weights[1] * (second * second_ref[rows, :])
        for k in range(0, PAIRS, 2):
            cos, sin = left(forward, beside(total[k * g : (k + 1) * g], total[(k + 1) * g : (k + 2) * g]))
            for j, (real, imag) in enumerate(zip(halves(cos), halves(sin))):
                lower, upper = regrouped(real, imag)
                store(work_a, start + k + j, [lower])
                store(work_a, start + k + j + half, [upper])

    potentials(g, phi_ref, first_ref, second_ref, tables, work_a, work_b, emit)

    step = g // 3
    for first in range(0, g, step):
        slabs = []
        for kx in range(first, first + step, 2):
            slabs += left_complex(forward, strided(work_a, kx, g), strided(work_a, kx + 1, g))
        spectrum = beside(*split(jnp.concatenate(slabs, 0)))
        both = dot(hot_ref[:, first * g : (first + step) * g], spectrum)
        both = both[:, :LANES] + both[:, LANES:]
        picked_ref[...] = both if first == 0 else picked_ref[...] + both

    stick_out = stick_out_ref[...].astype(BF16)
    for k in range(0, len(out_refs), 2):
        high, low = split(picked_ref[k * LANES : (k + 2) * LANES, :])
        lined = jnp.concatenate([high, low, high], 1)
        out = lax.dot_general(stick_out, lined, (((1,), (1,)), ((), ())), preferred_element_type=F32)
        out_refs[k][...], out_refs[k + 1][...] = halves(out)


def call(kernel, out_shapes, scratch, flops, *operands, space=pltpu.VMEM, out_space=pltpu.VMEM, grant=40):
    out_spec = pl.BlockSpec(memory_space=out_space)
    return pl.pallas_call(
        kernel,
        out_shape=out_shapes,
        in_specs=[pl.BlockSpec(memory_space=space)] * len(operands),
        out_specs=jax.tree.map(lambda _: out_spec, out_shapes),
        scratch_shapes=scratch,
        compiler_params=pltpu.CompilerParams(vmem_limit_bytes=grant * 2**20),
        cost_estimate=pl.CostEstimate(flops=flops, bytes_accessed=flops, transcendentals=0),
    )(*operands)


def after(x, *others):
    return lax.optimization_barrier((x, *others))[0]


def exchanged(blocks, order, before):
    owners = len(blocks)
    moved = [blocks[0]] + [None] * (owners - 1)
    for d in order:
        others = [moved[x] if isinstance(x, int) else x for x in before.get(d, ())]
        block = after(blocks[d], *others) if others else blocks[d]
        moved[d] = lax.ppermute(block, "stick", [(i, i ^ d) for i in range(owners)])
    return moved


def on_device(sticks, stick_columns):
    g = sticks.shape[1] // 2
    slots = stick_columns.shape[0]
    owners = lax.axis_size("stick")
    groups = lax.axis_size("band")
    t = {name: jnp.asarray(value) for name, value in make_tables(g).items()}
    rows = g * g
    field = jax.ShapeDtypeStruct((rows // 2, LANES), F32)
    work = pltpu.VMEM((rows, LANES), F32)
    pot_flops = 1

    def shifted(x, distance):
        return lax.ppermute(x, "band", [(i, (i - distance) % groups) for i in range(groups)])

    def swapped(x):
        return lax.ppermute(x, "band", [(i, i ^ 1) for i in range(groups)])

    sent = call(
        functools.partial(send_kernel, g),
        [jax.ShapeDtypeStruct((2 * g + 8, slots), F32)] * owners,
        [
            pltpu.VMEM((1, slots), jnp.int32),
            pltpu.SemaphoreType.DMA((owners,)),
            pltpu.SemaphoreType.DMA,
        ],
        1,
        sticks,
        stick_columns[None, :],
        space=pltpu.HBM,
        grant=SEND_GRANT,
    )
    shapes = [(2 * g + 8, slots), (LANES, 6 * g), (2 * g, 3 * g)]
    staged, *first_tables = call(
        functools.partial(early_kernel, g),
        [jax.ShapeDtypeStruct(shape, kind) for shape, kind in zip(shapes, (F32, BF16, BF16))],
        [],
        1,
        sent[0],
        after(t["early"], sent[0]),
    )
    half = owners // 2
    distant, close = list(range(half, owners)), list(range(1, half))
    mixed = [distant[0]] + [d for pair in zip(close, distant[1:]) for d in pair]
    before = {mixed[k]: (mixed[k - 3 - k % 2],) for k in range(WINDOW, len(mixed))}
    last = mixed[WINDOW]
    received = exchanged(sent, mixed, {**before, last: (*before[last], staged, *first_tables)})
    received[0] = staged
    order = [0] + distant + close
    relay, columns = call(
        functools.partial(relay_kernel, g),
        [jax.ShapeDtypeStruct((owners * 2 * g, slots), F32), jax.ShapeDtypeStruct((8, owners * slots), F32)],
        [],
        1,
        *[received[d] for d in order],
    )

    def orbital(blocks):
        return call(functools.partial(field_kernel, g), field, [work], 1, blocks, columns, *first_tables)

    phi = orbital(relay)
    near = swapped(phi)
    hot = call(
        functools.partial(pick_kernel, g), jax.ShapeDtypeStruct((owners * slots, rows), BF16), [], pot_flops, columns
    )
    pot_tables = [t["forward"], t["last_backward"], t["left_forward"], t["left_backward"], t["coulomb"]]

    def potential_sum(kernel, *operands):
        return call(functools.partial(kernel, g), field, [work, work], pot_flops, phi, *operands, *pot_tables)

    distances = (HALF,) if groups == 2 * HALF else (HALF, -HALF)
    fields = [orbital(after(shifted(relay, distance), hot)) for distance in distances]
    total = potential_sum(near_kernel, after(near, *fields))
    if groups == 2 * HALF:
        weights = (2.0, 1.0)
        first, second = fields[0], swapped(fields[0])
    else:
        weights = (1.0, 0.0)
        odd = lax.axis_index("band") % 2 == 1
        first = second = swapped(jnp.where(odd, fields[1], fields[0]))
        total = potential_sum(middle_kernel, *fields, total)
    result = call(
        functools.partial(far_kernel, g, weights),
        [jax.ShapeDtypeStruct((2 * g, slots), F32)] * owners,
        [work, work, pltpu.VMEM((owners * slots, LANES), F32)],
        pot_flops,
        phi,
        first,
        second,
        total,
        hot,
        t["stick_out"],
        *pot_tables,
    )
    result = [result[order.index(d)] for d in range(owners)]
    result = exchanged(result, mixed, before)
    return call(
        functools.partial(place_kernel, order),
        jax.ShapeDtypeStruct(sticks.shape, F32),
        [],
        1,
        *[result[d] for d in order],
    )


def solution(mesh):
    return jax.shard_map(
        on_device,
        mesh=mesh,
        in_specs=(P("band", None, "stick"), P("stick")),
        out_specs=P("band", None, "stick"),
        check_vma=False,
    )
```

```python
import functools
import math

import jax
import jax.numpy as jnp
import numpy as np
from jax import lax
from jax.experimental import pallas as pl
from jax.experimental.pallas import tpu as pltpu
from jax.sharding import PartitionSpec as P

HALF = 2
BOX_LENGTH = 18.0
LANES = 128
MID = 64
WINDOW = 5
SEND_GRANT = 60
PAIRS = 6

F32 = jnp.float32
BF16 = jnp.bfloat16


def rounded_parts(table):
    high = table.astype(BF16).astype(np.float64)
    low = (table - high).astype(BF16).astype(np.float64)
    return high, low


def across(table):
    high, low = rounded_parts(table)
    return np.concatenate([high, high, low], 1).astype(np.float32)


def down(table):
    high, low = rounded_parts(table)
    return np.block([[high, low], [high, np.zeros_like(low)]]).astype(np.float32)


def make_tables(g):
    angle = 2.0 * np.pi / g * (np.outer(np.arange(g), np.arange(g)) % g)
    c, s = np.cos(angle), np.sin(angle)
    lower, upper = slice(0, g), slice(MID, MID + g)

    forward, backward = np.zeros((2, LANES, LANES))
    forward[lower, lower], forward[lower, upper] = c, -s
    forward[upper, lower], forward[upper, upper] = s, c
    backward[lower, lower], backward[lower, upper] = c, s
    backward[upper, lower], backward[upper, upper] = -s, c
    stick_in = np.zeros((LANES, 2 * g))
    stick_in[lower, :g], stick_in[lower, g:] = c, -s
    stick_in[upper, :g], stick_in[upper, g:] = s, c
    stick_out = np.zeros((2 * g, LANES))
    stick_out[:g, lower], stick_out[:g, upper] = c, s
    stick_out[g:, lower], stick_out[g:, upper] = -s, c

    freq = np.arange(g)
    square = np.minimum(freq, g - freq) ** 2
    total = square[:, None, None] + square[None, :, None] + square[None, None, :]
    unit = (2.0 * math.pi / BOX_LENGTH) ** 2
    kernel = np.where(total > 0, 4.0 * math.pi / (unit * np.maximum(total, 1)), 0.0)
    coulomb = np.zeros((g, g, LANES), np.float32)
    coulomb[:, :, lower] = kernel
    coulomb[:, :, upper] = kernel
    stick_in, left_backward = across(stick_in), across(np.concatenate([c, s], 0))
    early = np.zeros((LANES + 2 * g, stick_in.shape[1]), np.float32)
    early[:LANES], early[LANES:, : left_backward.shape[1]] = stick_in, left_backward
    return dict(
        forward=down(forward),
        last_backward=down(backward / g**3),
        left_forward=across(np.concatenate([c, -s], 0)),
        left_backward=left_backward,
        early=early,
        stick_out=across(stick_out * g**-1.5),
        coulomb=coulomb.reshape(g * g, LANES),
    )


def split(x):
    high = x.astype(BF16)
    low = (x - high.astype(F32)).astype(BF16)
    return high, low


def stacked(x):
    high, low = split(x)
    return jnp.concatenate([high, low, high], 0)


def dot(a, b):
    return jnp.dot(a, b, preferred_element_type=F32)


def lane_halves(shape):
    return lax.broadcasted_iota(jnp.int32, shape, 1) % LANES < MID


def turned(x):
    return pltpu.roll(x, MID, 1)


def regrouped(a, b):
    low = lane_halves(a.shape)
    return jnp.where(low, a, turned(b)), jnp.where(low, turned(a), b)


def beside(a, b):
    return jnp.concatenate([a, b], 1)


def halves(x):
    return x[:, :LANES], x[:, LANES:]


def left(table, x):
    both = dot(table, stacked(x))
    g = both.shape[0] // 2
    return both[:g], both[g:]


def left_complex(table, a, b):
    cos, sin = left(table, beside(a, b))
    sign = jnp.where(lane_halves((1, LANES)), -1.0, 1.0)
    return [p + turned(q) * sign for p, q in zip(halves(cos), halves(sin))]


def right(x, table):
    both = dot(beside(*split(x)), table)
    width = both.shape[1] // 2
    return both[:, :width] + both[:, width:]


def strided(ref, first, g):
    return ref[pl.ds(first, g, stride=g), :]


def slab_rows(index, g, count=1):
    return pl.ds(index * g, count * g)


def one_hot(index, wanted):
    return jnp.where(index == wanted, jnp.asarray(1, BF16), jnp.asarray(0, BF16))


def send_kernel(g, sticks_ref, columns_ref, *refs):
    block_refs, (row_ref, sems, row_sem) = refs[:-3], refs[-3:]
    own = lax.axis_index("stick")
    row_copy = pltpu.make_async_copy(columns_ref, row_ref, row_sem)
    row_copy.start()
    copies = [
        pltpu.make_async_copy(sticks_ref.at[own ^ d], ref.at[pl.ds(0, 2 * g)], sems.at[d])
        for d, ref in enumerate(block_refs)
    ]
    for copy in copies:
        copy.start()
    row_copy.wait()
    columns = jnp.broadcast_to(row_ref[...].astype(F32), (8, LANES))
    for ref in block_refs:
        ref[2 * g :, :] = columns
    for copy in copies:
        copy.wait()


def early_kernel(g, own_ref, tables_ref, staged_ref, stick_in_ref, left_ref):
    staged_ref[...] = own_ref[...]
    stick_in_ref[...] = tables_ref[:LANES, : stick_in_ref.shape[1]].astype(BF16)
    left_ref[...] = tables_ref[LANES:, : left_ref.shape[1]].astype(BF16)


def place_kernel(order, *refs):
    own = lax.axis_index("stick")
    out_ref = refs[-1]
    for d, block_ref in zip(order, refs[:-1]):
        out_ref[own ^ d] = block_ref[...]


def store(ref, first, slabs):
    g = slabs[0].shape[0]
    for k, slab in enumerate(slabs):
        ref[slab_rows(first + k, g), :] = slab


def relay_kernel(g, *refs):
    blocks, (coefficients_ref, columns_ref) = refs[:-2], refs[-2:]
    for k, ref in enumerate(blocks):
        coefficients_ref[k * 2 * g : (k + 1) * 2 * g, :] = ref[: 2 * g, :]
        columns_ref[:, k * LANES : (k + 1) * LANES] = ref[2 * g :, :]


def placed(g, blocks_ref, columns_ref, stick_in_ref):
    columns = columns_ref[:1, :].astype(jnp.int32)
    stick_in = stick_in_ref[...]
    blocks = [blocks_ref[k : k + 2 * g, :] for k in range(0, blocks_ref.shape[0], 2 * g)]
    sticks = []
    for k in range(0, len(blocks), 2):
        sticks.append(beside(*split(dot(stick_in, stacked(beside(blocks[k], blocks[k + 1]))).T)))
    sticks = jnp.concatenate(sticks, 0)
    rows = g * g // 2
    index = lax.broadcasted_iota(jnp.int16, (rows, columns.shape[1]), 0)
    for first in (0, rows):
        both = dot(one_hot(index, (columns - first).astype(jnp.int16)), sticks)
        yield first, both[:, :LANES] + both[:, LANES:]


def place_sticks_kernel(g, blocks_ref, columns_ref, stick_in_ref, grid_ref):
    for first, part in placed(g, blocks_ref, columns_ref, stick_in_ref):
        grid_ref[first : first + part.shape[0], :] = part


def field_kernel(g, grid_ref, blocks_ref, columns_ref, stick_in_ref, left_ref, phi_ref, work_a):
    backward = left_ref[...]
    half = g // 2
    for first, part in placed(g, blocks_ref, columns_ref, stick_in_ref):
        part = part + grid_ref[first : first + part.shape[0], :]
        for k in range(0, half, 2):
            slabs = left_complex(backward, part[k * g : (k + 1) * g], part[(k + 1) * g : (k + 2) * g])
            store(work_a, first // g + k, slabs)

    for y in range(half):
        x = beside(strided(work_a, y, g), strided(work_a, y + half, g))
        (cos, cos_up), (sin, sin_up) = map(halves, left(backward, x))
        low = lane_halves(cos.shape)
        store(phi_ref, y, [jnp.where(low, cos - turned(sin), turned(cos_up) - sin_up)])


def pick_kernel(g, first_columns_ref, second_columns_ref, hot_ref):
    columns = beside(first_columns_ref[...], second_columns_ref[...])
    for k in range(0, columns.shape[1], LANES):
        block = columns[:, k : k + LANES]
        wanted = jnp.concatenate([block] * (LANES // block.shape[0]), 0).T.astype(jnp.int32)
        for c in range(0, hot_ref.shape[1], LANES):
            index = lax.broadcasted_iota(jnp.int16, (LANES, LANES), 1)
            hot_ref[k : k + LANES, c : c + LANES] = one_hot(index, (wanted - c).astype(jnp.int16))


def potentials(g, phi_ref, first_ref, second_ref, tables, work_a, work_b, emit, last=PAIRS):
    forward, last_backward, left_forward, left_backward = [ref[...].astype(BF16) for ref in tables[:4]]
    coulomb_ref = tables[4]
    half = g // 2
    for start in range(0, half, PAIRS):
        rows = slab_rows(start, g, PAIRS)
        phi = phi_ref[rows, :]
        lower, upper = regrouped(phi * first_ref[rows, :], phi * second_ref[rows, :])
        spectrum = right(jnp.concatenate([lower, upper], 0), forward)
        for k in range(PAIRS):
            a, b = left_complex(left_forward, *(spectrum[j * g : (j + 1) * g] for j in (k, k + PAIRS)))
            store(work_a, start + k, [a])
            store(work_a, start + k + half, [b])

    for kx in range(0, g, 2):
        slabs = left_complex(left_forward, strided(work_a, kx, g), strided(work_a, kx + 1, g))
        slabs = [slab * coulomb_ref[slab_rows(kx + j, g), :] for j, slab in enumerate(slabs)]
        store(work_b, kx, left_complex(left_backward, *slabs))

    for start in range(0, half, last):
        lower, upper = [], []
        for z in range(start, start + last):
            a, b = left_complex(left_backward, strided(work_b, z, g), strided(work_b, z + half, g))
            lower.append(a)
            upper.append(b)
        out = right(jnp.concatenate(lower + upper, 0), last_backward)
        emit(start, *regrouped(out[: last * g], out[last * g :]))


def near_kernel(g, phi_ref, other_ref, *refs):
    tables, (sum_ref, work_a, work_b) = refs[:5], refs[5:]

    def emit(start, own, other):
        rows = slab_rows(start, g, PAIRS)
        sum_ref[rows, :] = own * phi_ref[rows, :] + other * other_ref[rows, :]

    potentials(g, phi_ref, phi_ref, other_ref, tables, work_a, work_b, emit)


def middle_kernel(g, phi_ref, first_ref, second_ref, before_ref, *refs):
    tables, (sum_ref, work_a, work_b) = refs[:5], refs[5:]

    def emit(start, first, second):
        rows = slab_rows(start, g, PAIRS)
        sum_ref[rows, :] = before_ref[rows, :] + first * first_ref[rows, :] + second * second_ref[rows, :]

    potentials(g, phi_ref, first_ref, second_ref, tables, work_a, work_b, emit)


def far_kernel(g, weights, phi_ref, first_ref, second_ref, before_ref, hot_ref, stick_out_ref, *refs):
    tables, out_refs = refs[:5], refs[5:-3]
    work_a, work_b, picked_ref = refs[-3:]
    forward = tables[2][...].astype(BF16)
    half = g // 2

    def emit(start, first, second):
        rows = slab_rows(start, g, half)
        total = before_ref[rows, :] + weights[0] * (first * first_ref[rows, :])
        total = total + weights[1] * (second * second_ref[rows, :])
        for k in range(0, half, 2):
            cos, sin = left(forward, beside(total[k * g : (k + 1) * g], total[(k + 1) * g : (k + 2) * g]))
            for j, (real, imag) in enumerate(zip(halves(cos), halves(sin))):
                lower, upper = regrouped(real, imag)
                store(work_a, start + k + j, [lower])
                store(work_a, start + k + j + half, [upper])

    potentials(g, phi_ref, first_ref, second_ref, tables, work_a, work_b, emit, half)

    step = g // 3
    for first in range(0, g, step):
        slabs = []
        for kx in range(first, first + step, 2):
            slabs += left_complex(forward, strided(work_a, kx, g), strided(work_a, kx + 1, g))
        spectrum = beside(*split(jnp.concatenate(slabs, 0)))
        both = dot(hot_ref[:, first * g : (first + step) * g], spectrum)
        both = both[:, :LANES] + both[:, LANES:]
        picked_ref[...] = both if first == 0 else picked_ref[...] + both

    stick_out = stick_out_ref[...].astype(BF16)
    for k in range(0, len(out_refs), 2):
        high, low = split(picked_ref[k * LANES : (k + 2) * LANES, :])
        lined = jnp.concatenate([high, low, high], 1)
        out = lax.dot_general(stick_out, lined, (((1,), (1,)), ((), ())), preferred_element_type=F32)
        out_refs[k][...], out_refs[k + 1][...] = halves(out)


def call(kernel, out_shapes, scratch, flops, *operands, space=pltpu.VMEM, out_space=pltpu.VMEM, grant=40):
    out_spec = pl.BlockSpec(memory_space=out_space)
    return pl.pallas_call(
        kernel,
        out_shape=out_shapes,
        in_specs=[pl.BlockSpec(memory_space=space)] * len(operands),
        out_specs=jax.tree.map(lambda _: out_spec, out_shapes),
        scratch_shapes=scratch,
        compiler_params=pltpu.CompilerParams(vmem_limit_bytes=grant * 2**20),
        cost_estimate=pl.CostEstimate(flops=flops, bytes_accessed=flops, transcendentals=0),
    )(*operands)


def after(x, *others):
    return lax.optimization_barrier((x, *others))[0]


def exchanged(blocks, order, before):
    owners = len(blocks)
    moved = [blocks[0]] + [None] * (owners - 1)
    for d in order:
        others = [moved[x] if isinstance(x, int) else x for x in before.get(d, ())]
        block = after(blocks[d], *others) if others else blocks[d]
        moved[d] = lax.ppermute(block, "stick", [(i, i ^ d) for i in range(owners)])
    return moved


def on_device(sticks, stick_columns):
    g = sticks.shape[1] // 2
    slots = stick_columns.shape[0]
    owners = lax.axis_size("stick")
    groups = lax.axis_size("band")
    t = {name: jnp.asarray(value) for name, value in make_tables(g).items()}
    rows = g * g
    field = jax.ShapeDtypeStruct((rows // 2, LANES), F32)
    work = pltpu.VMEM((rows, LANES), F32)
    pot_flops = 1

    def shifted(x, distance):
        return lax.ppermute(x, "band", [(i, (i - distance) % groups) for i in range(groups)])

    def swapped(x):
        return lax.ppermute(x, "band", [(i, i ^ 1) for i in range(groups)])

    sent = call(
        functools.partial(send_kernel, g),
        [jax.ShapeDtypeStruct((2 * g + 8, slots), F32)] * owners,
        [
            pltpu.VMEM((1, slots), jnp.int32),
            pltpu.SemaphoreType.DMA((owners,)),
            pltpu.SemaphoreType.DMA,
        ],
        1,
        sticks,
        stick_columns[None, :],
        space=pltpu.HBM,
        grant=SEND_GRANT,
    )
    shapes = [(2 * g + 8, slots), (LANES, 6 * g), (2 * g, 3 * g)]
    staged, *first_tables = call(
        functools.partial(early_kernel, g),
        [jax.ShapeDtypeStruct(shape, kind) for shape, kind in zip(shapes, (F32, BF16, BF16))],
        [],
        1,
        sent[0],
        after(t["early"], sent[0]),
    )
    half = owners // 2
    distant, close = list(range(half, owners)), list(range(1, half))
    mixed = [distant[0]] + [d for pair in zip(close, distant[1:]) for d in pair]
    before = {mixed[k]: (mixed[k - 3 - k % 2],) for k in range(WINDOW, len(mixed))}
    last = mixed[WINDOW]
    received = exchanged(sent, mixed, {**before, last: (*before[last], staged, *first_tables)})
    received[0] = staged
    cut = owners * 3 // 4
    order = [0] + mixed
    order = order[:cut] + order[:cut - 1:-1]
    stick_in, left_table = first_tables

    def relayed(part):
        shapes = [(len(part) * 2 * g, slots), (8, len(part) * slots)]
        shapes = [jax.ShapeDtypeStruct(shape, F32) for shape in shapes]
        return call(functools.partial(relay_kernel, g), shapes, [], 1, *[received[d] for d in part])

    def on_grid(blocks):
        grid = jax.ShapeDtypeStruct((rows, LANES), F32)
        return call(functools.partial(place_sticks_kernel, g), grid, [], 1, blocks, columns[0], stick_in)

    def orbital(grid, rest):
        operands = (grid, rest, columns[1], stick_in, left_table)
        return call(functools.partial(field_kernel, g), field, [work], 1, *operands)

    first_blocks, first_columns = relayed(order[:cut])
    columns = [first_columns]
    own_grid = on_grid(first_blocks)
    received[order[cut]] = after(received[order[cut]], own_grid)
    last_blocks, last_columns = relayed(order[cut:])
    columns.append(last_columns)
    phi = orbital(own_grid, last_blocks)
    near = swapped(phi)
    hot = call(
        functools.partial(pick_kernel, g), jax.ShapeDtypeStruct((owners * slots, rows), BF16), [], pot_flops, *columns
    )
    pot_tables = [t["forward"], t["last_backward"], t["left_forward"], t["left_backward"], t["coulomb"]]

    def potential_sum(kernel, *operands):
        return call(functools.partial(kernel, g), field, [work, work], pot_flops, phi, *operands, *pot_tables)

    distances = (HALF,) if groups == 2 * HALF else (HALF, -HALF)
    fields = [orbital(on_grid(shifted(first_blocks, d)), shifted(last_blocks, d)) for d in distances]
    total = potential_sum(near_kernel, after(near, *fields))
    if groups == 2 * HALF:
        weights = (2.0, 1.0)
        first, second = fields[0], swapped(fields[0])
    else:
        weights = (1.0, 0.0)
        odd = lax.axis_index("band") % 2 == 1
        first = second = swapped(jnp.where(odd, fields[1], fields[0]))
        total = potential_sum(middle_kernel, *fields, total)
    result = call(
        functools.partial(far_kernel, g, weights),
        [jax.ShapeDtypeStruct((2 * g, slots), F32)] * owners,
        [work, work, pltpu.VMEM((owners * slots, LANES), F32)],
        pot_flops,
        phi,
        first,
        second,
        total,
        hot,
        t["stick_out"],
        *pot_tables,
    )
    result = [result[order.index(d)] for d in range(owners)]
    result = exchanged(result, mixed, before)
    out_order = [0] + distant + close
    return call(
        functools.partial(place_kernel, out_order),
        jax.ShapeDtypeStruct(sticks.shape, F32),
        [],
        1,
        *[result[d] for d in out_order],
    )


def solution(mesh):
    return jax.shard_map(
        on_device,
        mesh=mesh,
        in_specs=(P("band", None, "stick"), P("stick")),
        out_specs=P("band", None, "stick"),
        check_vma=False,
    )
```

```python
import functools
import math

import jax
import jax.numpy as jnp
import numpy as np
from jax import lax
from jax.experimental import pallas as pl
from jax.experimental.pallas import tpu as pltpu
from jax.sharding import PartitionSpec as P

HALF = 2
BOX_LENGTH = 18.0
LANES = 128
MID = 64
WINDOW = 5
SEND_GRANT = 60
PAIRS = 6

F32 = jnp.float32
BF16 = jnp.bfloat16


def rounded_parts(table):
    high = table.astype(BF16).astype(np.float64)
    low = (table - high).astype(BF16).astype(np.float64)
    return high, low


def across(table):
    high, low = rounded_parts(table)
    return np.concatenate([high, high, low], 1).astype(np.float32)


def down(table):
    high, low = rounded_parts(table)
    return np.block([[high, low], [high, np.zeros_like(low)]]).astype(np.float32)


def make_tables(g):
    angle = 2.0 * np.pi / g * (np.outer(np.arange(g), np.arange(g)) % g)
    c, s = np.cos(angle), np.sin(angle)
    lower, upper = slice(0, g), slice(MID, MID + g)

    forward, backward = np.zeros((2, LANES, LANES))
    forward[lower, lower], forward[lower, upper] = c, -s
    forward[upper, lower], forward[upper, upper] = s, c
    backward[lower, lower], backward[lower, upper] = c, s
    backward[upper, lower], backward[upper, upper] = -s, c
    stick_in = np.zeros((LANES, 2 * g))
    stick_in[lower, :g], stick_in[lower, g:] = c, -s
    stick_in[upper, :g], stick_in[upper, g:] = s, c
    stick_out = np.zeros((2 * g, LANES))
    stick_out[:g, lower], stick_out[:g, upper] = c, s
    stick_out[g:, lower], stick_out[g:, upper] = -s, c

    freq = np.arange(g)
    square = np.minimum(freq, g - freq) ** 2
    total = square[:, None, None] + square[None, :, None] + square[None, None, :]
    unit = (2.0 * math.pi / BOX_LENGTH) ** 2
    kernel = np.where(total > 0, 4.0 * math.pi / (unit * np.maximum(total, 1)), 0.0)
    coulomb = np.zeros((g, g, LANES), np.float32)
    coulomb[:, :, lower] = kernel
    coulomb[:, :, upper] = kernel
    stick_in, left_backward = across(stick_in), across(np.concatenate([c, s], 0))
    early = np.zeros((LANES + 2 * g, stick_in.shape[1]), np.float32)
    early[:LANES], early[LANES:, : left_backward.shape[1]] = stick_in, left_backward
    return dict(
        forward=down(forward),
        last_backward=down(backward / g**3),
        left_forward=across(np.concatenate([c, -s], 0)),
        left_backward=left_backward,
        early=early,
        stick_out=across(stick_out * g**-1.5),
        coulomb=coulomb.reshape(g * g, LANES),
    )


def split(x):
    high = x.astype(BF16)
    low = (x - high.astype(F32)).astype(BF16)
    return high, low


def stacked(x):
    high, low = split(x)
    return jnp.concatenate([high, low, high], 0)


def dot(a, b):
    return jnp.dot(a, b, preferred_element_type=F32)


def lane_halves(shape):
    return lax.broadcasted_iota(jnp.int32, shape, 1) % LANES < MID


def turned(x):
    return pltpu.roll(x, MID, 1)


def regrouped(a, b):
    low = lane_halves(a.shape)
    return jnp.where(low, a, turned(b)), jnp.where(low, turned(a), b)


def beside(a, b):
    return jnp.concatenate([a, b], 1)


def halves(x):
    return x[:, :LANES], x[:, LANES:]


def left(table, x):
    both = dot(table, stacked(x))
    g = both.shape[0] // 2
    return both[:g], both[g:]


def left_complex(table, a, b):
    cos, sin = left(table, beside(a, b))
    sign = jnp.where(lane_halves((1, LANES)), -1.0, 1.0)
    return [p + turned(q) * sign for p, q in zip(halves(cos), halves(sin))]


def right(x, table):
    both = dot(beside(*split(x)), table)
    width = both.shape[1] // 2
    return both[:, :width] + both[:, width:]


def strided(ref, first, g):
    return ref[pl.ds(first, g, stride=g), :]


def slab_rows(index, g, count=1):
    return pl.ds(index * g, count * g)


def one_hot(index, wanted):
    return jnp.where(index == wanted, jnp.asarray(1, BF16), jnp.asarray(0, BF16))


def send_kernel(g, sticks_ref, columns_ref, *refs):
    block_refs, (row_ref, sems, row_sem) = refs[:-3], refs[-3:]
    own = lax.axis_index("stick")
    row_copy = pltpu.make_async_copy(columns_ref, row_ref, row_sem)
    row_copy.start()
    copies = [
        pltpu.make_async_copy(sticks_ref.at[own ^ d], ref.at[pl.ds(0, 2 * g)], sems.at[d])
        for d, ref in enumerate(block_refs)
    ]
    for copy in copies:
        copy.start()
    row_copy.wait()
    columns = jnp.broadcast_to(row_ref[...].astype(F32), (8, LANES))
    for ref in block_refs:
        ref[2 * g :, :] = columns
    for copy in copies:
        copy.wait()


def early_kernel(g, own_ref, tables_ref, staged_ref, stick_in_ref, left_ref):
    staged_ref[...] = own_ref[...]
    stick_in_ref[...] = tables_ref[:LANES, : stick_in_ref.shape[1]].astype(BF16)
    left_ref[...] = tables_ref[LANES:, : left_ref.shape[1]].astype(BF16)


def place_kernel(order, *refs):
    own = lax.axis_index("stick")
    out_ref = refs[-1]
    for d, block_ref in zip(order, refs[:-1]):
        out_ref[own ^ d] = block_ref[...]


def store(ref, first, slabs):
    g = slabs[0].shape[0]
    for k, slab in enumerate(slabs):
        ref[slab_rows(first + k, g), :] = slab


def relay_kernel(g, *refs):
    blocks, (coefficients_ref, columns_ref) = refs[:-2], refs[-2:]
    for k, ref in enumerate(blocks):
        coefficients_ref[k * 2 * g : (k + 1) * 2 * g, :] = ref[: 2 * g, :]
        columns_ref[:, k * LANES : (k + 1) * LANES] = ref[2 * g :, :]


def placed(g, blocks_ref, columns_ref, stick_in_ref):
    columns = columns_ref[:1, :].astype(jnp.int32)
    stick_in = stick_in_ref[...]
    blocks = [blocks_ref[k : k + 2 * g, :] for k in range(0, blocks_ref.shape[0], 2 * g)]
    sticks = []
    for k in range(0, len(blocks), 2):
        sticks.append(beside(*split(dot(stick_in, stacked(beside(blocks[k], blocks[k + 1]))).T)))
    sticks = jnp.concatenate(sticks, 0)
    rows = g * g // 2
    index = lax.broadcasted_iota(jnp.int16, (rows, columns.shape[1]), 0)
    for first in (0, rows):
        both = dot(one_hot(index, (columns - first).astype(jnp.int16)), sticks)
        yield first, both[:, :LANES] + both[:, LANES:]


def place_sticks_kernel(g, blocks_ref, columns_ref, stick_in_ref, grid_ref):
    for first, part in placed(g, blocks_ref, columns_ref, stick_in_ref):
        grid_ref[first : first + part.shape[0], :] = part


def field_kernel(g, grid_ref, blocks_ref, columns_ref, stick_in_ref, left_ref, phi_ref, work_a):
    backward = left_ref[...]
    half = g // 2
    for first, part in placed(g, blocks_ref, columns_ref, stick_in_ref):
        part = part + grid_ref[first : first + part.shape[0], :]
        for k in range(0, half, 2):
            slabs = left_complex(backward, part[k * g : (k + 1) * g], part[(k + 1) * g : (k + 2) * g])
            store(work_a, first // g + k, slabs)

    for y in range(half):
        x = beside(strided(work_a, y, g), strided(work_a, y + half, g))
        (cos, cos_up), (sin, sin_up) = map(halves, left(backward, x))
        low = lane_halves(cos.shape)
        store(phi_ref, y, [jnp.where(low, cos - turned(sin), turned(cos_up) - sin_up)])


def pick_kernel(g, first_columns_ref, second_columns_ref, hot_ref):
    columns = beside(first_columns_ref[...], second_columns_ref[...])
    for k in range(0, columns.shape[1], LANES):
        block = columns[:, k : k + LANES]
        wanted = jnp.concatenate([block] * (LANES // block.shape[0]), 0).T.astype(jnp.int32)
        for c in range(0, hot_ref.shape[1], LANES):
            index = lax.broadcasted_iota(jnp.int16, (LANES, LANES), 1)
            hot_ref[k : k + LANES, c : c + LANES] = one_hot(index, (wanted - c).astype(jnp.int16))


def potentials(g, phi_ref, first_ref, second_ref, tables, work_a, work_b, emit, last=PAIRS):
    forward, last_backward, left_forward, left_backward = [ref[...].astype(BF16) for ref in tables[:4]]
    coulomb_ref = tables[4]
    half = g // 2
    for start in range(0, half, PAIRS):
        rows = slab_rows(start, g, PAIRS)
        phi = phi_ref[rows, :]
        lower, upper = regrouped(phi * first_ref[rows, :], phi * second_ref[rows, :])
        spectrum = right(jnp.concatenate([lower, upper], 0), forward)
        for k in range(PAIRS):
            a, b = left_complex(left_forward, *(spectrum[j * g : (j + 1) * g] for j in (k, k + PAIRS)))
            store(work_a, start + k, [a])
            store(work_a, start + k + half, [b])

    for kx in range(0, g, 2):
        slabs = left_complex(left_forward, strided(work_a, kx, g), strided(work_a, kx + 1, g))
        slabs = [slab * coulomb_ref[slab_rows(kx + j, g), :] for j, slab in enumerate(slabs)]
        store(work_b, kx, left_complex(left_backward, *slabs))

    for start in range(0, half, last):
        lower, upper = [], []
        for z in range(start, start + last):
            a, b = left_complex(left_backward, strided(work_b, z, g), strided(work_b, z + half, g))
            lower.append(a)
            upper.append(b)
        out = right(jnp.concatenate(lower + upper, 0), last_backward)
        emit(start, *regrouped(out[: last * g], out[last * g :]))


def near_kernel(g, phi_ref, other_ref, *refs):
    tables, (sum_ref, work_a, work_b) = refs[:5], refs[5:]

    def emit(start, own, other):
        rows = slab_rows(start, g, PAIRS)
        sum_ref[rows, :] = own * phi_ref[rows, :] + other * other_ref[rows, :]

    potentials(g, phi_ref, phi_ref, other_ref, tables, work_a, work_b, emit)


def middle_kernel(g, phi_ref, first_ref, second_ref, before_ref, *refs):
    tables, (sum_ref, work_a, work_b) = refs[:5], refs[5:]

    def emit(start, first, second):
        rows = slab_rows(start, g, PAIRS)
        sum_ref[rows, :] = before_ref[rows, :] + first * first_ref[rows, :] + second * second_ref[rows, :]

    potentials(g, phi_ref, first_ref, second_ref, tables, work_a, work_b, emit)


def far_kernel(g, weights, phi_ref, first_ref, second_ref, before_ref, hot_ref, stick_out_ref, *refs):
    tables, out_refs = refs[:5], refs[5:-3]
    work_a, work_b, picked_ref = refs[-3:]
    forward = tables[2][...].astype(BF16)
    half = g // 2

    def emit(start, first, second):
        rows = slab_rows(start, g, half)
        total = before_ref[rows, :] + weights[0] * (first * first_ref[rows, :])
        total = total + weights[1] * (second * second_ref[rows, :])
        for k in range(0, half, 2):
            cos, sin = left(forward, beside(total[k * g : (k + 1) * g], total[(k + 1) * g : (k + 2) * g]))
            for j, (real, imag) in enumerate(zip(halves(cos), halves(sin))):
                lower, upper = regrouped(real, imag)
                store(work_a, start + k + j, [lower])
                store(work_a, start + k + j + half, [upper])

    potentials(g, phi_ref, first_ref, second_ref, tables, work_a, work_b, emit, half)

    step = g // 3
    for first in range(0, g, step):
        slabs = []
        for kx in range(first, first + step, 2):
            slabs += left_complex(forward, strided(work_a, kx, g), strided(work_a, kx + 1, g))
        spectrum = beside(*split(jnp.concatenate(slabs, 0)))
        both = dot(hot_ref[:, first * g : (first + step) * g], spectrum)
        both = both[:, :LANES] + both[:, LANES:]
        picked_ref[...] = both if first == 0 else picked_ref[...] + both

    stick_out = stick_out_ref[...].astype(BF16)
    for k in range(0, len(out_refs), 2):
        high, low = split(picked_ref[k * LANES : (k + 2) * LANES, :])
        lined = jnp.concatenate([high, low, high], 1)
        out = lax.dot_general(stick_out, lined, (((1,), (1,)), ((), ())), preferred_element_type=F32)
        out_refs[k][...], out_refs[k + 1][...] = halves(out)


def call(kernel, out_shapes, scratch, flops, *operands, space=pltpu.VMEM, out_space=pltpu.VMEM, grant=40):
    out_spec = pl.BlockSpec(memory_space=out_space)
    return pl.pallas_call(
        kernel,
        out_shape=out_shapes,
        in_specs=[pl.BlockSpec(memory_space=space)] * len(operands),
        out_specs=jax.tree.map(lambda _: out_spec, out_shapes),
        scratch_shapes=scratch,
        compiler_params=pltpu.CompilerParams(vmem_limit_bytes=grant * 2**20),
        cost_estimate=pl.CostEstimate(flops=flops, bytes_accessed=flops, transcendentals=0),
    )(*operands)


def after(x, *others):
    return lax.optimization_barrier((x, *others))[0]


def exchanged(blocks, order, before):
    owners = len(blocks)
    moved = [blocks[0]] + [None] * (owners - 1)
    for d in order:
        others = [moved[x] if isinstance(x, int) else x for x in before.get(d, ())]
        block = after(blocks[d], *others) if others else blocks[d]
        moved[d] = lax.ppermute(block, "stick", [(i, i ^ d) for i in range(owners)])
    return moved


def on_device(sticks, stick_columns):
    g = sticks.shape[1] // 2
    slots = stick_columns.shape[0]
    owners = lax.axis_size("stick")
    groups = lax.axis_size("band")
    t = {name: jnp.asarray(value) for name, value in make_tables(g).items()}
    rows = g * g
    field = jax.ShapeDtypeStruct((rows // 2, LANES), F32)
    work = pltpu.VMEM((rows, LANES), F32)
    pot_flops = 1

    def shifted(x, distance):
        return lax.ppermute(x, "band", [(i, (i - distance) % groups) for i in range(groups)])

    def swapped(x):
        return lax.ppermute(x, "band", [(i, i ^ 1) for i in range(groups)])

    sent = call(
        functools.partial(send_kernel, g),
        [jax.ShapeDtypeStruct((2 * g + 8, slots), F32)] * owners,
        [
            pltpu.VMEM((1, slots), jnp.int32),
            pltpu.SemaphoreType.DMA((owners,)),
            pltpu.SemaphoreType.DMA,
        ],
        1,
        sticks,
        stick_columns[None, :],
        space=pltpu.HBM,
        grant=SEND_GRANT,
    )
    shapes = [(2 * g + 8, slots), (LANES, 6 * g), (2 * g, 3 * g)]
    staged, *first_tables = call(
        functools.partial(early_kernel, g),
        [jax.ShapeDtypeStruct(shape, kind) for shape, kind in zip(shapes, (F32, BF16, BF16))],
        [],
        1,
        sent[0],
        after(t["early"], sent[0]),
    )
    half = owners // 2
    distant, close = list(range(half, owners)), list(range(1, half))
    mixed = [distant[0]] + [d for pair in zip(close, distant[1:]) for d in pair]
    before = {mixed[k]: (mixed[k - 3 - k % 2],) for k in range(WINDOW, len(mixed))}
    last = mixed[WINDOW]
    received = exchanged(sent, mixed, {**before, last: (*before[last], staged, *first_tables)})
    received[0] = staged
    cut = owners * 3 // 4
    order = [0] + mixed
    order = order[:cut] + order[:cut - 1:-1]
    stick_in, left_table = first_tables

    def relayed(part):
        shapes = [(len(part) * 2 * g, slots), (8, len(part) * slots)]
        shapes = [jax.ShapeDtypeStruct(shape, F32) for shape in shapes]
        return call(functools.partial(relay_kernel, g), shapes, [], 1, *[received[d] for d in part])

    def on_grid(blocks, flops=1):
        grid = jax.ShapeDtypeStruct((rows, LANES), F32)
        return call(functools.partial(place_sticks_kernel, g), grid, [], flops, blocks, columns[0], stick_in)

    def orbital(grid, rest):
        operands = (grid, rest, columns[1], stick_in, left_table)
        return call(functools.partial(field_kernel, g), field, [work], 1, *operands)

    first_blocks, first_columns = relayed(order[:cut])
    columns = [first_columns]
    own_grid = on_grid(first_blocks, 5 * 10**9)
    received[order[cut]] = after(received[order[cut]], own_grid)
    last_blocks, last_columns = relayed(order[cut:])
    columns.append(last_columns)
    phi = orbital(own_grid, last_blocks)
    near = swapped(phi)
    hot = call(
        functools.partial(pick_kernel, g), jax.ShapeDtypeStruct((owners * slots, rows), BF16), [], pot_flops, *columns
    )
    pot_tables = [t["forward"], t["last_backward"], t["left_forward"], t["left_backward"], t["coulomb"]]

    def potential_sum(kernel, *operands):
        return call(functools.partial(kernel, g), field, [work, work], pot_flops, phi, *operands, *pot_tables)

    distances = (HALF,) if groups == 2 * HALF else (HALF, -HALF)
    fields = [orbital(on_grid(shifted(first_blocks, d)), shifted(last_blocks, d)) for d in distances]
    total = potential_sum(near_kernel, after(near, *fields))
    if groups == 2 * HALF:
        weights = (2.0, 1.0)
        first, second = fields[0], swapped(fields[0])
    else:
        weights = (1.0, 0.0)
        odd = lax.axis_index("band") % 2 == 1
        first = second = swapped(jnp.where(odd, fields[1], fields[0]))
        total = potential_sum(middle_kernel, *fields, total)
    result = call(
        functools.partial(far_kernel, g, weights),
        [jax.ShapeDtypeStruct((2 * g, slots), F32)] * owners,
        [work, work, pltpu.VMEM((owners * slots, LANES), F32)],
        pot_flops,
        phi,
        first,
        second,
        total,
        hot,
        t["stick_out"],
        *pot_tables,
    )
    result = [result[order.index(d)] for d in range(owners)]
    result = exchanged(result, mixed, before)
    out_order = [0] + distant + close
    return call(
        functools.partial(place_kernel, out_order),
        jax.ShapeDtypeStruct(sticks.shape, F32),
        [],
        1,
        *[result[d] for d in out_order],
    )


def solution(mesh):
    return jax.shard_map(
        on_device,
        mesh=mesh,
        in_specs=(P("band", None, "stick"), P("stick")),
        out_specs=P("band", None, "stick"),
        check_vma=False,
    )
```

```python
import functools
import math

import jax
import jax.numpy as jnp
import numpy as np
from jax import lax
from jax.experimental import pallas as pl
from jax.experimental.pallas import tpu as pltpu
from jax.sharding import PartitionSpec as P

HALF = 2
BOX_LENGTH = 18.0
LANES = 128
MID = 64
WINDOW = 5
SEND_GRANT = 60
PAIRS = 6

F32 = jnp.float32
BF16 = jnp.bfloat16


def rounded_parts(table):
    high = table.astype(BF16).astype(np.float64)
    low = (table - high).astype(BF16).astype(np.float64)
    return high, low


def across(table):
    high, low = rounded_parts(table)
    return np.concatenate([high, high, low], 1).astype(np.float32)


def down(table):
    high, low = rounded_parts(table)
    return np.block([[high, low], [high, np.zeros_like(low)]]).astype(np.float32)


def make_tables(g):
    angle = 2.0 * np.pi / g * (np.outer(np.arange(g), np.arange(g)) % g)
    c, s = np.cos(angle), np.sin(angle)
    lower, upper = slice(0, g), slice(MID, MID + g)

    forward, backward = np.zeros((2, LANES, LANES))
    forward[lower, lower], forward[lower, upper] = c, -s
    forward[upper, lower], forward[upper, upper] = s, c
    backward[lower, lower], backward[lower, upper] = c, s
    backward[upper, lower], backward[upper, upper] = -s, c
    stick_in = np.zeros((LANES, 2 * g))
    stick_in[lower, :g], stick_in[lower, g:] = c, -s
    stick_in[upper, :g], stick_in[upper, g:] = s, c
    stick_out = np.zeros((2 * g, LANES))
    stick_out[:g, lower], stick_out[:g, upper] = c, s
    stick_out[g:, lower], stick_out[g:, upper] = -s, c

    freq = np.arange(g)
    square = np.minimum(freq, g - freq) ** 2
    total = square[:, None, None] + square[None, :, None] + square[None, None, :]
    unit = (2.0 * math.pi / BOX_LENGTH) ** 2
    kernel = np.where(total > 0, 4.0 * math.pi / (unit * np.maximum(total, 1)), 0.0)
    coulomb = np.zeros((g, g, LANES), np.float32)
    coulomb[:, :, lower] = kernel
    coulomb[:, :, upper] = kernel
    stick_in, left_backward = across(stick_in), across(np.concatenate([c, s], 0))
    early = np.zeros((LANES + 2 * g, stick_in.shape[1]), np.float32)
    early[:LANES], early[LANES:, : left_backward.shape[1]] = stick_in, left_backward
    return dict(
        forward=down(forward),
        last_backward=down(backward / g**3),
        left_forward=across(np.concatenate([c, -s], 0)),
        left_backward=left_backward,
        early=early,
        stick_out=across(stick_out * g**-1.5),
        coulomb=coulomb.reshape(g * g, LANES),
    )


def split(x):
    high = x.astype(BF16)
    low = (x - high.astype(F32)).astype(BF16)
    return high, low


def stacked(x):
    high, low = split(x)
    return jnp.concatenate([high, low, high], 0)


def dot(a, b):
    return jnp.dot(a, b, preferred_element_type=F32)


def lane_halves(shape):
    return lax.broadcasted_iota(jnp.int32, shape, 1) % LANES < MID


def turned(x):
    return pltpu.roll(x, MID, 1)


def regrouped(a, b):
    low = lane_halves(a.shape)
    return jnp.where(low, a, turned(b)), jnp.where(low, turned(a), b)


def beside(a, b):
    return jnp.concatenate([a, b], 1)


def halves(x):
    return x[:, :LANES], x[:, LANES:]


def left(table, x):
    both = dot(table, stacked(x))
    g = both.shape[0] // 2
    return both[:g], both[g:]


def left_complex(table, a, b):
    cos, sin = left(table, beside(a, b))
    sign = jnp.where(lane_halves((1, LANES)), -1.0, 1.0)
    return [p + turned(q) * sign for p, q in zip(halves(cos), halves(sin))]


def right(x, table):
    both = dot(beside(*split(x)), table)
    width = both.shape[1] // 2
    return both[:, :width] + both[:, width:]


def strided(ref, first, g):
    return ref[pl.ds(first, g, stride=g), :]


def slab_rows(index, g, count=1):
    return pl.ds(index * g, count * g)


def one_hot(index, wanted):
    return jnp.where(index == wanted, jnp.asarray(1, BF16), jnp.asarray(0, BF16))


def send_kernel(g, sticks_ref, columns_ref, *refs):
    block_refs, (row_ref, sems, row_sem) = refs[:-3], refs[-3:]
    own = lax.axis_index("stick")
    row_copy = pltpu.make_async_copy(columns_ref, row_ref, row_sem)
    row_copy.start()
    copies = [
        pltpu.make_async_copy(sticks_ref.at[own ^ d], ref.at[pl.ds(0, 2 * g)], sems.at[d])
        for d, ref in enumerate(block_refs)
    ]
    for copy in copies:
        copy.start()
    row_copy.wait()
    columns = jnp.broadcast_to(row_ref[...].astype(F32), (8, LANES))
    for ref in block_refs:
        ref[2 * g :, :] = columns
    for copy in copies:
        copy.wait()


def early_kernel(g, tables_ref, stick_in_ref, left_ref):
    stick_in_ref[...] = tables_ref[:LANES, : stick_in_ref.shape[1]].astype(BF16)
    left_ref[...] = tables_ref[LANES:, : left_ref.shape[1]].astype(BF16)


def place_kernel(order, *refs):
    own = lax.axis_index("stick")
    out_ref = refs[-1]
    for d, block_ref in zip(order, refs[:-1]):
        out_ref[own ^ d] = block_ref[...]


def store(ref, first, slabs):
    g = slabs[0].shape[0]
    for k, slab in enumerate(slabs):
        ref[slab_rows(first + k, g), :] = slab


def relay_kernel(g, *refs):
    blocks, (coefficients_ref, columns_ref) = refs[:-2], refs[-2:]
    for k, ref in enumerate(blocks):
        coefficients_ref[k * 2 * g : (k + 1) * 2 * g, :] = ref[: 2 * g, :]
        columns_ref[:, k * LANES : (k + 1) * LANES] = ref[2 * g :, :]


def placed(g, blocks_ref, columns_ref, stick_in_ref):
    columns = columns_ref[:1, :].astype(jnp.int32)
    stick_in = stick_in_ref[...]
    blocks = [blocks_ref[k : k + 2 * g, :] for k in range(0, blocks_ref.shape[0], 2 * g)]
    sticks = []
    for k in range(0, len(blocks), 2):
        sticks.append(beside(*split(dot(stick_in, stacked(beside(blocks[k], blocks[k + 1]))).T)))
    sticks = jnp.concatenate(sticks, 0)
    rows = g * g // 2
    index = lax.broadcasted_iota(jnp.int16, (rows, columns.shape[1]), 0)
    for first in (0, rows):
        both = dot(one_hot(index, (columns - first).astype(jnp.int16)), sticks)
        yield first, both[:, :LANES] + both[:, LANES:]


def place_sticks_kernel(g, blocks_ref, columns_ref, stick_in_ref, grid_ref):
    for first, part in placed(g, blocks_ref, columns_ref, stick_in_ref):
        grid_ref[first : first + part.shape[0], :] = part


def field_kernel(g, grid_ref, blocks_ref, columns_ref, stick_in_ref, left_ref, phi_ref, work_a):
    backward = left_ref[...]
    half = g // 2
    for first, part in placed(g, blocks_ref, columns_ref, stick_in_ref):
        part = part + grid_ref[first : first + part.shape[0], :]
        for k in range(0, half, 2):
            slabs = left_complex(backward, part[k * g : (k + 1) * g], part[(k + 1) * g : (k + 2) * g])
            store(work_a, first // g + k, slabs)

    for y in range(half):
        x = beside(strided(work_a, y, g), strided(work_a, y + half, g))
        (cos, cos_up), (sin, sin_up) = map(halves, left(backward, x))
        low = lane_halves(cos.shape)
        store(phi_ref, y, [jnp.where(low, cos - turned(sin), turned(cos_up) - sin_up)])


def pick_kernel(g, columns_ref, hot_ref):
    for k in range(0, columns_ref.shape[1], LANES):
        block = columns_ref[:, k : k + LANES]
        wanted = jnp.concatenate([block] * (LANES // block.shape[0]), 0).T.astype(jnp.int32)
        for c in range(0, hot_ref.shape[1], LANES):
            index = lax.broadcasted_iota(jnp.int16, (LANES, LANES), 1)
            hot_ref[k : k + LANES, c : c + LANES] = one_hot(index, (wanted - c).astype(jnp.int16))


def potentials(g, phi_ref, first_ref, second_ref, tables, work_a, work_b, emit, last=PAIRS):
    forward, last_backward, left_forward, left_backward = [ref[...].astype(BF16) for ref in tables[:4]]
    coulomb_ref = tables[4]
    half = g // 2
    for start in range(0, half, PAIRS):
        rows = slab_rows(start, g, PAIRS)
        phi = phi_ref[rows, :]
        lower, upper = regrouped(phi * first_ref[rows, :], phi * second_ref[rows, :])
        spectrum = right(jnp.concatenate([lower, upper], 0), forward)
        for k in range(PAIRS):
            a, b = left_complex(left_forward, *(spectrum[j * g : (j + 1) * g] for j in (k, k + PAIRS)))
            store(work_a, start + k, [a])
            store(work_a, start + k + half, [b])

    for kx in range(0, g, 2):
        slabs = left_complex(left_forward, strided(work_a, kx, g), strided(work_a, kx + 1, g))
        slabs = [slab * coulomb_ref[slab_rows(kx + j, g), :] for j, slab in enumerate(slabs)]
        store(work_b, kx, left_complex(left_backward, *slabs))

    for start in range(0, half, last):
        lower, upper = [], []
        for z in range(start, start + last):
            a, b = left_complex(left_backward, strided(work_b, z, g), strided(work_b, z + half, g))
            lower.append(a)
            upper.append(b)
        out = right(jnp.concatenate(lower + upper, 0), last_backward)
        emit(start, *regrouped(out[: last * g], out[last * g :]))


def near_kernel(g, phi_ref, other_ref, *refs):
    tables, (sum_ref, work_a, work_b) = refs[:5], refs[5:]

    def emit(start, own, other):
        rows = slab_rows(start, g, PAIRS)
        sum_ref[rows, :] = own * phi_ref[rows, :] + other * other_ref[rows, :]

    potentials(g, phi_ref, phi_ref, other_ref, tables, work_a, work_b, emit)


def middle_kernel(g, phi_ref, first_ref, second_ref, before_ref, *refs):
    tables, (sum_ref, work_a, work_b) = refs[:5], refs[5:]

    def emit(start, first, second):
        rows = slab_rows(start, g, PAIRS)
        sum_ref[rows, :] = before_ref[rows, :] + first * first_ref[rows, :] + second * second_ref[rows, :]

    potentials(g, phi_ref, first_ref, second_ref, tables, work_a, work_b, emit)


def far_kernel(g, weights, phi_ref, first_ref, second_ref, before_ref, hot_ref, last_hot_ref, stick_out_ref, *refs):
    tables, out_refs = refs[:5], refs[5:-3]
    work_a, work_b, picked_ref = refs[-3:]
    forward = tables[2][...].astype(BF16)
    half = g // 2

    def emit(start, first, second):
        rows = slab_rows(start, g, half)
        total = before_ref[rows, :] + weights[0] * (first * first_ref[rows, :])
        total = total + weights[1] * (second * second_ref[rows, :])
        for k in range(0, half, 2):
            cos, sin = left(forward, beside(total[k * g : (k + 1) * g], total[(k + 1) * g : (k + 2) * g]))
            for j, (real, imag) in enumerate(zip(halves(cos), halves(sin))):
                lower, upper = regrouped(real, imag)
                store(work_a, start + k + j, [lower])
                store(work_a, start + k + j + half, [upper])

    potentials(g, phi_ref, first_ref, second_ref, tables, work_a, work_b, emit, half)

    step = g // 3
    for first in range(0, g, step):
        slabs = []
        for kx in range(first, first + step, 2):
            slabs += left_complex(forward, strided(work_a, kx, g), strided(work_a, kx + 1, g))
        spectrum = beside(*split(jnp.concatenate(slabs, 0)))
        start = 0
        for ref in (hot_ref, last_hot_ref):
            both = dot(ref[:, first * g : (first + step) * g], spectrum)
            both = both[:, :LANES] + both[:, LANES:]
            rows = slice(start, start + ref.shape[0])
            picked_ref[rows, :] = both if first == 0 else picked_ref[rows, :] + both
            start += ref.shape[0]

    stick_out = stick_out_ref[...].astype(BF16)
    for k in range(0, len(out_refs), 2):
        high, low = split(picked_ref[k * LANES : (k + 2) * LANES, :])
        lined = jnp.concatenate([high, low, high], 1)
        out = lax.dot_general(stick_out, lined, (((1,), (1,)), ((), ())), preferred_element_type=F32)
        out_refs[k][...], out_refs[k + 1][...] = halves(out)


def call(kernel, out_shapes, scratch, flops, *operands, space=pltpu.VMEM, out_space=pltpu.VMEM, grant=40):
    out_spec = pl.BlockSpec(memory_space=out_space)
    return pl.pallas_call(
        kernel,
        out_shape=out_shapes,
        in_specs=[pl.BlockSpec(memory_space=space)] * len(operands),
        out_specs=jax.tree.map(lambda _: out_spec, out_shapes),
        scratch_shapes=scratch,
        compiler_params=pltpu.CompilerParams(vmem_limit_bytes=grant * 2**20),
        cost_estimate=pl.CostEstimate(flops=flops, bytes_accessed=flops, transcendentals=0),
    )(*operands)


def after(x, *others):
    return lax.optimization_barrier((x, *others))[0]


def exchanged(blocks, order, before):
    owners = len(blocks)
    moved = [blocks[0]] + [None] * (owners - 1)
    for d in order:
        others = [moved[x] if isinstance(x, int) else x for x in before.get(d, ())]
        block = after(blocks[d], *others) if others else blocks[d]
        moved[d] = lax.ppermute(block, "stick", [(i, i ^ d) for i in range(owners)])
    return moved


def on_device(sticks, stick_columns):
    g = sticks.shape[1] // 2
    slots = stick_columns.shape[0]
    owners = lax.axis_size("stick")
    groups = lax.axis_size("band")
    t = {name: jnp.asarray(value) for name, value in make_tables(g).items()}
    rows = g * g
    field = jax.ShapeDtypeStruct((rows // 2, LANES), F32)
    work = pltpu.VMEM((rows, LANES), F32)
    pot_flops = 1

    def shifted(x, distance):
        return lax.ppermute(x, "band", [(i, (i - distance) % groups) for i in range(groups)])

    def swapped(x):
        return lax.ppermute(x, "band", [(i, i ^ 1) for i in range(groups)])

    sent = call(
        functools.partial(send_kernel, g),
        [jax.ShapeDtypeStruct((2 * g + 8, slots), F32)] * owners,
        [
            pltpu.VMEM((1, slots), jnp.int32),
            pltpu.SemaphoreType.DMA((owners,)),
            pltpu.SemaphoreType.DMA,
        ],
        1,
        sticks,
        stick_columns[None, :],
        space=pltpu.HBM,
        grant=SEND_GRANT,
    )
    half = owners // 2
    distant, close = list(range(half, owners)), list(range(1, half))
    mixed = [distant[0]] + [d for pair in zip(close, distant[1:]) for d in pair]
    before = {mixed[k]: (mixed[k - 2 if k % 2 else k - 5],) for k in range(WINDOW, len(mixed))}
    received = exchanged(sent, mixed, before)
    cut = owners * 3 // 4
    order = [0] + mixed
    order = order[:cut] + order[:cut - 1:-1]
    first_tables = call(
        functools.partial(early_kernel, g),
        [jax.ShapeDtypeStruct(shape, BF16) for shape in ((LANES, 6 * g), (2 * g, 3 * g))],
        [],
        1,
        after(t["early"], received[distant[-2]]),
    )
    stick_in, left_table = first_tables

    def relayed(part):
        shapes = [(len(part) * 2 * g, slots), (8, len(part) * slots)]
        shapes = [jax.ShapeDtypeStruct(shape, F32) for shape in shapes]
        return call(functools.partial(relay_kernel, g), shapes, [], 1, *[received[d] for d in part])

    def on_grid(blocks, flops=1):
        grid = jax.ShapeDtypeStruct((rows, LANES), F32)
        return call(functools.partial(place_sticks_kernel, g), grid, [], flops, blocks, columns[0], stick_in)

    def orbital(grid, rest):
        operands = (grid, rest, columns[1], stick_in, left_table)
        return call(functools.partial(field_kernel, g), field, [work], 1, *operands)

    first_blocks, first_columns = relayed(order[:cut])
    columns = [first_columns]
    own_grid = on_grid(first_blocks, 5 * 10**9)

    def hot_rows(columns):
        shape = jax.ShapeDtypeStruct((columns.shape[1], rows), BF16)
        return call(functools.partial(pick_kernel, g), shape, [], 1, columns)

    hot = [hot_rows(first_columns)]
    received[order[cut]] = after(received[order[cut]], own_grid, *hot)
    last_blocks, last_columns = relayed(order[cut:])
    columns.append(last_columns)
    hot.append(hot_rows(last_columns))
    phi = orbital(own_grid, last_blocks)
    near = swapped(phi)
    pot_tables = [t["forward"], t["last_backward"], t["left_forward"], t["left_backward"], t["coulomb"]]

    def potential_sum(kernel, *operands):
        return call(functools.partial(kernel, g), field, [work, work], pot_flops, phi, *operands, *pot_tables)

    distances = (HALF,) if groups == 2 * HALF else (HALF, -HALF)
    fields = [orbital(on_grid(shifted(first_blocks, d)), shifted(last_blocks, d)) for d in distances]
    total = potential_sum(near_kernel, after(near, *fields))
    if groups == 2 * HALF:
        weights = (2.0, 1.0)
        first, second = fields[0], swapped(fields[0])
    else:
        weights = (1.0, 0.0)
        odd = lax.axis_index("band") % 2 == 1
        first = second = swapped(jnp.where(odd, fields[1], fields[0]))
        total = potential_sum(middle_kernel, *fields, total)
    result = call(
        functools.partial(far_kernel, g, weights),
        [jax.ShapeDtypeStruct((2 * g, slots), F32)] * owners,
        [work, work, pltpu.VMEM((owners * slots, LANES), F32)],
        pot_flops,
        phi,
        first,
        second,
        total,
        *hot,
        t["stick_out"],
        *pot_tables,
    )
    result = [result[order.index(d)] for d in range(owners)]
    result = exchanged(result, mixed, before)
    out_order = [0] + distant + close
    return call(
        functools.partial(place_kernel, out_order),
        jax.ShapeDtypeStruct(sticks.shape, F32),
        [],
        1,
        *[result[d] for d in out_order],
    )


def solution(mesh):
    return jax.shard_map(
        on_device,
        mesh=mesh,
        in_specs=(P("band", None, "stick"), P("stick")),
        out_specs=P("band", None, "stick"),
        check_vma=False,
    )
```

```python
import functools
import math

import jax
import jax.numpy as jnp
import numpy as np
from jax import lax
from jax.experimental import pallas as pl
from jax.experimental.pallas import tpu as pltpu
from jax.sharding import PartitionSpec as P

HALF = 2
BOX_LENGTH = 18.0
LANES = 128
MID = 64
WINDOW = 5
SEND_GRANT = 60
PAIRS = 6

F32 = jnp.float32
BF16 = jnp.bfloat16


def rounded_parts(table):
    high = table.astype(BF16).astype(np.float64)
    low = (table - high).astype(BF16).astype(np.float64)
    return high, low


def across(table):
    high, low = rounded_parts(table)
    return np.concatenate([high, high, low], 1).astype(np.float32)


def down(table):
    high, low = rounded_parts(table)
    return np.block([[high, low], [high, np.zeros_like(low)]]).astype(np.float32)


def make_tables(g):
    angle = 2.0 * np.pi / g * (np.outer(np.arange(g), np.arange(g)) % g)
    c, s = np.cos(angle), np.sin(angle)
    lower, upper = slice(0, g), slice(MID, MID + g)

    forward, backward = np.zeros((2, LANES, LANES))
    forward[lower, lower], forward[lower, upper] = c, -s
    forward[upper, lower], forward[upper, upper] = s, c
    backward[lower, lower], backward[lower, upper] = c, s
    backward[upper, lower], backward[upper, upper] = -s, c
    stick_in = np.zeros((LANES, 2 * g))
    stick_in[lower, :g], stick_in[lower, g:] = c, -s
    stick_in[upper, :g], stick_in[upper, g:] = s, c
    stick_out = np.zeros((2 * g, LANES))
    stick_out[:g, lower], stick_out[:g, upper] = c, s
    stick_out[g:, lower], stick_out[g:, upper] = -s, c

    freq = np.arange(g)
    square = np.minimum(freq, g - freq) ** 2
    total = square[:, None, None] + square[None, :, None] + square[None, None, :]
    unit = (2.0 * math.pi / BOX_LENGTH) ** 2
    kernel = np.where(total > 0, 4.0 * math.pi / (unit * np.maximum(total, 1)), 0.0)
    coulomb = np.zeros((g, g, LANES), np.float32)
    coulomb[:, :, lower] = kernel
    coulomb[:, :, upper] = kernel
    stick_in, left_backward = across(stick_in), across(np.concatenate([c, s], 0))
    early = np.zeros((LANES + 2 * g, stick_in.shape[1]), np.float32)
    early[:LANES], early[LANES:, : left_backward.shape[1]] = stick_in, left_backward
    return dict(
        forward=down(forward),
        last_backward=down(backward / g**3),
        left_forward=across(np.concatenate([c, -s], 0)),
        left_backward=left_backward,
        early=early,
        stick_out=across(stick_out * g**-1.5),
        coulomb=coulomb.reshape(g * g, LANES),
    )


def split(x):
    high = x.astype(BF16)
    low = (x - high.astype(F32)).astype(BF16)
    return high, low


def stacked(x):
    high, low = split(x)
    return jnp.concatenate([high, low, high], 0)


def dot(a, b):
    return jnp.dot(a, b, preferred_element_type=F32)


def lane_halves(shape):
    return lax.broadcasted_iota(jnp.int32, shape, 1) % LANES < MID


def turned(x):
    return pltpu.roll(x, MID, 1)


def regrouped(a, b):
    low = lane_halves(a.shape)
    return jnp.where(low, a, turned(b)), jnp.where(low, turned(a), b)


def beside(a, b):
    return jnp.concatenate([a, b], 1)


def halves(x):
    return x[:, :LANES], x[:, LANES:]


def left(table, x):
    both = dot(table, stacked(x))
    g = both.shape[0] // 2
    return both[:g], both[g:]


def left_complex(table, a, b):
    cos, sin = left(table, beside(a, b))
    sign = jnp.where(lane_halves((1, LANES)), -1.0, 1.0)
    return [p + turned(q) * sign for p, q in zip(halves(cos), halves(sin))]


def right(x, table):
    both = dot(beside(*split(x)), table)
    width = both.shape[1] // 2
    return both[:, :width] + both[:, width:]


def strided(ref, first, g):
    return ref[pl.ds(first, g, stride=g), :]


def slab_rows(index, g, count=1):
    return pl.ds(index * g, count * g)


def one_hot(index, wanted):
    return jnp.where(index == wanted, jnp.asarray(1, BF16), jnp.asarray(0, BF16))


def send_kernel(g, sticks_ref, columns_ref, *refs):
    block_refs, (row_ref, sems, row_sem) = refs[:-3], refs[-3:]
    own = lax.axis_index("stick")
    row_copy = pltpu.make_async_copy(columns_ref, row_ref, row_sem)
    row_copy.start()
    copies = [
        pltpu.make_async_copy(sticks_ref.at[own ^ d], ref.at[pl.ds(0, 2 * g)], sems.at[d])
        for d, ref in enumerate(block_refs)
    ]
    for copy in copies:
        copy.start()
    row_copy.wait()
    columns = jnp.broadcast_to(row_ref[...].astype(F32), (8, LANES))
    for ref in block_refs:
        ref[2 * g :, :] = columns
    for copy in copies:
        copy.wait()


def early_kernel(g, own_ref, tables_ref, staged_ref, stick_in_ref, left_ref):
    staged_ref[...] = own_ref[...]
    stick_in_ref[...] = tables_ref[:LANES, : stick_in_ref.shape[1]].astype(BF16)
    left_ref[...] = tables_ref[LANES:, : left_ref.shape[1]].astype(BF16)


def place_kernel(order, *refs):
    own = lax.axis_index("stick")
    out_ref = refs[-1]
    for d, block_ref in zip(order, refs[:-1]):
        out_ref[own ^ d] = block_ref[...]


def store(ref, first, slabs):
    g = slabs[0].shape[0]
    for k, slab in enumerate(slabs):
        ref[slab_rows(first + k, g), :] = slab


def relay_kernel(g, *refs):
    blocks, (coefficients_ref, columns_ref) = refs[:-2], refs[-2:]
    for k, ref in enumerate(blocks):
        coefficients_ref[k * 2 * g : (k + 1) * 2 * g, :] = ref[: 2 * g, :]
        columns_ref[:, k * LANES : (k + 1) * LANES] = ref[2 * g :, :]


def placed(g, blocks_ref, columns_ref, stick_in_ref):
    columns = columns_ref[:1, :].astype(jnp.int32)
    stick_in = stick_in_ref[...]
    blocks = [blocks_ref[k : k + 2 * g, :] for k in range(0, blocks_ref.shape[0], 2 * g)]
    sticks = []
    for k in range(0, len(blocks), 2):
        sticks.append(beside(*split(dot(stick_in, stacked(beside(blocks[k], blocks[k + 1]))).T)))
    sticks = jnp.concatenate(sticks, 0)
    rows = g * g // 2
    index = lax.broadcasted_iota(jnp.int16, (rows, columns.shape[1]), 0)
    for first in (0, rows):
        both = dot(one_hot(index, (columns - first).astype(jnp.int16)), sticks)
        yield first, both[:, :LANES] + both[:, LANES:]


def place_sticks_kernel(g, blocks_ref, columns_ref, stick_in_ref, grid_ref):
    for first, part in placed(g, blocks_ref, columns_ref, stick_in_ref):
        grid_ref[first : first + part.shape[0], :] = part


def field_kernel(g, grid_ref, blocks_ref, columns_ref, stick_in_ref, left_ref, phi_ref, work_a):
    backward = left_ref[...]
    half = g // 2
    for first, part in placed(g, blocks_ref, columns_ref, stick_in_ref):
        part = part + grid_ref[first : first + part.shape[0], :]
        for k in range(0, half, 2):
            slabs = left_complex(backward, part[k * g : (k + 1) * g], part[(k + 1) * g : (k + 2) * g])
            store(work_a, first // g + k, slabs)

    for y in range(half):
        x = beside(strided(work_a, y, g), strided(work_a, y + half, g))
        (cos, cos_up), (sin, sin_up) = map(halves, left(backward, x))
        low = lane_halves(cos.shape)
        store(phi_ref, y, [jnp.where(low, cos - turned(sin), turned(cos_up) - sin_up)])


def pick_kernel(g, columns_ref, hot_ref):
    for k in range(0, columns_ref.shape[1], LANES):
        block = columns_ref[:, k : k + LANES]
        wanted = jnp.concatenate([block] * (LANES // block.shape[0]), 0).T.astype(jnp.int32)
        for c in range(0, hot_ref.shape[1], LANES):
            index = lax.broadcasted_iota(jnp.int16, (LANES, LANES), 1)
            hot_ref[k : k + LANES, c : c + LANES] = one_hot(index, (wanted - c).astype(jnp.int16))


def potentials(g, phi_ref, first_ref, second_ref, tables, work_a, work_b, emit, last=PAIRS):
    forward, last_backward, left_forward, left_backward = [ref[...].astype(BF16) for ref in tables[:4]]
    coulomb_ref = tables[4]
    half = g // 2
    for start in range(0, half, PAIRS):
        rows = slab_rows(start, g, PAIRS)
        phi = phi_ref[rows, :]
        lower, upper = regrouped(phi * first_ref[rows, :], phi * second_ref[rows, :])
        spectrum = right(jnp.concatenate([lower, upper], 0), forward)
        for k in range(PAIRS):
            a, b = left_complex(left_forward, *(spectrum[j * g : (j + 1) * g] for j in (k, k + PAIRS)))
            store(work_a, start + k, [a])
            store(work_a, start + k + half, [b])

    for kx in range(0, g, 2):
        slabs = left_complex(left_forward, strided(work_a, kx, g), strided(work_a, kx + 1, g))
        slabs = [slab * coulomb_ref[slab_rows(kx + j, g), :] for j, slab in enumerate(slabs)]
        store(work_b, kx, left_complex(left_backward, *slabs))

    for start in range(0, half, last):
        lower, upper = [], []
        for z in range(start, start + last):
            a, b = left_complex(left_backward, strided(work_b, z, g), strided(work_b, z + half, g))
            lower.append(a)
            upper.append(b)
        out = right(jnp.concatenate(lower + upper, 0), last_backward)
        emit(start, *regrouped(out[: last * g], out[last * g :]))


def near_kernel(g, phi_ref, other_ref, *refs):
    tables, (sum_ref, work_a, work_b) = refs[:5], refs[5:]

    def emit(start, own, other):
        rows = slab_rows(start, g, PAIRS)
        sum_ref[rows, :] = own * phi_ref[rows, :] + other * other_ref[rows, :]

    potentials(g, phi_ref, phi_ref, other_ref, tables, work_a, work_b, emit)


def middle_kernel(g, phi_ref, first_ref, second_ref, before_ref, *refs):
    tables, (sum_ref, work_a, work_b) = refs[:5], refs[5:]

    def emit(start, first, second):
        rows = slab_rows(start, g, PAIRS)
        sum_ref[rows, :] = before_ref[rows, :] + first * first_ref[rows, :] + second * second_ref[rows, :]

    potentials(g, phi_ref, first_ref, second_ref, tables, work_a, work_b, emit)


def far_kernel(g, weights, phi_ref, first_ref, second_ref, before_ref, hot_ref, last_hot_ref, stick_out_ref, *refs):
    tables, out_refs = refs[:5], refs[5:-3]
    work_a, work_b, picked_ref = refs[-3:]
    forward = tables[2][...].astype(BF16)
    half = g // 2

    def emit(start, first, second):
        rows = slab_rows(start, g, half)
        total = before_ref[rows, :] + weights[0] * (first * first_ref[rows, :])
        total = total + weights[1] * (second * second_ref[rows, :])
        for k in range(0, half, 2):
            cos, sin = left(forward, beside(total[k * g : (k + 1) * g], total[(k + 1) * g : (k + 2) * g]))
            for j, (real, imag) in enumerate(zip(halves(cos), halves(sin))):
                lower, upper = regrouped(real, imag)
                store(work_a, start + k + j, [lower])
                store(work_a, start + k + j + half, [upper])

    potentials(g, phi_ref, first_ref, second_ref, tables, work_a, work_b, emit, half)

    step = g // 3
    for first in range(0, g, step):
        slabs = []
        for kx in range(first, first + step, 2):
            slabs += left_complex(forward, strided(work_a, kx, g), strided(work_a, kx + 1, g))
        spectrum = beside(*split(jnp.concatenate(slabs, 0)))
        start = 0
        for ref in (hot_ref, last_hot_ref):
            both = dot(ref[:, first * g : (first + step) * g], spectrum)
            both = both[:, :LANES] + both[:, LANES:]
            rows = slice(start, start + ref.shape[0])
            picked_ref[rows, :] = both if first == 0 else picked_ref[rows, :] + both
            start += ref.shape[0]

    stick_out = stick_out_ref[...].astype(BF16)
    for k in range(0, len(out_refs), 2):
        high, low = split(picked_ref[k * LANES : (k + 2) * LANES, :])
        lined = jnp.concatenate([high, low, high], 1)
        out = lax.dot_general(stick_out, lined, (((1,), (1,)), ((), ())), preferred_element_type=F32)
        out_refs[k][...], out_refs[k + 1][...] = halves(out)


def call(kernel, out_shapes, scratch, flops, *operands, space=pltpu.VMEM, out_space=pltpu.VMEM, grant=40):
    out_spec = pl.BlockSpec(memory_space=out_space)
    return pl.pallas_call(
        kernel,
        out_shape=out_shapes,
        in_specs=[pl.BlockSpec(memory_space=space)] * len(operands),
        out_specs=jax.tree.map(lambda _: out_spec, out_shapes),
        scratch_shapes=scratch,
        compiler_params=pltpu.CompilerParams(vmem_limit_bytes=grant * 2**20),
        cost_estimate=pl.CostEstimate(flops=flops, bytes_accessed=flops, transcendentals=0),
    )(*operands)


def after(x, *others):
    return lax.optimization_barrier((x, *others))[0]


def exchanged(blocks, order, before):
    owners = len(blocks)
    moved = [blocks[0]] + [None] * (owners - 1)
    for d in order:
        others = [moved[x] if isinstance(x, int) else x for x in before.get(d, ())]
        block = after(blocks[d], *others) if others else blocks[d]
        moved[d] = lax.ppermute(block, "stick", [(i, i ^ d) for i in range(owners)])
    return moved


def on_device(sticks, stick_columns):
    g = sticks.shape[1] // 2
    slots = stick_columns.shape[0]
    owners = lax.axis_size("stick")
    groups = lax.axis_size("band")
    t = {name: jnp.asarray(value) for name, value in make_tables(g).items()}
    rows = g * g
    field = jax.ShapeDtypeStruct((rows // 2, LANES), F32)
    work = pltpu.VMEM((rows, LANES), F32)
    pot_flops = 1

    def shifted(x, distance):
        return lax.ppermute(x, "band", [(i, (i - distance) % groups) for i in range(groups)])

    def swapped(x):
        return lax.ppermute(x, "band", [(i, i ^ 1) for i in range(groups)])

    sent = call(
        functools.partial(send_kernel, g),
        [jax.ShapeDtypeStruct((2 * g + 8, slots), F32)] * owners,
        [
            pltpu.VMEM((1, slots), jnp.int32),
            pltpu.SemaphoreType.DMA((owners,)),
            pltpu.SemaphoreType.DMA,
        ],
        1,
        sticks,
        stick_columns[None, :],
        space=pltpu.HBM,
        grant=SEND_GRANT,
    )
    shapes = [(2 * g + 8, slots), (LANES, 6 * g), (2 * g, 3 * g)]
    staged, *first_tables = call(
        functools.partial(early_kernel, g),
        [jax.ShapeDtypeStruct(shape, kind) for shape, kind in zip(shapes, (F32, BF16, BF16))],
        [],
        1,
        sent[0],
        after(t["early"], sent[0]),
    )
    half = owners // 2
    distant, close = list(range(half, owners)), list(range(1, half))
    mixed = [distant[0]] + [d for pair in zip(close, distant[1:]) for d in pair]
    before = {mixed[k]: (mixed[k - 3 - k % 2],) for k in range(WINDOW, len(mixed))}
    last = mixed[WINDOW]
    received = exchanged(sent, mixed, {**before, last: (*before[last], staged, *first_tables)})
    received[0] = staged
    cut = owners * 3 // 4
    order = [0] + mixed
    order = order[:cut] + order[:cut - 1:-1]
    stick_in, left_table = first_tables

    def relayed(part):
        shapes = [(len(part) * 2 * g, slots), (8, len(part) * slots)]
        shapes = [jax.ShapeDtypeStruct(shape, F32) for shape in shapes]
        return call(functools.partial(relay_kernel, g), shapes, [], 1, *[received[d] for d in part])

    def on_grid(blocks, flops=1):
        grid = jax.ShapeDtypeStruct((rows, LANES), F32)
        return call(functools.partial(place_sticks_kernel, g), grid, [], flops, blocks, columns[0], stick_in)

    def orbital(grid, rest):
        operands = (grid, rest, columns[1], stick_in, left_table)
        return call(functools.partial(field_kernel, g), field, [work], 1, *operands)

    first_blocks, first_columns = relayed(order[:cut])
    columns = [first_columns]
    own_grid = on_grid(first_blocks, 5 * 10**9)

    def hot_rows(columns):
        shape = jax.ShapeDtypeStruct((columns.shape[1], rows), BF16)
        return call(functools.partial(pick_kernel, g), shape, [], 1, columns)

    hot = [hot_rows(first_columns)]
    received[order[cut]] = after(received[order[cut]], own_grid, *hot)
    last_blocks, last_columns = relayed(order[cut:])
    columns.append(last_columns)
    hot.append(hot_rows(last_columns))
    phi = orbital(own_grid, last_blocks)
    near = swapped(phi)
    pot_tables = [t["forward"], t["last_backward"], t["left_forward"], t["left_backward"], t["coulomb"]]

    def potential_sum(kernel, *operands):
        return call(functools.partial(kernel, g), field, [work, work], pot_flops, phi, *operands, *pot_tables)

    distances = (HALF,) if groups == 2 * HALF else (HALF, -HALF)
    fields = [orbital(on_grid(shifted(first_blocks, d)), shifted(last_blocks, d)) for d in distances]
    total = potential_sum(near_kernel, after(near, *fields))
    if groups == 2 * HALF:
        weights = (2.0, 1.0)
        first, second = fields[0], swapped(fields[0])
    else:
        weights = (1.0, 0.0)
        odd = lax.axis_index("band") % 2 == 1
        first = second = swapped(jnp.where(odd, fields[1], fields[0]))
        total = potential_sum(middle_kernel, *fields, total)
    result = call(
        functools.partial(far_kernel, g, weights),
        [jax.ShapeDtypeStruct((2 * g, slots), F32)] * owners,
        [work, work, pltpu.VMEM((owners * slots, LANES), F32)],
        pot_flops,
        phi,
        first,
        second,
        total,
        *hot,
        t["stick_out"],
        *pot_tables,
    )
    result = [result[order.index(d)] for d in range(owners)]
    result = exchanged(result, mixed, before)
    out_order = [0] + distant + close
    return call(
        functools.partial(place_kernel, out_order),
        jax.ShapeDtypeStruct(sticks.shape, F32),
        [],
        1,
        *[result[d] for d in out_order],
    )


def solution(mesh):
    return jax.shard_map(
        on_device,
        mesh=mesh,
        in_specs=(P("band", None, "stick"), P("stick")),
        out_specs=P("band", None, "stick"),
        check_vma=False,
    )
```

```python
import functools
import math

import jax
import jax.numpy as jnp
import numpy as np
from jax import lax
from jax.experimental import pallas as pl
from jax.experimental.pallas import tpu as pltpu
from jax.sharding import PartitionSpec as P

HALF = 2
BOX_LENGTH = 18.0
LANES = 128
MID = 64
WINDOW = 5
SEND_GRANT = 60
PAIRS = 6

F32 = jnp.float32
BF16 = jnp.bfloat16


def rounded_parts(table):
    high = table.astype(BF16).astype(np.float64)
    low = (table - high).astype(BF16).astype(np.float64)
    return high, low


def across(table):
    high, low = rounded_parts(table)
    return np.concatenate([high, high, low], 1).astype(np.float32)


def down(table):
    high, low = rounded_parts(table)
    return np.block([[high, low], [high, np.zeros_like(low)]]).astype(np.float32)


def make_tables(g):
    angle = 2.0 * np.pi / g * (np.outer(np.arange(g), np.arange(g)) % g)
    c, s = np.cos(angle), np.sin(angle)
    lower, upper = slice(0, g), slice(MID, MID + g)

    forward, backward = np.zeros((2, LANES, LANES))
    forward[lower, lower], forward[lower, upper] = c, -s
    forward[upper, lower], forward[upper, upper] = s, c
    backward[lower, lower], backward[lower, upper] = c, s
    backward[upper, lower], backward[upper, upper] = -s, c
    stick_in = np.zeros((LANES, 2 * g))
    stick_in[lower, :g], stick_in[lower, g:] = c, -s
    stick_in[upper, :g], stick_in[upper, g:] = s, c
    stick_out = np.zeros((2 * g, LANES))
    stick_out[:g, lower], stick_out[:g, upper] = c, s
    stick_out[g:, lower], stick_out[g:, upper] = -s, c

    freq = np.arange(g)
    square = np.minimum(freq, g - freq) ** 2
    total = square[:, None, None] + square[None, :, None] + square[None, None, :]
    unit = (2.0 * math.pi / BOX_LENGTH) ** 2
    kernel = np.where(total > 0, 4.0 * math.pi / (unit * np.maximum(total, 1)), 0.0)
    coulomb = np.zeros((g, g, LANES), np.float32)
    coulomb[:, :, lower] = kernel
    coulomb[:, :, upper] = kernel
    stick_in, left_backward = across(stick_in), across(np.concatenate([c, s], 0))
    early = np.zeros((LANES + 2 * g, stick_in.shape[1]), np.float32)
    early[:LANES], early[LANES:, : left_backward.shape[1]] = stick_in, left_backward
    return dict(
        forward=down(forward),
        last_backward=down(backward / g**3),
        left_forward=across(np.concatenate([c, -s], 0)),
        left_backward=left_backward,
        early=early,
        stick_out=across(stick_out * g**-1.5),
        coulomb=coulomb.reshape(g * g, LANES),
    )


def split(x):
    high = x.astype(BF16)
    low = (x - high.astype(F32)).astype(BF16)
    return high, low


def stacked(x):
    high, low = split(x)
    return jnp.concatenate([high, low, high], 0)


def dot(a, b):
    return jnp.dot(a, b, preferred_element_type=F32)


def lane_halves(shape):
    return lax.broadcasted_iota(jnp.int32, shape, 1) % LANES < MID


def turned(x):
    return pltpu.roll(x, MID, 1)


def regrouped(a, b):
    low = lane_halves(a.shape)
    return jnp.where(low, a, turned(b)), jnp.where(low, turned(a), b)


def beside(a, b):
    return jnp.concatenate([a, b], 1)


def halves(x):
    return x[:, :LANES], x[:, LANES:]


def left(table, x):
    both = dot(table, stacked(x))
    g = both.shape[0] // 2
    return both[:g], both[g:]


def left_complex(table, a, b):
    cos, sin = left(table, beside(a, b))
    sign = jnp.where(lane_halves((1, LANES)), -1.0, 1.0)
    return [p + turned(q) * sign for p, q in zip(halves(cos), halves(sin))]


def right(x, table):
    both = dot(beside(*split(x)), table)
    width = both.shape[1] // 2
    return both[:, :width] + both[:, width:]


def strided(ref, first, g):
    return ref[pl.ds(first, g, stride=g), :]


def slab_rows(index, g, count=1):
    return pl.ds(index * g, count * g)


def one_hot(index, wanted):
    return jnp.where(index == wanted, jnp.asarray(1, BF16), jnp.asarray(0, BF16))


def send_kernel(g, sticks_ref, columns_ref, *refs):
    block_refs, (row_ref, sems, row_sem) = refs[:-3], refs[-3:]
    own = lax.axis_index("stick")
    row_copy = pltpu.make_async_copy(columns_ref, row_ref, row_sem)
    row_copy.start()
    copies = [
        pltpu.make_async_copy(sticks_ref.at[own ^ d], ref.at[pl.ds(0, 2 * g)], sems.at[d])
        for d, ref in enumerate(block_refs)
    ]
    for copy in copies:
        copy.start()
    row_copy.wait()
    columns = jnp.broadcast_to(row_ref[...].astype(F32), (8, LANES))
    for ref in block_refs:
        ref[2 * g :, :] = columns
    for copy in copies:
        copy.wait()


def early_kernel(g, own_ref, tables_ref, staged_ref, stick_in_ref, left_ref):
    staged_ref[...] = own_ref[...]
    stick_in_ref[...] = tables_ref[:LANES, : stick_in_ref.shape[1]].astype(BF16)
    left_ref[...] = tables_ref[LANES:, : left_ref.shape[1]].astype(BF16)


def place_kernel(order, *refs):
    own = lax.axis_index("stick")
    out_ref = refs[-1]
    for d, block_ref in zip(order, refs[:-1]):
        out_ref[own ^ d] = block_ref[...]


def store(ref, first, slabs):
    g = slabs[0].shape[0]
    for k, slab in enumerate(slabs):
        ref[slab_rows(first + k, g), :] = slab


def relay_kernel(g, *refs):
    blocks, (coefficients_ref, columns_ref) = refs[:-2], refs[-2:]
    for k, ref in enumerate(blocks):
        coefficients_ref[k * 2 * g : (k + 1) * 2 * g, :] = ref[: 2 * g, :]
        columns_ref[:, k * LANES : (k + 1) * LANES] = ref[2 * g :, :]


def placed(g, blocks_ref, columns_ref, stick_in_ref):
    columns = columns_ref[:1, :].astype(jnp.int32)
    stick_in = stick_in_ref[...]
    blocks = [blocks_ref[k : k + 2 * g, :] for k in range(0, blocks_ref.shape[0], 2 * g)]
    sticks = []
    for k in range(0, len(blocks), 2):
        sticks.append(beside(*split(dot(stick_in, stacked(beside(blocks[k], blocks[k + 1]))).T)))
    sticks = jnp.concatenate(sticks, 0)
    rows = g * g // 2
    index = lax.broadcasted_iota(jnp.int16, (rows, columns.shape[1]), 0)
    for first in (0, rows):
        both = dot(one_hot(index, (columns - first).astype(jnp.int16)), sticks)
        yield first, both[:, :LANES] + both[:, LANES:]


def place_sticks_kernel(g, blocks_ref, columns_ref, stick_in_ref, grid_ref):
    for first, part in placed(g, blocks_ref, columns_ref, stick_in_ref):
        grid_ref[first : first + part.shape[0], :] = part


def field_kernel(g, grid_ref, blocks_ref, columns_ref, stick_in_ref, left_ref, phi_ref, work_a):
    backward = left_ref[...]
    half = g // 2
    for first, part in placed(g, blocks_ref, columns_ref, stick_in_ref):
        part = part + grid_ref[first : first + part.shape[0], :]
        for k in range(0, half, 2):
            slabs = left_complex(backward, part[k * g : (k + 1) * g], part[(k + 1) * g : (k + 2) * g])
            store(work_a, first // g + k, slabs)

    for y in range(half):
        x = beside(strided(work_a, y, g), strided(work_a, y + half, g))
        (cos, cos_up), (sin, sin_up) = map(halves, left(backward, x))
        low = lane_halves(cos.shape)
        store(phi_ref, y, [jnp.where(low, cos - turned(sin), turned(cos_up) - sin_up)])


def pick_kernel(g, columns_ref, hot_ref):
    for k in range(0, columns_ref.shape[1], LANES):
        block = columns_ref[:, k : k + LANES]
        wanted = jnp.concatenate([block] * (LANES // block.shape[0]), 0).T.astype(jnp.int32)
        for c in range(0, hot_ref.shape[1], LANES):
            index = lax.broadcasted_iota(jnp.int16, (LANES, LANES), 1)
            hot_ref[k : k + LANES, c : c + LANES] = one_hot(index, (wanted - c).astype(jnp.int16))


def potentials(g, phi_ref, first_ref, second_ref, tables, work_a, work_b, emit, last=PAIRS):
    forward, last_backward, left_forward, left_backward = [ref[...].astype(BF16) for ref in tables[:4]]
    coulomb_ref = tables[4]
    half = g // 2
    for start in range(0, half, PAIRS):
        rows = slab_rows(start, g, PAIRS)
        phi = phi_ref[rows, :]
        lower, upper = regrouped(phi * first_ref[rows, :], phi * second_ref[rows, :])
        spectrum = right(jnp.concatenate([lower, upper], 0), forward)
        for k in range(PAIRS):
            a, b = left_complex(left_forward, *(spectrum[j * g : (j + 1) * g] for j in (k, k + PAIRS)))
            store(work_a, start + k, [a])
            store(work_a, start + k + half, [b])

    for kx in range(0, g, 2):
        slabs = left_complex(left_forward, strided(work_a, kx, g), strided(work_a, kx + 1, g))
        slabs = [slab * coulomb_ref[slab_rows(kx + j, g), :] for j, slab in enumerate(slabs)]
        store(work_b, kx, left_complex(left_backward, *slabs))

    for start in range(0, half, last):
        lower, upper = [], []
        for z in range(start, start + last):
            a, b = left_complex(left_backward, strided(work_b, z, g), strided(work_b, z + half, g))
            lower.append(a)
            upper.append(b)
        out = right(jnp.concatenate(lower + upper, 0), last_backward)
        emit(start, *regrouped(out[: last * g], out[last * g :]))


def near_kernel(g, phi_ref, other_ref, *refs):
    tables, (sum_ref, work_a, work_b) = refs[:5], refs[5:]

    def emit(start, own, other):
        rows = slab_rows(start, g, PAIRS)
        sum_ref[rows, :] = own * phi_ref[rows, :] + other * other_ref[rows, :]

    potentials(g, phi_ref, phi_ref, other_ref, tables, work_a, work_b, emit)


def middle_kernel(g, phi_ref, first_ref, second_ref, before_ref, *refs):
    tables, (sum_ref, work_a, work_b) = refs[:5], refs[5:]

    def emit(start, first, second):
        rows = slab_rows(start, g, PAIRS)
        sum_ref[rows, :] = before_ref[rows, :] + first * first_ref[rows, :] + second * second_ref[rows, :]

    potentials(g, phi_ref, first_ref, second_ref, tables, work_a, work_b, emit)


def far_kernel(g, weights, phi_ref, first_ref, second_ref, before_ref, hot_ref, last_hot_ref, stick_out_ref, *refs):
    tables, out_refs = refs[:5], refs[5:-3]
    work_a, work_b, picked_ref = refs[-3:]
    forward = tables[2][...].astype(BF16)
    half = g // 2

    def emit(start, first, second):
        rows = slab_rows(start, g, half)
        total = before_ref[rows, :] + weights[0] * (first * first_ref[rows, :])
        total = total + weights[1] * (second * second_ref[rows, :])
        for k in range(0, half, 2):
            cos, sin = left(forward, beside(total[k * g : (k + 1) * g], total[(k + 1) * g : (k + 2) * g]))
            for j, (real, imag) in enumerate(zip(halves(cos), halves(sin))):
                lower, upper = regrouped(real, imag)
                store(work_a, start + k + j, [lower])
                store(work_a, start + k + j + half, [upper])

    potentials(g, phi_ref, first_ref, second_ref, tables, work_a, work_b, emit, half)

    step = g // 3
    for first in range(0, g, step):
        slabs = []
        for kx in range(first, first + step, 2):
            slabs += left_complex(forward, strided(work_a, kx, g), strided(work_a, kx + 1, g))
        spectrum = beside(*split(jnp.concatenate(slabs, 0)))
        start = 0
        for ref in (hot_ref, last_hot_ref):
            both = dot(ref[:, first * g : (first + step) * g], spectrum)
            both = both[:, :LANES] + both[:, LANES:]
            rows = slice(start, start + ref.shape[0])
            picked_ref[rows, :] = both if first == 0 else picked_ref[rows, :] + both
            start += ref.shape[0]

    stick_out = stick_out_ref[...].astype(BF16)
    for k in range(0, len(out_refs), 2):
        high, low = split(picked_ref[k * LANES : (k + 2) * LANES, :])
        lined = jnp.concatenate([high, low, high], 1)
        out = lax.dot_general(stick_out, lined, (((1,), (1,)), ((), ())), preferred_element_type=F32)
        out_refs[k][...], out_refs[k + 1][...] = halves(out)


def call(kernel, out_shapes, scratch, flops, *operands, space=pltpu.VMEM, out_space=pltpu.VMEM, grant=40):
    out_spec = pl.BlockSpec(memory_space=out_space)
    return pl.pallas_call(
        kernel,
        out_shape=out_shapes,
        in_specs=[pl.BlockSpec(memory_space=space)] * len(operands),
        out_specs=jax.tree.map(lambda _: out_spec, out_shapes),
        scratch_shapes=scratch,
        compiler_params=pltpu.CompilerParams(vmem_limit_bytes=grant * 2**20),
        cost_estimate=pl.CostEstimate(flops=flops, bytes_accessed=flops, transcendentals=0),
    )(*operands)


def after(x, *others):
    return lax.optimization_barrier((x, *others))[0]


def exchanged(blocks, order, before):
    owners = len(blocks)
    moved = [blocks[0]] + [None] * (owners - 1)
    for d in order:
        others = [moved[x] if isinstance(x, int) else x for x in before.get(d, ())]
        block = after(blocks[d], *others) if others else blocks[d]
        moved[d] = lax.ppermute(block, "stick", [(i, i ^ d) for i in range(owners)])
    return moved


def on_device(sticks, stick_columns):
    g = sticks.shape[1] // 2
    slots = stick_columns.shape[0]
    owners = lax.axis_size("stick")
    groups = lax.axis_size("band")
    t = {name: jnp.asarray(value) for name, value in make_tables(g).items()}
    rows = g * g
    field = jax.ShapeDtypeStruct((rows // 2, LANES), F32)
    work = pltpu.VMEM((rows, LANES), F32)
    pot_flops = 1

    def shifted(x, distance):
        return lax.ppermute(x, "band", [(i, (i - distance) % groups) for i in range(groups)])

    def swapped(x):
        return lax.ppermute(x, "band", [(i, i ^ 1) for i in range(groups)])

    sent = call(
        functools.partial(send_kernel, g),
        [jax.ShapeDtypeStruct((2 * g + 8, slots), F32)] * owners,
        [
            pltpu.VMEM((1, slots), jnp.int32),
            pltpu.SemaphoreType.DMA((owners,)),
            pltpu.SemaphoreType.DMA,
        ],
        1,
        sticks,
        stick_columns[None, :],
        space=pltpu.HBM,
        grant=SEND_GRANT,
    )
    shapes = [(2 * g + 8, slots), (LANES, 6 * g), (2 * g, 3 * g)]
    staged, *first_tables = call(
        functools.partial(early_kernel, g),
        [jax.ShapeDtypeStruct(shape, kind) for shape, kind in zip(shapes, (F32, BF16, BF16))],
        [],
        1,
        sent[0],
        after(t["early"], sent[0]),
    )
    half = owners // 2
    distant, close = list(range(half, owners)), list(range(1, half))
    mixed = [distant[0]] + [d for pair in zip(close, distant[1:]) for d in pair]
    before = {mixed[k]: (mixed[k - 3 - k % 2],) for k in range(WINDOW, len(mixed))}
    last = mixed[WINDOW]
    received = exchanged(sent, mixed, {d: (half, staged, *first_tables) if d == last else (half,) for d in before})
    received[0] = staged
    cut = owners * 3 // 4
    order = [0] + mixed
    order = order[:cut] + order[:cut - 1:-1]
    stick_in, left_table = first_tables

    def relayed(part):
        shapes = [(len(part) * 2 * g, slots), (8, len(part) * slots)]
        shapes = [jax.ShapeDtypeStruct(shape, F32) for shape in shapes]
        return call(functools.partial(relay_kernel, g), shapes, [], 1, *[received[d] for d in part])

    def on_grid(blocks, flops=1):
        grid = jax.ShapeDtypeStruct((rows, LANES), F32)
        return call(functools.partial(place_sticks_kernel, g), grid, [], flops, blocks, columns[0], stick_in)

    def orbital(grid, rest):
        operands = (grid, rest, columns[1], stick_in, left_table)
        return call(functools.partial(field_kernel, g), field, [work], 1, *operands)

    first_blocks, first_columns = relayed(order[:cut])
    columns = [first_columns]
    own_grid = on_grid(first_blocks, 5 * 10**9)

    def hot_rows(columns):
        shape = jax.ShapeDtypeStruct((columns.shape[1], rows), BF16)
        return call(functools.partial(pick_kernel, g), shape, [], 1, columns)

    hot = [hot_rows(first_columns)]
    received[order[cut]] = after(received[order[cut]], own_grid, *hot)
    last_blocks, last_columns = relayed(order[cut:])
    columns.append(last_columns)
    hot.append(hot_rows(last_columns))
    phi = orbital(own_grid, last_blocks)
    near = swapped(phi)
    pot_tables = [t["forward"], t["last_backward"], t["left_forward"], t["left_backward"], t["coulomb"]]

    def potential_sum(kernel, *operands):
        return call(functools.partial(kernel, g), field, [work, work], pot_flops, phi, *operands, *pot_tables)

    distances = (HALF,) if groups == 2 * HALF else (HALF, -HALF)
    fields = [orbital(on_grid(shifted(first_blocks, d)), shifted(last_blocks, d)) for d in distances]
    total = potential_sum(near_kernel, after(near, *fields))
    if groups == 2 * HALF:
        weights = (2.0, 1.0)
        first, second = fields[0], swapped(fields[0])
    else:
        weights = (1.0, 0.0)
        odd = lax.axis_index("band") % 2 == 1
        first = second = swapped(jnp.where(odd, fields[1], fields[0]))
        total = potential_sum(middle_kernel, *fields, total)
    result = call(
        functools.partial(far_kernel, g, weights),
        [jax.ShapeDtypeStruct((2 * g, slots), F32)] * owners,
        [work, work, pltpu.VMEM((owners * slots, LANES), F32)],
        pot_flops,
        phi,
        first,
        second,
        total,
        *hot,
        t["stick_out"],
        *pot_tables,
    )
    result = [result[order.index(d)] for d in range(owners)]
    result = exchanged(result, mixed, {d: (half,) for d in before})
    out_order = [0] + mixed
    return call(
        functools.partial(place_kernel, out_order),
        jax.ShapeDtypeStruct(sticks.shape, F32),
        [],
        1,
        *[result[d] for d in out_order],
    )


def solution(mesh):
    return jax.shard_map(
        on_device,
        mesh=mesh,
        in_specs=(P("band", None, "stick"), P("stick")),
        out_specs=P("band", None, "stick"),
        check_vma=False,
    )
```

```python
import functools
import math

import jax
import jax.numpy as jnp
import numpy as np
from jax import lax
from jax.experimental import pallas as pl
from jax.experimental.pallas import tpu as pltpu
from jax.sharding import PartitionSpec as P

HALF = 2
BOX_LENGTH = 18.0
LANES = 128
MID = 64
WINDOW = 5
SEND_GRANT = 60
PAIRS = 6

F32 = jnp.float32
BF16 = jnp.bfloat16


def rounded_parts(table):
    high = table.astype(BF16).astype(np.float64)
    low = (table - high).astype(BF16).astype(np.float64)
    return high, low


def across(table):
    high, low = rounded_parts(table)
    return np.concatenate([high, high, low], 1).astype(np.float32)


def down(table):
    high, low = rounded_parts(table)
    return np.block([[high, low], [high, np.zeros_like(low)]]).astype(np.float32)


def make_tables(g):
    angle = 2.0 * np.pi / g * (np.outer(np.arange(g), np.arange(g)) % g)
    c, s = np.cos(angle), np.sin(angle)
    lower, upper = slice(0, g), slice(MID, MID + g)

    forward, backward = np.zeros((2, LANES, LANES))
    forward[lower, lower], forward[lower, upper] = c, -s
    forward[upper, lower], forward[upper, upper] = s, c
    backward[lower, lower], backward[lower, upper] = c, s
    backward[upper, lower], backward[upper, upper] = -s, c
    stick_in = np.zeros((LANES, 2 * g))
    stick_in[lower, :g], stick_in[lower, g:] = c, -s
    stick_in[upper, :g], stick_in[upper, g:] = s, c
    stick_out = np.zeros((2 * g, LANES))
    stick_out[:g, lower], stick_out[:g, upper] = c, s
    stick_out[g:, lower], stick_out[g:, upper] = -s, c

    freq = np.arange(g)
    square = np.minimum(freq, g - freq) ** 2
    total = square[:, None, None] + square[None, :, None] + square[None, None, :]
    unit = (2.0 * math.pi / BOX_LENGTH) ** 2
    kernel = np.where(total > 0, 4.0 * math.pi / (unit * np.maximum(total, 1)), 0.0)
    coulomb = np.zeros((g, g, LANES), np.float32)
    coulomb[:, :, lower] = kernel
    coulomb[:, :, upper] = kernel
    stick_in, left_backward = across(stick_in), across(np.concatenate([c, s], 0))
    early = np.zeros((LANES + 2 * g, stick_in.shape[1]), np.float32)
    early[:LANES], early[LANES:, : left_backward.shape[1]] = stick_in, left_backward
    return dict(
        forward=down(forward),
        last_backward=down(backward / g**3),
        left_forward=across(np.concatenate([c, -s], 0)),
        left_backward=left_backward,
        early=early,
        stick_out=across(stick_out * g**-1.5),
        coulomb=coulomb.reshape(g * g, LANES),
    )


def split(x):
    high = x.astype(BF16)
    low = (x - high.astype(F32)).astype(BF16)
    return high, low


def stacked(x):
    high, low = split(x)
    return jnp.concatenate([high, low, high], 0)


def dot(a, b):
    return jnp.dot(a, b, preferred_element_type=F32)


def lane_halves(shape):
    return lax.broadcasted_iota(jnp.int32, shape, 1) % LANES < MID


def turned(x):
    return pltpu.roll(x, MID, 1)


def regrouped(a, b):
    low = lane_halves(a.shape)
    return jnp.where(low, a, turned(b)), jnp.where(low, turned(a), b)


def beside(a, b):
    return jnp.concatenate([a, b], 1)


def halves(x):
    return x[:, :LANES], x[:, LANES:]


def left(table, x):
    both = dot(table, stacked(x))
    g = both.shape[0] // 2
    return both[:g], both[g:]


def left_complex(table, a, b):
    cos, sin = left(table, beside(a, b))
    sign = jnp.where(lane_halves((1, LANES)), -1.0, 1.0)
    return [p + turned(q) * sign for p, q in zip(halves(cos), halves(sin))]


def right(x, table):
    both = dot(beside(*split(x)), table)
    width = both.shape[1] // 2
    return both[:, :width] + both[:, width:]


def strided(ref, first, g):
    return ref[pl.ds(first, g, stride=g), :]


def slab_rows(index, g, count=1):
    return pl.ds(index * g, count * g)


def one_hot(index, wanted):
    return jnp.where(index == wanted, jnp.asarray(1, BF16), jnp.asarray(0, BF16))


def send_kernel(g, sticks_ref, columns_ref, *refs):
    block_refs, (row_ref, sems, row_sem) = refs[:-3], refs[-3:]
    own = lax.axis_index("stick")
    row_copy = pltpu.make_async_copy(columns_ref, row_ref, row_sem)
    row_copy.start()
    copies = [
        pltpu.make_async_copy(sticks_ref.at[own ^ d], ref.at[pl.ds(0, 2 * g)], sems.at[d])
        for d, ref in enumerate(block_refs)
    ]
    for copy in copies:
        copy.start()
    row_copy.wait()
    columns = jnp.broadcast_to(row_ref[...].astype(F32), (8, LANES))
    for ref in block_refs:
        ref[2 * g :, :] = columns
    for copy in copies:
        copy.wait()


def early_kernel(g, own_ref, tables_ref, staged_ref, stick_in_ref, left_ref):
    staged_ref[...] = own_ref[...]
    stick_in_ref[...] = tables_ref[:LANES, : stick_in_ref.shape[1]].astype(BF16)
    left_ref[...] = tables_ref[LANES:, : left_ref.shape[1]].astype(BF16)


def place_kernel(order, *refs):
    own = lax.axis_index("stick")
    block_refs, (out_ref, sems) = refs[:-2], refs[-2:]
    copies = [
        pltpu.make_async_copy(ref, out_ref.at[own ^ d], sems.at[k]) for k, (d, ref) in enumerate(zip(order, block_refs))
    ]
    for copy in copies:
        copy.start()
    for copy in copies:
        copy.wait()


def store(ref, first, slabs):
    g = slabs[0].shape[0]
    for k, slab in enumerate(slabs):
        ref[slab_rows(first + k, g), :] = slab


def relay_kernel(g, *refs):
    blocks, (coefficients_ref, columns_ref) = refs[:-2], refs[-2:]
    for k, ref in enumerate(blocks):
        coefficients_ref[k * 2 * g : (k + 1) * 2 * g, :] = ref[: 2 * g, :]
        columns_ref[:, k * LANES : (k + 1) * LANES] = ref[2 * g :, :]


def placed(g, blocks_ref, columns_ref, stick_in_ref):
    columns = columns_ref[:1, :].astype(jnp.int32)
    stick_in = stick_in_ref[...]
    blocks = [blocks_ref[k : k + 2 * g, :] for k in range(0, blocks_ref.shape[0], 2 * g)]
    sticks = []
    for k in range(0, len(blocks), 2):
        sticks.append(beside(*split(dot(stick_in, stacked(beside(blocks[k], blocks[k + 1]))).T)))
    sticks = jnp.concatenate(sticks, 0)
    rows = g * g // 2
    index = lax.broadcasted_iota(jnp.int16, (rows, columns.shape[1]), 0)
    for first in (0, rows):
        both = dot(one_hot(index, (columns - first).astype(jnp.int16)), sticks)
        yield first, both[:, :LANES] + both[:, LANES:]


def place_sticks_kernel(g, blocks_ref, columns_ref, stick_in_ref, grid_ref):
    for first, part in placed(g, blocks_ref, columns_ref, stick_in_ref):
        grid_ref[first : first + part.shape[0], :] = part


def field_kernel(g, grid_ref, blocks_ref, columns_ref, stick_in_ref, left_ref, phi_ref, work_a):
    backward = left_ref[...]
    half = g // 2
    for first, part in placed(g, blocks_ref, columns_ref, stick_in_ref):
        part = part + grid_ref[first : first + part.shape[0], :]
        for k in range(0, half, 2):
            slabs = left_complex(backward, part[k * g : (k + 1) * g], part[(k + 1) * g : (k + 2) * g])
            store(work_a, first // g + k, slabs)

    for y in range(half):
        x = beside(strided(work_a, y, g), strided(work_a, y + half, g))
        (cos, cos_up), (sin, sin_up) = map(halves, left(backward, x))
        low = lane_halves(cos.shape)
        store(phi_ref, y, [jnp.where(low, cos - turned(sin), turned(cos_up) - sin_up)])


def pick_kernel(g, columns_ref, hot_ref):
    for k in range(0, columns_ref.shape[1], LANES):
        block = columns_ref[:, k : k + LANES]
        wanted = jnp.concatenate([block] * (LANES // block.shape[0]), 0).T.astype(jnp.int32)
        for c in range(0, hot_ref.shape[1], LANES):
            index = lax.broadcasted_iota(jnp.int16, (LANES, LANES), 1)
            hot_ref[k : k + LANES, c : c + LANES] = one_hot(index, (wanted - c).astype(jnp.int16))


def potentials(g, phi_ref, first_ref, second_ref, tables, work_a, work_b, emit, last=PAIRS):
    forward, last_backward, left_forward, left_backward = [ref[...].astype(BF16) for ref in tables[:4]]
    coulomb_ref = tables[4]
    half = g // 2
    for start in range(0, half, PAIRS):
        rows = slab_rows(start, g, PAIRS)
        phi = phi_ref[rows, :]
        lower, upper = regrouped(phi * first_ref[rows, :], phi * second_ref[rows, :])
        spectrum = right(jnp.concatenate([lower, upper], 0), forward)
        for k in range(PAIRS):
            a, b = left_complex(left_forward, *(spectrum[j * g : (j + 1) * g] for j in (k, k + PAIRS)))
            store(work_a, start + k, [a])
            store(work_a, start + k + half, [b])

    for kx in range(0, g, 2):
        slabs = left_complex(left_forward, strided(work_a, kx, g), strided(work_a, kx + 1, g))
        slabs = [slab * coulomb_ref[slab_rows(kx + j, g), :] for j, slab in enumerate(slabs)]
        store(work_b, kx, left_complex(left_backward, *slabs))

    for start in range(0, half, last):
        lower, upper = [], []
        for z in range(start, start + last):
            a, b = left_complex(left_backward, strided(work_b, z, g), strided(work_b, z + half, g))
            lower.append(a)
            upper.append(b)
        out = right(jnp.concatenate(lower + upper, 0), last_backward)
        emit(start, *regrouped(out[: last * g], out[last * g :]))


def near_kernel(g, phi_ref, other_ref, *refs):
    tables, (sum_ref, work_a, work_b) = refs[:5], refs[5:]

    def emit(start, own, other):
        rows = slab_rows(start, g, PAIRS)
        sum_ref[rows, :] = own * phi_ref[rows, :] + other * other_ref[rows, :]

    potentials(g, phi_ref, phi_ref, other_ref, tables, work_a, work_b, emit)


def middle_kernel(g, phi_ref, first_ref, second_ref, before_ref, *refs):
    tables, (sum_ref, work_a, work_b) = refs[:5], refs[5:]

    def emit(start, first, second):
        rows = slab_rows(start, g, PAIRS)
        sum_ref[rows, :] = before_ref[rows, :] + first * first_ref[rows, :] + second * second_ref[rows, :]

    potentials(g, phi_ref, first_ref, second_ref, tables, work_a, work_b, emit)


def far_kernel(g, weights, phi_ref, first_ref, second_ref, before_ref, hot_ref, last_hot_ref, stick_out_ref, *refs):
    tables, out_refs = refs[:5], refs[5:-3]
    work_a, work_b, picked_ref = refs[-3:]
    forward = tables[2][...].astype(BF16)
    half = g // 2

    def emit(start, first, second):
        rows = slab_rows(start, g, half)
        total = before_ref[rows, :] + weights[0] * (first * first_ref[rows, :])
        total = total + weights[1] * (second * second_ref[rows, :])
        for k in range(0, half, 2):
            cos, sin = left(forward, beside(total[k * g : (k + 1) * g], total[(k + 1) * g : (k + 2) * g]))
            for j, (real, imag) in enumerate(zip(halves(cos), halves(sin))):
                lower, upper = regrouped(real, imag)
                store(work_a, start + k + j, [lower])
                store(work_a, start + k + j + half, [upper])

    potentials(g, phi_ref, first_ref, second_ref, tables, work_a, work_b, emit, half)

    step = g // 3
    for first in range(0, g, step):
        slabs = []
        for kx in range(first, first + step, 2):
            slabs += left_complex(forward, strided(work_a, kx, g), strided(work_a, kx + 1, g))
        spectrum = beside(*split(jnp.concatenate(slabs, 0)))
        start = 0
        for ref in (hot_ref, last_hot_ref):
            both = dot(ref[:, first * g : (first + step) * g], spectrum)
            both = both[:, :LANES] + both[:, LANES:]
            rows = slice(start, start + ref.shape[0])
            picked_ref[rows, :] = both if first == 0 else picked_ref[rows, :] + both
            start += ref.shape[0]

    stick_out = stick_out_ref[...].astype(BF16)
    for k in range(0, len(out_refs), 2):
        high, low = split(picked_ref[k * LANES : (k + 2) * LANES, :])
        lined = jnp.concatenate([high, low, high], 1)
        out = lax.dot_general(stick_out, lined, (((1,), (1,)), ((), ())), preferred_element_type=F32)
        out_refs[k][...], out_refs[k + 1][...] = halves(out)


def call(kernel, out_shapes, scratch, flops, *operands, space=pltpu.VMEM, out_space=pltpu.VMEM, grant=40):
    out_spec = pl.BlockSpec(memory_space=out_space)
    return pl.pallas_call(
        kernel,
        out_shape=out_shapes,
        in_specs=[pl.BlockSpec(memory_space=space)] * len(operands),
        out_specs=jax.tree.map(lambda _: out_spec, out_shapes),
        scratch_shapes=scratch,
        compiler_params=pltpu.CompilerParams(vmem_limit_bytes=grant * 2**20),
        cost_estimate=pl.CostEstimate(flops=flops, bytes_accessed=flops, transcendentals=0),
    )(*operands)


def after(x, *others):
    return lax.optimization_barrier((x, *others))[0]


def exchanged(blocks, order, before):
    owners = len(blocks)
    moved = [blocks[0]] + [None] * (owners - 1)
    for d in order:
        others = [moved[x] if isinstance(x, int) else x for x in before.get(d, ())]
        block = after(blocks[d], *others) if others else blocks[d]
        moved[d] = lax.ppermute(block, "stick", [(i, i ^ d) for i in range(owners)])
    return moved


def on_device(sticks, stick_columns):
    g = sticks.shape[1] // 2
    slots = stick_columns.shape[0]
    owners = lax.axis_size("stick")
    groups = lax.axis_size("band")
    t = {name: jnp.asarray(value) for name, value in make_tables(g).items()}
    rows = g * g
    field = jax.ShapeDtypeStruct((rows // 2, LANES), F32)
    work = pltpu.VMEM((rows, LANES), F32)
    pot_flops = 1

    def shifted(x, distance):
        return lax.ppermute(x, "band", [(i, (i - distance) % groups) for i in range(groups)])

    def swapped(x):
        return lax.ppermute(x, "band", [(i, i ^ 1) for i in range(groups)])

    sent = call(
        functools.partial(send_kernel, g),
        [jax.ShapeDtypeStruct((2 * g + 8, slots), F32)] * owners,
        [
            pltpu.VMEM((1, slots), jnp.int32),
            pltpu.SemaphoreType.DMA((owners,)),
            pltpu.SemaphoreType.DMA,
        ],
        1,
        sticks,
        stick_columns[None, :],
        space=pltpu.HBM,
        grant=SEND_GRANT,
    )
    shapes = [(2 * g + 8, slots), (LANES, 6 * g), (2 * g, 3 * g)]
    staged, *first_tables = call(
        functools.partial(early_kernel, g),
        [jax.ShapeDtypeStruct(shape, kind) for shape, kind in zip(shapes, (F32, BF16, BF16))],
        [],
        1,
        sent[0],
        after(t["early"], sent[0]),
    )
    half = owners // 2
    distant, close = list(range(half, owners)), list(range(1, half))
    mixed = [distant[0]] + [d for pair in zip(close, distant[1:]) for d in pair]
    before = {mixed[k]: (mixed[k - 3 - k % 2],) for k in range(WINDOW, len(mixed))}
    last = mixed[WINDOW]
    received = exchanged(sent, mixed, {d: (half, staged, *first_tables) if d == last else (half,) for d in before})
    received[0] = staged
    cut = owners * 3 // 4
    order = [0] + mixed
    order = order[:cut] + order[:cut - 1:-1]
    stick_in, left_table = first_tables

    def relayed(part):
        shapes = [(len(part) * 2 * g, slots), (8, len(part) * slots)]
        shapes = [jax.ShapeDtypeStruct(shape, F32) for shape in shapes]
        return call(functools.partial(relay_kernel, g), shapes, [], 1, *[received[d] for d in part])

    def on_grid(blocks, flops=1):
        grid = jax.ShapeDtypeStruct((rows, LANES), F32)
        return call(functools.partial(place_sticks_kernel, g), grid, [], flops, blocks, columns[0], stick_in)

    def orbital(grid, rest):
        operands = (grid, rest, columns[1], stick_in, left_table)
        return call(functools.partial(field_kernel, g), field, [work], 1, *operands)

    first_blocks, first_columns = relayed(order[:cut])
    columns = [first_columns]
    own_grid = on_grid(first_blocks, 5 * 10**9)

    def hot_rows(columns):
        shape = jax.ShapeDtypeStruct((columns.shape[1], rows), BF16)
        return call(functools.partial(pick_kernel, g), shape, [], 1, columns)

    hot = [hot_rows(first_columns)]
    received[order[cut]] = after(received[order[cut]], own_grid, *hot)
    last_blocks, last_columns = relayed(order[cut:])
    columns.append(last_columns)
    hot.append(hot_rows(last_columns))
    phi = orbital(own_grid, last_blocks)
    near = swapped(phi)
    pot_tables = [t["forward"], t["last_backward"], t["left_forward"], t["left_backward"], t["coulomb"]]

    def potential_sum(kernel, *operands):
        return call(functools.partial(kernel, g), field, [work, work], pot_flops, phi, *operands, *pot_tables)

    distances = (HALF,) if groups == 2 * HALF else (HALF, -HALF)
    fields = [orbital(on_grid(shifted(first_blocks, d)), shifted(last_blocks, d)) for d in distances]
    total = potential_sum(near_kernel, after(near, *fields))
    if groups == 2 * HALF:
        weights = (2.0, 1.0)
        first, second = fields[0], swapped(fields[0])
    else:
        weights = (1.0, 0.0)
        odd = lax.axis_index("band") % 2 == 1
        first = second = swapped(jnp.where(odd, fields[1], fields[0]))
        total = potential_sum(middle_kernel, *fields, total)
    result = call(
        functools.partial(far_kernel, g, weights),
        [jax.ShapeDtypeStruct((2 * g, slots), F32)] * owners,
        [work, work, pltpu.VMEM((owners * slots, LANES), F32)],
        pot_flops,
        phi,
        first,
        second,
        total,
        *hot,
        t["stick_out"],
        *pot_tables,
    )
    result = [result[order.index(d)] for d in range(owners)]
    out_order = []
    for k in range(0, half, 2):
        out_order += distant[k : k + 2] + close[k // 2 : k // 2 + 1]
    out_order = [d for d in out_order if d not in close[half // 4 :]] + close[half // 4 :]
    result = exchanged(result, out_order, {d: (half,) for d in out_order[WINDOW:]})
    out_order = [0] + out_order
    return call(
        functools.partial(place_kernel, out_order),
        jax.ShapeDtypeStruct(sticks.shape, F32),
        [pltpu.SemaphoreType.DMA((owners,))],
        1,
        *[result[d] for d in out_order],
        out_space=pltpu.HBM,
    )


def solution(mesh):
    return jax.shard_map(
        on_device,
        mesh=mesh,
        in_specs=(P("band", None, "stick"), P("stick")),
        out_specs=P("band", None, "stick"),
        check_vma=False,
    )
```

```python
import functools
import math

import jax
import jax.numpy as jnp
import numpy as np
from jax import lax
from jax.experimental import pallas as pl
from jax.experimental.pallas import tpu as pltpu
from jax.sharding import PartitionSpec as P

HALF = 2
BOX_LENGTH = 18.0
LANES = 128
MID = 64
WINDOW = 5
SEND_GRANT = 60
PAIRS = 6

F32 = jnp.float32
BF16 = jnp.bfloat16


def rounded_parts(table):
    high = table.astype(BF16).astype(np.float64)
    low = (table - high).astype(BF16).astype(np.float64)
    return high, low


def across(table):
    high, low = rounded_parts(table)
    return np.concatenate([high, high, low], 1).astype(np.float32)


def down(table):
    high, low = rounded_parts(table)
    return np.block([[high, low], [high, np.zeros_like(low)]]).astype(np.float32)


def make_tables(g):
    angle = 2.0 * np.pi / g * (np.outer(np.arange(g), np.arange(g)) % g)
    c, s = np.cos(angle), np.sin(angle)
    lower, upper = slice(0, g), slice(MID, MID + g)

    forward, backward = np.zeros((2, LANES, LANES))
    forward[lower, lower], forward[lower, upper] = c, -s
    forward[upper, lower], forward[upper, upper] = s, c
    backward[lower, lower], backward[lower, upper] = c, s
    backward[upper, lower], backward[upper, upper] = -s, c
    stick_in = np.zeros((LANES, 2 * g))
    stick_in[lower, :g], stick_in[lower, g:] = c, -s
    stick_in[upper, :g], stick_in[upper, g:] = s, c
    stick_out = np.zeros((2 * g, LANES))
    stick_out[:g, lower], stick_out[:g, upper] = c, s
    stick_out[g:, lower], stick_out[g:, upper] = -s, c

    freq = np.arange(g)
    square = np.minimum(freq, g - freq) ** 2
    total = square[:, None, None] + square[None, :, None] + square[None, None, :]
    unit = (2.0 * math.pi / BOX_LENGTH) ** 2
    kernel = np.where(total > 0, 4.0 * math.pi / (unit * np.maximum(total, 1)), 0.0)
    coulomb = np.zeros((g, g, LANES), np.float32)
    coulomb[:, :, lower] = kernel
    coulomb[:, :, upper] = kernel
    stick_in, left_backward = across(stick_in), across(np.concatenate([c, s], 0))
    high, low = rounded_parts(np.concatenate([c, -s], 1))
    real_backward = np.block([[high, high], [low, np.zeros_like(low)]])
    early_parts = (stick_in, left_backward, real_backward)
    early = np.concatenate([np.pad(x, ((0, 0), (0, 6 * g - x.shape[1]))) for x in early_parts], 0).astype(np.float32)
    return dict(
        forward=down(forward),
        last_backward=down(backward / g**3),
        left_forward=across(np.concatenate([c, -s], 0)),
        left_backward=left_backward,
        early=early,
        stick_out=across(stick_out * g**-1.5),
        coulomb=coulomb.reshape(g * g, LANES),
    )


def split(x):
    high = x.astype(BF16)
    low = (x - high.astype(F32)).astype(BF16)
    return high, low


def stacked(x):
    high, low = split(x)
    return jnp.concatenate([high, low, high], 0)


def dot(a, b):
    return jnp.dot(a, b, preferred_element_type=F32)


def lane_halves(shape):
    return lax.broadcasted_iota(jnp.int32, shape, 1) % LANES < MID


def turned(x):
    return pltpu.roll(x, MID, 1)


def regrouped(a, b):
    low = lane_halves(a.shape)
    return jnp.where(low, a, turned(b)), jnp.where(low, turned(a), b)


def beside(a, b):
    return jnp.concatenate([a, b], 1)


def halves(x):
    return x[:, :LANES], x[:, LANES:]


def left(table, x):
    both = dot(table, stacked(x))
    g = both.shape[0] // 2
    return both[:g], both[g:]


def left_complex(table, a, b):
    cos, sin = left(table, beside(a, b))
    sign = jnp.where(lane_halves((1, LANES)), -1.0, 1.0)
    return [p + turned(q) * sign for p, q in zip(halves(cos), halves(sin))]


def right(x, table):
    both = dot(beside(*split(x)), table)
    width = both.shape[1] // 2
    return both[:, :width] + both[:, width:]


def strided(ref, first, g):
    return ref[pl.ds(first, g, stride=g), :]


def slab_rows(index, g, count=1):
    return pl.ds(index * g, count * g)


def one_hot(index, wanted):
    return jnp.where(index == wanted, jnp.asarray(1, BF16), jnp.asarray(0, BF16))


def send_kernel(g, sticks_ref, columns_ref, *refs):
    block_refs, (row_ref, sems, row_sem) = refs[:-3], refs[-3:]
    own = lax.axis_index("stick")
    row_copy = pltpu.make_async_copy(columns_ref, row_ref, row_sem)
    row_copy.start()
    copies = [
        pltpu.make_async_copy(sticks_ref.at[own ^ d], ref.at[pl.ds(0, 2 * g)], sems.at[d])
        for d, ref in enumerate(block_refs)
    ]
    for copy in copies:
        copy.start()
    row_copy.wait()
    columns = jnp.broadcast_to(row_ref[...].astype(F32), (8, LANES))
    for ref in block_refs:
        ref[2 * g :, :] = columns
    for copy in copies:
        copy.wait()


def early_kernel(g, own_ref, tables_ref, staged_ref, stick_in_ref, left_ref, real_ref):
    staged_ref[...] = own_ref[...]
    first = 0
    for ref in (stick_in_ref, left_ref, real_ref):
        ref[...] = tables_ref[first : first + ref.shape[0], : ref.shape[1]].astype(BF16)
        first += ref.shape[0]


def place_kernel(order, *refs):
    own = lax.axis_index("stick")
    out_ref = refs[-1]
    for d, block_ref in zip(order, refs[:-1]):
        out_ref[own ^ d] = block_ref[...]


def store(ref, first, slabs):
    g = slabs[0].shape[0]
    for k, slab in enumerate(slabs):
        ref[slab_rows(first + k, g), :] = slab


def relay_kernel(g, *refs):
    blocks, (coefficients_ref, columns_ref) = refs[:-2], refs[-2:]
    for k, ref in enumerate(blocks):
        coefficients_ref[k * 2 * g : (k + 1) * 2 * g, :] = ref[: 2 * g, :]
        columns_ref[:, k * LANES : (k + 1) * LANES] = ref[2 * g :, :]


def placed(g, blocks_ref, columns_ref, stick_in_ref):
    columns = columns_ref[:1, :].astype(jnp.int32)
    stick_in = stick_in_ref[...]
    blocks = [blocks_ref[k : k + 2 * g, :] for k in range(0, blocks_ref.shape[0], 2 * g)]
    sticks = []
    for k in range(0, len(blocks), 2):
        sticks.append(beside(*split(dot(stick_in, stacked(beside(blocks[k], blocks[k + 1]))).T)))
    sticks = jnp.concatenate(sticks, 0)
    rows = g * g // 2
    index = lax.broadcasted_iota(jnp.int16, (rows, columns.shape[1]), 0)
    for first in (0, rows):
        both = dot(one_hot(index, (columns - first).astype(jnp.int16)), sticks)
        yield first, both[:, :LANES] + both[:, LANES:]


def place_sticks_kernel(g, blocks_ref, columns_ref, stick_in_ref, grid_ref):
    for first, part in placed(g, blocks_ref, columns_ref, stick_in_ref):
        grid_ref[first : first + part.shape[0], :] = part


def field_kernel(g, grid_ref, blocks_ref, columns_ref, stick_in_ref, left_ref, real_ref, phi_ref, work_a):
    backward = left_ref[...]
    half = g // 2
    for first, part in placed(g, blocks_ref, columns_ref, stick_in_ref):
        part = part + grid_ref[first : first + part.shape[0], :]
        for k in range(0, half, 2):
            slabs = left_complex(backward, part[k * g : (k + 1) * g], part[(k + 1) * g : (k + 2) * g])
            store(work_a, first // g + k, slabs)

    for y in range(0, half, 2):
        real, imag = zip(*[regrouped(strided(work_a, j, g), strided(work_a, j + half, g)) for j in (y, y + 1)])
        parts = [split(beside(*real)), split(beside(*imag))]
        both = dot(real_ref[...], jnp.concatenate([x[k] for k in range(2) for x in parts], 0))
        store(phi_ref, y, halves(both[:g] + both[g:]))


def pick_kernel(g, columns_ref, hot_ref):
    for k in range(0, columns_ref.shape[1], LANES):
        block = columns_ref[:, k : k + LANES]
        wanted = jnp.concatenate([block] * (LANES // block.shape[0]), 0).T.astype(jnp.int32)
        for c in range(0, hot_ref.shape[1], LANES):
            index = lax.broadcasted_iota(jnp.int16, (LANES, LANES), 1)
            hot_ref[k : k + LANES, c : c + LANES] = one_hot(index, (wanted - c).astype(jnp.int16))


def potentials(g, phi_ref, first_ref, second_ref, tables, work_a, work_b, emit, last=PAIRS):
    forward, last_backward, left_forward, left_backward = [ref[...].astype(BF16) for ref in tables[:4]]
    coulomb_ref = tables[4]
    half = g // 2
    for start in range(0, half, PAIRS):
        rows = slab_rows(start, g, PAIRS)
        phi = phi_ref[rows, :]
        lower, upper = regrouped(phi * first_ref[rows, :], phi * second_ref[rows, :])
        spectrum = right(jnp.concatenate([lower, upper], 0), forward)
        for k in range(PAIRS):
            a, b = left_complex(left_forward, *(spectrum[j * g : (j + 1) * g] for j in (k, k + PAIRS)))
            store(work_a, start + k, [a])
            store(work_a, start + k + half, [b])

    for kx in range(0, g, 2):
        slabs = left_complex(left_forward, strided(work_a, kx, g), strided(work_a, kx + 1, g))
        slabs = [slab * coulomb_ref[slab_rows(kx + j, g), :] for j, slab in enumerate(slabs)]
        store(work_b, kx, left_complex(left_backward, *slabs))

    for start in range(0, half, last):
        lower, upper = [], []
        for z in range(start, start + last):
            a, b = left_complex(left_backward, strided(work_b, z, g), strided(work_b, z + half, g))
            lower.append(a)
            upper.append(b)
        out = right(jnp.concatenate(lower + upper, 0), last_backward)
        emit(start, *regrouped(out[: last * g], out[last * g :]))


def near_kernel(g, phi_ref, other_ref, *refs):
    tables, (sum_ref, work_a, work_b) = refs[:5], refs[5:]

    def emit(start, own, other):
        rows = slab_rows(start, g, PAIRS)
        sum_ref[rows, :] = own * phi_ref[rows, :] + other * other_ref[rows, :]

    potentials(g, phi_ref, phi_ref, other_ref, tables, work_a, work_b, emit)


def middle_kernel(g, phi_ref, first_ref, second_ref, before_ref, *refs):
    tables, (sum_ref, work_a, work_b) = refs[:5], refs[5:]

    def emit(start, first, second):
        rows = slab_rows(start, g, PAIRS)
        sum_ref[rows, :] = before_ref[rows, :] + first * first_ref[rows, :] + second * second_ref[rows, :]

    potentials(g, phi_ref, first_ref, second_ref, tables, work_a, work_b, emit)


def far_kernel(g, weights, phi_ref, first_ref, second_ref, before_ref, hot_ref, last_hot_ref, stick_out_ref, *refs):
    tables, out_refs = refs[:5], refs[5:-3]
    work_a, work_b, picked_ref = refs[-3:]
    forward = tables[2][...].astype(BF16)
    half = g // 2

    def emit(start, first, second):
        rows = slab_rows(start, g, half)
        total = before_ref[rows, :] + weights[0] * (first * first_ref[rows, :])
        total = total + weights[1] * (second * second_ref[rows, :])
        for k in range(0, half, 2):
            cos, sin = left(forward, beside(total[k * g : (k + 1) * g], total[(k + 1) * g : (k + 2) * g]))
            for j, (real, imag) in enumerate(zip(halves(cos), halves(sin))):
                lower, upper = regrouped(real, imag)
                store(work_a, start + k + j, [lower])
                store(work_a, start + k + j + half, [upper])

    potentials(g, phi_ref, first_ref, second_ref, tables, work_a, work_b, emit, half)

    step = g // 3
    for first in range(0, g, step):
        slabs = []
        for kx in range(first, first + step, 2):
            slabs += left_complex(forward, strided(work_a, kx, g), strided(work_a, kx + 1, g))
        spectrum = beside(*split(jnp.concatenate(slabs, 0)))
        start = 0
        for ref in (hot_ref, last_hot_ref):
            both = dot(ref[:, first * g : (first + step) * g], spectrum)
            both = both[:, :LANES] + both[:, LANES:]
            rows = slice(start, start + ref.shape[0])
            picked_ref[rows, :] = both if first == 0 else picked_ref[rows, :] + both
            start += ref.shape[0]

    stick_out = stick_out_ref[...].astype(BF16)
    for k in range(0, len(out_refs), 2):
        high, low = split(picked_ref[k * LANES : (k + 2) * LANES, :])
        lined = jnp.concatenate([high, low, high], 1)
        out = lax.dot_general(stick_out, lined, (((1,), (1,)), ((), ())), preferred_element_type=F32)
        out_refs[k][...], out_refs[k + 1][...] = halves(out)


def call(kernel, out_shapes, scratch, flops, *operands, space=pltpu.VMEM, out_space=pltpu.VMEM, grant=40):
    out_spec = pl.BlockSpec(memory_space=out_space)
    return pl.pallas_call(
        kernel,
        out_shape=out_shapes,
        in_specs=[pl.BlockSpec(memory_space=space)] * len(operands),
        out_specs=jax.tree.map(lambda _: out_spec, out_shapes),
        scratch_shapes=scratch,
        compiler_params=pltpu.CompilerParams(vmem_limit_bytes=grant * 2**20),
        cost_estimate=pl.CostEstimate(flops=flops, bytes_accessed=flops, transcendentals=0),
    )(*operands)


def after(x, *others):
    return lax.optimization_barrier((x, *others))[0]


def exchanged(blocks, order, before):
    owners = len(blocks)
    moved = [blocks[0]] + [None] * (owners - 1)
    for d in order:
        others = [moved[x] if isinstance(x, int) else x for x in before.get(d, ())]
        block = after(blocks[d], *others) if others else blocks[d]
        moved[d] = lax.ppermute(block, "stick", [(i, i ^ d) for i in range(owners)])
    return moved


def on_device(sticks, stick_columns):
    g = sticks.shape[1] // 2
    slots = stick_columns.shape[0]
    owners = lax.axis_size("stick")
    groups = lax.axis_size("band")
    t = {name: jnp.asarray(value) for name, value in make_tables(g).items()}
    rows = g * g
    field = jax.ShapeDtypeStruct((rows // 2, LANES), F32)
    work = pltpu.VMEM((rows, LANES), F32)
    pot_flops = 1

    def shifted(x, distance):
        return lax.ppermute(x, "band", [(i, (i - distance) % groups) for i in range(groups)])

    def swapped(x):
        return lax.ppermute(x, "band", [(i, i ^ 1) for i in range(groups)])

    sent = call(
        functools.partial(send_kernel, g),
        [jax.ShapeDtypeStruct((2 * g + 8, slots), F32)] * owners,
        [
            pltpu.VMEM((1, slots), jnp.int32),
            pltpu.SemaphoreType.DMA((owners,)),
            pltpu.SemaphoreType.DMA,
        ],
        1,
        sticks,
        stick_columns[None, :],
        space=pltpu.HBM,
        grant=SEND_GRANT,
    )
    shapes = [(2 * g + 8, slots), (LANES, 6 * g), (2 * g, 3 * g), (2 * g, 4 * g)]
    staged, *first_tables = call(
        functools.partial(early_kernel, g),
        [jax.ShapeDtypeStruct(shape, kind) for shape, kind in zip(shapes, (F32, BF16, BF16, BF16))],
        [],
        1,
        sent[0],
        after(t["early"], sent[0]),
    )
    half = owners // 2
    distant, close = list(range(half, owners)), list(range(1, half))
    mixed = [distant[0]] + [d for pair in zip(close, distant[1:]) for d in pair]
    before = {mixed[k]: (mixed[k - 3 - k % 2],) for k in range(WINDOW, len(mixed))}
    last = mixed[WINDOW]
    received = exchanged(sent, mixed, {d: (half, staged, *first_tables) if d == last else (half,) for d in before})
    received[0] = staged
    cut = owners * 3 // 4
    order = [0] + mixed
    order = order[:cut] + order[:cut - 1:-1]
    stick_in, *field_tables = first_tables

    def relayed(part):
        shapes = [(len(part) * 2 * g, slots), (8, len(part) * slots)]
        shapes = [jax.ShapeDtypeStruct(shape, F32) for shape in shapes]
        return call(functools.partial(relay_kernel, g), shapes, [], 1, *[received[d] for d in part])

    def on_grid(blocks, flops=1):
        grid = jax.ShapeDtypeStruct((rows, LANES), F32)
        return call(functools.partial(place_sticks_kernel, g), grid, [], flops, blocks, columns[0], stick_in)

    def orbital(grid, rest):
        operands = (grid, rest, columns[1], stick_in, *field_tables)
        return call(functools.partial(field_kernel, g), field, [work], 1, *operands)

    first_blocks, first_columns = relayed(order[:cut])
    columns = [first_columns]
    own_grid = on_grid(first_blocks, 5 * 10**9)

    def hot_rows(columns):
        shape = jax.ShapeDtypeStruct((columns.shape[1], rows), BF16)
        return call(functools.partial(pick_kernel, g), shape, [], 1, columns)

    hot = [hot_rows(first_columns)]
    received[order[cut]] = after(received[order[cut]], own_grid, *hot)
    last_blocks, last_columns = relayed(order[cut:])
    columns.append(last_columns)
    hot.append(hot_rows(last_columns))
    phi = orbital(own_grid, last_blocks)
    near = swapped(phi)
    pot_tables = [t["forward"], t["last_backward"], t["left_forward"], t["left_backward"], t["coulomb"]]

    def potential_sum(kernel, *operands):
        return call(functools.partial(kernel, g), field, [work, work], pot_flops, phi, *operands, *pot_tables)

    distances = (HALF,) if groups == 2 * HALF else (HALF, -HALF)
    fields = [orbital(on_grid(shifted(first_blocks, d)), shifted(last_blocks, d)) for d in distances]
    total = potential_sum(near_kernel, after(near, *fields))
    if groups == 2 * HALF:
        weights = (2.0, 1.0)
        first, second = fields[0], swapped(fields[0])
    else:
        weights = (1.0, 0.0)
        odd = lax.axis_index("band") % 2 == 1
        first = second = swapped(jnp.where(odd, fields[1], fields[0]))
        total = potential_sum(middle_kernel, *fields, total)
    result = call(
        functools.partial(far_kernel, g, weights),
        [jax.ShapeDtypeStruct((2 * g, slots), F32)] * owners,
        [work, work, pltpu.VMEM((owners * slots, LANES), F32)],
        pot_flops,
        phi,
        first,
        second,
        total,
        *hot,
        t["stick_out"],
        *pot_tables,
    )
    result = [result[order.index(d)] for d in range(owners)]
    result = exchanged(result, mixed, {d: (half,) for d in before})
    out_order = [0] + mixed
    return call(
        functools.partial(place_kernel, out_order),
        jax.ShapeDtypeStruct(sticks.shape, F32),
        [],
        1,
        *[result[d] for d in out_order],
    )


def solution(mesh):
    return jax.shard_map(
        on_device,
        mesh=mesh,
        in_specs=(P("band", None, "stick"), P("stick")),
        out_specs=P("band", None, "stick"),
        check_vma=False,
    )
```

```python
import functools
import math

import jax
import jax.numpy as jnp
import numpy as np
from jax import lax
from jax.experimental import pallas as pl
from jax.experimental.pallas import tpu as pltpu
from jax.sharding import PartitionSpec as P

HALF = 2
BOX_LENGTH = 18.0
LANES = 128
MID = 64
WINDOW = 5
SEND_GRANT = 60
PAIRS = 6

F32 = jnp.float32
BF16 = jnp.bfloat16


def rounded_parts(table):
    high = table.astype(BF16).astype(np.float64)
    low = (table - high).astype(BF16).astype(np.float64)
    return high, low


def across(table):
    high, low = rounded_parts(table)
    return np.concatenate([high, high, low], 1).astype(np.float32)


def down(table):
    high, low = rounded_parts(table)
    return np.block([[high, low], [high, np.zeros_like(low)]]).astype(np.float32)


def over_rows(table):
    high, low = rounded_parts(table)
    return np.block([[high, high], [low, np.zeros_like(low)]]).astype(np.float32)


def make_tables(g):
    angle = 2.0 * np.pi / g * (np.outer(np.arange(g), np.arange(g)) % g)
    c, s = np.cos(angle), np.sin(angle)
    lower, upper = slice(0, g), slice(MID, MID + g)

    forward, backward = np.zeros((2, LANES, LANES))
    forward[lower, lower], forward[lower, upper] = c, -s
    forward[upper, lower], forward[upper, upper] = s, c
    backward[lower, lower], backward[lower, upper] = c, s
    backward[upper, lower], backward[upper, upper] = -s, c
    stick_in = np.zeros((LANES, 2 * g))
    stick_in[lower, :g], stick_in[lower, g:] = c, -s
    stick_in[upper, :g], stick_in[upper, g:] = s, c
    stick_out = np.zeros((2 * g, LANES))
    stick_out[:g, lower], stick_out[:g, upper] = c, s
    stick_out[g:, lower], stick_out[g:, upper] = -s, c

    freq = np.arange(g)
    square = np.minimum(freq, g - freq) ** 2
    total = square[:, None, None] + square[None, :, None] + square[None, None, :]
    unit = (2.0 * math.pi / BOX_LENGTH) ** 2
    kernel = np.where(total > 0, 4.0 * math.pi / (unit * np.maximum(total, 1)), 0.0)
    coulomb = np.zeros((g, g, LANES), np.float32)
    coulomb[:, :, lower] = kernel
    coulomb[:, :, upper] = kernel
    stick_in = across(stick_in)
    real_backward = over_rows(np.concatenate([c, -s], 1))
    left_forward, left_backward = over_rows(np.block([[c, s], [-s, c]])), over_rows(np.block([[c, -s], [s, c]]))
    early_parts = (stick_in, left_backward, real_backward)
    early = np.concatenate([np.pad(x, ((0, 0), (0, 6 * g - x.shape[1]))) for x in early_parts], 0).astype(np.float32)
    return dict(
        forward=down(forward),
        last_backward=down(backward / g**3),
        real_forward=across(np.concatenate([c, -s], 0)),
        left_forward=left_forward,
        left_backward=left_backward,
        early=early,
        stick_out=across(stick_out * g**-1.5),
        coulomb=coulomb.reshape(g * g, LANES),
    )


def split(x):
    high = x.astype(BF16)
    low = (x - high.astype(F32)).astype(BF16)
    return high, low


def stacked(x):
    high, low = split(x)
    return jnp.concatenate([high, low, high], 0)


def dot(a, b):
    return jnp.dot(a, b, preferred_element_type=F32)


def lane_halves(shape):
    return lax.broadcasted_iota(jnp.int32, shape, 1) % LANES < MID


def turned(x):
    return pltpu.roll(x, MID, 1)


def regrouped(a, b):
    low = lane_halves(a.shape)
    return jnp.where(low, a, turned(b)), jnp.where(low, turned(a), b)


def beside(a, b):
    return jnp.concatenate([a, b], 1)


def halves(x):
    return x[:, :LANES], x[:, LANES:]


def left(table, x):
    both = dot(table, stacked(x))
    g = both.shape[0] // 2
    return both[:g], both[g:]


def packed(slabs):
    real, imag = zip(*[regrouped(slabs[k], slabs[k + 1]) for k in (0, 2)])
    return beside(*real), beside(*imag)


def unpacked(real, imag):
    slabs = []
    for pair in zip(halves(real), halves(imag)):
        slabs += regrouped(*pair)
    return slabs


def left_packed(table, real, imag):
    parts = [split(real), split(imag)]
    both = dot(table, jnp.concatenate([x[k] for k in range(2) for x in parts], 0))
    out = both[: both.shape[0] // 2] + both[both.shape[0] // 2 :]
    return out[: real.shape[0]], out[real.shape[0] :]


def left_complex(table, slabs):
    return unpacked(*left_packed(table, *packed(slabs)))


def right(x, table):
    both = dot(beside(*split(x)), table)
    width = both.shape[1] // 2
    return both[:, :width] + both[:, width:]


def strided(ref, first, g):
    return ref[pl.ds(first, g, stride=g), :]


def slab_rows(index, g, count=1):
    return pl.ds(index * g, count * g)


def one_hot(index, wanted):
    return jnp.where(index == wanted, jnp.asarray(1, BF16), jnp.asarray(0, BF16))


def send_kernel(g, sticks_ref, columns_ref, *refs):
    block_refs, (row_ref, sems, row_sem) = refs[:-3], refs[-3:]
    own = lax.axis_index("stick")
    row_copy = pltpu.make_async_copy(columns_ref, row_ref, row_sem)
    row_copy.start()
    copies = [
        pltpu.make_async_copy(sticks_ref.at[own ^ d], ref.at[pl.ds(0, 2 * g)], sems.at[d])
        for d, ref in enumerate(block_refs)
    ]
    for copy in copies:
        copy.start()
    row_copy.wait()
    columns = jnp.broadcast_to(row_ref[...].astype(F32), (8, LANES))
    for ref in block_refs:
        ref[2 * g :, :] = columns
    for copy in copies:
        copy.wait()


def early_kernel(g, own_ref, tables_ref, staged_ref, stick_in_ref, left_ref, real_ref):
    staged_ref[...] = own_ref[...]
    first = 0
    for ref in (stick_in_ref, left_ref, real_ref):
        ref[...] = tables_ref[first : first + ref.shape[0], : ref.shape[1]].astype(BF16)
        first += ref.shape[0]


def place_kernel(order, *refs):
    own = lax.axis_index("stick")
    out_ref = refs[-1]
    for d, block_ref in zip(order, refs[:-1]):
        out_ref[own ^ d] = block_ref[...]


def store(ref, first, slabs):
    g = slabs[0].shape[0]
    for k, slab in enumerate(slabs):
        ref[slab_rows(first + k, g), :] = slab


def relay_kernel(g, *refs):
    blocks, (coefficients_ref, columns_ref) = refs[:-2], refs[-2:]
    for k, ref in enumerate(blocks):
        coefficients_ref[k * 2 * g : (k + 1) * 2 * g, :] = ref[: 2 * g, :]
        columns_ref[:, k * LANES : (k + 1) * LANES] = ref[2 * g :, :]


def placed(g, blocks_ref, columns_ref, stick_in_ref):
    columns = columns_ref[:1, :].astype(jnp.int32)
    stick_in = stick_in_ref[...]
    blocks = [blocks_ref[k : k + 2 * g, :] for k in range(0, blocks_ref.shape[0], 2 * g)]
    sticks = []
    for k in range(0, len(blocks), 2):
        sticks.append(beside(*split(dot(stick_in, stacked(beside(blocks[k], blocks[k + 1]))).T)))
    sticks = jnp.concatenate(sticks, 0)
    rows = g * g // 2
    index = lax.broadcasted_iota(jnp.int16, (rows, columns.shape[1]), 0)
    for first in (0, rows):
        both = dot(one_hot(index, (columns - first).astype(jnp.int16)), sticks)
        yield first, both[:, :LANES] + both[:, LANES:]


def place_sticks_kernel(g, blocks_ref, columns_ref, stick_in_ref, grid_ref):
    for first, part in placed(g, blocks_ref, columns_ref, stick_in_ref):
        grid_ref[first : first + part.shape[0], :] = part


def field_kernel(g, grid_ref, blocks_ref, columns_ref, stick_in_ref, left_ref, real_ref, phi_ref, work_a):
    backward = left_ref[...]
    half = g // 2
    for first, part in placed(g, blocks_ref, columns_ref, stick_in_ref):
        part = part + grid_ref[first : first + part.shape[0], :]
        for k in range(0, half, 4):
            slabs = left_complex(backward, [part[j * g : (j + 1) * g] for j in range(k, k + 4)])
            store(work_a, first // g + k, slabs)

    for y in range(0, half, 2):
        real, imag = packed([strided(work_a, j, g) for j in (y, y + half, y + 1, y + 1 + half)])
        parts = [split(real), split(imag)]
        both = dot(real_ref[...], jnp.concatenate([x[k] for k in range(2) for x in parts], 0))
        store(phi_ref, y, halves(both[:g] + both[g:]))


def pick_kernel(g, columns_ref, hot_ref):
    for k in range(0, columns_ref.shape[1], LANES):
        block = columns_ref[:, k : k + LANES]
        wanted = jnp.concatenate([block] * (LANES // block.shape[0]), 0).T.astype(jnp.int32)
        for c in range(0, hot_ref.shape[1], LANES):
            index = lax.broadcasted_iota(jnp.int16, (LANES, LANES), 1)
            hot_ref[k : k + LANES, c : c + LANES] = one_hot(index, (wanted - c).astype(jnp.int16))


def potentials(g, phi_ref, first_ref, second_ref, tables, work_a, work_b, emit, last=PAIRS):
    forward, last_backward, left_forward, left_backward = [ref[...].astype(BF16) for ref in tables[:4]]
    coulomb_ref = tables[4]
    half = g // 2
    for start in range(0, half, PAIRS):
        rows = slab_rows(start, g, PAIRS)
        phi = phi_ref[rows, :]
        lower, upper = regrouped(phi * first_ref[rows, :], phi * second_ref[rows, :])
        spectrum = right(jnp.concatenate([lower, upper], 0), forward)
        for k in range(0, PAIRS, 2):
            chosen = (k, k + PAIRS, k + 1, k + 1 + PAIRS)
            slabs = left_complex(left_forward, [spectrum[j * g : (j + 1) * g] for j in chosen])
            store(work_a, start + k, slabs[::2])
            store(work_a, start + k + half, slabs[1::2])

    for kx in range(0, g, 4):
        real, imag = left_packed(left_forward, *packed([strided(work_a, kx + j, g) for j in range(4)]))
        factors = [coulomb_ref[slab_rows(kx + j, g), :] for j in range(4)]
        low = lane_halves(factors[0].shape)
        factor = beside(*[jnp.where(low, factors[j], factors[j + 1]) for j in (0, 2)])
        store(work_b, kx, unpacked(*left_packed(left_backward, real * factor, imag * factor)))

    for start in range(0, half, last):
        lower, upper = [], []
        for y in range(start, start + last, 2):
            slabs = left_complex(left_backward, [strided(work_b, j, g) for j in (y, y + half, y + 1, y + 1 + half)])
            lower += slabs[::2]
            upper += slabs[1::2]
        out = right(jnp.concatenate(lower + upper, 0), last_backward)
        emit(start, *regrouped(out[: last * g], out[last * g :]))


def near_kernel(g, phi_ref, other_ref, *refs):
    tables, (sum_ref, work_a, work_b) = refs[:5], refs[5:]

    def emit(start, own, other):
        rows = slab_rows(start, g, PAIRS)
        sum_ref[rows, :] = own * phi_ref[rows, :] + other * other_ref[rows, :]

    potentials(g, phi_ref, phi_ref, other_ref, tables, work_a, work_b, emit)


def middle_kernel(g, phi_ref, first_ref, second_ref, before_ref, *refs):
    tables, (sum_ref, work_a, work_b) = refs[:5], refs[5:]

    def emit(start, first, second):
        rows = slab_rows(start, g, PAIRS)
        sum_ref[rows, :] = before_ref[rows, :] + first * first_ref[rows, :] + second * second_ref[rows, :]

    potentials(g, phi_ref, first_ref, second_ref, tables, work_a, work_b, emit)


def far_kernel(g, weights, phi_ref, first_ref, second_ref, before_ref, hot_ref, last_hot_ref, stick_out_ref, real_forward_ref, *refs):
    tables, out_refs = refs[:5], refs[5:-3]
    work_a, work_b, picked_ref = refs[-3:]
    forward, real_forward = tables[2][...].astype(BF16), real_forward_ref[...].astype(BF16)
    half = g // 2

    def emit(start, first, second):
        rows = slab_rows(start, g, half)
        total = before_ref[rows, :] + weights[0] * (first * first_ref[rows, :])
        total = total + weights[1] * (second * second_ref[rows, :])
        for k in range(0, half, 2):
            cos, sin = left(real_forward, beside(total[k * g : (k + 1) * g], total[(k + 1) * g : (k + 2) * g]))
            for j, (real, imag) in enumerate(zip(halves(cos), halves(sin))):
                lower, upper = regrouped(real, imag)
                store(work_a, start + k + j, [lower])
                store(work_a, start + k + j + half, [upper])

    potentials(g, phi_ref, first_ref, second_ref, tables, work_a, work_b, emit, half)

    step = g // 3
    for first in range(0, g, step):
        slabs = []
        for kx in range(first, first + step, 4):
            slabs += left_complex(forward, [strided(work_a, kx + j, g) for j in range(4)])
        spectrum = beside(*split(jnp.concatenate(slabs, 0)))
        start = 0
        for ref in (hot_ref, last_hot_ref):
            both = dot(ref[:, first * g : (first + step) * g], spectrum)
            both = both[:, :LANES] + both[:, LANES:]
            rows = slice(start, start + ref.shape[0])
            picked_ref[rows, :] = both if first == 0 else picked_ref[rows, :] + both
            start += ref.shape[0]

    stick_out = stick_out_ref[...].astype(BF16)
    for k in range(0, len(out_refs), 2):
        high, low = split(picked_ref[k * LANES : (k + 2) * LANES, :])
        lined = jnp.concatenate([high, low, high], 1)
        out = lax.dot_general(stick_out, lined, (((1,), (1,)), ((), ())), preferred_element_type=F32)
        out_refs[k][...], out_refs[k + 1][...] = halves(out)


def call(kernel, out_shapes, scratch, flops, *operands, space=pltpu.VMEM, out_space=pltpu.VMEM, grant=40):
    out_spec = pl.BlockSpec(memory_space=out_space)
    return pl.pallas_call(
        kernel,
        out_shape=out_shapes,
        in_specs=[pl.BlockSpec(memory_space=space)] * len(operands),
        out_specs=jax.tree.map(lambda _: out_spec, out_shapes),
        scratch_shapes=scratch,
        compiler_params=pltpu.CompilerParams(vmem_limit_bytes=grant * 2**20),
        cost_estimate=pl.CostEstimate(flops=flops, bytes_accessed=flops, transcendentals=0),
    )(*operands)


def after(x, *others):
    return lax.optimization_barrier((x, *others))[0]


def exchanged(blocks, order, before):
    owners = len(blocks)
    moved = [blocks[0]] + [None] * (owners - 1)
    for d in order:
        others = [moved[x] if isinstance(x, int) else x for x in before.get(d, ())]
        block = after(blocks[d], *others) if others else blocks[d]
        moved[d] = lax.ppermute(block, "stick", [(i, i ^ d) for i in range(owners)])
    return moved


def on_device(sticks, stick_columns):
    g = sticks.shape[1] // 2
    slots = stick_columns.shape[0]
    owners = lax.axis_size("stick")
    groups = lax.axis_size("band")
    t = {name: jnp.asarray(value) for name, value in make_tables(g).items()}
    rows = g * g
    field = jax.ShapeDtypeStruct((rows // 2, LANES), F32)
    work = pltpu.VMEM((rows, LANES), F32)
    pot_flops = 1

    def shifted(x, distance):
        return lax.ppermute(x, "band", [(i, (i - distance) % groups) for i in range(groups)])

    def swapped(x):
        return lax.ppermute(x, "band", [(i, i ^ 1) for i in range(groups)])

    sent = call(
        functools.partial(send_kernel, g),
        [jax.ShapeDtypeStruct((2 * g + 8, slots), F32)] * owners,
        [
            pltpu.VMEM((1, slots), jnp.int32),
            pltpu.SemaphoreType.DMA((owners,)),
            pltpu.SemaphoreType.DMA,
        ],
        1,
        sticks,
        stick_columns[None, :],
        space=pltpu.HBM,
        grant=SEND_GRANT,
    )
    shapes = [(2 * g + 8, slots), (LANES, 6 * g), (4 * g, 4 * g), (2 * g, 4 * g)]
    staged, *first_tables = call(
        functools.partial(early_kernel, g),
        [jax.ShapeDtypeStruct(shape, kind) for shape, kind in zip(shapes, (F32, BF16, BF16, BF16))],
        [],
        1,
        sent[0],
        after(t["early"], sent[0]),
    )
    half = owners // 2
    distant, close = list(range(half, owners)), list(range(1, half))
    mixed = [distant[0]] + [d for pair in zip(close, distant[1:]) for d in pair]
    before = {mixed[k]: (mixed[k - 3 - k % 2],) for k in range(WINDOW, len(mixed))}
    last = mixed[WINDOW]
    received = exchanged(sent, mixed, {d: (half, staged, *first_tables) if d == last else (half,) for d in before})
    received[0] = staged
    cut = owners * 3 // 4
    order = [0] + mixed
    order = order[:cut] + order[:cut - 1:-1]
    stick_in, *field_tables = first_tables

    def relayed(part):
        shapes = [(len(part) * 2 * g, slots), (8, len(part) * slots)]
        shapes = [jax.ShapeDtypeStruct(shape, F32) for shape in shapes]
        return call(functools.partial(relay_kernel, g), shapes, [], 1, *[received[d] for d in part])

    def on_grid(blocks, flops=1):
        grid = jax.ShapeDtypeStruct((rows, LANES), F32)
        return call(functools.partial(place_sticks_kernel, g), grid, [], flops, blocks, columns[0], stick_in)

    def orbital(grid, rest):
        operands = (grid, rest, columns[1], stick_in, *field_tables)
        return call(functools.partial(field_kernel, g), field, [work], 1, *operands)

    first_blocks, first_columns = relayed(order[:cut])
    columns = [first_columns]
    own_grid = on_grid(first_blocks, 5 * 10**9)

    def hot_rows(columns):
        shape = jax.ShapeDtypeStruct((columns.shape[1], rows), BF16)
        return call(functools.partial(pick_kernel, g), shape, [], 1, columns)

    hot = [hot_rows(first_columns)]
    received[order[cut]] = after(received[order[cut]], own_grid, *hot)
    last_blocks, last_columns = relayed(order[cut:])
    columns.append(last_columns)
    hot.append(hot_rows(last_columns))
    phi = orbital(own_grid, last_blocks)
    near = swapped(phi)
    pot_tables = [t["forward"], t["last_backward"], t["left_forward"], t["left_backward"], t["coulomb"]]

    def potential_sum(kernel, *operands):
        return call(functools.partial(kernel, g), field, [work, work], pot_flops, phi, *operands, *pot_tables)

    distances = (HALF,) if groups == 2 * HALF else (HALF, -HALF)
    fields = [orbital(on_grid(shifted(first_blocks, d)), shifted(last_blocks, d)) for d in distances]
    total = potential_sum(near_kernel, after(near, *fields))
    if groups == 2 * HALF:
        weights = (2.0, 1.0)
        first, second = fields[0], swapped(fields[0])
    else:
        weights = (1.0, 0.0)
        odd = lax.axis_index("band") % 2 == 1
        first = second = swapped(jnp.where(odd, fields[1], fields[0]))
        total = potential_sum(middle_kernel, *fields, total)
    result = call(
        functools.partial(far_kernel, g, weights),
        [jax.ShapeDtypeStruct((2 * g, slots), F32)] * owners,
        [work, work, pltpu.VMEM((owners * slots, LANES), F32)],
        pot_flops,
        phi,
        first,
        second,
        total,
        *hot,
        t["stick_out"],
        t["real_forward"],
        *pot_tables,
    )
    result = [result[order.index(d)] for d in range(owners)]
    result = exchanged(result, mixed, {d: (half,) for d in before})
    out_order = [0] + mixed
    return call(
        functools.partial(place_kernel, out_order),
        jax.ShapeDtypeStruct(sticks.shape, F32),
        [],
        1,
        *[result[d] for d in out_order],
    )


def solution(mesh):
    return jax.shard_map(
        on_device,
        mesh=mesh,
        in_specs=(P("band", None, "stick"), P("stick")),
        out_specs=P("band", None, "stick"),
        check_vma=False,
    )
```

```python
import functools
import math

import jax
import jax.numpy as jnp
import numpy as np
from jax import lax
from jax.experimental import pallas as pl
from jax.experimental.pallas import tpu as pltpu
from jax.sharding import PartitionSpec as P

HALF = 2
BOX_LENGTH = 18.0
LANES = 128
MID = 64
WINDOW = 5
SEND_GRANT = 60
PAIRS = 6

F32 = jnp.float32
BF16 = jnp.bfloat16


def rounded_parts(table):
    high = table.astype(BF16).astype(np.float64)
    low = (table - high).astype(BF16).astype(np.float64)
    return high, low


def across(table):
    high, low = rounded_parts(table)
    return np.concatenate([high, high, low], 1).astype(np.float32)


def down(table):
    high, low = rounded_parts(table)
    return np.block([[high, low], [high, np.zeros_like(low)]]).astype(np.float32)


def make_tables(g):
    angle = 2.0 * np.pi / g * (np.outer(np.arange(g), np.arange(g)) % g)
    c, s = np.cos(angle), np.sin(angle)
    lower, upper = slice(0, g), slice(MID, MID + g)

    forward, backward = np.zeros((2, LANES, LANES))
    forward[lower, lower], forward[lower, upper] = c, -s
    forward[upper, lower], forward[upper, upper] = s, c
    backward[lower, lower], backward[lower, upper] = c, s
    backward[upper, lower], backward[upper, upper] = -s, c
    stick_in = np.zeros((LANES, 2 * g))
    stick_in[lower, :g], stick_in[lower, g:] = c, -s
    stick_in[upper, :g], stick_in[upper, g:] = s, c
    stick_out = np.zeros((2 * g, LANES))
    stick_out[:g, lower], stick_out[:g, upper] = c, s
    stick_out[g:, lower], stick_out[g:, upper] = -s, c

    freq = np.arange(g)
    square = np.minimum(freq, g - freq) ** 2
    total = square[:, None, None] + square[None, :, None] + square[None, None, :]
    unit = (2.0 * math.pi / BOX_LENGTH) ** 2
    kernel = np.where(total > 0, 4.0 * math.pi / (unit * np.maximum(total, 1)), 0.0)
    coulomb = np.zeros((g, g, LANES), np.float32)
    coulomb[:, :, lower] = kernel
    coulomb[:, :, upper] = kernel
    stick_in, left_backward = across(stick_in), across(np.concatenate([c, s], 0))
    high, low = rounded_parts(np.concatenate([c, -s], 1))
    real_backward = np.block([[high, high], [low, np.zeros_like(low)]])
    early_parts = (stick_in, left_backward, real_backward)
    early = np.concatenate([np.pad(x, ((0, 0), (0, 6 * g - x.shape[1]))) for x in early_parts], 0).astype(np.float32)
    return dict(
        forward=down(forward),
        last_backward=down(backward / g**3),
        left_forward=across(np.concatenate([c, -s], 0)),
        left_backward=left_backward,
        early=early,
        stick_out=across(stick_out * g**-1.5),
        coulomb=coulomb.reshape(g * g, LANES),
    )


def split(x):
    high = x.astype(BF16)
    low = (x - high.astype(F32)).astype(BF16)
    return high, low


def stacked(x):
    high, low = split(x)
    return jnp.concatenate([high, low, high], 0)


def dot(a, b):
    return jnp.dot(a, b, preferred_element_type=F32)


def lane_halves(shape):
    return lax.broadcasted_iota(jnp.int32, shape, 1) % LANES < MID


def turned(x):
    return pltpu.roll(x, MID, 1)


def regrouped(a, b):
    low = lane_halves(a.shape)
    return jnp.where(low, a, turned(b)), jnp.where(low, turned(a), b)


def beside(a, b):
    return jnp.concatenate([a, b], 1)


def halves(x):
    return x[:, :LANES], x[:, LANES:]


def left(table, x):
    both = dot(table, stacked(x))
    g = both.shape[0] // 2
    return both[:g], both[g:]


def left_complex(table, a, b):
    cos, sin = left(table, beside(a, b))
    sign = jnp.where(lane_halves((1, LANES)), -1.0, 1.0)
    return [p + turned(q) * sign for p, q in zip(halves(cos), halves(sin))]


def right(x, table):
    both = dot(beside(*split(x)), table)
    width = both.shape[1] // 2
    return both[:, :width] + both[:, width:]


def strided(ref, first, g):
    return ref[pl.ds(first, g, stride=g), :]


def slab_rows(index, g, count=1):
    return pl.ds(index * g, count * g)


def one_hot(index, wanted):
    return jnp.where(index == wanted, jnp.asarray(1, BF16), jnp.asarray(0, BF16))


def send_kernel(g, sticks_ref, columns_ref, *refs):
    block_refs, (row_ref, sems, row_sem) = refs[:-3], refs[-3:]
    own = lax.axis_index("stick")
    row_copy = pltpu.make_async_copy(columns_ref, row_ref, row_sem)
    row_copy.start()
    copies = [
        pltpu.make_async_copy(sticks_ref.at[own ^ d], ref.at[pl.ds(0, 2 * g)], sems.at[d])
        for d, ref in enumerate(block_refs)
    ]
    for copy in copies:
        copy.start()
    row_copy.wait()
    columns = jnp.broadcast_to(row_ref[...].astype(F32), (8, LANES))
    for ref in block_refs:
        ref[2 * g :, :] = columns
    for copy in copies:
        copy.wait()


def early_kernel(g, own_ref, tables_ref, staged_ref, stick_in_ref, left_ref, real_ref):
    staged_ref[...] = own_ref[...]
    first = 0
    for ref in (stick_in_ref, left_ref, real_ref):
        ref[...] = tables_ref[first : first + ref.shape[0], : ref.shape[1]].astype(BF16)
        first += ref.shape[0]


def place_kernel(order, *refs):
    own = lax.axis_index("stick")
    out_ref = refs[-1]
    for d, block_ref in zip(order, refs[:-1]):
        out_ref[own ^ d] = block_ref[...]


def store(ref, first, slabs):
    g = slabs[0].shape[0]
    for k, slab in enumerate(slabs):
        ref[slab_rows(first + k, g), :] = slab


def relay_kernel(g, *refs):
    blocks, (coefficients_ref, columns_ref) = refs[:-2], refs[-2:]
    for k, ref in enumerate(blocks):
        coefficients_ref[k * 2 * g : (k + 1) * 2 * g, :] = ref[: 2 * g, :]
        columns_ref[:, k * LANES : (k + 1) * LANES] = ref[2 * g :, :]


def placed(g, blocks_ref, columns_ref, stick_in_ref):
    columns = columns_ref[:1, :].astype(jnp.int32)
    stick_in = stick_in_ref[...]
    blocks = [blocks_ref[k : k + 2 * g, :] for k in range(0, blocks_ref.shape[0], 2 * g)]
    sticks = []
    for k in range(0, len(blocks), 2):
        sticks.append(beside(*split(dot(stick_in, stacked(beside(blocks[k], blocks[k + 1]))).T)))
    sticks = jnp.concatenate(sticks, 0)
    rows = g * g // 2
    index = lax.broadcasted_iota(jnp.int16, (rows, columns.shape[1]), 0)
    for first in (0, rows):
        both = dot(one_hot(index, (columns - first).astype(jnp.int16)), sticks)
        yield first, both[:, :LANES] + both[:, LANES:]


def place_sticks_kernel(g, blocks_ref, columns_ref, stick_in_ref, grid_ref):
    for first, part in placed(g, blocks_ref, columns_ref, stick_in_ref):
        grid_ref[first : first + part.shape[0], :] = part


def field_kernel(g, grid_ref, blocks_ref, columns_ref, stick_in_ref, left_ref, real_ref, phi_ref, work_a):
    backward = left_ref[...]
    half = g // 2
    for first, part in placed(g, blocks_ref, columns_ref, stick_in_ref):
        part = part + grid_ref[first : first + part.shape[0], :]
        for k in range(0, half, 2):
            slabs = left_complex(backward, part[k * g : (k + 1) * g], part[(k + 1) * g : (k + 2) * g])
            store(work_a, first // g + k, slabs)

    for y in range(0, half, 2):
        real, imag = zip(*[regrouped(strided(work_a, j, g), strided(work_a, j + half, g)) for j in (y, y + 1)])
        parts = [split(beside(*real)), split(beside(*imag))]
        both = dot(real_ref[...], jnp.concatenate([x[k] for k in range(2) for x in parts], 0))
        store(phi_ref, y, halves(both[:g] + both[g:]))


def pick_kernel(g, columns_ref, hot_ref):
    for k in range(0, columns_ref.shape[1], LANES):
        block = columns_ref[:, k : k + LANES]
        wanted = jnp.concatenate([block] * (LANES // block.shape[0]), 0).T.astype(jnp.int32)
        for c in range(0, hot_ref.shape[1], LANES):
            index = lax.broadcasted_iota(jnp.int16, (LANES, LANES), 1)
            hot_ref[k : k + LANES, c : c + LANES] = one_hot(index, (wanted - c).astype(jnp.int16))


def potentials(g, phi_ref, first_ref, second_ref, tables, work_a, work_b, emit, last=PAIRS):
    forward, last_backward, left_forward, left_backward = [ref[...].astype(BF16) for ref in tables[:4]]
    coulomb_ref = tables[4]
    half = g // 2
    for start in range(0, half, PAIRS):
        rows = slab_rows(start, g, PAIRS)
        phi = phi_ref[rows, :]
        lower, upper = regrouped(phi * first_ref[rows, :], phi * second_ref[rows, :])
        spectrum = right(jnp.concatenate([lower, upper], 0), forward)
        for k in range(PAIRS):
            a, b = left_complex(left_forward, *(spectrum[j * g : (j + 1) * g] for j in (k, k + PAIRS)))
            store(work_a, start + k, [a])
            store(work_a, start + k + half, [b])

    for kx in range(0, g, 2):
        slabs = left_complex(left_forward, strided(work_a, kx, g), strided(work_a, kx + 1, g))
        slabs = [slab * coulomb_ref[slab_rows(kx + j, g), :] for j, slab in enumerate(slabs)]
        store(work_b, kx, left_complex(left_backward, *slabs))

    for start in range(0, half, last):
        lower, upper = [], []
        for z in range(start, start + last):
            a, b = left_complex(left_backward, strided(work_b, z, g), strided(work_b, z + half, g))
            lower.append(a)
            upper.append(b)
        out = right(jnp.concatenate(lower + upper, 0), last_backward)
        emit(start, *regrouped(out[: last * g], out[last * g :]))


def near_kernel(g, phi_ref, other_ref, *refs):
    tables, (sum_ref, work_a, work_b) = refs[:5], refs[5:]

    def emit(start, own, other):
        rows = slab_rows(start, g, PAIRS)
        sum_ref[rows, :] = own * phi_ref[rows, :] + other * other_ref[rows, :]

    potentials(g, phi_ref, phi_ref, other_ref, tables, work_a, work_b, emit)


def middle_kernel(g, phi_ref, first_ref, second_ref, before_ref, *refs):
    tables, (sum_ref, work_a, work_b) = refs[:5], refs[5:]

    def emit(start, first, second):
        rows = slab_rows(start, g, PAIRS)
        sum_ref[rows, :] = before_ref[rows, :] + first * first_ref[rows, :] + second * second_ref[rows, :]

    potentials(g, phi_ref, first_ref, second_ref, tables, work_a, work_b, emit)


def far_kernel(g, weights, phi_ref, first_ref, second_ref, before_ref, hot_ref, last_hot_ref, stick_out_ref, *refs):
    tables, out_refs = refs[:5], refs[5:-3]
    work_a, work_b, picked_ref = refs[-3:]
    forward = tables[2][...].astype(BF16)
    half = g // 2

    def emit(start, first, second):
        rows = slab_rows(start, g, half)
        total = before_ref[rows, :] + weights[0] * (first * first_ref[rows, :])
        total = total + weights[1] * (second * second_ref[rows, :])
        for k in range(0, half, 2):
            cos, sin = left(forward, beside(total[k * g : (k + 1) * g], total[(k + 1) * g : (k + 2) * g]))
            for j, (real, imag) in enumerate(zip(halves(cos), halves(sin))):
                lower, upper = regrouped(real, imag)
                store(work_a, start + k + j, [lower])
                store(work_a, start + k + j + half, [upper])

    potentials(g, phi_ref, first_ref, second_ref, tables, work_a, work_b, emit, half)

    step = g // 3
    for first in range(0, g, step):
        slabs = []
        for kx in range(first, first + step, 2):
            slabs += left_complex(forward, strided(work_a, kx, g), strided(work_a, kx + 1, g))
        spectrum = beside(*split(jnp.concatenate(slabs, 0)))
        start = 0
        for ref in (hot_ref, last_hot_ref):
            both = dot(ref[:, first * g : (first + step) * g], spectrum)
            both = both[:, :LANES] + both[:, LANES:]
            rows = slice(start, start + ref.shape[0])
            picked_ref[rows, :] = both if first == 0 else picked_ref[rows, :] + both
            start += ref.shape[0]

    stick_out = stick_out_ref[...].astype(BF16)
    for k in range(0, len(out_refs), 2):
        lined = beside(*[picked_ref[j * LANES : (j + 1) * LANES, :].T for j in (k, k + 1)])
        out_refs[k][...], out_refs[k + 1][...] = halves(dot(stick_out, stacked(lined)))


def call(kernel, out_shapes, scratch, flops, *operands, space=pltpu.VMEM, out_space=pltpu.VMEM, grant=40):
    out_spec = pl.BlockSpec(memory_space=out_space)
    return pl.pallas_call(
        kernel,
        out_shape=out_shapes,
        in_specs=[pl.BlockSpec(memory_space=space)] * len(operands),
        out_specs=jax.tree.map(lambda _: out_spec, out_shapes),
        scratch_shapes=scratch,
        compiler_params=pltpu.CompilerParams(vmem_limit_bytes=grant * 2**20),
        cost_estimate=pl.CostEstimate(flops=flops, bytes_accessed=flops, transcendentals=0),
    )(*operands)


def after(x, *others):
    return lax.optimization_barrier((x, *others))[0]


def exchanged(blocks, order, before):
    owners = len(blocks)
    moved = [blocks[0]] + [None] * (owners - 1)
    for d in order:
        others = [moved[x] if isinstance(x, int) else x for x in before.get(d, ())]
        block = after(blocks[d], *others) if others else blocks[d]
        moved[d] = lax.ppermute(block, "stick", [(i, i ^ d) for i in range(owners)])
    return moved


def on_device(sticks, stick_columns):
    g = sticks.shape[1] // 2
    slots = stick_columns.shape[0]
    owners = lax.axis_size("stick")
    groups = lax.axis_size("band")
    t = {name: jnp.asarray(value) for name, value in make_tables(g).items()}
    rows = g * g
    field = jax.ShapeDtypeStruct((rows // 2, LANES), F32)
    work = pltpu.VMEM((rows, LANES), F32)
    pot_flops = 1

    def shifted(x, distance):
        return lax.ppermute(x, "band", [(i, (i - distance) % groups) for i in range(groups)])

    def swapped(x):
        return lax.ppermute(x, "band", [(i, i ^ 1) for i in range(groups)])

    sent = call(
        functools.partial(send_kernel, g),
        [jax.ShapeDtypeStruct((2 * g + 8, slots), F32)] * owners,
        [
            pltpu.VMEM((1, slots), jnp.int32),
            pltpu.SemaphoreType.DMA((owners,)),
            pltpu.SemaphoreType.DMA,
        ],
        1,
        sticks,
        stick_columns[None, :],
        space=pltpu.HBM,
        grant=SEND_GRANT,
    )
    shapes = [(2 * g + 8, slots), (LANES, 6 * g), (2 * g, 3 * g), (2 * g, 4 * g)]
    staged, *first_tables = call(
        functools.partial(early_kernel, g),
        [jax.ShapeDtypeStruct(shape, kind) for shape, kind in zip(shapes, (F32, BF16, BF16, BF16))],
        [],
        1,
        sent[0],
        after(t["early"], sent[0]),
    )
    half = owners // 2
    distant, close = list(range(half, owners)), list(range(1, half))
    mixed = [distant[0]] + [d for pair in zip(close, distant[1:]) for d in pair]
    before = {mixed[k]: (mixed[k - 3 - k % 2],) for k in range(WINDOW, len(mixed))}
    last = mixed[WINDOW]
    received = exchanged(sent, mixed, {d: (half, staged, *first_tables) if d == last else (half,) for d in before})
    received[0] = staged
    cut = owners * 3 // 4
    order = [0] + mixed
    order = order[:cut] + order[:cut - 1:-1]
    stick_in, *field_tables = first_tables

    def relayed(part):
        shapes = [(len(part) * 2 * g, slots), (8, len(part) * slots)]
        shapes = [jax.ShapeDtypeStruct(shape, F32) for shape in shapes]
        return call(functools.partial(relay_kernel, g), shapes, [], 1, *[received[d] for d in part])

    def on_grid(blocks, flops=1):
        grid = jax.ShapeDtypeStruct((rows, LANES), F32)
        return call(functools.partial(place_sticks_kernel, g), grid, [], flops, blocks, columns[0], stick_in)

    def orbital(grid, rest):
        operands = (grid, rest, columns[1], stick_in, *field_tables)
        return call(functools.partial(field_kernel, g), field, [work], 1, *operands)

    first_blocks, first_columns = relayed(order[:cut])
    columns = [first_columns]
    own_grid = on_grid(first_blocks, 5 * 10**9)

    def hot_rows(columns):
        shape = jax.ShapeDtypeStruct((columns.shape[1], rows), BF16)
        return call(functools.partial(pick_kernel, g), shape, [], 1, columns)

    hot = [hot_rows(first_columns)]
    received[order[cut]] = after(received[order[cut]], own_grid, *hot)
    last_blocks, last_columns = relayed(order[cut:])
    columns.append(last_columns)
    hot.append(hot_rows(last_columns))
    phi = orbital(own_grid, last_blocks)
    near = swapped(phi)
    pot_tables = [t["forward"], t["last_backward"], t["left_forward"], t["left_backward"], t["coulomb"]]

    def potential_sum(kernel, *operands):
        return call(functools.partial(kernel, g), field, [work, work], pot_flops, phi, *operands, *pot_tables)

    distances = (HALF,) if groups == 2 * HALF else (HALF, -HALF)
    fields = [orbital(on_grid(shifted(first_blocks, d)), shifted(last_blocks, d)) for d in distances]
    total = potential_sum(near_kernel, after(near, *fields))
    if groups == 2 * HALF:
        weights = (2.0, 1.0)
        first, second = fields[0], swapped(fields[0])
    else:
        weights = (1.0, 0.0)
        odd = lax.axis_index("band") % 2 == 1
        first = second = swapped(jnp.where(odd, fields[1], fields[0]))
        total = potential_sum(middle_kernel, *fields, total)
    result = call(
        functools.partial(far_kernel, g, weights),
        [jax.ShapeDtypeStruct((2 * g, slots), F32)] * owners,
        [work, work, pltpu.VMEM((owners * slots, LANES), F32)],
        pot_flops,
        phi,
        first,
        second,
        total,
        *hot,
        t["stick_out"],
        *pot_tables,
    )
    result = [result[order.index(d)] for d in range(owners)]
    result = exchanged(result, mixed, {d: (half,) for d in before})
    out_order = order
    return call(
        functools.partial(place_kernel, out_order),
        jax.ShapeDtypeStruct(sticks.shape, F32),
        [],
        1,
        *[result[d] for d in out_order],
    )


def solution(mesh):
    return jax.shard_map(
        on_device,
        mesh=mesh,
        in_specs=(P("band", None, "stick"), P("stick")),
        out_specs=P("band", None, "stick"),
        check_vma=False,
    )
```
